32 devices in a mesh: seq: 8 (over y, x, core), head: 4 (over z).
Axes of the slice: x: 2, y: 2, z: 4, core: 2. Of those that a mesh axis runs over, the one named last changes fastest.
Arguments:
- tokens: bfloat16 [4096, 2, 2048], P(('seq', 'head')), may hold values from -6 to 6
- cotangent: bfloat16 [4096, 2, 2048], P(('seq', 'head')), may hold values from -6 to 6
- lengths: int32 [2], replicated, may hold values from 1024 to 4096, as said below
- query_weight: bfloat16 [2048, 2048], P(None, 'head'), may hold values from -0.125 to 0.125
- key_weight: bfloat16 [2048, 1024], P(None, 'head'), may hold values from -0.125 to 0.125
- value_weight: bfloat16 [2048, 1024], P(None, 'head'), may hold values from -0.125 to 0.125
- gating_weight: bfloat16 [2048, 2048], P(None, 'head'), may hold values from -0.125 to 0.125
- output_weight: bfloat16 [2048, 2048], P('head'), may hold values from -1.5 to 1.5
- swiglu_gate: bfloat16 [2048, 6144], P(None, 'head'), may hold values from -0.125 to 0.125
- swiglu_lift: bfloat16 [2048, 6144], P(None, 'head'), may hold values from -0.125 to 0.125
- swiglu_down: bfloat16 [6144, 2048], P('head'), may hold values from -0.078125 to 0.078125
- input_gain: float32 [2048], replicated, may hold values from 0.25 to 1.75
- middle_gain: float32 [2048], replicated, may hold values from 0.25 to 1.75
- query_gain: float32 [128], replicated, may hold values from 0.25 to 1.75
- key_gain: float32 [128], replicated, may hold values from 0.25 to 1.75
Outputs:
- output: bfloat16 [4096, 2, 2048], P(('seq', 'head'))
- input_grad: float32 [4096, 2, 2048], P(('seq', 'head'))
- query_weight_grad: float32 [2048, 2048], P(None, 'head')
- key_weight_grad: float32 [2048, 1024], P(None, 'head')
- value_weight_grad: float32 [2048, 1024], P(None, 'head')
- gating_weight_grad: float32 [2048, 2048], P(None, 'head')
- output_weight_grad: float32 [2048, 2048], P('head')
- swiglu_gate_grad: float32 [2048, 6144], P(None, 'head')
- swiglu_lift_grad: float32 [2048, 6144], P(None, 'head')
- swiglu_down_grad: float32 [6144, 2048], P('head')
- input_gain_grad: float32 [2048], P('head')
- middle_gain_grad: float32 [2048], P('head')
- query_gain_grad: float32 [128], P('head')
- key_gain_grad: float32 [128], P('head')
The draws below stay inside these ranges and needn't reach their ends.
Inputs may be any that keep to these rules, and one draw needn't show every extreme that they name: `lengths`: one sequence, chosen by the seed, has exactly 4096 tokens; the others have 4096 // 4 or more.
All inputs are finite; a program needn't handle non-finite values.
Results may differ from the reference program's by a relative error of at most 0.024.
Values may be sent and summed in bfloat16 or wider, within the bound.
A program may use at most 320 MiB of HBM per device.

```python
import math
import jax
import jax.numpy as jnp
from jax import lax

D = 2048
HEADS = 16
KV_HEADS = 8
HD = 128
FF = 6144
SEQS = 2
SEQ_LEN = 4096


def draw_lengths(key, part):
    key = jax.random.fold_in(key, 7)
    key_pick = jax.random.fold_in(key, 1)
    key_chosen = jax.random.fold_in(key, 2)
    raw_picks = jax.random.randint(key_pick, (SEQS,), 1, SEQ_LEN + 1)
    spread = SEQ_LEN // 4 + raw_picks * raw_picks // SEQ_LEN * 3 // 4
    chosen = jax.random.randint(key_chosen, (), 0, SEQS)
    return jnp.where(jnp.arange(SEQS) == chosen, SEQ_LEN, spread).astype(jnp.int32)


def block_levels(stream_key, dims, shards, smallest, largest):
    loudness = 1.0
    for position, blocks in shards:
        steps = jax.random.uniform(jax.random.fold_in(jax.random.fold_in(stream_key, 6), position), (blocks,), jnp.float32, smallest / len(shards), largest / len(shards))
        loudness = loudness * jnp.repeat(jnp.exp(steps), dims[position] // blocks).reshape((-1,) + (1,) * (len(dims) - 1 - position))
    return loudness


def scatter_about(stream_key, extent, deviation, bound, pieces=(), kind=jnp.bfloat16):
    drawn = deviation * jax.random.normal(stream_key, extent, jnp.float32)
    if pieces:
        drawn = drawn * block_levels(stream_key, extent, pieces, -0.22, 0.18)
    return jnp.clip(drawn, -bound, bound).astype(kind)


def setup_inputs(seed: int = 0) -> dict:
    streams_of = jax.random.split(jax.random.key(seed), 16)
    tokens = scatter_about(streams_of[0], (SEQ_LEN, SEQS, D), 1.0, 6.0, ((0, 32),))
    cotangent = scatter_about(streams_of[1], (SEQ_LEN, SEQS, D), 1.0, 6.0, ((0, 32),))
    lengths = draw_lengths(jax.random.fold_in(streams_of[15], 71), 0)
    query_weight = scatter_about(streams_of[3], (D, HEADS * HD), D ** -0.5, 0.125, ((1, 4),))
    key_weight = scatter_about(streams_of[4], (D, KV_HEADS * HD), D ** -0.5, 0.125, ((1, 4),))
    value_weight = scatter_about(streams_of[5], (D, KV_HEADS * HD), D ** -0.5, 0.125, ((1, 4),))
    gating_weight = scatter_about(streams_of[6], (D, HEADS * HD), D ** -0.5, 0.125, ((1, 4),))
    output_weight = scatter_about(streams_of[7], (HEADS * HD, D), 16 ** -0.5, 1.5, ((0, 4),))
    swiglu_gate = scatter_about(streams_of[8], (D, FF), D ** -0.5, 0.125, ((1, 4),))
    swiglu_lift = scatter_about(streams_of[9], (D, FF), D ** -0.5, 0.125, ((1, 4),))
    swiglu_down = scatter_about(streams_of[10], (FF, D), FF ** -0.5, 0.078125, ((0, 4),))
    input_gain = jnp.clip(1.0 + 0.15 * jax.random.normal(streams_of[11], (D,), jnp.float32), 0.25, 1.75)
    middle_gain = jnp.clip(1.0 + 0.15 * jax.random.normal(streams_of[12], (D,), jnp.float32), 0.25, 1.75)
    query_gain = jnp.clip(1.0 + 0.15 * jax.random.normal(streams_of[13], (HD,), jnp.float32), 0.25, 1.75)
    key_gain = jnp.clip(1.0 + 0.15 * jax.random.normal(streams_of[14], (HD,), jnp.float32), 0.25, 1.75)
    return dict(tokens=tokens, cotangent=cotangent, lengths=lengths, query_weight=query_weight, key_weight=key_weight, value_weight=value_weight, gating_weight=gating_weight, output_weight=output_weight, swiglu_gate=swiglu_gate, swiglu_lift=swiglu_lift, swiglu_down=swiglu_down, input_gain=input_gain, middle_gain=middle_gain, query_gain=query_gain, key_gain=key_gain)


EPS = 1e-06
THETA = 1000000.0

@jax.custom_vjp
def low(v):
    return lax.optimization_barrier(v.astype(jnp.bfloat16)).astype(jnp.float32)

@jax.custom_vjp
def low_back(v):
    return v

def low_keep(v):
    return (low(v), None)

def low_pass(kept, grad):
    return (grad,)

def back_keep(v):
    return (v, None)

def back_low(kept, grad):
    return (low(grad),)
low.defvjp(low_keep, low_pass)
low_back.defvjp(back_keep, back_low)

def product(left, right):
    return jnp.dot(left, right, precision=lax.Precision.HIGHEST, preferred_element_type=jnp.float32)

def norm_rows(values, norm_gain):
    return values * lax.rsqrt(lax.optimization_barrier(jnp.mean(values * values, axis=-1, keepdims=True)) + EPS) * norm_gain

def rotate_norm(raw_part, norm_gain, cosine, sine):
    normed = norm_rows(raw_part, norm_gain)
    half_dim = raw_part.shape[-1] // 2
    first = normed[..., :half_dim]
    second = normed[..., half_dim:]
    return jnp.concatenate([first * cosine - second * sine, second * cosine + first * sine], axis=-1)

def turn_tables(row_count):
    positions = jnp.arange(row_count, dtype=jnp.int32).astype(jnp.float32)
    inverse = THETA ** (-(jnp.arange(HD // 2, dtype=jnp.float32) * 2.0) / HD)
    angles = positions[:, None] * inverse[None, :]
    return (jnp.cos(angles)[:, None, :], jnp.sin(angles)[:, None, :])

def attend(queries, keys_all, value_all, length_now):
    row_count = queries.shape[0]
    group_size = HEADS // KV_HEADS
    block_len = math.gcd(row_count, 512)
    scale_factor = HD ** (-0.5)
    grouped = queries.reshape(row_count // block_len, block_len, KV_HEADS, group_size, HD)
    key_pos = jnp.arange(row_count, dtype=jnp.int32)

    def one_block(block_item):
        query_block, anchor = block_item
        query_pos = anchor + jnp.arange(block_len, dtype=jnp.int32)
        raw_scores = low_back(jnp.einsum('qcgd,kcd->cgqk', query_block, keys_all, precision=lax.Precision.HIGHEST, preferred_element_type=jnp.float32))
        allowed = (key_pos[None, :] <= query_pos[:, None]) & (key_pos[None, :] < length_now)
        weights_now = jnp.where(allowed[None, None], jnp.exp(raw_scores * scale_factor), 0.0)
        summed = lax.optimization_barrier(jnp.sum(weights_now, axis=-1))
        unscaled = low_back(jnp.einsum('cgqk,kcd->qcgd', low(weights_now), value_all, precision=lax.Precision.HIGHEST, preferred_element_type=jnp.float32))
        return unscaled * jnp.transpose(1.0 / summed, (2, 0, 1))[..., None]
    anchors = jnp.arange(row_count // block_len, dtype=jnp.int32) * block_len
    result = lax.map(jax.checkpoint(one_block), (grouped, anchors))
    return result.reshape(row_count, HEADS * HD)

def layer_one(inputs, length_now, params):
    query_weight, key_weight, value_weight, gating_weight, output_weight, swiglu_gate, swiglu_lift, swiglu_down, input_gain, middle_gain, query_gain, key_gain = params
    row_count = inputs.shape[0]
    cosine, sine = turn_tables(row_count)
    valid = (jnp.arange(row_count, dtype=jnp.int32) < length_now).astype(jnp.float32)[:, None]
    normed = low(norm_rows(inputs, input_gain))
    query_raw = low_back(product(normed, query_weight)).reshape(row_count, HEADS, HD)
    key_raw = low_back(product(normed, key_weight)).reshape(row_count, KV_HEADS, HD)
    value_all = low(low_back(product(normed, value_weight))).reshape(row_count, KV_HEADS, HD)
    gate_raw = low_back(product(normed, gating_weight))
    queries = low(rotate_norm(query_raw, query_gain, cosine, sine))
    keys_all = low(rotate_norm(key_raw, key_gain, cosine, sine))
    attended = attend(queries, keys_all, value_all, length_now)
    acted = low(attended * jax.nn.sigmoid(gate_raw))
    middle = inputs + low_back(product(acted, output_weight))
    normed_mid = low(norm_rows(low(middle), middle_gain))
    gate_units = low_back(product(normed_mid, swiglu_gate))
    lift_units = low_back(product(normed_mid, swiglu_lift))
    hidden = low(jax.nn.silu(gate_units) * lift_units)
    return valid * (middle + low_back(product(hidden, swiglu_down)))

def reference(tokens, cotangent, lengths, query_weight, key_weight, value_weight, gating_weight, output_weight, swiglu_gate, swiglu_lift, swiglu_down, input_gain, middle_gain, query_gain, key_gain):
    matrices = tuple((weight_now.astype(jnp.float32) for weight_now in (query_weight, key_weight, value_weight, gating_weight, output_weight, swiglu_gate, swiglu_lift, swiglu_down)))
    gains = (input_gain.astype(jnp.float32), middle_gain.astype(jnp.float32), query_gain.astype(jnp.float32), key_gain.astype(jnp.float32))
    inputs = jnp.transpose(tokens.astype(jnp.float32), (1, 0, 2))

    def forward(inputs_now, *params):

        def one_sequence(seq_item):
            return layer_one(seq_item[0], seq_item[1], params)
        return lax.map(jax.checkpoint(one_sequence), (inputs_now, lengths))
    result, pull_back = jax.vjp(forward, inputs, *matrices + gains)
    grads = pull_back(jnp.transpose(cotangent.astype(jnp.float32), (1, 0, 2)))
    output = jnp.transpose(result, (1, 0, 2)).astype(jnp.bfloat16)
    input_grad = jnp.transpose(grads[0], (1, 0, 2))
    return (output, input_grad, grads[1], grads[2], grads[3], grads[4], grads[5], grads[6], grads[7], grads[8], grads[9], grads[10], grads[11], grads[12])
```

```python
import functools

import jax
import jax.numpy as jnp
from jax import lax
from jax.experimental import pallas as pl
from jax.experimental.pallas import tpu as pltpu
from jax.sharding import PartitionSpec as P

EPS = 1e-06
THETA = 1000000.0
LOG2E = 1.4426950408889634
VMEM_LIMIT = 58 * 1024 * 1024
LOW = jnp.bfloat16
F32 = jnp.float32


def mm(left, right):
    return jnp.dot(left, right, preferred_element_type=F32)


def mm_t(left, right):
    return lax.dot_general(left, right, (((1,), (1,)), ((), ())), preferred_element_type=F32)


def t_mm(left, right):
    return lax.dot_general(left, right, (((0,), (0,)), ((), ())), preferred_element_type=F32)


def shape_of(rows, columns, kind):
    return jax.ShapeDtypeStruct((rows, columns), kind)


def params(**extra):
    return pltpu.CompilerParams(vmem_limit_bytes=VMEM_LIMIT, **extra)


def cost(flops, moved, exps=0):
    return pl.CostEstimate(flops=int(flops), bytes_accessed=int(moved), transcendentals=int(exps))


WHOLE = pl.BlockSpec(memory_space=pltpu.VMEM)
SCALARS = pl.BlockSpec(memory_space=pltpu.SMEM)


def full_block(array):
    return pl.BlockSpec(array.shape, lambda i: (0,) * len(array.shape))


def inverse_rms(values):
    return lax.rsqrt(jnp.mean(values * values, axis=-1, keepdims=True) + EPS)


def turn(values, cosine, sine):
    return values * cosine + pltpu.roll(values, values.shape[-1] // 2, 1) * sine


def turn_back(grads, cosine, sine):
    return grads * cosine + pltpu.roll(grads * sine, grads.shape[-1] // 2, 1)


def project_kernel(
    head_dim,
    x_ref, gain_ref, cos_ref, sin_ref, qgain_ref, kgain_ref, wq_ref, wk_ref, wv_ref, wg_ref,
    normed_ref, qraw_ref, q_ref, kraw_ref, kv_ref, gate_ref,
):
    x = x_ref[...].astype(F32)
    normed = (x * inverse_rms(x) * gain_ref[...]).astype(LOW)
    normed_ref[...] = normed
    cosine, sine = cos_ref[...], sin_ref[...]
    raw = mm(normed, wk_ref[...])
    kraw_ref[...] = raw
    for h in range(raw.shape[1] // head_dim):
        part = raw[:, h * head_dim : (h + 1) * head_dim]
        part = part * inverse_rms(part) * kgain_ref[...]
        kv_ref[:, h * head_dim : (h + 1) * head_dim] = turn(part, cosine, sine).astype(LOW)
    kv_ref[:, raw.shape[1] :] = mm(normed, wv_ref[...]).astype(LOW)
    raw = mm(normed, wq_ref[...])
    qraw_ref[...] = raw
    for h in range(raw.shape[1] // head_dim):
        part = raw[:, h * head_dim : (h + 1) * head_dim]
        part = part * inverse_rms(part) * qgain_ref[...]
        q_ref[:, h * head_dim : (h + 1) * head_dim] = turn(part, cosine, sine).astype(LOW)
    gate_ref[...] = mm(normed, wg_ref[...])


def project(x, gain, cosine, sine, qgain, kgain, wq, wk, wv, wg):
    rows, model = x.shape
    head_dim = qgain.shape[1]
    tile = min(rows, 256)
    nq, nk = wq.shape[1], wk.shape[1]

    def by_row(columns):
        return pl.BlockSpec((tile, columns), lambda i: (i, 0))

    return pl.pallas_call(
        functools.partial(project_kernel, head_dim),
        grid=(rows // tile,),
        in_specs=[
            by_row(model), full_block(gain), by_row(head_dim), by_row(head_dim),
            full_block(qgain), full_block(kgain),
            full_block(wq), full_block(wk), full_block(wv), full_block(wg),
        ],
        out_specs=[by_row(model), by_row(nq), by_row(nq), by_row(nk), by_row(2 * nk), by_row(nq)],
        out_shape=[
            shape_of(rows, model, LOW), shape_of(rows, nq, F32), shape_of(rows, nq, LOW),
            shape_of(rows, nk, F32), shape_of(rows, 2 * nk, LOW), shape_of(rows, nq, F32),
        ],
        compiler_params=params(),
        cost_estimate=cost(2 * rows * model * 2 * (nq + nk), model * 2 * (nq + nk) * 2),
        name="project",
    )(x, gain, cosine, sine, qgain, kgain, wq, wk, wv, wg)


def live_blocks(place_ref, rows):
    start, length = place_ref[0], place_ref[1]
    whole = jnp.minimum(start // rows, length // rows)
    end = jnp.minimum(start // rows + 1, (length + rows - 1) // rows)
    end = jnp.where(start < length, end, 0)
    return jnp.minimum(whole, end), end


def attend_kernel(
    group, head_dim, place_ref, q_ref, kv_ref, gate_ref, att_ref, acted_ref, inv_ref, acc_ref, sum_ref
):
    rows = q_ref.shape[0]
    heads = q_ref.shape[1] // head_dim
    kv_heads = heads // group
    factor = head_dim ** (-0.5) * LOG2E
    start, length = place_ref[0], place_ref[1]
    acc_ref[...] = jnp.zeros_like(acc_ref)
    sum_ref[...] = jnp.zeros_like(sum_ref)
    whole, end = live_blocks(place_ref, rows)

    def one_block(j, masked):
        span = pl.ds(pl.multiple_of(j * rows, rows), rows)
        if masked:
            key_pos = j * rows + lax.broadcasted_iota(jnp.int32, (rows, rows), 1)
            query_pos = start + lax.broadcasted_iota(jnp.int32, (rows, rows), 0)
            allowed = (key_pos <= query_pos) & (key_pos < length)
        for h in range(heads):
            c = h // group
            keys = kv_ref[span, c * head_dim : (c + 1) * head_dim]
            values = kv_ref[span, (kv_heads + c) * head_dim : (kv_heads + c + 1) * head_dim]
            weights = jnp.exp2(mm_t(q_ref[:, h * head_dim : (h + 1) * head_dim], keys) * factor)
            if masked:
                weights = jnp.where(allowed, weights, 0.0)
            total = weights[:, :128]
            for piece in range(1, rows // 128):
                total = total + weights[:, piece * 128 : (piece + 1) * 128]
            sum_ref[h] = sum_ref[h] + total
            acc_ref[h] = acc_ref[h] + mm(weights.astype(LOW), values)

    def plain(j, carry):
        one_block(j, False)
        return carry

    def edge(j, carry):
        one_block(j, True)
        return carry

    lax.fori_loop(0, whole, plain, 0)
    lax.fori_loop(whole, end, edge, 0)
    lane = lax.broadcasted_iota(jnp.int32, inv_ref.shape, 1)
    kept = jnp.zeros(inv_ref.shape, F32)
    for h in range(heads):
        total = jnp.sum(sum_ref[h], axis=1, keepdims=True)
        inverse = 1.0 / jnp.where(total > 0.0, total, 1.0)
        attended = acc_ref[h] * inverse
        columns = slice(h * head_dim, (h + 1) * head_dim)
        att_ref[:, columns] = attended
        acted_ref[:, columns] = (attended * jax.nn.sigmoid(gate_ref[:, columns])).astype(LOW)
        kept = jnp.where(lane == h, inverse, kept)
    inv_ref[...] = kept


def attend(place, q, kv, gate, group, head_dim):
    rows, width = q.shape
    heads = width // head_dim
    return pl.pallas_call(
        functools.partial(attend_kernel, group, head_dim),
        in_specs=[SCALARS, WHOLE, WHOLE, WHOLE],
        out_specs=[WHOLE, WHOLE, WHOLE],
        out_shape=[shape_of(rows, width, F32), shape_of(rows, width, LOW), shape_of(rows, 128, F32)],
        scratch_shapes=[
            pltpu.VMEM((heads, rows, head_dim), F32),
            pltpu.VMEM((heads, rows, 128), F32),
        ],
        compiler_params=params(),
        cost_estimate=cost(4 * rows * kv.shape[0] * width, kv.size * 2, rows * kv.shape[0] * heads),
        name="attend",
    )(place, q, kv, gate)


def attend_back_kernel(
    group, head_dim,
    place_ref, q_ref, kv_ref, r_ref, wo_ref, att_ref, gate_ref, inv_ref,
    dq_ref, dkv_ref, dgate_ref,
    scaled_ref, corr_ref, acc_ref,
):
    rows = q_ref.shape[0]
    heads = q_ref.shape[1] // head_dim
    kv_heads = heads // group
    scale = head_dim ** (-0.5)
    start, length = place_ref[0], place_ref[1]
    acted_grad = mm_t(r_ref[...], wo_ref[...])
    lane = lax.broadcasted_iota(jnp.int32, inv_ref.shape, 1)
    kept = jnp.zeros(inv_ref.shape, F32)
    for h in range(heads):
        columns = slice(h * head_dim, (h + 1) * head_dim)
        sigmoid = jax.nn.sigmoid(gate_ref[:, columns])
        attended = att_ref[:, columns]
        grad = acted_grad[:, columns]
        dgate_ref[:, columns] = (grad * attended * sigmoid * (1.0 - sigmoid)).astype(LOW)
        grad = grad * sigmoid
        inverse = inv_ref[:, h : h + 1]
        scaled_ref[:, columns] = (grad * inverse).astype(LOW)
        kept = jnp.where(
            lane == h, jnp.sum(grad * attended, axis=1, keepdims=True) * inverse, kept
        )
    corr_ref[...] = kept.T
    acc_ref[...] = jnp.zeros_like(acc_ref)
    whole, end = live_blocks(place_ref, rows)

    def one_block(j, masked):
        span = pl.ds(pl.multiple_of(j * rows, rows), rows)
        if masked:
            key_pos = j * rows + lax.broadcasted_iota(jnp.int32, (rows, rows), 0)
            query_pos = start + lax.broadcasted_iota(jnp.int32, (rows, rows), 1)
            allowed = (key_pos <= query_pos) & (key_pos < length)
        for c in range(kv_heads):
            key_columns = slice(c * head_dim, (c + 1) * head_dim)
            value_columns = slice((kv_heads + c) * head_dim, (kv_heads + c + 1) * head_dim)
            keys = kv_ref[span, key_columns]
            values = kv_ref[span, value_columns]
            dk = jnp.zeros((rows, head_dim), F32)
            dv = jnp.zeros((rows, head_dim), F32)
            for h in range(c * group, (c + 1) * group):
                columns = slice(h * head_dim, (h + 1) * head_dim)
                queries = q_ref[:, columns]
                scaled = scaled_ref[:, columns]
                weights = jnp.exp2(mm_t(keys, queries) * (scale * LOG2E))
                if masked:
                    weights = jnp.where(allowed, weights, 0.0)
                dv = dv + mm(weights.astype(LOW), scaled)
                score = (weights * (mm_t(values, scaled) - corr_ref[h : h + 1, :])).astype(LOW)
                dk = dk + mm(score, queries)
                acc_ref[h] = acc_ref[h] + t_mm(score, keys)
            dkv_ref[span, key_columns] = (dk * scale).astype(LOW)
            dkv_ref[span, value_columns] = dv.astype(LOW)

    def plain(j, carry):
        one_block(j, False)
        return carry

    def edge(j, carry):
        one_block(j, True)
        return carry

    def empty(j, carry):
        span = pl.ds(pl.multiple_of(j * rows, rows), rows)
        dkv_ref[span, :] = jnp.zeros((rows, dkv_ref.shape[1]), LOW)
        return carry

    lax.fori_loop(0, whole, plain, 0)
    lax.fori_loop(whole, end, edge, 0)
    lax.fori_loop(end, dkv_ref.shape[0] // rows, empty, 0)
    for h in range(heads):
        dq_ref[:, h * head_dim : (h + 1) * head_dim] = acc_ref[h] * scale


def attend_back(place, q, kv, r, wo, att, gate, inv, group, head_dim):
    rows, width = q.shape
    heads = width // head_dim
    return pl.pallas_call(
        functools.partial(attend_back_kernel, group, head_dim),
        in_specs=[SCALARS] + [WHOLE] * 7,
        out_specs=[WHOLE] * 3,
        out_shape=[
            shape_of(rows, width, F32), shape_of(kv.shape[0], kv.shape[1], LOW), shape_of(rows, width, LOW)
        ],
        scratch_shapes=[
            pltpu.VMEM((rows, width), LOW),
            pltpu.VMEM((128, rows), F32),
            pltpu.VMEM((heads, rows, head_dim), F32),
        ],
        compiler_params=params(),
        cost_estimate=cost(10 * rows * kv.shape[0] * width, kv.size * 4, rows * kv.shape[0] * heads),
        name="attend_back",
    )(place, q, kv, r, wo, att, gate, inv)


def units_kernel(
    mid_ref, masked_ref, gain_ref, wg_ref, wl_ref, wd_ref,
    normed_ref, hidden_ref, dg_ref, dl_ref, dn_ref, dgain_ref,
    acc_ref,
):
    step = pl.program_id(0)

    @pl.when(step == 0)
    def _():
        x = mid_ref[...].astype(F32)
        normed_ref[...] = (x * inverse_rms(x) * gain_ref[...]).astype(LOW)

    normed = normed_ref[...]
    gate = mm(normed, wg_ref[...])
    lift = mm(normed, wl_ref[...])
    grad = mm_t(masked_ref[...], wd_ref[...])
    sigmoid = jax.nn.sigmoid(gate)
    silu = gate * sigmoid
    hidden_ref[...] = (silu * lift).astype(LOW)
    lift_grad = (grad * silu).astype(LOW)
    gate_grad = (grad * lift * (sigmoid + silu * (1.0 - sigmoid))).astype(LOW)
    dg_ref[...] = gate_grad
    dl_ref[...] = lift_grad
    part = mm_t(gate_grad, wg_ref[...]) + mm_t(lift_grad, wl_ref[...])

    @pl.when(step == 0)
    def _():
        acc_ref[...] = part

    @pl.when(step > 0)
    def _():
        acc_ref[...] = acc_ref[...] + part

    @pl.when(step == pl.num_programs(0) - 1)
    def _():
        total = acc_ref[...]
        dn_ref[...] = total.astype(LOW)
        x = mid_ref[...].astype(F32)
        dgain_ref[...] = jnp.sum(total * x * inverse_rms(x), axis=0, keepdims=True)


def units(mid, masked, gain, wg, wl, wd):
    rows, model = mid.shape
    hidden = wg.shape[1]
    tile = 256
    whole = pl.BlockSpec((rows, model), lambda i: (0, 0))
    tall = pl.BlockSpec((model, tile), lambda i: (0, i))
    wide = pl.BlockSpec((tile, model), lambda i: (i, 0))
    part = pl.BlockSpec((rows, tile), lambda i: (0, i))
    return pl.pallas_call(
        units_kernel,
        grid=(hidden // tile,),
        in_specs=[whole, whole, full_block(gain), tall, tall, wide],
        out_specs=[whole, part, part, part, whole, pl.BlockSpec((1, model), lambda i: (0, 0))],
        out_shape=[
            shape_of(rows, model, LOW), shape_of(rows, hidden, LOW), shape_of(rows, hidden, LOW),
            shape_of(rows, hidden, LOW), shape_of(rows, model, LOW), shape_of(1, model, F32),
        ],
        scratch_shapes=[pltpu.VMEM((rows, model), F32)],
        compiler_params=params(),
        cost_estimate=cost(10 * rows * model * hidden, 6 * model * hidden),
        name="units",
    )(mid, masked, gain, wg, wl, wd)


def unproject_kernel(
    head_dim,
    x_ref, gain_ref, cos_ref, sin_ref, qgain_ref, kgain_ref, wq_ref, wk_ref, wv_ref, wg_ref,
    dq_ref, qraw_ref, dkv_ref, kraw_ref, dgate_ref,
    dall_ref, dn_ref, dgain_ref, dqgain_ref, dkgain_ref,
):
    step = pl.program_id(0)
    cosine, sine = cos_ref[...], sin_ref[...]
    nq, nk = qraw_ref.shape[1], kraw_ref.shape[1]

    def heads_back(grad_ref, raw_ref, head_gain, count, place):
        gain_total = jnp.zeros((1, head_dim), F32)
        for h in range(count):
            columns = slice(h * head_dim, (h + 1) * head_dim)
            grad = turn_back(grad_ref[:, columns].astype(F32), cosine, sine)
            raw = raw_ref[:, columns]
            inverse = inverse_rms(raw)
            gain_total = gain_total + jnp.sum(grad * raw * inverse, axis=0, keepdims=True)
            grad = grad * head_gain
            mean = jnp.mean(grad * raw, axis=-1, keepdims=True)
            grad = inverse * (grad - raw * (inverse * inverse * mean))
            dall_ref[:, place + h * head_dim : place + (h + 1) * head_dim] = grad.astype(LOW)
        return gain_total

    dqgain = heads_back(dq_ref, qraw_ref, qgain_ref[...], nq // head_dim, 0)
    dkgain = heads_back(dkv_ref, kraw_ref, kgain_ref[...], nk // head_dim, nq)
    dall_ref[:, nq + nk : nq + 2 * nk] = dkv_ref[:, nk:]
    dall_ref[:, nq + 2 * nk :] = dgate_ref[...]
    total = (
        mm_t(dall_ref[:, :nq], wq_ref[...])
        + mm_t(dall_ref[:, nq : nq + nk], wk_ref[...])
        + mm_t(dall_ref[:, nq + nk : nq + 2 * nk], wv_ref[...])
        + mm_t(dall_ref[:, nq + 2 * nk :], wg_ref[...])
    )
    dn_ref[...] = total.astype(LOW)
    x = x_ref[...].astype(F32)
    dgain = jnp.sum(total * x * inverse_rms(x), axis=0, keepdims=True)

    @pl.when(step == 0)
    def _():
        dgain_ref[...] = dgain
        dqgain_ref[...] = dqgain
        dkgain_ref[...] = dkgain

    @pl.when(step > 0)
    def _():
        dgain_ref[...] = dgain_ref[...] + dgain
        dqgain_ref[...] = dqgain_ref[...] + dqgain
        dkgain_ref[...] = dkgain_ref[...] + dkgain


def unproject(x, gain, cosine, sine, qgain, kgain, wq, wk, wv, wg, dq, qraw, dkv, kraw, dgate):
    rows, model = x.shape
    head_dim = qgain.shape[1]
    tile = min(rows, 256)
    nq, nk = wq.shape[1], wk.shape[1]

    def by_row(columns):
        return pl.BlockSpec((tile, columns), lambda i: (i, 0))

    def line(columns):
        return pl.BlockSpec((1, columns), lambda i: (0, 0))

    return pl.pallas_call(
        functools.partial(unproject_kernel, head_dim),
        grid=(rows // tile,),
        in_specs=[
            by_row(model), full_block(gain), by_row(head_dim), by_row(head_dim),
            full_block(qgain), full_block(kgain),
            full_block(wq), full_block(wk), full_block(wv), full_block(wg),
            by_row(nq), by_row(nq), by_row(2 * nk), by_row(nk), by_row(nq),
        ],
        out_specs=[by_row(2 * nq + 2 * nk), by_row(model), line(model), line(head_dim), line(head_dim)],
        out_shape=[
            shape_of(rows, 2 * nq + 2 * nk, LOW), shape_of(rows, model, LOW),
            shape_of(1, model, F32), shape_of(1, head_dim, F32), shape_of(1, head_dim, F32),
        ],
        compiler_params=params(),
        cost_estimate=cost(2 * rows * model * 2 * (nq + nk), model * 2 * (nq + nk) * 2),
        name="unproject",
    )(x, gain, cosine, sine, qgain, kgain, wq, wk, wv, wg, dq, qraw, dkv, kraw, dgate)


def turn_tables(positions, head_dim):
    half_dim = head_dim // 2
    inverse = THETA ** (-(jnp.arange(half_dim, dtype=F32) * 2.0) / head_dim)
    angles = positions.astype(F32)[:, None] * inverse[None, :]
    cosine, sine = jnp.cos(angles), jnp.sin(angles)
    return jnp.concatenate([cosine, cosine], axis=1), jnp.concatenate([-sine, sine], axis=1)


def norm_back(grad, values, gain):
    inverse = inverse_rms(values)
    grad = grad * gain
    mean = jnp.mean(grad * values, axis=-1, keepdims=True)
    return inverse * (grad - values * (inverse * inverse * mean))


def gather(value, axis):
    return lax.all_gather(value, axis, axis=0, tiled=True)


def scatter(value, axis):
    return lax.psum_scatter(value, axis, scatter_dimension=0, tiled=True)


def on_device(
    tokens, cotangent, lengths,
    query_weight, key_weight, value_weight, gating_weight, output_weight,
    swiglu_gate, swiglu_lift, swiglu_down,
    input_gain, middle_gain, query_gain, key_gain,
):
    block_index = lax.axis_index("seq")
    part_index = lax.axis_index("head")
    parts = lax.axis_size("head")
    local_rows, batch, model = tokens.shape
    head_dim = query_gain.shape[0]
    block_rows = local_rows * parts
    group = query_weight.shape[1] // key_weight.shape[1]
    nq, nk = query_weight.shape[1], key_weight.shape[1]
    query_start = block_index * block_rows
    positions = query_start + jnp.arange(block_rows, dtype=jnp.int32)
    cosine, sine = turn_tables(positions, head_dim)
    gain_in, gain_mid = input_gain[None, :], middle_gain[None, :]
    gain_q, gain_k = query_gain[None, :], key_gain[None, :]
    local_pos = query_start + part_index * local_rows + jnp.arange(local_rows, dtype=jnp.int32)
    seqs = range(batch)
    places = [jnp.stack([query_start, lengths[b]]).astype(jnp.int32) for b in seqs]
    valid = [(local_pos < lengths[b]).astype(F32)[:, None] for b in seqs]
    own = [tokens[:, b, :] for b in seqs]
    own_masked = [valid[b] * cotangent[:, b, :].astype(F32) for b in seqs]

    rows_in = [gather(own[b], "head") for b in seqs]
    projected = [
        project(
            rows_in[b], gain_in, cosine, sine, gain_q, gain_k,
            query_weight, key_weight, value_weight, gating_weight,
        )
        for b in seqs
    ]
    normed, qraw, q, kraw, kv_own, gate = [list(x) for x in zip(*projected)]
    kv = [gather(kv_own[b], "seq") for b in seqs]
    masked = [gather(own_masked[b].astype(LOW), "head") for b in seqs]
    attended = [attend(places[b], q[b], kv[b], gate[b], group, head_dim) for b in seqs]
    att, acted, inv = [list(x) for x in zip(*attended)]
    middle = [
        own[b].astype(F32)
        + scatter(mm(acted[b], output_weight).astype(LOW), "head").astype(F32)
        for b in seqs
    ]
    mid = [gather(middle[b].astype(LOW), "head") for b in seqs]
    forward = [units(mid[b], masked[b], gain_mid, swiglu_gate, swiglu_lift, swiglu_down) for b in seqs]
    normed_mid, hidden, dg, dl, dn_mid, dgain_mid = [list(x) for x in zip(*forward)]
    residual = [
        own_masked[b]
        + norm_back(
            scatter(dn_mid[b], "head").astype(F32), middle[b].astype(LOW).astype(F32), gain_mid
        )
        for b in seqs
    ]
    r = [gather(residual[b].astype(LOW), "head") for b in seqs]

    def both(pair):
        return jnp.concatenate(pair, axis=0)

    normed_mid_all, masked_all = both(normed_mid), both(masked)
    ff_grads = (
        t_mm(normed_mid_all, both(dg)).astype(LOW),
        t_mm(normed_mid_all, both(dl)).astype(LOW),
        t_mm(both(hidden), masked_all).astype(LOW),
    )
    ff_grads = [x.astype(F32) for x in lax.psum(ff_grads, "seq")]
    units_out = [scatter(mm(hidden[b], swiglu_down).astype(LOW), "head").astype(F32) for b in seqs]
    output = jnp.stack(
        [(valid[b] * (middle[b] + units_out[b])).astype(LOW) for b in seqs], axis=1
    )

    back = [
        attend_back(places[b], q[b], kv[b], r[b], output_weight, att[b], gate[b], inv[b], group, head_dim)
        for b in seqs
    ]
    dq, dkv_all, dgate = [list(x) for x in zip(*back)]
    dkv = [scatter(dkv_all[b], "seq") for b in seqs]
    last = [
        unproject(
            rows_in[b], gain_in, cosine, sine, gain_q, gain_k,
            query_weight, key_weight, value_weight, gating_weight,
            dq[b], qraw[b], dkv[b], kraw[b], dgate[b],
        )
        for b in seqs
    ]
    dall, dn_in, dgain_in, dgain_q, dgain_k = [list(x) for x in zip(*last)]
    input_grad = jnp.stack(
        [
            residual[b] + norm_back(scatter(dn_in[b], "head").astype(F32), own[b].astype(F32), gain_in)
            for b in seqs
        ],
        axis=1,
    )
    out_grad = t_mm(both(acted), both(r)).astype(LOW)
    proj_grad = t_mm(both(normed), both(dall)).astype(LOW)
    out_grad = gather(scatter(out_grad, "seq"), "seq").astype(F32)
    proj_grad = gather(scatter(proj_grad, "seq"), "seq")
    gains = jnp.concatenate(
        [sum(dgain_in)[0], sum(dgain_mid)[0], sum(dgain_q)[0], sum(dgain_k)[0]]
    )
    gains = lax.psum(gains, ("seq", "head"))

    def share(start, width):
        piece = width // parts
        return lax.dynamic_slice(gains, (start + part_index * piece,), (piece,))

    return (
        output,
        input_grad,
        proj_grad[:, :nq].astype(F32),
        proj_grad[:, nq : nq + nk].astype(F32),
        proj_grad[:, nq + nk : nq + 2 * nk].astype(F32),
        proj_grad[:, nq + 2 * nk :].astype(F32),
        out_grad,
        ff_grads[0],
        ff_grads[1],
        ff_grads[2],
        share(0, model),
        share(model, model),
        share(2 * model, head_dim),
        share(2 * model + head_dim, head_dim),
    )


def solution(mesh):
    return jax.shard_map(
        on_device,
        mesh=mesh,
        in_specs=(
            P(("seq", "head"), None, None),
            P(("seq", "head"), None, None),
            P(),
            P(None, "head"),
            P(None, "head"),
            P(None, "head"),
            P(None, "head"),
            P("head", None),
            P(None, "head"),
            P(None, "head"),
            P("head", None),
            P(),
            P(),
            P(),
            P(),
        ),
        out_specs=(
            P(("seq", "head"), None, None),
            P(("seq", "head"), None, None),
            P(None, "head"),
            P(None, "head"),
            P(None, "head"),
            P(None, "head"),
            P("head", None),
            P(None, "head"),
            P(None, "head"),
            P("head", None),
            P("head"),
            P("head"),
            P("head"),
            P("head"),
        ),
        check_vma=False,
    )
```

```python
import functools

import jax
import jax.numpy as jnp
from jax import lax
from jax.experimental import pallas as pl
from jax.experimental.pallas import tpu as pltpu
from jax.sharding import PartitionSpec as P

EPS = 1e-06
THETA = 1000000.0
LOG2E = 1.4426950408889634
VMEM_LIMIT = 58 * 1024 * 1024
LOW = jnp.bfloat16
F32 = jnp.float32
MESH = pl.DeviceIdType.MESH


def mm(left, right):
    return jnp.dot(left, right, preferred_element_type=F32)


def mm_t(left, right):
    return lax.dot_general(left, right, (((1,), (1,)), ((), ())), preferred_element_type=F32)


def t_mm(left, right):
    return lax.dot_general(left, right, (((0,), (0,)), ((), ())), preferred_element_type=F32)


def shape_of(rows, columns, kind):
    return jax.ShapeDtypeStruct((rows, columns), kind)


def params(**extra):
    return pltpu.CompilerParams(vmem_limit_bytes=VMEM_LIMIT, **extra)


def takes(microseconds):
    return pl.CostEstimate(
        flops=int(microseconds * 1.15e9), bytes_accessed=int(microseconds * 3.69e6), transcendentals=0
    )


WHOLE = pl.BlockSpec(memory_space=pltpu.VMEM)
SCALARS = pl.BlockSpec(memory_space=pltpu.SMEM)


def full_block(array):
    return pl.BlockSpec(array.shape, lambda i: (0,) * len(array.shape))


def inverse_rms(values):
    return lax.rsqrt(jnp.mean(values * values, axis=-1, keepdims=True) + EPS)


def turn(values, cosine, sine):
    return values * cosine + pltpu.roll(values, values.shape[-1] // 2, 1) * sine


def turn_back(grads, cosine, sine):
    return grads * cosine + pltpu.roll(grads * sine, grads.shape[-1] // 2, 1)


def project_kernel(
    head_dim,
    x_ref, gain_ref, cos_ref, sin_ref, qgain_ref, kgain_ref, wq_ref, wk_ref, wv_ref, wg_ref,
    normed_ref, qraw_ref, q_ref, kraw_ref, kv_ref, gate_ref,
):
    x = x_ref[...].astype(F32)
    normed = (x * inverse_rms(x) * gain_ref[...]).astype(LOW)
    normed_ref[...] = normed
    cosine, sine = cos_ref[...], sin_ref[...]
    raw = mm(normed, wk_ref[...])
    kraw_ref[...] = raw
    for h in range(raw.shape[1] // head_dim):
        part = raw[:, h * head_dim : (h + 1) * head_dim]
        part = part * inverse_rms(part) * kgain_ref[...]
        kv_ref[:, h * head_dim : (h + 1) * head_dim] = turn(part, cosine, sine).astype(LOW)
    kv_ref[:, raw.shape[1] :] = mm(normed, wv_ref[...]).astype(LOW)
    raw = mm(normed, wq_ref[...])
    qraw_ref[...] = raw
    for h in range(raw.shape[1] // head_dim):
        part = raw[:, h * head_dim : (h + 1) * head_dim]
        part = part * inverse_rms(part) * qgain_ref[...]
        q_ref[:, h * head_dim : (h + 1) * head_dim] = turn(part, cosine, sine).astype(LOW)
    gate_ref[...] = mm(normed, wg_ref[...])


def project(x, gain, cosine, sine, qgain, kgain, wq, wk, wv, wg):
    rows, model = x.shape
    head_dim = qgain.shape[1]
    tile = min(rows, 256)
    nq, nk = wq.shape[1], wk.shape[1]

    def by_row(columns):
        return pl.BlockSpec((tile, columns), lambda i: (i, 0))

    return pl.pallas_call(
        functools.partial(project_kernel, head_dim),
        grid=(rows // tile,),
        in_specs=[
            by_row(model), full_block(gain), by_row(head_dim), by_row(head_dim),
            full_block(qgain), full_block(kgain),
            full_block(wq), full_block(wk), full_block(wv), full_block(wg),
        ],
        out_specs=[by_row(model), by_row(nq), by_row(nq), by_row(nk), by_row(2 * nk), by_row(nq)],
        out_shape=[
            shape_of(rows, model, LOW), shape_of(rows, nq, F32), shape_of(rows, nq, LOW),
            shape_of(rows, nk, F32), shape_of(rows, 2 * nk, LOW), shape_of(rows, nq, F32),
        ],
        compiler_params=params(),
        cost_estimate=takes(9),
        name="project",
    )(x, gain, cosine, sine, qgain, kgain, wq, wk, wv, wg)


def live_blocks(place_ref, rows):
    start, length = place_ref[0], place_ref[1]
    whole = jnp.minimum(start // rows, length // rows)
    end = jnp.minimum(start // rows + 1, (length + rows - 1) // rows)
    end = jnp.where(start < length, end, 0)
    return jnp.minimum(whole, end), end


def attend_kernel(
    group, head_dim, place_ref, q_ref, kv_ref, gate_ref, att_ref, acted_ref, inv_ref, acc_ref, sum_ref
):
    rows = q_ref.shape[0]
    heads = q_ref.shape[1] // head_dim
    kv_heads = heads // group
    factor = head_dim ** (-0.5) * LOG2E
    start, length = place_ref[0], place_ref[1]
    acc_ref[...] = jnp.zeros_like(acc_ref)
    sum_ref[...] = jnp.zeros_like(sum_ref)
    whole, end = live_blocks(place_ref, rows)

    def one_block(j, masked):
        span = pl.ds(pl.multiple_of(j * rows, rows), rows)
        if masked:
            key_pos = j * rows + lax.broadcasted_iota(jnp.int32, (rows, rows), 1)
            query_pos = start + lax.broadcasted_iota(jnp.int32, (rows, rows), 0)
            allowed = (key_pos <= query_pos) & (key_pos < length)
        for h in range(heads):
            c = h // group
            keys = kv_ref[span, c * head_dim : (c + 1) * head_dim]
            values = kv_ref[span, (kv_heads + c) * head_dim : (kv_heads + c + 1) * head_dim]
            weights = jnp.exp2(mm_t(q_ref[:, h * head_dim : (h + 1) * head_dim], keys) * factor)
            if masked:
                weights = jnp.where(allowed, weights, 0.0)
            total = weights[:, :128]
            for piece in range(1, rows // 128):
                total = total + weights[:, piece * 128 : (piece + 1) * 128]
            sum_ref[h] = sum_ref[h] + total
            acc_ref[h] = acc_ref[h] + mm(weights.astype(LOW), values)

    def plain(j, carry):
        one_block(j, False)
        return carry

    def edge(j, carry):
        one_block(j, True)
        return carry

    lax.fori_loop(0, whole, plain, 0)
    lax.fori_loop(whole, end, edge, 0)
    lane = lax.broadcasted_iota(jnp.int32, inv_ref.shape, 1)
    kept = jnp.zeros(inv_ref.shape, F32)
    for h in range(heads):
        total = jnp.sum(sum_ref[h], axis=1, keepdims=True)
        inverse = 1.0 / jnp.where(total > 0.0, total, 1.0)
        attended = acc_ref[h] * inverse
        columns = slice(h * head_dim, (h + 1) * head_dim)
        att_ref[:, columns] = attended
        acted_ref[:, columns] = (attended * jax.nn.sigmoid(gate_ref[:, columns])).astype(LOW)
        kept = jnp.where(lane == h, inverse, kept)
    inv_ref[...] = kept


def attend(place, q, kv, gate, group, head_dim):
    rows, width = q.shape
    heads = width // head_dim
    return pl.pallas_call(
        functools.partial(attend_kernel, group, head_dim),
        in_specs=[SCALARS, WHOLE, WHOLE, WHOLE],
        out_specs=[WHOLE, WHOLE, WHOLE],
        out_shape=[shape_of(rows, width, F32), shape_of(rows, width, LOW), shape_of(rows, 128, F32)],
        scratch_shapes=[
            pltpu.VMEM((heads, rows, head_dim), F32),
            pltpu.VMEM((heads, rows, 128), F32),
        ],
        compiler_params=params(),
        cost_estimate=takes(9),
        name="attend",
    )(place, q, kv, gate)


def attend_back_kernel(
    group, head_dim,
    place_ref, q_ref, kv_ref, r_ref, wo_ref, att_ref, gate_ref, inv_ref,
    dq_ref, dkv_ref, dgate_ref,
    scaled_ref, corr_ref, acc_ref,
):
    rows = q_ref.shape[0]
    heads = q_ref.shape[1] // head_dim
    kv_heads = heads // group
    scale = head_dim ** (-0.5)
    start, length = place_ref[0], place_ref[1]
    acted_grad = mm_t(r_ref[...], wo_ref[...])
    lane = lax.broadcasted_iota(jnp.int32, inv_ref.shape, 1)
    kept = jnp.zeros(inv_ref.shape, F32)
    for h in range(heads):
        columns = slice(h * head_dim, (h + 1) * head_dim)
        sigmoid = jax.nn.sigmoid(gate_ref[:, columns])
        attended = att_ref[:, columns]
        grad = acted_grad[:, columns]
        dgate_ref[:, columns] = (grad * attended * sigmoid * (1.0 - sigmoid)).astype(LOW)
        grad = grad * sigmoid
        inverse = inv_ref[:, h : h + 1]
        scaled_ref[:, columns] = (grad * inverse).astype(LOW)
        kept = jnp.where(
            lane == h, jnp.sum(grad * attended, axis=1, keepdims=True) * inverse, kept
        )
    corr_ref[...] = kept.T
    acc_ref[...] = jnp.zeros_like(acc_ref)
    whole, end = live_blocks(place_ref, rows)

    def one_block(j, masked):
        span = pl.ds(pl.multiple_of(j * rows, rows), rows)
        if masked:
            key_pos = j * rows + lax.broadcasted_iota(jnp.int32, (rows, rows), 0)
            query_pos = start + lax.broadcasted_iota(jnp.int32, (rows, rows), 1)
            allowed = (key_pos <= query_pos) & (key_pos < length)
        for c in range(kv_heads):
            key_columns = slice(c * head_dim, (c + 1) * head_dim)
            value_columns = slice((kv_heads + c) * head_dim, (kv_heads + c + 1) * head_dim)
            keys = kv_ref[span, key_columns]
            values = kv_ref[span, value_columns]
            dk = jnp.zeros((rows, head_dim), F32)
            dv = jnp.zeros((rows, head_dim), F32)
            for h in range(c * group, (c + 1) * group):
                columns = slice(h * head_dim, (h + 1) * head_dim)
                queries = q_ref[:, columns]
                scaled = scaled_ref[:, columns]
                weights = jnp.exp2(mm_t(keys, queries) * (scale * LOG2E))
                if masked:
                    weights = jnp.where(allowed, weights, 0.0)
                dv = dv + mm(weights.astype(LOW), scaled)
                score = (weights * (mm_t(values, scaled) - corr_ref[h : h + 1, :])).astype(LOW)
                dk = dk + mm(score, queries)
                acc_ref[h] = acc_ref[h] + t_mm(score, keys)
            dkv_ref[span, key_columns] = (dk * scale).astype(LOW)
            dkv_ref[span, value_columns] = dv.astype(LOW)

    def plain(j, carry):
        one_block(j, False)
        return carry

    def edge(j, carry):
        one_block(j, True)
        return carry

    def empty(j, carry):
        span = pl.ds(pl.multiple_of(j * rows, rows), rows)
        dkv_ref[span, :] = jnp.zeros((rows, dkv_ref.shape[1]), LOW)
        return carry

    lax.fori_loop(0, whole, plain, 0)
    lax.fori_loop(whole, end, edge, 0)
    lax.fori_loop(end, dkv_ref.shape[0] // rows, empty, 0)
    for h in range(heads):
        dq_ref[:, h * head_dim : (h + 1) * head_dim] = acc_ref[h] * scale


def attend_back(place, q, kv, r, wo, att, gate, inv, group, head_dim):
    rows, width = q.shape
    heads = width // head_dim
    return pl.pallas_call(
        functools.partial(attend_back_kernel, group, head_dim),
        in_specs=[SCALARS] + [WHOLE] * 7,
        out_specs=[WHOLE] * 3,
        out_shape=[
            shape_of(rows, width, F32), shape_of(kv.shape[0], kv.shape[1], LOW), shape_of(rows, width, LOW)
        ],
        scratch_shapes=[
            pltpu.VMEM((rows, width), LOW),
            pltpu.VMEM((128, rows), F32),
            pltpu.VMEM((heads, rows, head_dim), F32),
        ],
        compiler_params=params(),
        cost_estimate=takes(20),
        name="attend_back",
    )(place, q, kv, r, wo, att, gate, inv)


def unproject_kernel(
    head_dim,
    x_ref, gain_ref, cos_ref, sin_ref, qgain_ref, kgain_ref, wq_ref, wk_ref, wv_ref, wg_ref,
    dq_ref, qraw_ref, dkv_ref, kraw_ref, dgate_ref,
    dall_ref, dn_ref, dgain_ref, dqgain_ref, dkgain_ref,
):
    step = pl.program_id(0)
    cosine, sine = cos_ref[...], sin_ref[...]
    nq, nk = qraw_ref.shape[1], kraw_ref.shape[1]

    def heads_back(grad_ref, raw_ref, head_gain, count, place):
        gain_total = jnp.zeros((1, head_dim), F32)
        for h in range(count):
            columns = slice(h * head_dim, (h + 1) * head_dim)
            grad = turn_back(grad_ref[:, columns].astype(F32), cosine, sine)
            raw = raw_ref[:, columns]
            inverse = inverse_rms(raw)
            gain_total = gain_total + jnp.sum(grad * raw * inverse, axis=0, keepdims=True)
            grad = grad * head_gain
            mean = jnp.mean(grad * raw, axis=-1, keepdims=True)
            grad = inverse * (grad - raw * (inverse * inverse * mean))
            dall_ref[:, place + h * head_dim : place + (h + 1) * head_dim] = grad.astype(LOW)
        return gain_total

    dqgain = heads_back(dq_ref, qraw_ref, qgain_ref[...], nq // head_dim, 0)
    dkgain = heads_back(dkv_ref, kraw_ref, kgain_ref[...], nk // head_dim, nq)
    dall_ref[:, nq + nk : nq + 2 * nk] = dkv_ref[:, nk:]
    dall_ref[:, nq + 2 * nk :] = dgate_ref[...]
    total = (
        mm_t(dall_ref[:, :nq], wq_ref[...])
        + mm_t(dall_ref[:, nq : nq + nk], wk_ref[...])
        + mm_t(dall_ref[:, nq + nk : nq + 2 * nk], wv_ref[...])
        + mm_t(dall_ref[:, nq + 2 * nk :], wg_ref[...])
    )
    dn_ref[...] = total.astype(LOW)
    x = x_ref[...].astype(F32)
    dgain = jnp.sum(total * x * inverse_rms(x), axis=0, keepdims=True)

    @pl.when(step == 0)
    def _():
        dgain_ref[...] = dgain
        dqgain_ref[...] = dqgain
        dkgain_ref[...] = dkgain

    @pl.when(step > 0)
    def _():
        dgain_ref[...] = dgain_ref[...] + dgain
        dqgain_ref[...] = dqgain_ref[...] + dqgain
        dkgain_ref[...] = dkgain_ref[...] + dkgain


def unproject(x, gain, cosine, sine, qgain, kgain, wq, wk, wv, wg, dq, qraw, dkv, kraw, dgate):
    rows, model = x.shape
    head_dim = qgain.shape[1]
    tile = min(rows, 256)
    nq, nk = wq.shape[1], wk.shape[1]

    def by_row(columns):
        return pl.BlockSpec((tile, columns), lambda i: (i, 0))

    def line(columns):
        return pl.BlockSpec((1, columns), lambda i: (0, 0))

    return pl.pallas_call(
        functools.partial(unproject_kernel, head_dim),
        grid=(rows // tile,),
        in_specs=[
            by_row(model), full_block(gain), by_row(head_dim), by_row(head_dim),
            full_block(qgain), full_block(kgain),
            full_block(wq), full_block(wk), full_block(wv), full_block(wg),
            by_row(nq), by_row(nq), by_row(2 * nk), by_row(nk), by_row(nq),
        ],
        out_specs=[by_row(2 * nq + 2 * nk), by_row(model), line(model), line(head_dim), line(head_dim)],
        out_shape=[
            shape_of(rows, 2 * nq + 2 * nk, LOW), shape_of(rows, model, LOW),
            shape_of(1, model, F32), shape_of(1, head_dim, F32), shape_of(1, head_dim, F32),
        ],
        compiler_params=params(),
        cost_estimate=takes(13),
        name="unproject",
    )(x, gain, cosine, sine, qgain, kgain, wq, wk, wv, wg, dq, qraw, dkv, kraw, dgate)


class Line:
    def __init__(self, pieces, count, part_ref, own_ref, right_ref, left_ref, sems, spread=None):
        self.pieces, self.count = pieces, count
        self.place = lax.axis_index("head")
        self.part_ref, self.own_ref = part_ref, own_ref
        self.right_ref, self.left_ref = right_ref, left_ref
        self.sems = sems
        self.spread = spread

    def barrier(self):
        sem = pltpu.get_barrier_semaphore()
        place, count = self.place, self.count

        @pl.when(place > 0)
        def _():
            pl.semaphore_signal(sem, inc=1, device_id={"head": place - 1}, device_id_type=MESH)

        @pl.when(place < count - 1)
        def _():
            pl.semaphore_signal(sem, inc=1, device_id={"head": place + 1}, device_id_type=MESH)

        inside = (place > 0) & (place < count - 1)

        @pl.when(inside)
        def _():
            pl.semaphore_wait(sem, 2)

        @pl.when(jnp.logical_not(inside))
        def _():
            pl.semaphore_wait(sem, 1)

    def copy(self, ref, send, receive, p, t, step):
        return pltpu.make_async_remote_copy(
            src_ref=ref,
            dst_ref=ref,
            send_sem=self.sems[send].at[p, t],
            recv_sem=self.sems[receive].at[p, t],
            device_id={"head": jnp.clip(self.place + step, 0, self.count - 1)},
            device_id_type=MESH,
        )

    def sum_copy(self, p, t, step):
        ref = self.right_ref if step > 0 else self.left_ref
        base = 0 if step > 0 else 2
        return self.copy(ref.at[p, t], base, base + 1, p, t, step)

    def spread_copy(self, p, t, step):
        return self.copy(self.spread(p, t), 4 if step > 0 else 5, 6, p, t, step)

    def send_sums(self, p, distance):
        place, count = self.place, self.count
        for step, ref in ((1, self.right_ref), (-1, self.left_ref)):
            t = place + step * distance
            first = place == (0 if step > 0 else count - 1)

            @pl.when((t >= 0) & (t < count))
            def _(t=t, step=step, ref=ref, first=first):
                @pl.when(first)
                def _():
                    ref[p, t] = self.part_ref[t].astype(LOW)

                @pl.when(jnp.logical_not(first))
                def _():
                    self.sum_copy(p, t, step).wait_recv()
                    ref[p, t] = (ref[p, t].astype(F32) + self.part_ref[t].astype(F32)).astype(LOW)

                self.sum_copy(p, t, step).start()

    def keep_own(self, p):
        self.own_ref[p] = self.part_ref[self.place].astype(F32)

    def finish_own(self, p):
        place, count = self.place, self.count
        for step, ref, inner in ((1, self.right_ref, place > 0), (-1, self.left_ref, place < count - 1)):

            @pl.when(inner)
            def _(step=step, ref=ref):
                self.sum_copy(p, place, step).wait_recv()
                self.own_ref[p] = self.own_ref[p] + ref[p, place].astype(F32)

    def hand_out(self, p):
        place, count = self.place, self.count

        @pl.when(place < count - 1)
        def _():
            self.spread_copy(p, place, 1).start()

        @pl.when(place > 0)
        def _():
            self.spread_copy(p, place, -1).start()

    def hand_on(self, p, distance):
        place, count = self.place, self.count
        for step, more in ((1, place < count - 1), (-1, place > 0)):
            t = place - step * distance

            @pl.when((t >= 0) & (t < count))
            def _(t=t, step=step, more=more):
                self.spread_copy(p, t, step).wait_recv()

                @pl.when(more)
                def _():
                    self.spread_copy(p, t, step).start()

    def drain(self):
        place, count = self.place, self.count

        def one(p, carry):
            for t in range(count):

                @pl.when(t > place)
                def _(t=t):
                    self.sum_copy(p, t, 1).wait_send()

                @pl.when(t < place)
                def _(t=t):
                    self.sum_copy(p, t, -1).wait_send()

                if self.spread is not None:

                    @pl.when((t <= place) & (place < count - 1))
                    def _(t=t):
                        self.spread_copy(p, t, 1).wait_send()

                    @pl.when((t >= place) & (place > 0))
                    def _(t=t):
                        self.spread_copy(p, t, -1).wait_send()

            return carry

        lax.fori_loop(0, self.pieces, one, 0)


def line_scratch(pieces, count, rows, model, part_kind, spread):
    slots = (pieces, count)
    scratch = [
        pltpu.VMEM((pieces, rows, model), F32),
        pltpu.VMEM((pieces, count, rows, model), LOW),
        pltpu.VMEM((pieces, count, rows, model), LOW),
    ] + [pltpu.SemaphoreType.DMA(slots)] * (7 if spread else 4)
    if part_kind is not None:
        scratch = [pltpu.VMEM((count, rows, model), part_kind)] + scratch
    return scratch


def both_ways(index, limit, body):
    @pl.when((index >= 0) & (index < limit))
    def _():
        body(index)


def middle_kernel(
    pieces, count,
    acted_ref, tok_ref, gain_ref, wo_ref, masked_hbm, wg_hbm, wl_hbm, wd_hbm,
    middle_ref, dgain_ref, normed_hbm, hidden_hbm, dg_hbm, dl_hbm, dn_hbm,
    mid_ref, wg_ref, wl_ref, wd_ref, masked_ref, normed_ref, hidden_ref, dg_ref, dl_ref, dn_ref, acc_ref,
    load_sem, masked_sem, store_sem,
    part_ref, own_ref, right_ref, left_ref, *sems,
):
    rows, model = own_ref.shape[1], own_ref.shape[2]
    tall = count * rows
    hidden = wg_ref.shape[1]
    line = Line(
        pieces, count, part_ref, own_ref, right_ref, left_ref, sems, spread=lambda p, t: mid_ref.at[p, t]
    )
    place = line.place
    loads = [
        pltpu.make_async_copy(source, target, load_sem.at[i])
        for i, (source, target) in enumerate(((wg_hbm, wg_ref), (wl_hbm, wl_ref), (wd_hbm, wd_ref)))
    ]
    line.barrier()
    for load in loads:
        load.start()
    dgain_ref[...] = jnp.zeros_like(dgain_ref)
    tiles = 3
    tile = hidden // tiles

    def masked_copy(p):
        return pltpu.make_async_copy(masked_hbm.at[:, p], masked_ref, masked_sem)

    def stores(p):
        pairs = (
            (normed_ref, normed_hbm), (hidden_ref, hidden_hbm), (dg_ref, dg_hbm), (dl_ref, dl_hbm),
            (dn_ref, dn_hbm),
        )
        return [
            pltpu.make_async_copy(source, target.at[:, p], store_sem.at[i])
            for i, (source, target) in enumerate(pairs)
        ]

    def begin(p):
        acted = acted_ref[p // 2, :, p % 2].reshape(tall, acted_ref.shape[-1])
        part_ref[...] = mm(acted, wo_ref[...]).reshape(count, rows, model)
        line.keep_own(p)

    def own(p):
        line.finish_own(p)
        middle = own_ref[p] + tok_ref[p].astype(F32)
        middle_ref[p] = middle
        mid_ref[p, place] = middle.astype(LOW)
        line.hand_out(p)

    def units_begin(p):
        line.hand_on(p, count - 1)

        @pl.when(p > 0)
        def _():
            for store in stores(p - 1):
                store.wait()

        x = mid_ref[p].reshape(tall, model).astype(F32)
        normed = (x * inverse_rms(x) * gain_ref[...]).astype(LOW)
        normed_ref[...] = normed.reshape(count, rows, model)
        masked_copy(p).wait()

        @pl.when(p == 0)
        def _():
            for load in loads:
                load.wait()

    def units_tile(i):
        span = slice(i * tile, (i + 1) * tile)
        normed = normed_ref[...].reshape(tall, model)
        gate = mm(normed, wg_ref[:, span])
        lift = mm(normed, wl_ref[:, span])
        grad = mm_t(masked_ref[...].reshape(tall, model), wd_ref[span, :])
        sigmoid = jax.nn.sigmoid(gate)
        silu = gate * sigmoid
        lift_grad = (grad * silu).astype(LOW)
        gate_grad = (grad * lift * (sigmoid + silu * (1.0 - sigmoid))).astype(LOW)
        hidden_ref[:, :, span] = (silu * lift).astype(LOW).reshape(count, rows, tile)
        dg_ref[:, :, span] = gate_grad.reshape(count, rows, tile)
        dl_ref[:, :, span] = lift_grad.reshape(count, rows, tile)
        part = mm_t(gate_grad, wg_ref[:, span]) + mm_t(lift_grad, wl_ref[:, span])
        if i == 0:
            acc_ref[...] = part
        else:
            acc_ref[...] = acc_ref[...] + part

    def units_end(p):
        total = acc_ref[...]
        dn_ref[...] = total.astype(LOW).reshape(count, rows, model)
        x = mid_ref[p].reshape(tall, model).astype(F32)
        dgain_ref[...] = dgain_ref[...] + jnp.sum(total * x * inverse_rms(x), axis=0, keepdims=True)
        for store in stores(p):
            store.start()

        @pl.when(p < pieces - 1)
        def _():
            masked_copy(p + 1).start()

    masked_copy(0).start()

    def turn_once(k, carry):
        both_ways(k, pieces, begin)
        for i in range(max(tiles, count - 1)):
            if i < count - 1:
                both_ways(k, pieces, lambda p, i=i: line.send_sums(p, count - 1 - i))
            if i == 0:
                both_ways(k - 1, pieces, own)
                both_ways(k - 2, pieces, units_begin)
            elif i < count - 1:
                both_ways(k - 1, pieces, lambda p, i=i: line.hand_on(p, i))
            if i < tiles:
                both_ways(k - 2, pieces, lambda p, i=i: units_tile(i))
        both_ways(k - 2, pieces, units_end)
        return carry

    lax.fori_loop(0, pieces + 2, turn_once, 0)
    for store in stores(pieces - 1):
        store.wait()
    line.drain()


def middle_step(acted, tok, gain, wo, masked, wg, wl, wd, count):
    pieces, rows, model = tok.shape
    hidden = wg.shape[1]
    any_place = pl.BlockSpec(memory_space=pl.ANY)

    def wide(columns, kind=LOW):
        return jax.ShapeDtypeStruct((count, pieces, rows, columns), kind)

    def room(columns, kind=LOW):
        return pltpu.VMEM((count, rows, columns), kind)

    return pl.pallas_call(
        functools.partial(middle_kernel, pieces, count),
        in_specs=[WHOLE] * 4 + [any_place] * 4,
        out_specs=[WHOLE] * 2 + [any_place] * 5,
        out_shape=[
            jax.ShapeDtypeStruct((pieces, rows, model), F32), shape_of(1, model, F32),
            wide(model), wide(hidden), wide(hidden), wide(hidden), wide(model),
        ],
        scratch_shapes=[
            pltpu.VMEM((pieces, count, rows, model), LOW),
            pltpu.VMEM(wg.shape, LOW), pltpu.VMEM(wl.shape, LOW), pltpu.VMEM(wd.shape, LOW),
            room(model), room(model), room(hidden), room(hidden), room(hidden), room(model),
            pltpu.VMEM((count * rows, model), F32),
            pltpu.SemaphoreType.DMA((3,)), pltpu.SemaphoreType.DMA, pltpu.SemaphoreType.DMA((5,)),
        ]
        + line_scratch(pieces, count, rows, model, F32, True),
        compiler_params=params(collective_id=0, has_side_effects=True),
        cost_estimate=takes(128),
        name="middle",
    )(acted, tok, gain, wo, masked, wg, wl, wd)


def residual_kernel(
    pieces, count,
    dn_ref, middle_ref, masked_ref, gain_ref, residual_ref, r_ref,
    part_ref, own_ref, right_ref, left_ref, *sems,
):
    line = Line(
        pieces, count, part_ref, own_ref, right_ref, left_ref, sems,
        spread=lambda p, t: r_ref.at[p // 2, t, p % 2],
    )
    line.barrier()

    def begin(p):
        part_ref[...] = dn_ref[:, p]
        line.keep_own(p)

    def own(p):
        line.finish_own(p)
        x = middle_ref[p].astype(LOW).astype(F32)
        residual = masked_ref[p] + norm_back(own_ref[p], x, gain_ref[...])
        residual_ref[p] = residual
        r_ref[p // 2, line.place, p % 2] = residual.astype(LOW)
        line.hand_out(p)

    def turn_once(k, carry):
        both_ways(k, pieces, begin)
        for i in range(count - 1):
            both_ways(k, pieces, lambda p, i=i: line.send_sums(p, count - 1 - i))
            if i == 0:
                both_ways(k - 1, pieces, own)
            else:
                both_ways(k - 1, pieces, lambda p, i=i: line.hand_on(p, i))
        both_ways(k - 1, pieces, lambda p: line.hand_on(p, count - 1))
        return carry

    lax.fori_loop(0, pieces + 1, turn_once, 0)
    line.drain()


def residual_step(dn, middle, masked, gain):
    count, pieces, rows, model = dn.shape
    return pl.pallas_call(
        functools.partial(residual_kernel, pieces, count),
        in_specs=[WHOLE] * 4,
        out_specs=[WHOLE] * 2,
        out_shape=[
            jax.ShapeDtypeStruct((pieces, rows, model), F32),
            jax.ShapeDtypeStruct((pieces // 2, count, 2, rows, model), LOW),
        ],
        scratch_shapes=line_scratch(pieces, count, rows, model, LOW, True),
        compiler_params=params(collective_id=1, has_side_effects=True),
        cost_estimate=takes(120),
        name="residual",
    )(dn, middle, masked, gain)


def input_kernel(
    pieces, count,
    dn_ref, tok_ref, residual_ref, gain_ref, grad_ref,
    part_ref, own_ref, right_ref, left_ref, *sems,
):
    line = Line(pieces, count, part_ref, own_ref, right_ref, left_ref, sems)
    line.barrier()

    def begin(p):
        part_ref[...] = dn_ref[p // 2, :, p % 2]
        line.keep_own(p)

    def own(p):
        line.finish_own(p)
        x = tok_ref[p].astype(F32)
        grad_ref[p] = residual_ref[p] + norm_back(own_ref[p], x, gain_ref[...])

    def turn_once(k, carry):
        both_ways(k, pieces, begin)
        for i in range(count - 1):
            both_ways(k, pieces, lambda p, i=i: line.send_sums(p, count - 1 - i))
            if i == 0:
                both_ways(k - 1, pieces, own)
        return carry

    lax.fori_loop(0, pieces + 1, turn_once, 0)
    line.drain()


def input_step(dn, tok, residual, gain):
    batch, count, halves, rows, model = dn.shape
    pieces = batch * halves
    return pl.pallas_call(
        functools.partial(input_kernel, pieces, count),
        in_specs=[WHOLE] * 4,
        out_specs=WHOLE,
        out_shape=jax.ShapeDtypeStruct((pieces, rows, model), F32),
        scratch_shapes=line_scratch(pieces, count, rows, model, LOW, False),
        compiler_params=params(collective_id=2, has_side_effects=True),
        cost_estimate=takes(110),
        name="input_grad",
    )(dn, tok, residual, gain)


def flipped(place, mask):
    bit = 1
    while bit <= mask:
        if mask & bit:
            place = place + (1 - 2 * (place // bit % 2)) * bit
        bit *= 2
    return place


def digit_orders(count, batch):
    upper = [1 << i for i in range(1, count.bit_length() - 1)]
    return [(upper if b % 2 == 0 else upper[::-1]) + [1] for b in range(batch)]


def greet(place, digits):
    sem = pltpu.get_barrier_semaphore()
    for digit in digits:
        pl.semaphore_signal(sem, inc=1, device_id={"seq": flipped(place, digit)}, device_id_type=MESH)
    pl.semaphore_wait(sem, len(digits))


def gather_kernel(count, batch, *refs):
    own, out = refs[:batch], refs[batch : 2 * batch]
    local_sem, send_sem, receive_sem = refs[2 * batch :]
    place = lax.axis_index("seq")
    orders = digit_orders(count, batch)
    greet(place, orders[0])
    local = [pltpu.make_async_copy(own[b], out[b].at[place], local_sem.at[b]) for b in range(batch)]
    for copy in local:
        copy.start()

    def block(b, mask):
        return out[b].at[flipped(place, mask)]

    def send(b, mask, step):
        digit = orders[b][step]
        return pltpu.make_async_remote_copy(
            src_ref=own[b] if mask == 0 else block(b, mask),
            dst_ref=block(b, mask),
            send_sem=send_sem.at[b, step, mask],
            recv_sem=receive_sem.at[b, mask | digit],
            device_id={"seq": flipped(place, digit)},
            device_id_type=MESH,
        )

    def arrival(b, mask):
        return pltpu.make_async_remote_copy(
            src_ref=block(b, mask),
            dst_ref=block(b, mask),
            send_sem=send_sem.at[b, 0, mask],
            recv_sem=receive_sem.at[b, mask],
            device_id={"seq": flipped(place, mask)},
            device_id_type=MESH,
        )

    steps = len(orders[0])
    started = []
    for level in range(-1, steps):
        masks = [0] if level < 0 else range(1 << level)
        for turn in masks:
            for b in range(batch):
                mask = 0
                if level >= 0:
                    mask = orders[b][level]
                    for i in range(level):
                        if turn >> i & 1:
                            mask |= orders[b][i]
                    arrival(b, mask).wait_recv()
                for step in range(level + 1, steps):
                    copy = send(b, mask, step)
                    copy.start()
                    started.append(copy)
    for copy in started:
        copy.wait_send()
    for copy in local:
        copy.wait()


def gather_blocks(own):
    count, batch = lax.axis_size("seq"), len(own)
    rows, columns = own[0].shape
    steps = count.bit_length() - 1
    any_place = pl.BlockSpec(memory_space=pl.ANY)
    return pl.pallas_call(
        functools.partial(gather_kernel, count, batch),
        in_specs=[any_place] * batch,
        out_specs=[any_place] * batch,
        out_shape=[jax.ShapeDtypeStruct((count, rows, columns), LOW)] * batch,
        scratch_shapes=[
            pltpu.SemaphoreType.DMA((batch,)),
            pltpu.SemaphoreType.DMA((batch, steps, count)),
            pltpu.SemaphoreType.DMA((batch, count)),
        ],
        compiler_params=params(collective_id=3, has_side_effects=True),
        cost_estimate=takes(41),
        name="gather_blocks",
    )(*own)


def scatter_kernel(count, batch, *refs):
    parts, out = refs[:batch], refs[batch : 2 * batch]
    slots, send_sem, receive_sem = refs[2 * batch :]
    place = lax.axis_index("seq")
    orders = [order[::-1] for order in digit_orders(count, batch)]
    steps = len(orders[0])
    greet(place, orders[0])

    def masks_at(b, step):
        found = [0]
        for digit in orders[b][step + 1 :][::-1]:
            found = [mask | digit for mask in found] + found
        return found

    numbers = {}
    for b in range(batch):
        place_in = 0
        for step in range(steps):
            for mask in masks_at(b, step):
                numbers[b, step, mask] = place_in
                place_in += 1

    def slot(b, step, mask):
        return slots.at[b, numbers[b, step, mask]]

    def transfer(b, step, mask):
        digit = orders[b][step]
        number = numbers[b, step, mask]
        if step == 0:
            source = parts[b].at[flipped(place, mask | digit)]
        else:
            source = slot(b, step - 1, mask | digit)
        return pltpu.make_async_remote_copy(
            src_ref=source,
            dst_ref=slots.at[b, number],
            send_sem=send_sem.at[b, number],
            recv_sem=receive_sem.at[b, number],
            device_id={"seq": flipped(place, digit)},
            device_id_type=MESH,
        )

    started = []
    for turn in range(count // 2):
        for b in range(batch):
            copy = transfer(b, 0, masks_at(b, 0)[turn])
            copy.start()
            started.append(copy)
    for step in range(steps):
        for turn in range(len(masks_at(0, step))):
            for b in range(batch):
                mask = masks_at(b, step)[turn]
                transfer(b, step, mask).wait_recv()
                held = parts[b].at[flipped(place, mask)] if step == 0 else slot(b, step - 1, mask)
                total = held[...].astype(F32) + slot(b, step, mask)[...].astype(F32)
                if step == steps - 1:
                    out[b][...] = total.astype(LOW)
                else:
                    slot(b, step, mask)[...] = total.astype(LOW)
                    if mask & orders[b][step + 1]:
                        copy = transfer(b, step + 1, mask & ~orders[b][step + 1])
                        copy.start()
                        started.append(copy)
    for copy in started:
        copy.wait_send()


def scatter_blocks(parts):
    count, batch = lax.axis_size("seq"), len(parts)
    rows, columns = parts[0].shape[0] // count, parts[0].shape[1]
    return pl.pallas_call(
        functools.partial(scatter_kernel, count, batch),
        in_specs=[WHOLE] * batch,
        out_specs=[WHOLE] * batch,
        out_shape=[shape_of(rows, columns, LOW)] * batch,
        scratch_shapes=[
            pltpu.VMEM((batch, count - 1, rows, columns), LOW),
            pltpu.SemaphoreType.DMA((batch, count - 1)),
            pltpu.SemaphoreType.DMA((batch, count - 1)),
        ],
        compiler_params=params(collective_id=4, has_side_effects=True),
        cost_estimate=takes(52),
        name="scatter_blocks",
    )(*[part.reshape(count, rows, columns) for part in parts])


def turn_tables(positions, head_dim):
    half_dim = head_dim // 2
    inverse = THETA ** (-(jnp.arange(half_dim, dtype=F32) * 2.0) / head_dim)
    angles = positions.astype(F32)[:, None] * inverse[None, :]
    cosine, sine = jnp.cos(angles), jnp.sin(angles)
    return jnp.concatenate([cosine, cosine], axis=1), jnp.concatenate([-sine, sine], axis=1)


def norm_back(grad, values, gain):
    inverse = inverse_rms(values)
    grad = grad * gain
    mean = jnp.mean(grad * values, axis=-1, keepdims=True)
    return inverse * (grad - values * (inverse * inverse * mean))


def gather(value, axis):
    return lax.all_gather(value, axis, axis=0, tiled=True)


def scatter(value, axis):
    return lax.psum_scatter(value, axis, scatter_dimension=0, tiled=True)


def on_device(
    tokens, cotangent, lengths,
    query_weight, key_weight, value_weight, gating_weight, output_weight,
    swiglu_gate, swiglu_lift, swiglu_down,
    input_gain, middle_gain, query_gain, key_gain,
):
    block_index = lax.axis_index("seq")
    part_index = lax.axis_index("head")
    parts = lax.axis_size("head")
    local_rows, batch, model = tokens.shape
    head_dim = query_gain.shape[0]
    block_rows = local_rows * parts
    group = query_weight.shape[1] // key_weight.shape[1]
    nq, nk = query_weight.shape[1], key_weight.shape[1]
    query_start = block_index * block_rows
    positions = query_start + jnp.arange(block_rows, dtype=jnp.int32)
    cosine, sine = turn_tables(positions, head_dim)
    gain_in, gain_mid = input_gain[None, :], middle_gain[None, :]
    gain_q, gain_k = query_gain[None, :], key_gain[None, :]
    local_pos = query_start + part_index * local_rows + jnp.arange(local_rows, dtype=jnp.int32)
    seqs = range(batch)
    places = [jnp.stack([query_start, lengths[b]]).astype(jnp.int32) for b in seqs]
    valid = [(local_pos < lengths[b]).astype(F32)[:, None] for b in seqs]
    own = [tokens[:, b, :] for b in seqs]
    own_masked = [valid[b] * cotangent[:, b, :].astype(F32) for b in seqs]

    rows_in = [gather(own[b], "head") for b in seqs]
    projected = [
        project(
            rows_in[b], gain_in, cosine, sine, gain_q, gain_k,
            query_weight, key_weight, value_weight, gating_weight,
        )
        for b in seqs
    ]
    normed, qraw, q, kraw, kv_own, gate = [list(x) for x in zip(*projected)]
    kv = [x.reshape(-1, 2 * nk) for x in gather_blocks(kv_own)]
    masked = gather(jnp.concatenate([x.astype(LOW) for x in own_masked], axis=0), "head")
    attended = [attend(places[b], q[b], kv[b], gate[b], group, head_dim) for b in seqs]
    att, acted, inv = [list(x) for x in zip(*attended)]
    halves = 2
    rows = local_rows // halves
    pieces = batch * halves
    acted_all = jnp.stack(acted).reshape(batch, parts, halves, rows, nq)
    tok = jnp.stack(own).reshape(pieces, rows, model)
    masked_own = jnp.stack(own_masked).reshape(pieces, rows, model)
    middle, dgain_mid, normed_mid, hidden, dg, dl, dn_mid = middle_step(
        acted_all, tok, gain_mid, output_weight,
        masked.reshape(parts, pieces, rows, model), swiglu_gate, swiglu_lift, swiglu_down, parts,
    )
    flat_rows = block_rows * batch

    def flat(array):
        return array.reshape(flat_rows, array.shape[-1])

    normed_mid, hidden, dg, dl = flat(normed_mid), flat(hidden), flat(dg), flat(dl)
    ff_grads = (
        t_mm(normed_mid, dg).astype(LOW),
        t_mm(normed_mid, dl).astype(LOW),
        t_mm(hidden, masked).astype(LOW),
    )
    dn_mid, ff_grads = lax.optimization_barrier((dn_mid, ff_grads))
    ff_grads = lax.psum(ff_grads, "seq")
    residual, r_all = residual_step(dn_mid, middle, masked_own, gain_mid)
    r_all, hidden = lax.optimization_barrier((r_all, hidden))
    r_all = r_all.reshape(batch, block_rows, model)
    r = [r_all[b] for b in seqs]
    units_out = scatter(mm(hidden, swiglu_down).astype(LOW), "head").astype(F32)
    units_out = units_out.reshape(batch, local_rows, model)
    middle = middle.reshape(batch, local_rows, model)
    output = jnp.stack(
        [(valid[b] * (middle[b] + units_out[b])).astype(LOW) for b in seqs], axis=1
    )

    back = [
        attend_back(places[b], q[b], kv[b], r[b], output_weight, att[b], gate[b], inv[b], group, head_dim)
        for b in seqs
    ]
    dq, dkv_all, dgate = [list(x) for x in zip(*back)]
    dkv = scatter_blocks(dkv_all)
    last = [
        unproject(
            rows_in[b], gain_in, cosine, sine, gain_q, gain_k,
            query_weight, key_weight, value_weight, gating_weight,
            dq[b], qraw[b], dkv[b], kraw[b], dgate[b],
        )
        for b in seqs
    ]
    dall, dn_in, dgain_in, dgain_q, dgain_k = [list(x) for x in zip(*last)]
    input_grad = input_step(
        jnp.stack(dn_in).reshape(batch, parts, halves, rows, model), tok, residual, gain_in
    )
    input_grad = jnp.transpose(input_grad.reshape(batch, local_rows, model), (1, 0, 2))

    def both(pair):
        return jnp.concatenate(pair, axis=0)

    ff_grads, dall = lax.optimization_barrier((ff_grads, dall))
    out_grad = t_mm(both(acted), r_all.reshape(flat_rows, model)).astype(LOW)
    proj_grad = t_mm(both(normed), both(dall)).astype(LOW)
    out_grad, proj_grad = lax.psum((out_grad, proj_grad), "seq")
    gains = jnp.concatenate(
        [sum(dgain_in)[0], dgain_mid[0], sum(dgain_q)[0], sum(dgain_k)[0]]
    )
    gains = lax.psum(gains, ("seq", "head"))

    def share(start, width):
        piece = width // parts
        return lax.dynamic_slice(gains, (start + part_index * piece,), (piece,))

    return (
        output,
        input_grad,
        proj_grad[:, :nq].astype(F32),
        proj_grad[:, nq : nq + nk].astype(F32),
        proj_grad[:, nq + nk : nq + 2 * nk].astype(F32),
        proj_grad[:, nq + 2 * nk :].astype(F32),
        out_grad.astype(F32),
        ff_grads[0].astype(F32),
        ff_grads[1].astype(F32),
        ff_grads[2].astype(F32),
        share(0, model),
        share(model, model),
        share(2 * model, head_dim),
        share(2 * model + head_dim, head_dim),
    )


def solution(mesh):
    return jax.shard_map(
        on_device,
        mesh=mesh,
        in_specs=(
            P(("seq", "head"), None, None),
            P(("seq", "head"), None, None),
            P(),
            P(None, "head"),
            P(None, "head"),
            P(None, "head"),
            P(None, "head"),
            P("head", None),
            P(None, "head"),
            P(None, "head"),
            P("head", None),
            P(),
            P(),
            P(),
            P(),
        ),
        out_specs=(
            P(("seq", "head"), None, None),
            P(("seq", "head"), None, None),
            P(None, "head"),
            P(None, "head"),
            P(None, "head"),
            P(None, "head"),
            P("head", None),
            P(None, "head"),
            P(None, "head"),
            P("head", None),
            P("head"),
            P("head"),
            P("head"),
            P("head"),
        ),
        check_vma=False,
    )
```

```python
import functools

import jax
import jax.numpy as jnp
from jax import lax
from jax.experimental import pallas as pl
from jax.experimental.pallas import tpu as pltpu
from jax.sharding import PartitionSpec as P

EPS = 1e-06
THETA = 1000000.0
LOG2E = 1.4426950408889634
VMEM_LIMIT = 58 * 1024 * 1024
LOW = jnp.bfloat16
F32 = jnp.float32
MESH = pl.DeviceIdType.MESH


def mm(left, right):
    return jnp.dot(left, right, preferred_element_type=F32)


def mm_t(left, right):
    return lax.dot_general(left, right, (((1,), (1,)), ((), ())), preferred_element_type=F32)


def t_mm(left, right):
    return lax.dot_general(left, right, (((0,), (0,)), ((), ())), preferred_element_type=F32)


def shape_of(rows, columns, kind):
    return jax.ShapeDtypeStruct((rows, columns), kind)


def params(**extra):
    return pltpu.CompilerParams(vmem_limit_bytes=VMEM_LIMIT, **extra)


def takes(microseconds):
    return pl.CostEstimate(
        flops=int(microseconds * 1.15e9), bytes_accessed=int(microseconds * 3.69e6), transcendentals=0
    )


WHOLE = pl.BlockSpec(memory_space=pltpu.VMEM)
SCALARS = pl.BlockSpec(memory_space=pltpu.SMEM)


def full_block(array):
    return pl.BlockSpec(array.shape, lambda i: (0,) * len(array.shape))


def inverse_rms(values):
    return lax.rsqrt(jnp.mean(values * values, axis=-1, keepdims=True) + EPS)


def turn(values, cosine, sine):
    return values * cosine + pltpu.roll(values, values.shape[-1] // 2, 1) * sine


def turn_back(grads, cosine, sine):
    return grads * cosine + pltpu.roll(grads * sine, grads.shape[-1] // 2, 1)


def project_kernel(
    head_dim,
    x_ref, gain_ref, cos_ref, sin_ref, qgain_ref, kgain_ref, wq_ref, wk_ref, wv_ref, wg_ref,
    normed_ref, qraw_ref, q_ref, kraw_ref, kv_ref, gate_ref,
):
    x = x_ref[...].astype(F32)
    normed = (x * inverse_rms(x) * gain_ref[...]).astype(LOW)
    normed_ref[...] = normed
    cosine, sine = cos_ref[...], sin_ref[...]
    raw = mm(normed, wk_ref[...])
    kraw_ref[...] = raw
    for h in range(raw.shape[1] // head_dim):
        part = raw[:, h * head_dim : (h + 1) * head_dim]
        part = part * inverse_rms(part) * kgain_ref[...]
        kv_ref[:, h * head_dim : (h + 1) * head_dim] = turn(part, cosine, sine).astype(LOW)
    kv_ref[:, raw.shape[1] :] = mm(normed, wv_ref[...]).astype(LOW)
    raw = mm(normed, wq_ref[...])
    qraw_ref[...] = raw
    for h in range(raw.shape[1] // head_dim):
        part = raw[:, h * head_dim : (h + 1) * head_dim]
        part = part * inverse_rms(part) * qgain_ref[...]
        q_ref[:, h * head_dim : (h + 1) * head_dim] = turn(part, cosine, sine).astype(LOW)
    gate_ref[...] = mm(normed, wg_ref[...])


def project(x, gain, cosine, sine, qgain, kgain, wq, wk, wv, wg):
    rows, model = x.shape
    head_dim = qgain.shape[1]
    tile = min(rows, 256)
    nq, nk = wq.shape[1], wk.shape[1]

    def by_row(columns):
        return pl.BlockSpec((tile, columns), lambda i: (i, 0))

    return pl.pallas_call(
        functools.partial(project_kernel, head_dim),
        grid=(rows // tile,),
        in_specs=[
            by_row(model), full_block(gain), by_row(head_dim), by_row(head_dim),
            full_block(qgain), full_block(kgain),
            full_block(wq), full_block(wk), full_block(wv), full_block(wg),
        ],
        out_specs=[by_row(model), by_row(nq), by_row(nq), by_row(nk), by_row(2 * nk), by_row(nq)],
        out_shape=[
            shape_of(rows, model, LOW), shape_of(rows, nq, F32), shape_of(rows, nq, LOW),
            shape_of(rows, nk, F32), shape_of(rows, 2 * nk, LOW), shape_of(rows, nq, F32),
        ],
        compiler_params=params(),
        cost_estimate=takes(9),
        name="project",
    )(x, gain, cosine, sine, qgain, kgain, wq, wk, wv, wg)


def live_blocks(place_ref, rows):
    start, length = place_ref[0], place_ref[1]
    whole = jnp.minimum(start // rows, length // rows)
    end = jnp.minimum(start // rows + 1, (length + rows - 1) // rows)
    end = jnp.where(start < length, end, 0)
    return jnp.minimum(whole, end), end


def attend_kernel(
    group, head_dim, place_ref, q_ref, kv_ref, gate_ref, att_ref, acted_ref, inv_ref, acc_ref, sum_ref
):
    rows = q_ref.shape[0]
    heads = q_ref.shape[1] // head_dim
    kv_heads = heads // group
    factor = head_dim ** (-0.5) * LOG2E
    start, length = place_ref[0], place_ref[1]
    acc_ref[...] = jnp.zeros_like(acc_ref)
    sum_ref[...] = jnp.zeros_like(sum_ref)
    whole, end = live_blocks(place_ref, rows)

    def one_block(j, masked):
        span = pl.ds(pl.multiple_of(j * rows, rows), rows)
        if masked:
            key_pos = j * rows + lax.broadcasted_iota(jnp.int32, (rows, rows), 1)
            query_pos = start + lax.broadcasted_iota(jnp.int32, (rows, rows), 0)
            allowed = (key_pos <= query_pos) & (key_pos < length)
        for h in range(heads):
            c = h // group
            keys = kv_ref[span, c * head_dim : (c + 1) * head_dim]
            values = kv_ref[span, (kv_heads + c) * head_dim : (kv_heads + c + 1) * head_dim]
            weights = jnp.exp2(mm_t(q_ref[:, h * head_dim : (h + 1) * head_dim], keys) * factor)
            if masked:
                weights = jnp.where(allowed, weights, 0.0)
            total = weights[:, :128]
            for piece in range(1, rows // 128):
                total = total + weights[:, piece * 128 : (piece + 1) * 128]
            sum_ref[h] = sum_ref[h] + total
            acc_ref[h] = acc_ref[h] + mm(weights.astype(LOW), values)

    def plain(j, carry):
        one_block(j, False)
        return carry

    def edge(j, carry):
        one_block(j, True)
        return carry

    lax.fori_loop(0, whole, plain, 0)
    lax.fori_loop(whole, end, edge, 0)
    lane = lax.broadcasted_iota(jnp.int32, inv_ref.shape, 1)
    kept = jnp.zeros(inv_ref.shape, F32)
    for h in range(heads):
        total = jnp.sum(sum_ref[h], axis=1, keepdims=True)
        inverse = 1.0 / jnp.where(total > 0.0, total, 1.0)
        attended = acc_ref[h] * inverse
        columns = slice(h * head_dim, (h + 1) * head_dim)
        att_ref[:, columns] = attended
        acted_ref[:, columns] = (attended * jax.nn.sigmoid(gate_ref[:, columns])).astype(LOW)
        kept = jnp.where(lane == h, inverse, kept)
    inv_ref[...] = kept


def attend(place, q, kv, gate, group, head_dim):
    rows, width = q.shape
    heads = width // head_dim
    return pl.pallas_call(
        functools.partial(attend_kernel, group, head_dim),
        in_specs=[SCALARS, WHOLE, WHOLE, WHOLE],
        out_specs=[WHOLE, WHOLE, WHOLE],
        out_shape=[shape_of(rows, width, F32), shape_of(rows, width, LOW), shape_of(rows, 128, F32)],
        scratch_shapes=[
            pltpu.VMEM((heads, rows, head_dim), F32),
            pltpu.VMEM((heads, rows, 128), F32),
        ],
        compiler_params=params(),
        cost_estimate=takes(9),
        name="attend",
    )(place, q, kv, gate)


def attend_back_kernel(
    group, head_dim,
    place_ref, q_ref, kv_ref, r_ref, wo_ref, att_ref, gate_ref, inv_ref,
    dq_ref, dkv_ref, dgate_ref,
    scaled_ref, corr_ref, acc_ref,
):
    rows = q_ref.shape[0]
    heads = q_ref.shape[1] // head_dim
    kv_heads = heads // group
    scale = head_dim ** (-0.5)
    start, length = place_ref[0], place_ref[1]
    acted_grad = mm_t(r_ref[...], wo_ref[...])
    lane = lax.broadcasted_iota(jnp.int32, inv_ref.shape, 1)
    kept = jnp.zeros(inv_ref.shape, F32)
    for h in range(heads):
        columns = slice(h * head_dim, (h + 1) * head_dim)
        sigmoid = jax.nn.sigmoid(gate_ref[:, columns])
        attended = att_ref[:, columns]
        grad = acted_grad[:, columns]
        dgate_ref[:, columns] = (grad * attended * sigmoid * (1.0 - sigmoid)).astype(LOW)
        grad = grad * sigmoid
        inverse = inv_ref[:, h : h + 1]
        scaled_ref[:, columns] = (grad * inverse).astype(LOW)
        kept = jnp.where(
            lane == h, jnp.sum(grad * attended, axis=1, keepdims=True) * inverse, kept
        )
    corr_ref[...] = kept.T
    acc_ref[...] = jnp.zeros_like(acc_ref)
    whole, end = live_blocks(place_ref, rows)

    def one_block(j, masked):
        span = pl.ds(pl.multiple_of(j * rows, rows), rows)
        if masked:
            key_pos = j * rows + lax.broadcasted_iota(jnp.int32, (rows, rows), 0)
            query_pos = start + lax.broadcasted_iota(jnp.int32, (rows, rows), 1)
            allowed = (key_pos <= query_pos) & (key_pos < length)
        for c in range(kv_heads):
            key_columns = slice(c * head_dim, (c + 1) * head_dim)
            value_columns = slice((kv_heads + c) * head_dim, (kv_heads + c + 1) * head_dim)
            keys = kv_ref[span, key_columns]
            values = kv_ref[span, value_columns]
            dk = jnp.zeros((rows, head_dim), F32)
            dv = jnp.zeros((rows, head_dim), F32)
            for h in range(c * group, (c + 1) * group):
                columns = slice(h * head_dim, (h + 1) * head_dim)
                queries = q_ref[:, columns]
                scaled = scaled_ref[:, columns]
                weights = jnp.exp2(mm_t(keys, queries) * (scale * LOG2E))
                if masked:
                    weights = jnp.where(allowed, weights, 0.0)
                dv = dv + mm(weights.astype(LOW), scaled)
                score = (weights * (mm_t(values, scaled) - corr_ref[h : h + 1, :])).astype(LOW)
                dk = dk + mm(score, queries)
                acc_ref[h] = acc_ref[h] + t_mm(score, keys)
            dkv_ref[span, key_columns] = (dk * scale).astype(LOW)
            dkv_ref[span, value_columns] = dv.astype(LOW)

    def plain(j, carry):
        one_block(j, False)
        return carry

    def edge(j, carry):
        one_block(j, True)
        return carry

    def empty(j, carry):
        span = pl.ds(pl.multiple_of(j * rows, rows), rows)
        dkv_ref[span, :] = jnp.zeros((rows, dkv_ref.shape[1]), LOW)
        return carry

    lax.fori_loop(0, whole, plain, 0)
    lax.fori_loop(whole, end, edge, 0)
    lax.fori_loop(end, dkv_ref.shape[0] // rows, empty, 0)
    for h in range(heads):
        dq_ref[:, h * head_dim : (h + 1) * head_dim] = acc_ref[h] * scale


def attend_back(place, q, kv, r, wo, att, gate, inv, group, head_dim):
    rows, width = q.shape
    heads = width // head_dim
    return pl.pallas_call(
        functools.partial(attend_back_kernel, group, head_dim),
        in_specs=[SCALARS] + [WHOLE] * 7,
        out_specs=[WHOLE] * 3,
        out_shape=[
            shape_of(rows, width, F32), shape_of(kv.shape[0], kv.shape[1], LOW), shape_of(rows, width, LOW)
        ],
        scratch_shapes=[
            pltpu.VMEM((rows, width), LOW),
            pltpu.VMEM((128, rows), F32),
            pltpu.VMEM((heads, rows, head_dim), F32),
        ],
        compiler_params=params(),
        cost_estimate=takes(3),
        name="attend_back",
    )(place, q, kv, r, wo, att, gate, inv)


def unproject_kernel(
    head_dim,
    x_ref, gain_ref, cos_ref, sin_ref, qgain_ref, kgain_ref, wq_ref, wk_ref, wv_ref, wg_ref,
    dq_ref, qraw_ref, dkv_ref, kraw_ref, dgate_ref,
    dall_ref, dn_ref, dgain_ref, dqgain_ref, dkgain_ref,
):
    step = pl.program_id(0)
    cosine, sine = cos_ref[...], sin_ref[...]
    nq, nk = qraw_ref.shape[1], kraw_ref.shape[1]

    def heads_back(grad_ref, raw_ref, head_gain, count, place):
        gain_total = jnp.zeros((1, head_dim), F32)
        for h in range(count):
            columns = slice(h * head_dim, (h + 1) * head_dim)
            grad = turn_back(grad_ref[:, columns].astype(F32), cosine, sine)
            raw = raw_ref[:, columns]
            inverse = inverse_rms(raw)
            gain_total = gain_total + jnp.sum(grad * raw * inverse, axis=0, keepdims=True)
            grad = grad * head_gain
            mean = jnp.mean(grad * raw, axis=-1, keepdims=True)
            grad = inverse * (grad - raw * (inverse * inverse * mean))
            dall_ref[:, place + h * head_dim : place + (h + 1) * head_dim] = grad.astype(LOW)
        return gain_total

    dqgain = heads_back(dq_ref, qraw_ref, qgain_ref[...], nq // head_dim, 0)
    dkgain = heads_back(dkv_ref, kraw_ref, kgain_ref[...], nk // head_dim, nq)
    dall_ref[:, nq + nk : nq + 2 * nk] = dkv_ref[:, nk:]
    dall_ref[:, nq + 2 * nk :] = dgate_ref[...]
    total = (
        mm_t(dall_ref[:, :nq], wq_ref[...])
        + mm_t(dall_ref[:, nq : nq + nk], wk_ref[...])
        + mm_t(dall_ref[:, nq + nk : nq + 2 * nk], wv_ref[...])
        + mm_t(dall_ref[:, nq + 2 * nk :], wg_ref[...])
    )
    dn_ref[...] = total.astype(LOW)
    x = x_ref[...].astype(F32)
    dgain = jnp.sum(total * x * inverse_rms(x), axis=0, keepdims=True)

    @pl.when(step == 0)
    def _():
        dgain_ref[...] = dgain
        dqgain_ref[...] = dqgain
        dkgain_ref[...] = dkgain

    @pl.when(step > 0)
    def _():
        dgain_ref[...] = dgain_ref[...] + dgain
        dqgain_ref[...] = dqgain_ref[...] + dqgain
        dkgain_ref[...] = dkgain_ref[...] + dkgain


def unproject(x, gain, cosine, sine, qgain, kgain, wq, wk, wv, wg, dq, qraw, dkv, kraw, dgate):
    rows, model = x.shape
    head_dim = qgain.shape[1]
    tile = min(rows, 256)
    nq, nk = wq.shape[1], wk.shape[1]

    def by_row(columns):
        return pl.BlockSpec((tile, columns), lambda i: (i, 0))

    def line(columns):
        return pl.BlockSpec((1, columns), lambda i: (0, 0))

    return pl.pallas_call(
        functools.partial(unproject_kernel, head_dim),
        grid=(rows // tile,),
        in_specs=[
            by_row(model), full_block(gain), by_row(head_dim), by_row(head_dim),
            full_block(qgain), full_block(kgain),
            full_block(wq), full_block(wk), full_block(wv), full_block(wg),
            by_row(nq), by_row(nq), by_row(2 * nk), by_row(nk), by_row(nq),
        ],
        out_specs=[by_row(2 * nq + 2 * nk), by_row(model), line(model), line(head_dim), line(head_dim)],
        out_shape=[
            shape_of(rows, 2 * nq + 2 * nk, LOW), shape_of(rows, model, LOW),
            shape_of(1, model, F32), shape_of(1, head_dim, F32), shape_of(1, head_dim, F32),
        ],
        compiler_params=params(),
        cost_estimate=takes(3),
        name="unproject",
    )(x, gain, cosine, sine, qgain, kgain, wq, wk, wv, wg, dq, qraw, dkv, kraw, dgate)


class Line:
    def __init__(self, pieces, count, part_ref, own_ref, right_ref, left_ref, sems, spread=None):
        self.pieces, self.count = pieces, count
        self.place = lax.axis_index("head")
        self.part_ref, self.own_ref = part_ref, own_ref
        self.right_ref, self.left_ref = right_ref, left_ref
        self.sems = sems
        self.spread = spread

    def barrier(self, digits=()):
        sem = pltpu.get_barrier_semaphore()
        place, count = self.place, self.count
        for digit in digits:
            partner = flipped(lax.axis_index("seq"), digit)
            pl.semaphore_signal(sem, inc=1, device_id={"seq": partner}, device_id_type=MESH)

        @pl.when(place > 0)
        def _():
            pl.semaphore_signal(sem, inc=1, device_id={"head": place - 1}, device_id_type=MESH)

        @pl.when(place < count - 1)
        def _():
            pl.semaphore_signal(sem, inc=1, device_id={"head": place + 1}, device_id_type=MESH)

        inside = (place > 0) & (place < count - 1)

        @pl.when(inside)
        def _():
            pl.semaphore_wait(sem, 2 + len(digits))

        @pl.when(jnp.logical_not(inside))
        def _():
            pl.semaphore_wait(sem, 1 + len(digits))

    def copy(self, ref, send, receive, p, t, step):
        return pltpu.make_async_remote_copy(
            src_ref=ref,
            dst_ref=ref,
            send_sem=self.sems[send].at[p, t],
            recv_sem=self.sems[receive].at[p, t],
            device_id={"head": jnp.clip(self.place + step, 0, self.count - 1)},
            device_id_type=MESH,
        )

    def sum_copy(self, p, t, step):
        ref = self.right_ref if step > 0 else self.left_ref
        base = 0 if step > 0 else 2
        return self.copy(ref.at[p, t], base, base + 1, p, t, step)

    def spread_copy(self, p, t, step):
        return self.copy(self.spread(p, t), 4 if step > 0 else 5, 6, p, t, step)

    def send_sums(self, p, distance):
        place, count = self.place, self.count
        for step, ref in ((1, self.right_ref), (-1, self.left_ref)):
            t = place + step * distance
            first = place == (0 if step > 0 else count - 1)

            @pl.when((t >= 0) & (t < count))
            def _(t=t, step=step, ref=ref, first=first):
                @pl.when(first)
                def _():
                    ref[p, t] = self.part_ref[t].astype(LOW)

                @pl.when(jnp.logical_not(first))
                def _():
                    self.sum_copy(p, t, step).wait_recv()
                    ref[p, t] = (ref[p, t].astype(F32) + self.part_ref[t].astype(F32)).astype(LOW)

                self.sum_copy(p, t, step).start()

    def keep_own(self, p):
        self.own_ref[p] = self.part_ref[self.place].astype(F32)

    def finish_own(self, p):
        place, count = self.place, self.count
        for step, ref, inner in ((1, self.right_ref, place > 0), (-1, self.left_ref, place < count - 1)):

            @pl.when(inner)
            def _(step=step, ref=ref):
                self.sum_copy(p, place, step).wait_recv()
                self.own_ref[p] = self.own_ref[p] + ref[p, place].astype(F32)

    def hand_out(self, p):
        place, count = self.place, self.count

        @pl.when(place < count - 1)
        def _():
            self.spread_copy(p, place, 1).start()

        @pl.when(place > 0)
        def _():
            self.spread_copy(p, place, -1).start()

    def hand_on(self, p, distance):
        place, count = self.place, self.count
        for step, more in ((1, place < count - 1), (-1, place > 0)):
            t = place - step * distance

            @pl.when((t >= 0) & (t < count))
            def _(t=t, step=step, more=more):
                self.spread_copy(p, t, step).wait_recv()

                @pl.when(more)
                def _():
                    self.spread_copy(p, t, step).start()

    def drain(self):
        place, count = self.place, self.count

        def one(p, carry):
            for t in range(count):

                @pl.when(t > place)
                def _(t=t):
                    self.sum_copy(p, t, 1).wait_send()

                @pl.when(t < place)
                def _(t=t):
                    self.sum_copy(p, t, -1).wait_send()

                if self.spread is not None:

                    @pl.when((t <= place) & (place < count - 1))
                    def _(t=t):
                        self.spread_copy(p, t, 1).wait_send()

                    @pl.when((t >= place) & (place > 0))
                    def _(t=t):
                        self.spread_copy(p, t, -1).wait_send()

            return carry

        lax.fori_loop(0, self.pieces, one, 0)


def line_scratch(pieces, count, rows, model, part_kind, spread):
    slots = (pieces, count)
    scratch = [
        pltpu.VMEM((pieces, rows, model), F32),
        pltpu.VMEM((pieces, count, rows, model), LOW),
        pltpu.VMEM((pieces, count, rows, model), LOW),
    ] + [pltpu.SemaphoreType.DMA(slots)] * (7 if spread else 4)
    if part_kind is not None:
        scratch = [pltpu.VMEM((count, rows, model), part_kind)] + scratch
    return scratch


def both_ways(index, limit, body):
    @pl.when((index >= 0) & (index < limit))
    def _():
        body(index)


def middle_kernel(
    pieces, count,
    acted_ref, tok_ref, gain_ref, wo_ref, masked_hbm, wg_hbm, wl_hbm, wd_hbm,
    middle_ref, dgain_ref, normed_hbm, hidden_hbm, dg_hbm, dl_hbm, dn_hbm,
    mid_ref, wg_ref, wl_ref, wd_ref, masked_ref, normed_ref, hidden_ref, dg_ref, dl_ref, dn_ref, acc_ref,
    load_sem, masked_sem, store_sem,
    part_ref, own_ref, right_ref, left_ref, *sems,
):
    rows, model = own_ref.shape[1], own_ref.shape[2]
    tall = count * rows
    hidden = wg_ref.shape[1]
    line = Line(
        pieces, count, part_ref, own_ref, right_ref, left_ref, sems, spread=lambda p, t: mid_ref.at[p, t]
    )
    place = line.place
    loads = [
        pltpu.make_async_copy(source, target, load_sem.at[i])
        for i, (source, target) in enumerate(((wg_hbm, wg_ref), (wl_hbm, wl_ref), (wd_hbm, wd_ref)))
    ]
    line.barrier()
    for load in loads:
        load.start()
    dgain_ref[...] = jnp.zeros_like(dgain_ref)
    tiles = 3
    tile = hidden // tiles

    def masked_copy(p):
        return pltpu.make_async_copy(masked_hbm.at[:, p], masked_ref, masked_sem)

    def stores(p):
        pairs = (
            (normed_ref, normed_hbm), (hidden_ref, hidden_hbm), (dg_ref, dg_hbm), (dl_ref, dl_hbm),
            (dn_ref, dn_hbm),
        )
        return [
            pltpu.make_async_copy(source, target.at[:, p], store_sem.at[i])
            for i, (source, target) in enumerate(pairs)
        ]

    def begin(p):
        acted = acted_ref[p // 2, :, p % 2].reshape(tall, acted_ref.shape[-1])
        part_ref[...] = mm(acted, wo_ref[...]).reshape(count, rows, model)
        line.keep_own(p)

    def own(p):
        line.finish_own(p)
        middle = own_ref[p] + tok_ref[p].astype(F32)
        middle_ref[p] = middle
        mid_ref[p, place] = middle.astype(LOW)
        line.hand_out(p)

    def units_begin(p):
        line.hand_on(p, count - 1)

        @pl.when(p > 0)
        def _():
            for store in stores(p - 1):
                store.wait()

        x = mid_ref[p].reshape(tall, model).astype(F32)
        normed = (x * inverse_rms(x) * gain_ref[...]).astype(LOW)
        normed_ref[...] = normed.reshape(count, rows, model)
        masked_copy(p).wait()

        @pl.when(p == 0)
        def _():
            for load in loads:
                load.wait()

    def units_tile(i):
        span = slice(i * tile, (i + 1) * tile)
        normed = normed_ref[...].reshape(tall, model)
        gate = mm(normed, wg_ref[:, span])
        lift = mm(normed, wl_ref[:, span])
        grad = mm_t(masked_ref[...].reshape(tall, model), wd_ref[span, :])
        sigmoid = jax.nn.sigmoid(gate)
        silu = gate * sigmoid
        lift_grad = (grad * silu).astype(LOW)
        gate_grad = (grad * lift * (sigmoid + silu * (1.0 - sigmoid))).astype(LOW)
        hidden_ref[:, :, span] = (silu * lift).astype(LOW).reshape(count, rows, tile)
        dg_ref[:, :, span] = gate_grad.reshape(count, rows, tile)
        dl_ref[:, :, span] = lift_grad.reshape(count, rows, tile)
        part = mm_t(gate_grad, wg_ref[:, span]) + mm_t(lift_grad, wl_ref[:, span])
        if i == 0:
            acc_ref[...] = part
        else:
            acc_ref[...] = acc_ref[...] + part

    def units_end(p):
        total = acc_ref[...]
        dn_ref[...] = total.astype(LOW).reshape(count, rows, model)
        x = mid_ref[p].reshape(tall, model).astype(F32)
        dgain_ref[...] = dgain_ref[...] + jnp.sum(total * x * inverse_rms(x), axis=0, keepdims=True)
        for store in stores(p):
            store.start()

        @pl.when(p < pieces - 1)
        def _():
            masked_copy(p + 1).start()

    masked_copy(0).start()

    def turn_once(k, carry):
        both_ways(k, pieces, begin)
        for i in range(max(tiles, count - 1)):
            if i < count - 1:
                both_ways(k, pieces, lambda p, i=i: line.send_sums(p, count - 1 - i))
            if i == 0:
                both_ways(k - 1, pieces, own)
                both_ways(k - 2, pieces, units_begin)
            elif i < count - 1:
                both_ways(k - 1, pieces, lambda p, i=i: line.hand_on(p, i))
            if i < tiles:
                both_ways(k - 2, pieces, lambda p, i=i: units_tile(i))
        both_ways(k - 2, pieces, units_end)
        return carry

    lax.fori_loop(0, pieces + 2, turn_once, 0)
    for store in stores(pieces - 1):
        store.wait()
    line.drain()


def middle_step(acted, tok, gain, wo, masked, wg, wl, wd, count):
    pieces, rows, model = tok.shape
    hidden = wg.shape[1]
    any_place = pl.BlockSpec(memory_space=pl.ANY)

    def wide(columns, kind=LOW):
        return jax.ShapeDtypeStruct((count, pieces, rows, columns), kind)

    def room(columns, kind=LOW):
        return pltpu.VMEM((count, rows, columns), kind)

    return pl.pallas_call(
        functools.partial(middle_kernel, pieces, count),
        in_specs=[WHOLE] * 4 + [any_place] * 4,
        out_specs=[WHOLE] * 2 + [any_place] * 5,
        out_shape=[
            jax.ShapeDtypeStruct((pieces, rows, model), F32), shape_of(1, model, F32),
            wide(model), wide(hidden), wide(hidden), wide(hidden), wide(model),
        ],
        scratch_shapes=[
            pltpu.VMEM((pieces, count, rows, model), LOW),
            pltpu.VMEM(wg.shape, LOW), pltpu.VMEM(wl.shape, LOW), pltpu.VMEM(wd.shape, LOW),
            room(model), room(model), room(hidden), room(hidden), room(hidden), room(model),
            pltpu.VMEM((count * rows, model), F32),
            pltpu.SemaphoreType.DMA((3,)), pltpu.SemaphoreType.DMA, pltpu.SemaphoreType.DMA((5,)),
        ]
        + line_scratch(pieces, count, rows, model, F32, True),
        compiler_params=params(collective_id=0, has_side_effects=True),
        cost_estimate=takes(128),
        name="middle",
    )(acted, tok, gain, wo, masked, wg, wl, wd)


def residual_kernel(
    pieces, count,
    dn_ref, middle_ref, masked_ref, gain_ref, residual_ref, r_ref,
    part_ref, own_ref, right_ref, left_ref, *sems,
):
    line = Line(
        pieces, count, part_ref, own_ref, right_ref, left_ref, sems,
        spread=lambda p, t: r_ref.at[p // 2, t, p % 2],
    )
    line.barrier()

    def begin(p):
        part_ref[...] = dn_ref[:, p]
        line.keep_own(p)

    def own(p):
        line.finish_own(p)
        x = middle_ref[p].astype(LOW).astype(F32)
        residual = masked_ref[p] + norm_back(own_ref[p], x, gain_ref[...])
        residual_ref[p] = residual
        r_ref[p // 2, line.place, p % 2] = residual.astype(LOW)
        line.hand_out(p)

    def turn_once(k, carry):
        both_ways(k, pieces, begin)
        for i in range(count - 1):
            both_ways(k, pieces, lambda p, i=i: line.send_sums(p, count - 1 - i))
            if i == 0:
                both_ways(k - 1, pieces, own)
            else:
                both_ways(k - 1, pieces, lambda p, i=i: line.hand_on(p, i))
        both_ways(k - 1, pieces, lambda p: line.hand_on(p, count - 1))
        return carry

    lax.fori_loop(0, pieces + 1, turn_once, 0)
    line.drain()


def residual_step(dn, middle, masked, gain):
    count, pieces, rows, model = dn.shape
    return pl.pallas_call(
        functools.partial(residual_kernel, pieces, count),
        in_specs=[WHOLE] * 4,
        out_specs=[WHOLE] * 2,
        out_shape=[
            jax.ShapeDtypeStruct((pieces, rows, model), F32),
            jax.ShapeDtypeStruct((pieces // 2, count, 2, rows, model), LOW),
        ],
        scratch_shapes=line_scratch(pieces, count, rows, model, LOW, True),
        compiler_params=params(collective_id=1, has_side_effects=True),
        cost_estimate=takes(10),
        name="residual",
    )(dn, middle, masked, gain)


def input_kernel(
    pieces, count,
    dn_ref, tok_ref, residual_ref, gain_ref, grad_ref,
    part_ref, own_ref, right_ref, left_ref, *sems,
):
    line = Line(pieces, count, part_ref, own_ref, right_ref, left_ref, sems)
    line.barrier()

    def begin(p):
        part_ref[...] = dn_ref[p // 2, :, p % 2]
        line.keep_own(p)

    def own(p):
        line.finish_own(p)
        x = tok_ref[p].astype(F32)
        grad_ref[p] = residual_ref[p] + norm_back(own_ref[p], x, gain_ref[...])

    def turn_once(k, carry):
        both_ways(k, pieces, begin)
        for i in range(count - 1):
            both_ways(k, pieces, lambda p, i=i: line.send_sums(p, count - 1 - i))
            if i == 0:
                both_ways(k - 1, pieces, own)
        return carry

    lax.fori_loop(0, pieces + 1, turn_once, 0)
    line.drain()


def input_step(dn, tok, residual, gain):
    batch, count, halves, rows, model = dn.shape
    pieces = batch * halves
    return pl.pallas_call(
        functools.partial(input_kernel, pieces, count),
        in_specs=[WHOLE] * 4,
        out_specs=WHOLE,
        out_shape=jax.ShapeDtypeStruct((pieces, rows, model), F32),
        scratch_shapes=line_scratch(pieces, count, rows, model, LOW, False),
        compiler_params=params(collective_id=2, has_side_effects=True),
        cost_estimate=takes(110),
        name="input_grad",
    )(dn, tok, residual, gain)


def flipped(place, mask):
    bit = 1
    while bit <= mask:
        if mask & bit:
            place = place + (1 - 2 * (place // bit % 2)) * bit
        bit *= 2
    return place


def digit_orders(count, batch):
    upper = [1 << i for i in range(1, count.bit_length() - 1)]
    return [(upper if b % 2 == 0 else upper[::-1]) + [1] for b in range(batch)]


def greet(place, digits):
    sem = pltpu.get_barrier_semaphore()
    for digit in digits:
        pl.semaphore_signal(sem, inc=1, device_id={"seq": flipped(place, digit)}, device_id_type=MESH)
    pl.semaphore_wait(sem, len(digits))


def gather_kernel(count, batch, *refs):
    own, out = refs[:batch], refs[batch : 2 * batch]
    local_sem, send_sem, receive_sem = refs[2 * batch :]
    place = lax.axis_index("seq")
    orders = digit_orders(count, batch)
    greet(place, orders[0])
    local = [pltpu.make_async_copy(own[b], out[b].at[place], local_sem.at[b]) for b in range(batch)]
    for copy in local:
        copy.start()

    def block(b, mask):
        return out[b].at[flipped(place, mask)]

    def send(b, mask, step):
        digit = orders[b][step]
        return pltpu.make_async_remote_copy(
            src_ref=own[b] if mask == 0 else block(b, mask),
            dst_ref=block(b, mask),
            send_sem=send_sem.at[b, step, mask],
            recv_sem=receive_sem.at[b, mask | digit],
            device_id={"seq": flipped(place, digit)},
            device_id_type=MESH,
        )

    def arrival(b, mask):
        return pltpu.make_async_remote_copy(
            src_ref=block(b, mask),
            dst_ref=block(b, mask),
            send_sem=send_sem.at[b, 0, mask],
            recv_sem=receive_sem.at[b, mask],
            device_id={"seq": flipped(place, mask)},
            device_id_type=MESH,
        )

    steps = len(orders[0])
    started = []
    for level in range(-1, steps):
        masks = [0] if level < 0 else range(1 << level)
        for turn in masks:
            for b in range(batch):
                mask = 0
                if level >= 0:
                    mask = orders[b][level]
                    for i in range(level):
                        if turn >> i & 1:
                            mask |= orders[b][i]
                    arrival(b, mask).wait_recv()
                for step in range(level + 1, steps):
                    copy = send(b, mask, step)
                    copy.start()
                    started.append(copy)
    for copy in started:
        copy.wait_send()
    for copy in local:
        copy.wait()


def gather_blocks(own):
    count, batch = lax.axis_size("seq"), len(own)
    rows, columns = own[0].shape
    steps = count.bit_length() - 1
    any_place = pl.BlockSpec(memory_space=pl.ANY)
    return pl.pallas_call(
        functools.partial(gather_kernel, count, batch),
        in_specs=[any_place] * batch,
        out_specs=[any_place] * batch,
        out_shape=[jax.ShapeDtypeStruct((count, rows, columns), LOW)] * batch,
        scratch_shapes=[
            pltpu.SemaphoreType.DMA((batch,)),
            pltpu.SemaphoreType.DMA((batch, steps, count)),
            pltpu.SemaphoreType.DMA((batch, count)),
        ],
        compiler_params=params(collective_id=3, has_side_effects=True),
        cost_estimate=takes(41),
        name="gather_blocks",
    )(*own)


def block_sums(count, batch, parts, out, slots, send_sem, receive_sem):
    place = lax.axis_index("seq")
    orders = [order[::-1] for order in digit_orders(count, batch)]
    steps = len(orders[0])

    def masks_at(b, step):
        found = [0]
        for digit in orders[b][step + 1 :][::-1]:
            found = [mask | digit for mask in found] + found
        return found

    numbers = {}
    for b in range(batch):
        place_in = 0
        for step in range(steps):
            for mask in masks_at(b, step):
                numbers[b, step, mask] = place_in
                place_in += 1

    def slot(b, step, mask):
        return slots.at[b, numbers[b, step, mask]]

    def transfer(b, step, mask):
        digit = orders[b][step]
        number = numbers[b, step, mask]
        if step == 0:
            source = parts[b].at[flipped(place, mask | digit)]
        else:
            source = slot(b, step - 1, mask | digit)
        return pltpu.make_async_remote_copy(
            src_ref=source,
            dst_ref=slots.at[b, number],
            send_sem=send_sem.at[b, number],
            recv_sem=receive_sem.at[b, number],
            device_id={"seq": flipped(place, digit)},
            device_id_type=MESH,
        )

    started = []

    def begin():
        for turn in range(count // 2):
            for b in range(batch):
                copy = transfer(b, 0, masks_at(b, 0)[turn])
                copy.start()
                started.append(copy)

    def take(b, step, mask):
        transfer(b, step, mask).wait_recv()
        held = parts[b].at[flipped(place, mask)] if step == 0 else slot(b, step - 1, mask)
        total = held[...].astype(F32) + slot(b, step, mask)[...].astype(F32)
        if step == steps - 1:
            out[b][...] = total.astype(LOW)
        else:
            slot(b, step, mask)[...] = total.astype(LOW)
            if mask & orders[b][step + 1]:
                copy = transfer(b, step + 1, mask & ~orders[b][step + 1])
                copy.start()
                started.append(copy)

    events = [begin]
    for step in range(steps):
        for turn in range(len(masks_at(0, step))):
            for b in range(batch):
                events.append(functools.partial(take, b, step, masks_at(b, step)[turn]))

    def drain():
        for copy in started:
            copy.wait_send()

    return events, drain


def interleaved(first, second):
    taken = 0
    for i, call in enumerate(first):
        call()
        due = (i + 1) * len(second) // len(first)
        while taken < due:
            second[taken]()
            taken += 1


def scatter_kernel(pieces, count, seq_count, batch, *refs):
    parts, refs = refs[:batch], refs[batch:]
    hidden_hbm, wd_hbm, middle_ref, valid_ref = refs[:4]
    out, output_ref = refs[4 : 4 + batch], refs[4 + batch]
    (
        wd_ref, hidden_ref, load_sem, hidden_sem, slots, send_sem, receive_sem,
        part_ref, own_ref, right_ref, left_ref, *sems,
    ) = refs[5 + batch :]
    rows, model = own_ref.shape[1], own_ref.shape[2]
    tall = count * rows
    line = Line(pieces, count, part_ref, own_ref, right_ref, left_ref, sems)
    load = pltpu.make_async_copy(wd_hbm, wd_ref, load_sem)

    def hidden_copy(p):
        return pltpu.make_async_copy(hidden_hbm.at[:, p], hidden_ref.at[p % 2], hidden_sem.at[p % 2])

    load.start()
    hidden_copy(0).start()
    line.barrier(digit_orders(seq_count, batch)[0])
    events, drain = block_sums(seq_count, batch, parts, out, slots, send_sem, receive_sem)

    def begin(p):
        if p == 0:
            load.wait()
        if p + 1 < pieces:
            hidden_copy(p + 1).start()
        hidden_copy(p).wait()
        hidden = hidden_ref[p % 2].reshape(tall, hidden_ref.shape[-1])
        part_ref[...] = mm(hidden, wd_ref[...]).reshape(count, rows, model)
        line.keep_own(p)

    def own(p):
        line.finish_own(p)
        output_ref[p] = (valid_ref[p] * (middle_ref[p] + own_ref[p])).astype(LOW)

    steps = []
    for k in range(pieces + 1):
        for i in range(count - 1):
            if i == 0 and k < pieces:
                steps.append(functools.partial(begin, k))
            if k < pieces:
                steps.append(functools.partial(line.send_sums, k, count - 1 - i))
            if i == 0 and k > 0:
                steps.append(functools.partial(own, k - 1))
    events[0]()
    interleaved(steps, events[1:])
    drain()
    line.drain()


def scatter_blocks(parts, hidden, wd, middle, valid):
    seq_count, batch = lax.axis_size("seq"), len(parts)
    rows, columns = parts[0].shape[0] // seq_count, parts[0].shape[1]
    count, pieces, piece_rows, units = hidden.shape
    model = wd.shape[1]
    any_place = pl.BlockSpec(memory_space=pl.ANY)
    *sums, output = pl.pallas_call(
        functools.partial(scatter_kernel, pieces, count, seq_count, batch),
        in_specs=[WHOLE] * batch + [any_place, any_place, WHOLE, WHOLE],
        out_specs=[WHOLE] * (batch + 1),
        out_shape=[shape_of(rows, columns, LOW)] * batch
        + [jax.ShapeDtypeStruct((pieces, piece_rows, model), LOW)],
        scratch_shapes=[
            pltpu.VMEM(wd.shape, LOW),
            pltpu.VMEM((2, count, piece_rows, units), LOW),
            pltpu.SemaphoreType.DMA,
            pltpu.SemaphoreType.DMA((2,)),
            pltpu.VMEM((batch, seq_count - 1, rows, columns), LOW),
            pltpu.SemaphoreType.DMA((batch, seq_count - 1)),
            pltpu.SemaphoreType.DMA((batch, seq_count - 1)),
        ]
        + line_scratch(pieces, count, piece_rows, model, F32, False),
        compiler_params=params(collective_id=4, has_side_effects=True),
        cost_estimate=takes(10),
        name="scatter_blocks",
    )(*[part.reshape(seq_count, rows, columns) for part in parts], hidden, wd, middle, valid)
    return sums, output


def turn_tables(positions, head_dim):
    half_dim = head_dim // 2
    inverse = THETA ** (-(jnp.arange(half_dim, dtype=F32) * 2.0) / head_dim)
    angles = positions.astype(F32)[:, None] * inverse[None, :]
    cosine, sine = jnp.cos(angles), jnp.sin(angles)
    return jnp.concatenate([cosine, cosine], axis=1), jnp.concatenate([-sine, sine], axis=1)


def norm_back(grad, values, gain):
    inverse = inverse_rms(values)
    grad = grad * gain
    mean = jnp.mean(grad * values, axis=-1, keepdims=True)
    return inverse * (grad - values * (inverse * inverse * mean))


def gather(value, axis):
    return lax.all_gather(value, axis, axis=0, tiled=True)


def scatter(value, axis):
    return lax.psum_scatter(value, axis, scatter_dimension=0, tiled=True)


def on_device(
    tokens, cotangent, lengths,
    query_weight, key_weight, value_weight, gating_weight, output_weight,
    swiglu_gate, swiglu_lift, swiglu_down,
    input_gain, middle_gain, query_gain, key_gain,
):
    block_index = lax.axis_index("seq")
    part_index = lax.axis_index("head")
    parts = lax.axis_size("head")
    local_rows, batch, model = tokens.shape
    head_dim = query_gain.shape[0]
    block_rows = local_rows * parts
    group = query_weight.shape[1] // key_weight.shape[1]
    nq, nk = query_weight.shape[1], key_weight.shape[1]
    query_start = block_index * block_rows
    positions = query_start + jnp.arange(block_rows, dtype=jnp.int32)
    cosine, sine = turn_tables(positions, head_dim)
    gain_in, gain_mid = input_gain[None, :], middle_gain[None, :]
    gain_q, gain_k = query_gain[None, :], key_gain[None, :]
    local_pos = query_start + part_index * local_rows + jnp.arange(local_rows, dtype=jnp.int32)
    seqs = range(batch)
    places = [jnp.stack([query_start, lengths[b]]).astype(jnp.int32) for b in seqs]
    valid = [(local_pos < lengths[b]).astype(F32)[:, None] for b in seqs]
    own = [tokens[:, b, :] for b in seqs]
    own_masked = [valid[b] * cotangent[:, b, :].astype(F32) for b in seqs]

    rows_in = [gather(own[b], "head") for b in seqs]
    projected = [
        project(
            rows_in[b], gain_in, cosine, sine, gain_q, gain_k,
            query_weight, key_weight, value_weight, gating_weight,
        )
        for b in seqs
    ]
    normed, qraw, q, kraw, kv_own, gate = [list(x) for x in zip(*projected)]
    kv = [x.reshape(-1, 2 * nk) for x in gather_blocks(kv_own)]
    masked = gather(jnp.concatenate([x.astype(LOW) for x in own_masked], axis=0), "head")
    attended = [attend(places[b], q[b], kv[b], gate[b], group, head_dim) for b in seqs]
    att, acted, inv = [list(x) for x in zip(*attended)]
    halves = 2
    rows = local_rows // halves
    pieces = batch * halves
    acted_all = jnp.stack(acted).reshape(batch, parts, halves, rows, nq)
    tok = jnp.stack(own).reshape(pieces, rows, model)
    masked_own = jnp.stack(own_masked).reshape(pieces, rows, model)
    middle, dgain_mid, normed_mid, hidden, dg, dl, dn_mid = middle_step(
        acted_all, tok, gain_mid, output_weight,
        masked.reshape(parts, pieces, rows, model), swiglu_gate, swiglu_lift, swiglu_down, parts,
    )
    flat_rows = block_rows * batch

    def flat(array):
        return array.reshape(flat_rows, array.shape[-1])

    normed_mid, hidden, dg, dl = flat(normed_mid), flat(hidden), flat(dg), flat(dl)
    ff_grads = (
        t_mm(normed_mid, dg).astype(LOW),
        t_mm(normed_mid, dl).astype(LOW),
        t_mm(hidden, masked).astype(LOW),
    )
    dn_mid, ff_grads = lax.optimization_barrier((dn_mid, ff_grads))
    ff_grads = lax.psum(ff_grads, "seq")
    residual, r_all = residual_step(dn_mid, middle, masked_own, gain_mid)
    r_all = r_all.reshape(batch, block_rows, model)
    r = [r_all[b] for b in seqs]
    back = [
        attend_back(places[b], q[b], kv[b], r[b], output_weight, att[b], gate[b], inv[b], group, head_dim)
        for b in seqs
    ]
    dq, dkv_all, dgate = [list(x) for x in zip(*back)]
    dkv, output = scatter_blocks(
        dkv_all,
        hidden.reshape(parts, pieces, rows, -1),
        swiglu_down,
        middle,
        jnp.stack(valid).reshape(pieces, rows, 1),
    )
    output = jnp.transpose(output.reshape(batch, local_rows, model), (1, 0, 2))
    last = [
        unproject(
            rows_in[b], gain_in, cosine, sine, gain_q, gain_k,
            query_weight, key_weight, value_weight, gating_weight,
            dq[b], qraw[b], dkv[b], kraw[b], dgate[b],
        )
        for b in seqs
    ]
    dall, dn_in, dgain_in, dgain_q, dgain_k = [list(x) for x in zip(*last)]
    def both(pair):
        return jnp.concatenate(pair, axis=0)

    ff_sums, dall = lax.optimization_barrier((ff_grads, dall))
    out_grad = t_mm(both(acted), r_all.reshape(flat_rows, model)).astype(LOW)
    proj_grad = t_mm(both(normed), both(dall)).astype(LOW)
    out_grad, proj_grad = lax.psum((out_grad, proj_grad), "seq")
    input_grad = input_step(
        jnp.stack(dn_in).reshape(batch, parts, halves, rows, model), tok, residual, gain_in
    )
    input_grad, ff_sums = lax.optimization_barrier((input_grad, ff_sums))
    ff_sums = [x.astype(F32) for x in ff_sums]
    input_grad = jnp.transpose(input_grad.reshape(batch, local_rows, model), (1, 0, 2))

    gains = jnp.concatenate(
        [sum(dgain_in)[0], dgain_mid[0], sum(dgain_q)[0], sum(dgain_k)[0]]
    )
    ff_sums, gains = lax.optimization_barrier((ff_sums, gains))
    gains = lax.psum(gains, ("seq", "head"))

    def share(start, width):
        piece = width // parts
        return lax.dynamic_slice(gains, (start + part_index * piece,), (piece,))

    return (
        output,
        input_grad,
        proj_grad[:, :nq].astype(F32),
        proj_grad[:, nq : nq + nk].astype(F32),
        proj_grad[:, nq + nk : nq + 2 * nk].astype(F32),
        proj_grad[:, nq + 2 * nk :].astype(F32),
        out_grad.astype(F32),
        ff_sums[0],
        ff_sums[1],
        ff_sums[2],
        share(0, model),
        share(model, model),
        share(2 * model, head_dim),
        share(2 * model + head_dim, head_dim),
    )


def solution(mesh):
    return jax.shard_map(
        on_device,
        mesh=mesh,
        in_specs=(
            P(("seq", "head"), None, None),
            P(("seq", "head"), None, None),
            P(),
            P(None, "head"),
            P(None, "head"),
            P(None, "head"),
            P(None, "head"),
            P("head", None),
            P(None, "head"),
            P(None, "head"),
            P("head", None),
            P(),
            P(),
            P(),
            P(),
        ),
        out_specs=(
            P(("seq", "head"), None, None),
            P(("seq", "head"), None, None),
            P(None, "head"),
            P(None, "head"),
            P(None, "head"),
            P(None, "head"),
            P("head", None),
            P(None, "head"),
            P(None, "head"),
            P("head", None),
            P("head"),
            P("head"),
            P("head"),
            P("head"),
        ),
        check_vma=False,
    )
```

```python
import functools

import jax
import jax.numpy as jnp
from jax import lax
from jax.experimental import pallas as pl
from jax.experimental.pallas import tpu as pltpu
from jax.sharding import PartitionSpec as P

EPS = 1e-06
THETA = 1000000.0
LOG2E = 1.4426950408889634
VMEM_LIMIT = 58 * 1024 * 1024
LOW = jnp.bfloat16
F32 = jnp.float32
MESH = pl.DeviceIdType.MESH


def mm(left, right):
    return jnp.dot(left, right, preferred_element_type=F32)


def mm_t(left, right):
    return lax.dot_general(left, right, (((1,), (1,)), ((), ())), preferred_element_type=F32)


def t_mm(left, right):
    return lax.dot_general(left, right, (((0,), (0,)), ((), ())), preferred_element_type=F32)


def shape_of(rows, columns, kind):
    return jax.ShapeDtypeStruct((rows, columns), kind)


def params(**extra):
    return pltpu.CompilerParams(vmem_limit_bytes=VMEM_LIMIT, **extra)


def takes(microseconds):
    return pl.CostEstimate(
        flops=int(microseconds * 1.15e9), bytes_accessed=int(microseconds * 3.69e6), transcendentals=0
    )


WHOLE = pl.BlockSpec(memory_space=pltpu.VMEM)
SCALARS = pl.BlockSpec(memory_space=pltpu.SMEM)


def full_block(array):
    return pl.BlockSpec(array.shape, lambda i: (0,) * len(array.shape))


def inverse_rms(values):
    return lax.rsqrt(jnp.mean(values * values, axis=-1, keepdims=True) + EPS)


def turn(values, cosine, sine):
    return values * cosine + pltpu.roll(values, values.shape[-1] // 2, 1) * sine


def turn_back(grads, cosine, sine):
    return grads * cosine + pltpu.roll(grads * sine, grads.shape[-1] // 2, 1)


def live_blocks(place_ref, rows):
    start, length = place_ref[0], place_ref[1 + pl.program_id(0)]
    whole = jnp.minimum(start // rows, length // rows)
    end = jnp.minimum(start // rows + 1, (length + rows - 1) // rows)
    end = jnp.where(start < length, end, 0)
    return jnp.minimum(whole, end), end, start, length


def attend_kernel(
    group, head_dim, place_ref, q_ref, kv_ref, gate_ref, att_ref, acted_ref, inv_ref, acc_ref, sum_ref
):
    rows = q_ref.shape[1]
    heads = q_ref.shape[2] // head_dim
    kv_heads = heads // group
    factor = head_dim ** (-0.5) * LOG2E
    acc_ref[...] = jnp.zeros_like(acc_ref)
    sum_ref[...] = jnp.zeros_like(sum_ref)
    whole, end, start, length = live_blocks(place_ref, rows)

    def one_block(j, masked):
        span = pl.ds(pl.multiple_of(j * rows, rows), rows)
        if masked:
            key_pos = j * rows + lax.broadcasted_iota(jnp.int32, (rows, rows), 1)
            query_pos = start + lax.broadcasted_iota(jnp.int32, (rows, rows), 0)
            allowed = (key_pos <= query_pos) & (key_pos < length)
        for h in range(heads):
            c = h // group
            keys = kv_ref[0, span, c * head_dim : (c + 1) * head_dim]
            values = kv_ref[0, span, (kv_heads + c) * head_dim : (kv_heads + c + 1) * head_dim]
            weights = jnp.exp2(mm_t(q_ref[0, :, h * head_dim : (h + 1) * head_dim], keys) * factor)
            if masked:
                weights = jnp.where(allowed, weights, 0.0)
            total = weights[:, :128]
            for piece in range(1, rows // 128):
                total = total + weights[:, piece * 128 : (piece + 1) * 128]
            sum_ref[h] = sum_ref[h] + total
            acc_ref[h] = acc_ref[h] + mm(weights.astype(LOW), values)

    def plain(j, carry):
        one_block(j, False)
        return carry

    def edge(j, carry):
        one_block(j, True)
        return carry

    lax.fori_loop(0, whole, plain, 0)
    lax.fori_loop(whole, end, edge, 0)
    lane = lax.broadcasted_iota(jnp.int32, inv_ref.shape[1:], 1)
    kept = jnp.zeros(inv_ref.shape[1:], F32)
    for h in range(heads):
        total = jnp.sum(sum_ref[h], axis=1, keepdims=True)
        inverse = 1.0 / jnp.where(total > 0.0, total, 1.0)
        attended = acc_ref[h] * inverse
        columns = slice(h * head_dim, (h + 1) * head_dim)
        att_ref[0, :, columns] = attended
        acted_ref[0, :, columns] = (attended * jax.nn.sigmoid(gate_ref[0, :, columns])).astype(LOW)
        kept = jnp.where(lane == h, inverse, kept)
    inv_ref[0] = kept


def by_sequence(array):
    return pl.BlockSpec((1,) + array.shape[1:], lambda b: (b,) + (0,) * (len(array.shape) - 1))


def attend(place, q, kv, gate, group, head_dim):
    batch, rows, width = q.shape
    heads = width // head_dim
    outs = [
        jax.ShapeDtypeStruct((batch, rows, width), F32),
        jax.ShapeDtypeStruct((batch, rows, width), LOW),
        jax.ShapeDtypeStruct((batch, rows, 128), F32),
    ]
    return pl.pallas_call(
        functools.partial(attend_kernel, group, head_dim),
        grid=(batch,),
        in_specs=[SCALARS, by_sequence(q), by_sequence(kv), by_sequence(gate)],
        out_specs=[by_sequence(x) for x in outs],
        out_shape=outs,
        scratch_shapes=[
            pltpu.VMEM((heads, rows, head_dim), F32),
            pltpu.VMEM((heads, rows, 128), F32),
        ],
        compiler_params=params(),
        cost_estimate=takes(18),
        name="attend",
    )(place, q, kv, gate)


def norm_turn_back(grad, raw, head_gain, cosine, sine):
    grad = turn_back(grad, cosine, sine)
    inverse = inverse_rms(raw)
    gain_grad = jnp.sum(grad * raw * inverse, axis=0, keepdims=True)
    grad = grad * head_gain
    mean = jnp.mean(grad * raw, axis=-1, keepdims=True)
    return inverse * (grad - raw * (inverse * inverse * mean)), gain_grad


def attend_back_kernel(
    group, head_dim,
    place_ref, q_ref, kv_ref, r_ref, wo_ref, att_ref, gate_ref, inv_ref, qraw_ref, cos_ref, sin_ref, qgain_ref,
    dq_ref, dkv_ref, dgate_ref, dqgain_ref,
    scaled_ref, corr_ref, acc_ref,
):
    rows = q_ref.shape[1]
    heads = q_ref.shape[2] // head_dim
    kv_heads = heads // group
    scale = head_dim ** (-0.5)
    acted_grad = mm_t(r_ref[0], wo_ref[...])
    lane = lax.broadcasted_iota(jnp.int32, inv_ref.shape[1:], 1)
    kept = jnp.zeros(inv_ref.shape[1:], F32)
    for h in range(heads):
        columns = slice(h * head_dim, (h + 1) * head_dim)
        sigmoid = jax.nn.sigmoid(gate_ref[0, :, columns])
        attended = att_ref[0, :, columns]
        grad = acted_grad[:, columns]
        dgate_ref[0, :, columns] = (grad * attended * sigmoid * (1.0 - sigmoid)).astype(LOW)
        grad = grad * sigmoid
        inverse = inv_ref[0, :, h : h + 1]
        scaled_ref[:, columns] = (grad * inverse).astype(LOW)
        kept = jnp.where(
            lane == h, jnp.sum(grad * attended, axis=1, keepdims=True) * inverse, kept
        )
    corr_ref[...] = kept.T
    acc_ref[...] = jnp.zeros_like(acc_ref)
    whole, end, start, length = live_blocks(place_ref, rows)

    def one_block(j, masked):
        span = pl.ds(pl.multiple_of(j * rows, rows), rows)
        if masked:
            key_pos = j * rows + lax.broadcasted_iota(jnp.int32, (rows, rows), 0)
            query_pos = start + lax.broadcasted_iota(jnp.int32, (rows, rows), 1)
            allowed = (key_pos <= query_pos) & (key_pos < length)
        for c in range(kv_heads):
            key_columns = slice(c * head_dim, (c + 1) * head_dim)
            value_columns = slice((kv_heads + c) * head_dim, (kv_heads + c + 1) * head_dim)
            keys = kv_ref[0, span, key_columns]
            values = kv_ref[0, span, value_columns]
            dk = jnp.zeros((rows, head_dim), F32)
            dv = jnp.zeros((rows, head_dim), F32)
            for h in range(c * group, (c + 1) * group):
                columns = slice(h * head_dim, (h + 1) * head_dim)
                queries = q_ref[0, :, columns]
                scaled = scaled_ref[:, columns]
                weights = jnp.exp2(mm_t(keys, queries) * (scale * LOG2E))
                if masked:
                    weights = jnp.where(allowed, weights, 0.0)
                dv = dv + mm(weights.astype(LOW), scaled)
                score = (weights * (mm_t(values, scaled) - corr_ref[h : h + 1, :])).astype(LOW)
                dk = dk + mm(score, queries)
                acc_ref[h] = acc_ref[h] + t_mm(score, keys)
            dkv_ref[0, span, key_columns] = (dk * scale).astype(LOW)
            dkv_ref[0, span, value_columns] = dv.astype(LOW)

    def plain(j, carry):
        one_block(j, False)
        return carry

    def edge(j, carry):
        one_block(j, True)
        return carry

    def empty(j, carry):
        span = pl.ds(pl.multiple_of(j * rows, rows), rows)
        dkv_ref[0, span, :] = jnp.zeros((rows, dkv_ref.shape[2]), LOW)
        return carry

    lax.fori_loop(0, whole, plain, 0)
    lax.fori_loop(whole, end, edge, 0)
    lax.fori_loop(end, dkv_ref.shape[1] // rows, empty, 0)
    gain_total = jnp.zeros((1, head_dim), F32)
    for h in range(heads):
        columns = slice(h * head_dim, (h + 1) * head_dim)
        grad, gain_grad = norm_turn_back(
            acc_ref[h] * scale, qraw_ref[0, :, columns], qgain_ref[...], cos_ref[...], sin_ref[...]
        )
        dq_ref[0, :, columns] = grad.astype(LOW)
        gain_total = gain_total + gain_grad

    @pl.when(pl.program_id(0) == 0)
    def _():
        dqgain_ref[...] = gain_total

    @pl.when(pl.program_id(0) > 0)
    def _():
        dqgain_ref[...] = dqgain_ref[...] + gain_total


def attend_back(place, q, kv, r, wo, att, gate, inv, qraw, cosine, sine, qgain, group):
    batch, rows, width = q.shape
    head_dim = qgain.shape[1]
    heads = width // head_dim
    outs = [
        jax.ShapeDtypeStruct(q.shape, LOW),
        jax.ShapeDtypeStruct(kv.shape, LOW),
        jax.ShapeDtypeStruct(q.shape, LOW),
    ]
    line = pl.BlockSpec((1, head_dim), lambda b: (0, 0))
    return pl.pallas_call(
        functools.partial(attend_back_kernel, group, head_dim),
        grid=(batch,),
        in_specs=[SCALARS, by_sequence(q), by_sequence(kv), by_sequence(r), full_block(wo)]
        + [by_sequence(x) for x in (att, gate, inv, qraw)]
        + [full_block(x) for x in (cosine, sine, qgain)],
        out_specs=[by_sequence(x) for x in outs] + [line],
        out_shape=outs + [shape_of(1, head_dim, F32)],
        scratch_shapes=[
            pltpu.VMEM((rows, width), LOW),
            pltpu.VMEM((128, rows), F32),
            pltpu.VMEM((heads, rows, head_dim), F32),
        ],
        compiler_params=params(),
        cost_estimate=takes(3),
        name="attend_back",
    )(place, q, kv, r, wo, att, gate, inv, qraw, cosine, sine, qgain)


class Line:
    def __init__(self, pieces, count, part_ref, own_ref, right_ref, left_ref, sems, spread=None):
        self.sums = part_ref is not None
        self.pieces, self.count = pieces, count
        self.place = lax.axis_index("head")
        self.part_ref, self.own_ref = part_ref, own_ref
        self.right_ref, self.left_ref = right_ref, left_ref
        self.sems = sems
        self.spread = spread

    def barrier(self, digits=()):
        sem = pltpu.get_barrier_semaphore()
        place, count = self.place, self.count
        for digit in digits:
            partner = flipped(lax.axis_index("seq"), digit)
            pl.semaphore_signal(sem, inc=1, device_id={"seq": partner}, device_id_type=MESH)

        @pl.when(place > 0)
        def _():
            pl.semaphore_signal(sem, inc=1, device_id={"head": place - 1}, device_id_type=MESH)

        @pl.when(place < count - 1)
        def _():
            pl.semaphore_signal(sem, inc=1, device_id={"head": place + 1}, device_id_type=MESH)

        inside = (place > 0) & (place < count - 1)

        @pl.when(inside)
        def _():
            pl.semaphore_wait(sem, 2 + len(digits))

        @pl.when(jnp.logical_not(inside))
        def _():
            pl.semaphore_wait(sem, 1 + len(digits))

    def barrier_all(self, digits):
        sem = pltpu.get_barrier_semaphore()
        for digit in digits:
            partner = flipped(lax.axis_index("seq"), digit)
            pl.semaphore_signal(sem, inc=1, device_id={"seq": partner}, device_id_type=MESH)
        for distance in range(1, self.count):
            other = lax.rem(self.place + distance, self.count)
            pl.semaphore_signal(sem, inc=1, device_id={"head": other}, device_id_type=MESH)
        pl.semaphore_wait(sem, self.count - 1 + len(digits))

    def copy(self, ref, send, receive, p, t, step):
        return pltpu.make_async_remote_copy(
            src_ref=ref,
            dst_ref=ref,
            send_sem=self.sems[send].at[p, t],
            recv_sem=self.sems[receive].at[p, t],
            device_id={"head": jnp.clip(self.place + step, 0, self.count - 1)},
            device_id_type=MESH,
        )

    def sum_copy(self, p, t, step):
        ref = self.right_ref if step > 0 else self.left_ref
        base = 0 if step > 0 else 2
        return self.copy(ref.at[p, t], base, base + 1, p, t, step)

    def spread_copy(self, p, t, step):
        first = 4 if self.sums else 0
        return self.copy(self.spread(p, t), first if step > 0 else first + 1, first + 2, p, t, step)

    def send_sums(self, p, distance):
        place, count = self.place, self.count
        for step, ref in ((1, self.right_ref), (-1, self.left_ref)):
            t = place + step * distance
            first = place == (0 if step > 0 else count - 1)

            @pl.when((t >= 0) & (t < count))
            def _(t=t, step=step, ref=ref, first=first):
                @pl.when(first)
                def _():
                    ref[p, t] = self.part_ref[t].astype(LOW)

                @pl.when(jnp.logical_not(first))
                def _():
                    self.sum_copy(p, t, step).wait_recv()
                    ref[p, t] = (ref[p, t].astype(F32) + self.part_ref[t].astype(F32)).astype(LOW)

                self.sum_copy(p, t, step).start()

    def keep_own(self, p):
        self.own_ref[p] = self.part_ref[self.place].astype(F32)

    def finish_own(self, p):
        place, count = self.place, self.count
        for step, ref, inner in ((1, self.right_ref, place > 0), (-1, self.left_ref, place < count - 1)):

            @pl.when(inner)
            def _(step=step, ref=ref):
                self.sum_copy(p, place, step).wait_recv()
                self.own_ref[p] = self.own_ref[p] + ref[p, place].astype(F32)

    def hand_out(self, p):
        place, count = self.place, self.count

        @pl.when(place < count - 1)
        def _():
            self.spread_copy(p, place, 1).start()

        @pl.when(place > 0)
        def _():
            self.spread_copy(p, place, -1).start()

    def hand_on(self, p, distance):
        place, count = self.place, self.count
        for step, more in ((1, place < count - 1), (-1, place > 0)):
            t = place - step * distance

            @pl.when((t >= 0) & (t < count))
            def _(t=t, step=step, more=more):
                self.spread_copy(p, t, step).wait_recv()

                @pl.when(more)
                def _():
                    self.spread_copy(p, t, step).start()

    def drain(self):
        place, count = self.place, self.count

        def one(p, carry):
            for t in range(count):
                if self.sums:

                    @pl.when(t > place)
                    def _(t=t):
                        self.sum_copy(p, t, 1).wait_send()

                    @pl.when(t < place)
                    def _(t=t):
                        self.sum_copy(p, t, -1).wait_send()

                if self.spread is not None:

                    @pl.when((t <= place) & (place < count - 1))
                    def _(t=t):
                        self.spread_copy(p, t, 1).wait_send()

                    @pl.when((t >= place) & (place > 0))
                    def _(t=t):
                        self.spread_copy(p, t, -1).wait_send()

            return carry

        lax.fori_loop(0, self.pieces, one, 0)


def line_scratch(pieces, count, rows, model, part_kind, spread):
    slots = (pieces, count)
    scratch = [
        pltpu.VMEM((pieces, rows, model), F32),
        pltpu.VMEM((pieces, count, rows, model), LOW),
        pltpu.VMEM((pieces, count, rows, model), LOW),
    ] + [pltpu.SemaphoreType.DMA(slots)] * (7 if spread else 4)
    if part_kind is not None:
        scratch = [pltpu.VMEM((count, rows, model), part_kind)] + scratch
    return scratch


def both_ways(index, limit, body):
    @pl.when((index >= 0) & (index < limit))
    def _():
        body(index)


def front_kernel(
    pieces, count, head_dim,
    tok_ref, gain_ref, cos_ref, sin_ref, qgain_ref, kgain_ref, wq_ref, wk_ref, wv_ref, wg_ref,
    normed_ref, qraw_ref, q_ref, kraw_ref, kv_ref, gate_ref,
    all_ref, *sems,
):
    rows, model = tok_ref.shape[1], tok_ref.shape[2]
    tall = count * rows
    line = Line(pieces, count, None, None, None, None, sems, spread=lambda p, t: all_ref.at[p, t])
    line.barrier()
    for p in range(pieces):
        all_ref[p, line.place] = tok_ref[p]

    def project(p):
        b, half = p // 2, p % 2

        def keep(ref, value):
            ref[b, :, half] = value.astype(ref.dtype).reshape(count, rows, value.shape[-1])

        x = all_ref[p].reshape(tall, model).astype(F32)
        normed = (x * inverse_rms(x) * gain_ref[...]).astype(LOW)
        keep(normed_ref, normed)
        cosine = cos_ref[:, half].reshape(tall, head_dim)
        sine = sin_ref[:, half].reshape(tall, head_dim)

        def turned(raw, head_gain):
            parts = []
            for h in range(raw.shape[1] // head_dim):
                part = raw[:, h * head_dim : (h + 1) * head_dim]
                parts.append(turn(part * inverse_rms(part) * head_gain, cosine, sine).astype(LOW))
            return parts

        raw = mm(normed, wk_ref[...])
        keep(kraw_ref, raw)
        values = mm(normed, wv_ref[...]).astype(LOW)
        keep(kv_ref, jnp.concatenate(turned(raw, kgain_ref[...]) + [values], axis=1))
        raw = mm(normed, wq_ref[...])
        keep(qraw_ref, raw)
        keep(q_ref, jnp.concatenate(turned(raw, qgain_ref[...]), axis=1))
        keep(gate_ref, mm(normed, wg_ref[...]))

    def turn_once(k, carry):
        both_ways(k, pieces, line.hand_out)
        for distance in range(1, count):
            both_ways(k - 1, pieces, lambda p, d=distance: line.hand_on(p, d))
        both_ways(k - 1, pieces, project)
        return carry

    lax.fori_loop(0, pieces + 1, turn_once, 0)
    line.drain()


def front_step(tok, gain, cosine, sine, qgain, kgain, wq, wk, wv, wg, count):
    pieces, rows, model = tok.shape
    batch = pieces // 2
    head_dim = qgain.shape[1]
    nq, nk = wq.shape[1], wk.shape[1]

    def wide(columns, kind):
        return jax.ShapeDtypeStruct((batch, count, 2, rows, columns), kind)

    slots = (pieces, count)
    return pl.pallas_call(
        functools.partial(front_kernel, pieces, count, head_dim),
        in_specs=[WHOLE] * 10,
        out_specs=[WHOLE] * 6,
        out_shape=[
            wide(model, LOW), wide(nq, F32), wide(nq, LOW), wide(nk, F32), wide(2 * nk, LOW), wide(nq, F32)
        ],
        scratch_shapes=[pltpu.VMEM((pieces, count, rows, model), LOW)]
        + [pltpu.SemaphoreType.DMA(slots)] * 3,
        compiler_params=params(collective_id=2, has_side_effects=True),
        cost_estimate=takes(95),
        name="front",
    )(
        tok, gain, cosine.reshape(count, 2, rows, head_dim), sine.reshape(count, 2, rows, head_dim),
        qgain, kgain, wq, wk, wv, wg,
    )


def middle_kernel(
    pieces, count,
    acted_ref, tok_ref, gain_ref, wo_ref, masked_hbm, wg_hbm, wl_hbm, wd_hbm,
    middle_ref, dgain_ref, normed_hbm, hidden_hbm, dg_hbm, dl_hbm, dn_hbm,
    mid_ref, wg_ref, wl_ref, wd_ref, masked_ref, normed_ref, hidden_ref, dg_ref, dl_ref, dn_ref, acc_ref,
    load_sem, masked_sem, store_sem,
    part_ref, own_ref, right_ref, left_ref, *sems,
):
    rows, model = own_ref.shape[1], own_ref.shape[2]
    tall = count * rows
    hidden = wg_ref.shape[1]
    line = Line(
        pieces, count, part_ref, own_ref, right_ref, left_ref, sems, spread=lambda p, t: mid_ref.at[p, t]
    )
    place = line.place
    loads = [
        pltpu.make_async_copy(source, target, load_sem.at[i])
        for i, (source, target) in enumerate(((wg_hbm, wg_ref), (wl_hbm, wl_ref), (wd_hbm, wd_ref)))
    ]
    line.barrier()
    for load in loads:
        load.start()
    dgain_ref[...] = jnp.zeros_like(dgain_ref)
    tiles = 3
    tile = hidden // tiles

    def masked_copy(p):
        return pltpu.make_async_copy(masked_hbm.at[:, p], masked_ref, masked_sem)

    def stores(p):
        pairs = (
            (normed_ref, normed_hbm), (hidden_ref, hidden_hbm), (dg_ref, dg_hbm), (dl_ref, dl_hbm),
            (dn_ref, dn_hbm),
        )
        return [
            pltpu.make_async_copy(source, target.at[:, p], store_sem.at[i])
            for i, (source, target) in enumerate(pairs)
        ]

    def begin(p):
        acted = acted_ref[p // 2, :, p % 2].reshape(tall, acted_ref.shape[-1])
        part_ref[...] = mm(acted, wo_ref[...]).reshape(count, rows, model)
        line.keep_own(p)

    def own(p):
        line.finish_own(p)
        middle = own_ref[p] + tok_ref[p].astype(F32)
        middle_ref[p] = middle
        mid_ref[p, place] = middle.astype(LOW)
        line.hand_out(p)

    def units_begin(p):
        line.hand_on(p, count - 1)

        @pl.when(p > 0)
        def _():
            for store in stores(p - 1):
                store.wait()

        x = mid_ref[p].reshape(tall, model).astype(F32)
        normed = (x * inverse_rms(x) * gain_ref[...]).astype(LOW)
        normed_ref[...] = normed.reshape(count, rows, model)
        masked_copy(p).wait()

        @pl.when(p == 0)
        def _():
            for load in loads:
                load.wait()

    def units_tile(i):
        span = slice(i * tile, (i + 1) * tile)
        normed = normed_ref[...].reshape(tall, model)
        gate = mm(normed, wg_ref[:, span])
        lift = mm(normed, wl_ref[:, span])
        grad = mm_t(masked_ref[...].reshape(tall, model), wd_ref[span, :])
        sigmoid = jax.nn.sigmoid(gate)
        silu = gate * sigmoid
        lift_grad = (grad * silu).astype(LOW)
        gate_grad = (grad * lift * (sigmoid + silu * (1.0 - sigmoid))).astype(LOW)
        hidden_ref[:, :, span] = (silu * lift).astype(LOW).reshape(count, rows, tile)
        dg_ref[:, :, span] = gate_grad.reshape(count, rows, tile)
        dl_ref[:, :, span] = lift_grad.reshape(count, rows, tile)
        part = mm_t(gate_grad, wg_ref[:, span]) + mm_t(lift_grad, wl_ref[:, span])
        if i == 0:
            acc_ref[...] = part
        else:
            acc_ref[...] = acc_ref[...] + part

    def units_end(p):
        total = acc_ref[...]
        dn_ref[...] = total.astype(LOW).reshape(count, rows, model)
        x = mid_ref[p].reshape(tall, model).astype(F32)
        dgain_ref[...] = dgain_ref[...] + jnp.sum(total * x * inverse_rms(x), axis=0, keepdims=True)
        for store in stores(p):
            store.start()

        @pl.when(p < pieces - 1)
        def _():
            masked_copy(p + 1).start()

    masked_copy(0).start()

    def turn_once(k, carry):
        both_ways(k, pieces, begin)
        for i in range(max(tiles, count - 1)):
            if i < count - 1:
                both_ways(k, pieces, lambda p, i=i: line.send_sums(p, count - 1 - i))
            if i == 0:
                both_ways(k - 1, pieces, own)
                both_ways(k - 2, pieces, units_begin)
            elif i < count - 1:
                both_ways(k - 1, pieces, lambda p, i=i: line.hand_on(p, i))
            if i < tiles:
                both_ways(k - 2, pieces, lambda p, i=i: units_tile(i))
        both_ways(k - 2, pieces, units_end)
        return carry

    lax.fori_loop(0, pieces + 2, turn_once, 0)
    for store in stores(pieces - 1):
        store.wait()
    line.drain()


def middle_step(acted, tok, gain, wo, masked, wg, wl, wd, count):
    pieces, rows, model = tok.shape
    hidden = wg.shape[1]
    any_place = pl.BlockSpec(memory_space=pl.ANY)

    def wide(columns, kind=LOW):
        return jax.ShapeDtypeStruct((count, pieces, rows, columns), kind)

    def room(columns, kind=LOW):
        return pltpu.VMEM((count, rows, columns), kind)

    return pl.pallas_call(
        functools.partial(middle_kernel, pieces, count),
        in_specs=[WHOLE] * 4 + [any_place] * 4,
        out_specs=[WHOLE] * 2 + [any_place] * 5,
        out_shape=[
            jax.ShapeDtypeStruct((pieces, rows, model), F32), shape_of(1, model, F32),
            wide(model), wide(hidden), wide(hidden), wide(hidden), wide(model),
        ],
        scratch_shapes=[
            pltpu.VMEM((pieces, count, rows, model), LOW),
            pltpu.VMEM(wg.shape, LOW), pltpu.VMEM(wl.shape, LOW), pltpu.VMEM(wd.shape, LOW),
            room(model), room(model), room(hidden), room(hidden), room(hidden), room(model),
            pltpu.VMEM((count * rows, model), F32),
            pltpu.SemaphoreType.DMA((3,)), pltpu.SemaphoreType.DMA, pltpu.SemaphoreType.DMA((5,)),
        ]
        + line_scratch(pieces, count, rows, model, F32, True),
        compiler_params=params(collective_id=0, has_side_effects=True),
        cost_estimate=takes(128),
        name="middle",
    )(acted, tok, gain, wo, masked, wg, wl, wd)


def residual_kernel(
    pieces, count, halves,
    dn_ref, middle_ref, masked_ref, gain_ref, residual_ref, r_ref,
    part_ref, own_ref, right_ref, left_ref, *sems,
):
    line = Line(
        pieces, count, part_ref, own_ref, right_ref, left_ref, sems,
        spread=lambda p, t: r_ref.at[p // halves, t, p % halves],
    )
    line.barrier()

    def begin(p):
        part_ref[...] = dn_ref[:, p]
        line.keep_own(p)

    def own(p):
        line.finish_own(p)
        x = middle_ref[p].astype(LOW).astype(F32)
        residual = masked_ref[p] + norm_back(own_ref[p], x, gain_ref[...])
        residual_ref[p] = residual
        r_ref[p // halves, line.place, p % halves] = residual.astype(LOW)
        line.hand_out(p)

    def turn_once(k, carry):
        both_ways(k, pieces, begin)
        for i in range(count - 1):
            both_ways(k, pieces, lambda p, i=i: line.send_sums(p, count - 1 - i))
            if i == 0:
                both_ways(k - 1, pieces, own)
            else:
                both_ways(k - 1, pieces, lambda p, i=i: line.hand_on(p, i))
        both_ways(k - 1, pieces, lambda p: line.hand_on(p, count - 1))
        return carry

    lax.fori_loop(0, pieces + 1, turn_once, 0)
    line.drain()


def residual_step(dn, middle, masked, gain, batch):
    count, pieces, rows, model = dn.shape
    halves = pieces // batch
    return pl.pallas_call(
        functools.partial(residual_kernel, pieces, count, halves),
        in_specs=[WHOLE] * 4,
        out_specs=[WHOLE] * 2,
        out_shape=[
            jax.ShapeDtypeStruct((pieces, rows, model), F32),
            jax.ShapeDtypeStruct((batch, count, halves, rows, model), LOW),
        ],
        scratch_shapes=line_scratch(pieces, count, rows, model, LOW, True),
        compiler_params=params(collective_id=1, has_side_effects=True),
        cost_estimate=takes(10),
        name="residual",
    )(dn, middle, masked, gain)


def flipped(place, mask):
    bit = 1
    while bit <= mask:
        if mask & bit:
            place = place + (1 - 2 * (place // bit % 2)) * bit
        bit *= 2
    return place


def digit_orders(count, batch):
    upper = [1 << i for i in range(1, count.bit_length() - 1)]
    return [(upper if b % 2 == 0 else upper[::-1]) + [1] for b in range(batch)]


def greet(place, digits):
    sem = pltpu.get_barrier_semaphore()
    for digit in digits:
        pl.semaphore_signal(sem, inc=1, device_id={"seq": flipped(place, digit)}, device_id_type=MESH)
    pl.semaphore_wait(sem, len(digits))


def block_gathers(count, batch, out, sources, send_sem, receive_sem):
    place = lax.axis_index("seq")
    orders = digit_orders(count, batch)
    steps = len(orders[0])
    started = []

    def copy(b, mask, step):
        digit = orders[b][step]
        block = out(b).at[flipped(place, mask)]
        return pltpu.make_async_remote_copy(
            src_ref=sources(b) if mask == 0 else block,
            dst_ref=block,
            send_sem=send_sem.at[b, step, mask],
            recv_sem=receive_sem.at[b, mask | digit],
            device_id={"seq": flipped(place, digit)},
            device_id_type=MESH,
        )

    def pass_on(b, mask, first):
        for step in range(first, steps):
            one = copy(b, mask, step)
            one.start()
            started.append(one)

    def arrive(b, mask, level):
        block = out(b).at[flipped(place, mask)]
        pltpu.make_async_remote_copy(
            src_ref=block,
            dst_ref=block,
            send_sem=send_sem.at[b, 0, mask],
            recv_sem=receive_sem.at[b, mask],
            device_id={"seq": flipped(place, orders[b][level])},
            device_id_type=MESH,
        ).wait_recv()
        pass_on(b, mask, level + 1)

    begins = [functools.partial(pass_on, b, 0, 0) for b in range(batch)]
    arrivals = []
    for level in range(steps):
        for turn in range(1 << level):
            for b in range(batch):
                mask = orders[b][level]
                for i in range(level):
                    if turn >> i & 1:
                        mask |= orders[b][i]
                arrivals.append(functools.partial(arrive, b, mask, level))

    def drain():
        for one in started:
            one.wait_send()

    return begins, arrivals, drain


def gather_kernel(count, batch, own_ref, out_ref, local_sem, send_sem, receive_sem):
    place = lax.axis_index("seq")
    greet(place, digit_orders(count, 1)[0])
    local = [
        pltpu.make_async_copy(own_ref.at[b], out_ref.at[b, place], local_sem.at[b]) for b in range(batch)
    ]
    for copy in local:
        copy.start()
    begins, arrivals, drain = block_gathers(
        count, batch, lambda b: out_ref.at[b], lambda b: own_ref.at[b], send_sem, receive_sem
    )
    for event in begins + arrivals:
        event()
    drain()
    for copy in local:
        copy.wait()


def gather_blocks(own):
    batch, rows, columns = own.shape
    count = lax.axis_size("seq")
    steps = count.bit_length() - 1
    any_place = pl.BlockSpec(memory_space=pl.ANY)
    out = pl.pallas_call(
        functools.partial(gather_kernel, count, batch),
        in_specs=[any_place],
        out_specs=any_place,
        out_shape=jax.ShapeDtypeStruct((batch, count, rows, columns), LOW),
        scratch_shapes=[
            pltpu.SemaphoreType.DMA((batch,)),
            pltpu.SemaphoreType.DMA((batch, steps, count)),
            pltpu.SemaphoreType.DMA((batch, count)),
        ],
        compiler_params=params(collective_id=3, has_side_effects=True),
        cost_estimate=takes(41),
        name="gather_blocks",
    )(own)
    return out.reshape(batch, count * rows, columns)


def block_sums(count, batch, parts, finish, slots, send_sem, receive_sem):
    place = lax.axis_index("seq")
    orders = [order[::-1] for order in digit_orders(count, batch)]
    steps = len(orders[0])

    def masks_at(b, step):
        found = [0]
        for digit in orders[b][step + 1 :][::-1]:
            found = [mask | digit for mask in found] + found
        return found

    numbers = {}
    for b in range(batch):
        place_in = 0
        for step in range(steps):
            for mask in masks_at(b, step):
                numbers[b, step, mask] = place_in
                place_in += 1

    def slot(b, step, mask):
        return slots.at[b, numbers[b, step, mask]]

    def transfer(b, step, mask):
        digit = orders[b][step]
        number = numbers[b, step, mask]
        if step == 0:
            source = parts(b).at[flipped(place, mask | digit)]
        else:
            source = slot(b, step - 1, mask | digit)
        return pltpu.make_async_remote_copy(
            src_ref=source,
            dst_ref=slots.at[b, number],
            send_sem=send_sem.at[b, number],
            recv_sem=receive_sem.at[b, number],
            device_id={"seq": flipped(place, digit)},
            device_id_type=MESH,
        )

    started = []

    def begin():
        for turn in range(count // 2):
            for b in range(batch):
                copy = transfer(b, 0, masks_at(b, 0)[turn])
                copy.start()
                started.append(copy)

    def take(b, step, mask):
        transfer(b, step, mask).wait_recv()
        held = parts(b).at[flipped(place, mask)] if step == 0 else slot(b, step - 1, mask)
        total = held[...].astype(F32) + slot(b, step, mask)[...].astype(F32)
        if step == steps - 1:
            finish(b, total)
        else:
            slot(b, step, mask)[...] = total.astype(LOW)
            if mask & orders[b][step + 1]:
                copy = transfer(b, step + 1, mask & ~orders[b][step + 1])
                copy.start()
                started.append(copy)

    events = []
    for step in range(steps):
        for turn in range(len(masks_at(0, step))):
            for b in range(batch):
                events.append(functools.partial(take, b, step, masks_at(b, step)[turn]))

    def drain():
        for copy in started:
            copy.wait_send()

    return begin, events, drain


def interleaved(first, second):
    taken = 0
    for i, call in enumerate(first):
        call()
        due = (i + 1) * len(second) // len(first)
        while taken < due:
            second[taken]()
            taken += 1


def scatter_kernel(
    pieces, count, seq_count, batch, head_dim,
    parts_ref, hidden_hbm, wd_hbm, middle_ref, valid_ref, kraw_ref, cos_ref, sin_ref, kgain_ref,
    dkv_ref, output_ref, dkgain_ref,
    wd_ref, hidden_ref, load_sem, hidden_sem, slots, send_sem, receive_sem,
    part_ref, own_ref, right_ref, left_ref, *sems,
):
    rows, model = own_ref.shape[1], own_ref.shape[2]
    tall = count * rows
    keys = kraw_ref.shape[2]
    line = Line(pieces, count, part_ref, own_ref, right_ref, left_ref, sems)
    load = pltpu.make_async_copy(wd_hbm, wd_ref, load_sem)

    def hidden_copy(p):
        return pltpu.make_async_copy(hidden_hbm.at[:, p], hidden_ref.at[p % 2], hidden_sem.at[p % 2])

    load.start()
    hidden_copy(0).start()
    dkgain_ref[...] = jnp.zeros_like(dkgain_ref)
    line.barrier(digit_orders(seq_count, 1)[0])

    def finish(b, total):
        for h in range(keys // head_dim):
            columns = slice(h * head_dim, (h + 1) * head_dim)
            grad, gain_grad = norm_turn_back(
                total[:, columns], kraw_ref[b, :, columns], kgain_ref[...], cos_ref[...], sin_ref[...]
            )
            dkv_ref[b, :, columns] = grad.astype(LOW)
            dkgain_ref[...] = dkgain_ref[...] + gain_grad
        dkv_ref[b, :, keys:] = total[:, keys:].astype(LOW)

    first, events, drain = block_sums(
        seq_count, batch, lambda b: parts_ref.at[b], finish, slots, send_sem, receive_sem
    )

    def begin(p):
        if p == 0:
            load.wait()
        if p + 1 < pieces:
            hidden_copy(p + 1).start()
        hidden_copy(p).wait()
        hidden = hidden_ref[p % 2].reshape(tall, hidden_ref.shape[-1])
        part_ref[...] = mm(hidden, wd_ref[...]).reshape(count, rows, model)
        line.keep_own(p)

    def own(p):
        line.finish_own(p)
        output_ref[p] = (valid_ref[p] * (middle_ref[p] + own_ref[p])).astype(LOW)

    first()
    interleaved(line_steps(line, begin, own), events)
    drain()
    line.drain()


def line_steps(line, begin, own):
    steps = []
    for k in range(line.pieces + 1):
        for i in range(line.count - 1):
            if i == 0 and k < line.pieces:
                steps.append(functools.partial(begin, k))
            if k < line.pieces:
                steps.append(functools.partial(line.send_sums, k, line.count - 1 - i))
            if i == 0 and k > 0:
                steps.append(functools.partial(own, k - 1))
    return steps


def scatter_blocks(parts, hidden, wd, middle, valid, kraw, cosine, sine, kgain):
    seq_count, batch = lax.axis_size("seq"), parts.shape[0]
    rows, columns = parts.shape[1] // seq_count, parts.shape[2]
    count, pieces, piece_rows, units = hidden.shape
    model, head_dim = wd.shape[1], kgain.shape[1]
    any_place = pl.BlockSpec(memory_space=pl.ANY)
    return pl.pallas_call(
        functools.partial(scatter_kernel, pieces, count, seq_count, batch, head_dim),
        in_specs=[WHOLE, any_place, any_place] + [WHOLE] * 6,
        out_specs=[WHOLE] * 3,
        out_shape=[
            jax.ShapeDtypeStruct((batch, rows, columns), LOW),
            jax.ShapeDtypeStruct((pieces, piece_rows, model), LOW),
            shape_of(1, head_dim, F32),
        ],
        scratch_shapes=[
            pltpu.VMEM(wd.shape, LOW),
            pltpu.VMEM((2, count, piece_rows, units), LOW),
            pltpu.SemaphoreType.DMA,
            pltpu.SemaphoreType.DMA((2,)),
            pltpu.VMEM((batch, seq_count - 1, rows, columns), LOW),
            pltpu.SemaphoreType.DMA((batch, seq_count - 1)),
            pltpu.SemaphoreType.DMA((batch, seq_count - 1)),
        ]
        + line_scratch(pieces, count, piece_rows, model, F32, False),
        compiler_params=params(collective_id=4, has_side_effects=True),
        cost_estimate=takes(10),
        name="scatter_blocks",
    )(
        parts.reshape(batch, seq_count, rows, columns), hidden, wd, middle, valid, kraw, cosine, sine, kgain
    )


def last_kernel(
    pieces, count, seq_count, streams, halves,
    dq_ref, dkv_ref, dgate_ref, wq_ref, wk_ref, wv_ref, wg_ref, tok_ref, residual_ref, gain_ref,
    dmid_ref, dqgain_ref, dkgain_ref, *refs,
):
    grads, refs = refs[:streams], refs[streams:]
    input_ref, total_ref, sums = refs[0], refs[1], refs[2 : 2 + streams]
    (
        slots, scatter_send, scatter_receive, gather_send, gather_receive,
        dgain_ref, turns_ref, round_ref, mixed_ref, round_send, round_receive, mixed_send, mixed_receive,
        part_ref, own_ref, right_ref, left_ref, *sems,
    ) = refs[2 + streams :]
    rows, model = own_ref.shape[1], own_ref.shape[2]
    tall = count * rows
    place_seq = lax.axis_index("seq")
    digits = digit_orders(seq_count, 1)[0]
    line = Line(pieces, count, part_ref, own_ref, right_ref, left_ref, sems)
    line.barrier_all(digits)
    dgain_ref[...] = jnp.zeros_like(dgain_ref)

    begins, arrivals, gather_drain = block_gathers(
        seq_count, streams, lambda b: sums[b], lambda b: sums[b].at[place_seq], gather_send, gather_receive
    )

    def finish(b, total):
        sums[b][place_seq] = total.astype(LOW)
        begins[b]()

    first, events, scatter_drain = block_sums(
        seq_count, streams, lambda b: grads[b], finish, slots, scatter_send, scatter_receive
    )

    def begin(p):
        b, half = p // halves, p % halves
        dq = dq_ref[b, :, half].reshape(tall, dq_ref.shape[-1])
        dkv = dkv_ref[b, :, half].reshape(tall, dkv_ref.shape[-1])
        dgate = dgate_ref[b, :, half].reshape(tall, dgate_ref.shape[-1])
        nk = dkv.shape[1] // 2
        total = mm_t(dq, wq_ref[...]) + mm_t(dgate, wg_ref[...])
        total = total + mm_t(dkv[:, :nk], wk_ref[...]) + mm_t(dkv[:, nk:], wv_ref[...])
        part_ref[...] = total.reshape(count, rows, model)
        line.keep_own(p)

    def own(p):
        line.finish_own(p)
        x = tok_ref[p].astype(F32)
        grad = own_ref[p]
        inverse = inverse_rms(x)
        dgain_ref[...] = dgain_ref[...] + jnp.sum(grad * x * inverse, axis=0, keepdims=True)
        input_ref[p] = residual_ref[p] + norm_back(grad, x, gain_ref[...])

    first()
    interleaved(line_steps(line, begin, own), events + arrivals)

    width = model // count
    lines = width // 128
    turns_ref[0] = jnp.zeros(turns_ref.shape[1:], F32)
    for t in range(count):
        for i in range(lines):
            span = slice(t * width + i * 128, t * width + (i + 1) * 128)
            turns_ref[0, t, i : i + 1, :] = dgain_ref[:, span]
            turns_ref[0, t, lines + i : lines + i + 1, :] = dmid_ref[:, span]
        turns_ref[0, t, 2 * lines : 2 * lines + 1, :] = dqgain_ref[...]
        turns_ref[0, t, 2 * lines + 1 : 2 * lines + 2, :] = dkgain_ref[...]
    copies = []
    for i, digit in enumerate(digits):
        copy = pltpu.make_async_remote_copy(
            src_ref=turns_ref.at[i],
            dst_ref=round_ref.at[i],
            send_sem=round_send.at[i],
            recv_sem=round_receive.at[i],
            device_id={"seq": flipped(place_seq, digit)},
            device_id_type=MESH,
        )
        copy.start()
        copies.append(copy)
        copy.wait_recv()
        turns_ref[i + 1] = turns_ref[i] + round_ref[i]
    done = len(digits)
    for distance in range(1, count):
        other = lax.rem(line.place + distance, count)
        copy = pltpu.make_async_remote_copy(
            src_ref=turns_ref.at[done, other],
            dst_ref=mixed_ref.at[distance - 1],
            send_sem=mixed_send.at[distance - 1],
            recv_sem=mixed_receive.at[distance - 1],
            device_id={"head": other},
            device_id_type=MESH,
        )
        copy.start()
        copies.append(copy)
    total = turns_ref[done, line.place]
    for distance in range(1, count):
        copies[done + distance - 1].wait_recv()
        total = total + mixed_ref[distance - 1]
    total_ref[...] = total
    for copy in copies:
        copy.wait_send()
    scatter_drain()
    gather_drain()
    line.drain()


def last_step(dq, dkv, dgate, wq, wk, wv, wg, tok, residual, gain, dmid, dqgain, dkgain, grads):
    batch, count, halves, rows, nq = dq.shape
    pieces, model = batch * halves, wq.shape[0]
    seq_count, streams = lax.axis_size("seq"), len(grads)
    tall, columns = grads[0].shape
    block = tall // seq_count
    steps = seq_count.bit_length() - 1
    lines = 8 * ((2 * (model // count // 128) + 2 + 7) // 8)
    return pl.pallas_call(
        functools.partial(last_kernel, pieces, count, seq_count, streams, halves),
        in_specs=[WHOLE] * (13 + streams),
        out_specs=[WHOLE] * (2 + streams),
        out_shape=[jax.ShapeDtypeStruct((pieces, rows, model), F32), shape_of(lines, 128, F32)]
        + [jax.ShapeDtypeStruct((seq_count, block, columns), LOW)] * streams,
        scratch_shapes=[
            pltpu.VMEM((streams, seq_count - 1, block, columns), LOW),
            pltpu.SemaphoreType.DMA((streams, seq_count - 1)),
            pltpu.SemaphoreType.DMA((streams, seq_count - 1)),
            pltpu.SemaphoreType.DMA((streams, steps, seq_count)),
            pltpu.SemaphoreType.DMA((streams, seq_count)),
            pltpu.VMEM((1, model), F32),
            pltpu.VMEM((steps + 1, count, lines, 128), F32),
            pltpu.VMEM((steps, count, lines, 128), F32),
            pltpu.VMEM((count - 1, lines, 128), F32),
            pltpu.SemaphoreType.DMA((steps,)),
            pltpu.SemaphoreType.DMA((steps,)),
            pltpu.SemaphoreType.DMA((count - 1,)),
            pltpu.SemaphoreType.DMA((count - 1,)),
        ]
        + line_scratch(pieces, count, rows, model, F32, False),
        compiler_params=params(collective_id=5, has_side_effects=True),
        cost_estimate=takes(5),
        name="last",
    )(
        dq, dkv, dgate, wq, wk, wv, wg, tok, residual, gain, dmid, dqgain, dkgain,
        *[grad.reshape(seq_count, block, columns) for grad in grads],
    )


def widen_kernel(input_ref, dq_ref, dkv_ref, dgate_ref, out_ref, *refs):
    ff_refs, refs = refs[:3], refs[3:]
    input_out, dq_out, dk_out, dv_out, dgate_out, out_out, *ff_outs = refs
    keys = dk_out.shape[1]
    input_out[...] = jnp.stack([input_ref[b] for b in range(input_ref.shape[0])], axis=1)
    dq_out[...] = dq_ref[...].astype(F32)
    dk_out[...] = dkv_ref[:, :keys].astype(F32)
    dv_out[...] = dkv_ref[:, keys:].astype(F32)
    dgate_out[...] = dgate_ref[...].astype(F32)
    out_out[...] = out_ref[...].astype(F32).T
    for ref, out in zip(ff_refs, ff_outs):
        out[...] = ref[...].astype(F32)


def widen(input_grad, dq, dkv, dgate, out, ff, steps=8):
    batch, rows, model = input_grad.shape
    columns, keys = dq.shape[1], dkv.shape[1] // 2

    def tall(array):
        return pl.BlockSpec((array.shape[0] // steps, array.shape[1]), lambda i: (i, 0))

    def wide(array):
        return jax.ShapeDtypeStruct(array.shape, F32)

    outs = [
        jax.ShapeDtypeStruct((rows, batch, model), F32),
        wide(dq), shape_of(model, keys, F32), shape_of(model, keys, F32), wide(dgate), shape_of(columns, model, F32),
    ] + [wide(x) for x in ff]
    specs = [pl.BlockSpec((rows // steps, batch, model), lambda i: (i, 0, 0))]
    specs += [tall(x) for x in outs[1:5]]
    specs += [pl.BlockSpec((columns, model // steps), lambda i: (0, i))]
    specs += [tall(x) for x in ff]
    return pl.pallas_call(
        widen_kernel,
        grid=(steps,),
        in_specs=[pl.BlockSpec((batch, rows // steps, model), lambda i: (0, i, 0))]
        + [tall(x) for x in (dq, dkv, dgate, out, *ff)],
        out_specs=specs,
        out_shape=outs,
        compiler_params=params(),
        cost_estimate=takes(25),
        name="widen",
    )(input_grad, dq, dkv, dgate, out, *ff)


def turn_tables(positions, head_dim):
    half_dim = head_dim // 2
    inverse = THETA ** (-(jnp.arange(half_dim, dtype=F32) * 2.0) / head_dim)
    angles = positions.astype(F32)[:, None] * inverse[None, :]
    cosine, sine = jnp.cos(angles), jnp.sin(angles)
    return jnp.concatenate([cosine, cosine], axis=1), jnp.concatenate([-sine, sine], axis=1)


def norm_back(grad, values, gain):
    inverse = inverse_rms(values)
    grad = grad * gain
    mean = jnp.mean(grad * values, axis=-1, keepdims=True)
    return inverse * (grad - values * (inverse * inverse * mean))


def gather(value, axis):
    return lax.all_gather(value, axis, axis=0, tiled=True)


def on_device(
    tokens, cotangent, lengths,
    query_weight, key_weight, value_weight, gating_weight, output_weight,
    swiglu_gate, swiglu_lift, swiglu_down,
    input_gain, middle_gain, query_gain, key_gain,
):
    block_index = lax.axis_index("seq")
    part_index = lax.axis_index("head")
    parts = lax.axis_size("head")
    local_rows, batch, model = tokens.shape
    head_dim = query_gain.shape[0]
    block_rows = local_rows * parts
    flat_rows = block_rows * batch
    group = query_weight.shape[1] // key_weight.shape[1]
    nq, nk = query_weight.shape[1], key_weight.shape[1]
    halves = 2
    pieces, rows = batch * halves, local_rows // halves

    query_start = block_index * block_rows
    positions = query_start + jnp.arange(block_rows, dtype=jnp.int32)
    cosine, sine = turn_tables(positions, head_dim)
    gain_in, gain_mid = input_gain[None, :], middle_gain[None, :]
    gain_q, gain_k = query_gain[None, :], key_gain[None, :]
    local_pos = query_start + part_index * local_rows + jnp.arange(local_rows, dtype=jnp.int32)
    place = jnp.concatenate([query_start[None], lengths]).astype(jnp.int32)
    valid = (local_pos[None, :] < lengths[:, None]).astype(F32)[..., None]
    tok = jnp.transpose(tokens, (1, 0, 2)).reshape(pieces, rows, model)

    normed, qraw, q, kraw, kv_own, gate = [
        x.reshape(batch, block_rows, x.shape[-1])
        for x in front_step(
            tok, gain_in, cosine, sine, gain_q, gain_k,
            query_weight, key_weight, value_weight, gating_weight, parts,
        )
    ]
    kv_own, masked_own = lax.optimization_barrier(
        (kv_own, valid * jnp.transpose(cotangent, (1, 0, 2)).astype(F32))
    )
    kv = gather_blocks(kv_own)
    masked = gather(masked_own.astype(LOW).reshape(batch * local_rows, model), "head")
    att, acted, inv = attend(place, q, kv, gate, group, head_dim)
    middle, dgain_mid, normed_mid, hidden, dg, dl, dn_mid = middle_step(
        acted.reshape(batch, parts, halves, rows, nq), tok, gain_mid, output_weight,
        masked.reshape(parts, pieces, rows, model), swiglu_gate, swiglu_lift, swiglu_down, parts,
    )

    def flat(array):
        return array.reshape(flat_rows, array.shape[-1])

    normed_mid = flat(normed_mid)
    ff_grads = (
        t_mm(normed_mid, flat(dg)).astype(LOW),
        t_mm(normed_mid, flat(dl)).astype(LOW),
        t_mm(flat(hidden), masked).astype(LOW),
    )
    dn_mid, ff_grads = lax.optimization_barrier((dn_mid, ff_grads))
    ff_grads = lax.psum(ff_grads, "seq")
    residual, r = residual_step(
        dn_mid, middle, masked_own.reshape(pieces, rows, model), gain_mid, batch
    )
    r = r.reshape(batch, block_rows, model)
    dq, dkv_all, dgate, dgain_q = attend_back(
        place, q, kv, r, output_weight, att, gate, inv, qraw, cosine, sine, gain_q, group
    )
    dkv, output, dgain_k = scatter_blocks(
        dkv_all, hidden, swiglu_down, middle, valid.reshape(pieces, rows, 1), kraw, cosine, sine, gain_k
    )
    output = jnp.transpose(output.reshape(batch, local_rows, model), (1, 0, 2))
    grads = [
        t_mm(flat(normed), flat(dq)).astype(LOW),
        t_mm(flat(normed), flat(dkv)).astype(LOW),
        t_mm(flat(normed), flat(dgate)).astype(LOW),
        t_mm(flat(r), flat(acted)).astype(LOW),
    ]

    def pieced(array):
        return array.reshape(batch, parts, halves, rows, array.shape[-1])

    input_grad, gains, *grads = last_step(
        pieced(dq), pieced(dkv), pieced(dgate), query_weight, key_weight, value_weight, gating_weight,
        tok, residual, gain_in, dgain_mid, dgain_q, dgain_k, grads,
    )
    input_grad, dq_weight, dk_weight, dv_weight, dgate_weight, out_weight, *ff_sums = widen(
        input_grad.reshape(batch, local_rows, model), *[x.reshape(model, x.shape[-1]) for x in grads], ff_grads
    )
    share = model // parts
    lines = share // 128
    head_share = head_dim // parts

    def head_gain(line):
        return lax.dynamic_slice(gains[line], (part_index * head_share,), (head_share,))

    return (
        output,
        input_grad,
        dq_weight,
        dk_weight,
        dv_weight,
        dgate_weight,
        out_weight,
        *ff_sums,
        gains[:lines].reshape(share),
        gains[lines : 2 * lines].reshape(share),
        head_gain(2 * lines),
        head_gain(2 * lines + 1),
    )


def solution(mesh):
    return jax.shard_map(
        on_device,
        mesh=mesh,
        in_specs=(
            P(("seq", "head"), None, None),
            P(("seq", "head"), None, None),
            P(),
            P(None, "head"),
            P(None, "head"),
            P(None, "head"),
            P(None, "head"),
            P("head", None),
            P(None, "head"),
            P(None, "head"),
            P("head", None),
            P(),
            P(),
            P(),
            P(),
        ),
        out_specs=(
            P(("seq", "head"), None, None),
            P(("seq", "head"), None, None),
            P(None, "head"),
            P(None, "head"),
            P(None, "head"),
            P(None, "head"),
            P("head", None),
            P(None, "head"),
            P(None, "head"),
            P("head", None),
            P("head"),
            P("head"),
            P("head"),
            P("head"),
        ),
        check_vma=False,
    )
```

```python
import functools

import jax
import jax.numpy as jnp
from jax import lax
from jax.experimental import pallas as pl
from jax.experimental.pallas import tpu as pltpu
from jax.sharding import PartitionSpec as P

EPS = 1e-06
THETA = 1000000.0
LOG2E = 1.4426950408889634
MIB = 1024 * 1024
LOW = jnp.bfloat16
F32 = jnp.float32
MESH = pl.DeviceIdType.MESH


def mm(left, right):
    return jnp.dot(left, right, preferred_element_type=F32)


def mm_t(left, right):
    return lax.dot_general(left, right, (((1,), (1,)), ((), ())), preferred_element_type=F32)


def t_mm(left, right):
    return lax.dot_general(left, right, (((0,), (0,)), ((), ())), preferred_element_type=F32)


def shape_of(rows, columns, kind):
    return jax.ShapeDtypeStruct((rows, columns), kind)


def params(mib, **extra):
    return pltpu.CompilerParams(vmem_limit_bytes=mib * MIB, **extra)


def takes(microseconds):
    return pl.CostEstimate(
        flops=int(microseconds * 1.15e9), bytes_accessed=int(microseconds * 3.69e6), transcendentals=0
    )


WHOLE = pl.BlockSpec(memory_space=pltpu.VMEM)
SCALARS = pl.BlockSpec(memory_space=pltpu.SMEM)


def full_block(array):
    return pl.BlockSpec(array.shape, lambda i: (0,) * len(array.shape))


def inverse_rms(values):
    return lax.rsqrt(jnp.mean(values * values, axis=-1, keepdims=True) + EPS)


def turn(values, cosine, sine):
    return values * cosine + pltpu.roll(values, values.shape[-1] // 2, 1) * sine


def turn_back(grads, cosine, sine):
    return grads * cosine + pltpu.roll(grads * sine, grads.shape[-1] // 2, 1)


def live_blocks(place_ref, rows):
    start, length = place_ref[0], place_ref[1 + pl.program_id(0)]
    whole = jnp.minimum(start // rows, length // rows)
    end = jnp.minimum(start // rows + 1, (length + rows - 1) // rows)
    end = jnp.where(start < length, end, 0)
    return jnp.minimum(whole, end), end, start, length


def attend_kernel(
    group, head_dim, place_ref, q_ref, kv_ref, gate_ref, att_ref, acted_ref, inv_ref, acc_ref, sum_ref
):
    rows = q_ref.shape[1]
    heads = q_ref.shape[2] // head_dim
    kv_heads = heads // group
    factor = head_dim ** (-0.5) * LOG2E
    acc_ref[...] = jnp.zeros_like(acc_ref)
    sum_ref[...] = jnp.zeros_like(sum_ref)
    whole, end, start, length = live_blocks(place_ref, rows)

    def one_block(j, masked, width=1):
        tall = width * rows
        span = pl.ds(pl.multiple_of(j * rows, rows), tall)
        if masked:
            key_pos = j * rows + lax.broadcasted_iota(jnp.int32, (rows, rows), 1)
            query_pos = start + lax.broadcasted_iota(jnp.int32, (rows, rows), 0)
            allowed = (key_pos <= query_pos) & (key_pos < length)
        for h in range(heads):
            c = h // group
            keys = kv_ref[0, span, c * head_dim : (c + 1) * head_dim]
            values = kv_ref[0, span, (kv_heads + c) * head_dim : (kv_heads + c + 1) * head_dim]
            weights = jnp.exp2(mm_t(q_ref[0, :, h * head_dim : (h + 1) * head_dim], keys) * factor)
            if masked:
                weights = jnp.where(allowed, weights, 0.0)
            total = weights[:, :128]
            for piece in range(1, tall // 128):
                total = total + weights[:, piece * 128 : (piece + 1) * 128]
            sum_ref[h] = sum_ref[h] + total
            acc_ref[h] = acc_ref[h] + mm(weights.astype(LOW), values)

    def plain(j, carry):
        one_block(j, False)
        return carry

    def pair(j, carry):
        one_block(2 * j, False, 2)
        return carry

    def edge(j, carry):
        one_block(j, True)
        return carry

    lax.fori_loop(0, whole // 2, pair, 0)
    lax.fori_loop(whole // 2 * 2, whole, plain, 0)
    lax.fori_loop(whole, end, edge, 0)
    lane = lax.broadcasted_iota(jnp.int32, inv_ref.shape[1:], 1)
    kept = jnp.zeros(inv_ref.shape[1:], F32)
    for h in range(heads):
        total = jnp.sum(sum_ref[h], axis=1, keepdims=True)
        inverse = 1.0 / jnp.where(total > 0.0, total, 1.0)
        attended = acc_ref[h] * inverse
        columns = slice(h * head_dim, (h + 1) * head_dim)
        att_ref[0, :, columns] = attended
        acted_ref[0, :, columns] = (attended * jax.nn.sigmoid(gate_ref[0, :, columns])).astype(LOW)
        kept = jnp.where(lane == h, inverse, kept)
    inv_ref[0] = kept


def by_sequence(array):
    return pl.BlockSpec((1,) + array.shape[1:], lambda b: (b,) + (0,) * (len(array.shape) - 1))


def attend(place, q, kv, gate, group, head_dim):
    batch, rows, width = q.shape
    heads = width // head_dim
    outs = [
        jax.ShapeDtypeStruct((batch, rows, width), F32),
        jax.ShapeDtypeStruct((batch, rows, width), LOW),
        jax.ShapeDtypeStruct((batch, rows, 128), F32),
    ]
    return pl.pallas_call(
        functools.partial(attend_kernel, group, head_dim),
        grid=(batch,),
        in_specs=[SCALARS, by_sequence(q), by_sequence(kv), by_sequence(gate)],
        out_specs=[by_sequence(x) for x in outs],
        out_shape=outs,
        scratch_shapes=[
            pltpu.VMEM((heads, rows, head_dim), F32),
            pltpu.VMEM((heads, rows, 128), F32),
        ],
        compiler_params=params(58),
        cost_estimate=takes(18),
        name="attend",
    )(place, q, kv, gate)


def norm_turn_back(grad, raw, head_gain, cosine, sine):
    grad = turn_back(grad, cosine, sine)
    inverse = inverse_rms(raw)
    gain_grad = jnp.sum(grad * raw * inverse, axis=0, keepdims=True)
    grad = grad * head_gain
    mean = jnp.mean(grad * raw, axis=-1, keepdims=True)
    return inverse * (grad - raw * (inverse * inverse * mean)), gain_grad


def attend_back_kernel(
    group, head_dim,
    place_ref, q_ref, kv_ref, r_ref, wo_ref, att_ref, gate_ref, inv_ref, qraw_ref, cos_ref, sin_ref, qgain_ref,
    dq_ref, dkv_ref, dgate_ref, dqgain_ref,
    scaled_ref, corr_ref, acc_ref,
):
    rows = q_ref.shape[1]
    heads = q_ref.shape[2] // head_dim
    kv_heads = heads // group
    scale = head_dim ** (-0.5)
    acted_grad = mm_t(r_ref[0], wo_ref[...])
    lane = lax.broadcasted_iota(jnp.int32, inv_ref.shape[1:], 1)
    kept = jnp.zeros(inv_ref.shape[1:], F32)
    for h in range(heads):
        columns = slice(h * head_dim, (h + 1) * head_dim)
        sigmoid = jax.nn.sigmoid(gate_ref[0, :, columns])
        attended = att_ref[0, :, columns]
        grad = acted_grad[:, columns]
        dgate_ref[0, :, columns] = (grad * attended * sigmoid * (1.0 - sigmoid)).astype(LOW)
        grad = grad * sigmoid
        inverse = inv_ref[0, :, h : h + 1]
        scaled_ref[:, columns] = (grad * inverse).astype(LOW)
        kept = jnp.where(
            lane == h, jnp.sum(grad * attended, axis=1, keepdims=True) * inverse, kept
        )
    corr_ref[...] = kept.T
    acc_ref[...] = jnp.zeros_like(acc_ref)
    whole, end, start, length = live_blocks(place_ref, rows)

    def one_block(j, masked, width=1):
        tall = width * rows
        span = pl.ds(pl.multiple_of(j * rows, rows), tall)
        if masked:
            key_pos = j * rows + lax.broadcasted_iota(jnp.int32, (rows, rows), 0)
            query_pos = start + lax.broadcasted_iota(jnp.int32, (rows, rows), 1)
            allowed = (key_pos <= query_pos) & (key_pos < length)
        for c in range(kv_heads):
            key_columns = slice(c * head_dim, (c + 1) * head_dim)
            value_columns = slice((kv_heads + c) * head_dim, (kv_heads + c + 1) * head_dim)
            keys = kv_ref[0, span, key_columns]
            values = kv_ref[0, span, value_columns]
            dk = jnp.zeros((tall, head_dim), F32)
            dv = jnp.zeros((tall, head_dim), F32)
            for h in range(c * group, (c + 1) * group):
                columns = slice(h * head_dim, (h + 1) * head_dim)
                queries = q_ref[0, :, columns]
                scaled = scaled_ref[:, columns]
                weights = jnp.exp2(mm_t(keys, queries) * (scale * LOG2E))
                if masked:
                    weights = jnp.where(allowed, weights, 0.0)
                dv = dv + mm(weights.astype(LOW), scaled)
                score = (weights * (mm_t(values, scaled) - corr_ref[h : h + 1, :])).astype(LOW)
                dk = dk + mm(score, queries)
                acc_ref[h] = acc_ref[h] + t_mm(keys, score)
            dkv_ref[0, span, key_columns] = (dk * scale).astype(LOW)
            dkv_ref[0, span, value_columns] = dv.astype(LOW)

    def plain(j, carry):
        one_block(j, False)
        return carry

    def pair(j, carry):
        one_block(2 * j, False, 2)
        return carry

    def edge(j, carry):
        one_block(j, True)
        return carry

    def empty(j, carry):
        span = pl.ds(pl.multiple_of(j * rows, rows), rows)
        dkv_ref[0, span, :] = jnp.zeros((rows, dkv_ref.shape[2]), LOW)
        return carry

    lax.fori_loop(0, whole // 2, pair, 0)
    lax.fori_loop(whole // 2 * 2, whole, plain, 0)
    lax.fori_loop(whole, end, edge, 0)
    lax.fori_loop(end, dkv_ref.shape[1] // rows, empty, 0)
    gain_total = jnp.zeros((1, head_dim), F32)
    for h in range(heads):
        columns = slice(h * head_dim, (h + 1) * head_dim)
        grad, gain_grad = norm_turn_back(
            acc_ref[h].T * scale, qraw_ref[0, :, columns], qgain_ref[...], cos_ref[...], sin_ref[...]
        )
        dq_ref[0, :, columns] = grad.astype(LOW)
        gain_total = gain_total + gain_grad

    @pl.when(pl.program_id(0) == 0)
    def _():
        dqgain_ref[...] = gain_total

    @pl.when(pl.program_id(0) > 0)
    def _():
        dqgain_ref[...] = dqgain_ref[...] + gain_total


def attend_back(place, q, kv, r, wo, att, gate, inv, qraw, cosine, sine, qgain, group):
    batch, rows, width = q.shape
    head_dim = qgain.shape[1]
    heads = width // head_dim
    outs = [
        jax.ShapeDtypeStruct(q.shape, LOW),
        jax.ShapeDtypeStruct(kv.shape, LOW),
        jax.ShapeDtypeStruct(q.shape, LOW),
    ]
    line = pl.BlockSpec((1, head_dim), lambda b: (0, 0))
    return pl.pallas_call(
        functools.partial(attend_back_kernel, group, head_dim),
        grid=(batch,),
        in_specs=[SCALARS, by_sequence(q), by_sequence(kv), by_sequence(r), full_block(wo)]
        + [by_sequence(x) for x in (att, gate, inv, qraw)]
        + [full_block(x) for x in (cosine, sine, qgain)],
        out_specs=[by_sequence(x) for x in outs] + [line],
        out_shape=outs + [shape_of(1, head_dim, F32)],
        scratch_shapes=[
            pltpu.VMEM((rows, width), LOW),
            pltpu.VMEM((128, rows), F32),
            pltpu.VMEM((heads, head_dim, rows), F32),
        ],
        compiler_params=params(58),
        cost_estimate=takes(3),
        name="attend_back",
    )(place, q, kv, r, wo, att, gate, inv, qraw, cosine, sine, qgain)


class Line:
    def __init__(self, pieces, count, part_ref, own_ref, right_ref, left_ref, sems, spread=None):
        self.sums = part_ref is not None
        self.pieces, self.count = pieces, count
        self.place = lax.axis_index("head")
        self.part_ref, self.own_ref = part_ref, own_ref
        self.right_ref, self.left_ref = right_ref, left_ref
        self.sems = sems
        self.spread = spread

    def barrier(self, digits=()):
        sem = pltpu.get_barrier_semaphore()
        place, count = self.place, self.count
        for digit in digits:
            partner = flipped(lax.axis_index("seq"), digit)
            pl.semaphore_signal(sem, inc=1, device_id={"seq": partner}, device_id_type=MESH)

        @pl.when(place > 0)
        def _():
            pl.semaphore_signal(sem, inc=1, device_id={"head": place - 1}, device_id_type=MESH)

        @pl.when(place < count - 1)
        def _():
            pl.semaphore_signal(sem, inc=1, device_id={"head": place + 1}, device_id_type=MESH)

        inside = (place > 0) & (place < count - 1)

        @pl.when(inside)
        def _():
            pl.semaphore_wait(sem, 2 + len(digits))

        @pl.when(jnp.logical_not(inside))
        def _():
            pl.semaphore_wait(sem, 1 + len(digits))

    def barrier_all(self, digits):
        sem = pltpu.get_barrier_semaphore()
        for digit in digits:
            partner = flipped(lax.axis_index("seq"), digit)
            pl.semaphore_signal(sem, inc=1, device_id={"seq": partner}, device_id_type=MESH)
        for distance in range(1, self.count):
            other = lax.rem(self.place + distance, self.count)
            pl.semaphore_signal(sem, inc=1, device_id={"head": other}, device_id_type=MESH)
        pl.semaphore_wait(sem, self.count - 1 + len(digits))

    def copy(self, ref, send, receive, p, t, step):
        return pltpu.make_async_remote_copy(
            src_ref=ref,
            dst_ref=ref,
            send_sem=self.sems[send].at[p, t],
            recv_sem=self.sems[receive].at[p, t],
            device_id={"head": jnp.clip(self.place + step, 0, self.count - 1)},
            device_id_type=MESH,
        )

    def sum_copy(self, p, t, step):
        ref = self.right_ref if step > 0 else self.left_ref
        base = 0 if step > 0 else 2
        return self.copy(ref.at[p, t], base, base + 1, p, t, step)

    def spread_copy(self, p, t, step):
        first = 4 if self.sums else 0
        return self.copy(self.spread(p, t), first if step > 0 else first + 1, first + 2, p, t, step)

    def send_sums(self, p, distance):
        place, count = self.place, self.count
        for step, ref in ((1, self.right_ref), (-1, self.left_ref)):
            t = place + step * distance
            first = place == (0 if step > 0 else count - 1)

            @pl.when((t >= 0) & (t < count))
            def _(t=t, step=step, ref=ref, first=first):
                @pl.when(first)
                def _():
                    ref[p, t] = self.part_ref[t].astype(LOW)

                @pl.when(jnp.logical_not(first))
                def _():
                    self.sum_copy(p, t, step).wait_recv()
                    ref[p, t] = (ref[p, t].astype(F32) + self.part_ref[t].astype(F32)).astype(LOW)

                self.sum_copy(p, t, step).start()

    def keep_own(self, p):
        self.own_ref[p] = self.part_ref[self.place].astype(F32)

    def finish_own(self, p):
        place, count = self.place, self.count
        for step, ref, inner in ((1, self.right_ref, place > 0), (-1, self.left_ref, place < count - 1)):

            @pl.when(inner)
            def _(step=step, ref=ref):
                self.sum_copy(p, place, step).wait_recv()
                self.own_ref[p] = self.own_ref[p] + ref[p, place].astype(F32)

    def hand_out(self, p):
        place, count = self.place, self.count

        @pl.when(place < count - 1)
        def _():
            self.spread_copy(p, place, 1).start()

        @pl.when(place > 0)
        def _():
            self.spread_copy(p, place, -1).start()

    def hand_on(self, p, distance):
        place, count = self.place, self.count
        for step, more in ((1, place < count - 1), (-1, place > 0)):
            t = place - step * distance

            @pl.when((t >= 0) & (t < count))
            def _(t=t, step=step, more=more):
                self.spread_copy(p, t, step).wait_recv()

                @pl.when(more)
                def _():
                    self.spread_copy(p, t, step).start()

    def drain(self):
        place, count = self.place, self.count

        def one(p, carry):
            for t in range(count):
                if self.sums:

                    @pl.when(t > place)
                    def _(t=t):
                        self.sum_copy(p, t, 1).wait_send()

                    @pl.when(t < place)
                    def _(t=t):
                        self.sum_copy(p, t, -1).wait_send()

                if self.spread is not None:

                    @pl.when((t <= place) & (place < count - 1))
                    def _(t=t):
                        self.spread_copy(p, t, 1).wait_send()

                    @pl.when((t >= place) & (place > 0))
                    def _(t=t):
                        self.spread_copy(p, t, -1).wait_send()

            return carry

        lax.fori_loop(0, self.pieces, one, 0)


def line_scratch(pieces, count, rows, model, part_kind, spread):
    slots = (pieces, count)
    scratch = [
        pltpu.VMEM((pieces, rows, model), F32),
        pltpu.VMEM((pieces, count, rows, model), LOW),
        pltpu.VMEM((pieces, count, rows, model), LOW),
    ] + [pltpu.SemaphoreType.DMA(slots)] * (7 if spread else 4)
    if part_kind is not None:
        scratch = [pltpu.VMEM((count, rows, model), part_kind)] + scratch
    return scratch


def both_ways(index, limit, body):
    @pl.when((index >= 0) & (index < limit))
    def _():
        body(index)


def front_kernel(
    pieces, count, head_dim,
    tok_ref, gain_ref, cos_ref, sin_ref, qgain_ref, kgain_ref, wq_ref, wk_ref, wv_ref, wg_ref,
    normed_ref, qraw_ref, q_ref, kraw_ref, kv_ref, gate_ref,
    all_ref, *sems,
):
    rows, model = tok_ref.shape[1], tok_ref.shape[2]
    tall = count * rows
    line = Line(pieces, count, None, None, None, None, sems, spread=lambda p, t: all_ref.at[p, t])
    line.barrier()
    for p in range(pieces):
        all_ref[p, line.place] = tok_ref[p]

    def project(p):
        b, half = p // 2, p % 2

        def keep(ref, value):
            ref[b, :, half] = value.astype(ref.dtype).reshape(count, rows, value.shape[-1])

        x = all_ref[p].reshape(tall, model).astype(F32)
        normed = (x * inverse_rms(x) * gain_ref[...]).astype(LOW)
        keep(normed_ref, normed)
        cosine = cos_ref[:, half].reshape(tall, head_dim)
        sine = sin_ref[:, half].reshape(tall, head_dim)

        def turned(raw, head_gain):
            parts = []
            for h in range(raw.shape[1] // head_dim):
                part = raw[:, h * head_dim : (h + 1) * head_dim]
                parts.append(turn(part * inverse_rms(part) * head_gain, cosine, sine).astype(LOW))
            return parts

        raw = mm(normed, wk_ref[...])
        keep(kraw_ref, raw)
        values = mm(normed, wv_ref[...]).astype(LOW)
        keep(kv_ref, jnp.concatenate(turned(raw, kgain_ref[...]) + [values], axis=1))
        raw = mm(normed, wq_ref[...])
        keep(qraw_ref, raw)
        keep(q_ref, jnp.concatenate(turned(raw, qgain_ref[...]), axis=1))
        keep(gate_ref, mm(normed, wg_ref[...]))

    def turn_once(k, carry):
        both_ways(k, pieces, line.hand_out)
        for distance in range(1, count):
            both_ways(k - 1, pieces, lambda p, d=distance: line.hand_on(p, d))
        both_ways(k - 1, pieces, project)
        return carry

    lax.fori_loop(0, pieces + 1, turn_once, 0)
    line.drain()


def front_step(tok, gain, cosine, sine, qgain, kgain, wq, wk, wv, wg, count):
    pieces, rows, model = tok.shape
    batch = pieces // 2
    head_dim = qgain.shape[1]
    nq, nk = wq.shape[1], wk.shape[1]

    def wide(columns, kind):
        return jax.ShapeDtypeStruct((batch, count, 2, rows, columns), kind)

    slots = (pieces, count)
    return pl.pallas_call(
        functools.partial(front_kernel, pieces, count, head_dim),
        in_specs=[WHOLE] * 10,
        out_specs=[WHOLE] * 6,
        out_shape=[
            wide(model, LOW), wide(nq, F32), wide(nq, LOW), wide(nk, F32), wide(2 * nk, LOW), wide(nq, F32)
        ],
        scratch_shapes=[pltpu.VMEM((pieces, count, rows, model), LOW)]
        + [pltpu.SemaphoreType.DMA(slots)] * 3,
        compiler_params=params(34, collective_id=2, has_side_effects=True),
        cost_estimate=takes(95),
        name="front",
    )(
        tok, gain, cosine.reshape(count, 2, rows, head_dim), sine.reshape(count, 2, rows, head_dim),
        qgain, kgain, wq, wk, wv, wg,
    )


def middle_kernel(
    pieces, count,
    acted_ref, tok_ref, gain_ref, wo_ref, masked_hbm, wg_hbm, wl_hbm, wd_hbm,
    middle_ref, dgain_ref, normed_hbm, hidden_hbm, dg_hbm, dl_hbm, dn_hbm,
    mid_ref, wg_ref, wl_ref, wd_ref, masked_ref, normed_ref, hidden_ref, dg_ref, dl_ref, dn_ref, acc_ref,
    load_sem, masked_sem, store_sem,
    part_ref, own_ref, right_ref, left_ref, *sems,
):
    rows, model = own_ref.shape[1], own_ref.shape[2]
    tall = count * rows
    hidden = wg_ref.shape[1]
    line = Line(
        pieces, count, part_ref, own_ref, right_ref, left_ref, sems, spread=lambda p, t: mid_ref.at[p, t]
    )
    place = line.place
    loads = [
        pltpu.make_async_copy(source, target, load_sem.at[i])
        for i, (source, target) in enumerate(((wg_hbm, wg_ref), (wl_hbm, wl_ref), (wd_hbm, wd_ref)))
    ]
    line.barrier()
    for load in loads:
        load.start()
    dgain_ref[...] = jnp.zeros_like(dgain_ref)
    tiles = 3
    tile = hidden // tiles

    def masked_copy(p):
        return pltpu.make_async_copy(masked_hbm.at[:, p], masked_ref, masked_sem)

    def stores(p):
        pairs = (
            (normed_ref, normed_hbm), (hidden_ref, hidden_hbm), (dg_ref, dg_hbm), (dl_ref, dl_hbm),
            (dn_ref, dn_hbm),
        )
        return [
            pltpu.make_async_copy(source, target.at[:, p], store_sem.at[i])
            for i, (source, target) in enumerate(pairs)
        ]

    def begin(p):
        acted = acted_ref[p // 2, :, p % 2].reshape(tall, acted_ref.shape[-1])
        part_ref[...] = mm(acted, wo_ref[...]).reshape(count, rows, model)
        line.keep_own(p)

    def own(p):
        line.finish_own(p)
        middle = own_ref[p] + tok_ref[p].astype(F32)
        middle_ref[p] = middle
        mid_ref[p, place] = middle.astype(LOW)
        line.hand_out(p)

    def units_begin(p):
        line.hand_on(p, count - 1)

        @pl.when(p > 0)
        def _():
            for store in stores(p - 1):
                store.wait()

        x = mid_ref[p].reshape(tall, model).astype(F32)
        normed = (x * inverse_rms(x) * gain_ref[...]).astype(LOW)
        normed_ref[...] = normed.reshape(count, rows, model)
        masked_copy(p).wait()

        @pl.when(p == 0)
        def _():
            for load in loads:
                load.wait()

    def units_tile(i):
        span = slice(i * tile, (i + 1) * tile)
        normed = normed_ref[...].reshape(tall, model)
        gate = mm(normed, wg_ref[:, span])
        lift = mm(normed, wl_ref[:, span])
        grad = mm_t(masked_ref[...].reshape(tall, model), wd_ref[span, :])
        sigmoid = jax.nn.sigmoid(gate)
        silu = gate * sigmoid
        lift_grad = (grad * silu).astype(LOW)
        gate_grad = (grad * lift * (sigmoid + silu * (1.0 - sigmoid))).astype(LOW)
        hidden_ref[:, :, span] = (silu * lift).astype(LOW).reshape(count, rows, tile)
        dg_ref[:, :, span] = gate_grad.reshape(count, rows, tile)
        dl_ref[:, :, span] = lift_grad.reshape(count, rows, tile)
        part = mm_t(gate_grad, wg_ref[:, span]) + mm_t(lift_grad, wl_ref[:, span])
        if i == 0:
            acc_ref[...] = part
        else:
            acc_ref[...] = acc_ref[...] + part

    def units_end(p):
        total = acc_ref[...]
        dn_ref[...] = total.astype(LOW).reshape(count, rows, model)
        x = mid_ref[p].reshape(tall, model).astype(F32)
        dgain_ref[...] = dgain_ref[...] + jnp.sum(total * x * inverse_rms(x), axis=0, keepdims=True)
        for store in stores(p):
            store.start()

        @pl.when(p < pieces - 1)
        def _():
            masked_copy(p + 1).start()

    masked_copy(0).start()

    def turn_once(k, carry):
        both_ways(k, pieces, begin)
        for i in range(max(tiles, count - 1)):
            if i < count - 1:
                both_ways(k, pieces, lambda p, i=i: line.send_sums(p, count - 1 - i))
            if i == 0:
                both_ways(k - 1, pieces, own)
                both_ways(k - 2, pieces, units_begin)
            elif i < count - 1:
                both_ways(k - 1, pieces, lambda p, i=i: line.hand_on(p, i))
            if i < tiles:
                both_ways(k - 2, pieces, lambda p, i=i: units_tile(i))
        both_ways(k - 2, pieces, units_end)
        return carry

    lax.fori_loop(0, pieces + 2, turn_once, 0)
    for store in stores(pieces - 1):
        store.wait()
    line.drain()


def middle_step(acted, tok, gain, wo, masked, wg, wl, wd, count):
    pieces, rows, model = tok.shape
    hidden = wg.shape[1]
    any_place = pl.BlockSpec(memory_space=pl.ANY)

    def wide(columns, kind=LOW):
        return jax.ShapeDtypeStruct((count, pieces, rows, columns), kind)

    def room(columns, kind=LOW):
        return pltpu.VMEM((count, rows, columns), kind)

    return pl.pallas_call(
        functools.partial(middle_kernel, pieces, count),
        in_specs=[WHOLE] * 4 + [any_place] * 4,
        out_specs=[WHOLE] * 2 + [any_place] * 5,
        out_shape=[
            jax.ShapeDtypeStruct((pieces, rows, model), F32), shape_of(1, model, F32),
            wide(model), wide(hidden), wide(hidden), wide(hidden), wide(model),
        ],
        scratch_shapes=[
            pltpu.VMEM((pieces, count, rows, model), LOW),
            pltpu.VMEM(wg.shape, LOW), pltpu.VMEM(wl.shape, LOW), pltpu.VMEM(wd.shape, LOW),
            room(model), room(model), room(hidden), room(hidden), room(hidden), room(model),
            pltpu.VMEM((count * rows, model), F32),
            pltpu.SemaphoreType.DMA((3,)), pltpu.SemaphoreType.DMA, pltpu.SemaphoreType.DMA((5,)),
        ]
        + line_scratch(pieces, count, rows, model, F32, True),
        compiler_params=params(58, collective_id=0, has_side_effects=True),
        cost_estimate=takes(128),
        name="middle",
    )(acted, tok, gain, wo, masked, wg, wl, wd)


def residual_kernel(
    pieces, count, halves,
    dn_ref, middle_ref, masked_ref, gain_ref, residual_ref, r_ref,
    part_ref, own_ref, right_ref, left_ref, *sems,
):
    line = Line(
        pieces, count, part_ref, own_ref, right_ref, left_ref, sems,
        spread=lambda p, t: r_ref.at[p // halves, t, p % halves],
    )
    line.barrier()

    def begin(p):
        part_ref[...] = dn_ref[:, p]
        line.keep_own(p)

    def own(p):
        line.finish_own(p)
        x = middle_ref[p].astype(LOW).astype(F32)
        residual = masked_ref[p] + norm_back(own_ref[p], x, gain_ref[...])
        residual_ref[p] = residual
        r_ref[p // halves, line.place, p % halves] = residual.astype(LOW)
        line.hand_out(p)

    def turn_once(k, carry):
        both_ways(k, pieces, begin)
        for i in range(count - 1):
            both_ways(k, pieces, lambda p, i=i: line.send_sums(p, count - 1 - i))
            if i == 0:
                both_ways(k - 1, pieces, own)
            else:
                both_ways(k - 1, pieces, lambda p, i=i: line.hand_on(p, i))
        both_ways(k - 1, pieces, lambda p: line.hand_on(p, count - 1))
        return carry

    lax.fori_loop(0, pieces + 1, turn_once, 0)
    line.drain()


def residual_step(dn, middle, masked, gain, batch):
    count, pieces, rows, model = dn.shape
    halves = pieces // batch
    return pl.pallas_call(
        functools.partial(residual_kernel, pieces, count, halves),
        in_specs=[WHOLE] * 4,
        out_specs=[WHOLE] * 2,
        out_shape=[
            jax.ShapeDtypeStruct((pieces, rows, model), F32),
            jax.ShapeDtypeStruct((batch, count, halves, rows, model), LOW),
        ],
        scratch_shapes=line_scratch(pieces, count, rows, model, LOW, True),
        compiler_params=params(36, collective_id=1, has_side_effects=True),
        cost_estimate=takes(10),
        name="residual",
    )(dn, middle, masked, gain)


def flipped(place, mask):
    bit = 1
    while bit <= mask:
        if mask & bit:
            place = place + (1 - 2 * (place // bit % 2)) * bit
        bit *= 2
    return place


def digit_orders(count, batch):
    upper = [1 << i for i in range(1, count.bit_length() - 1)]
    return [(upper if b % 2 == 0 else upper[::-1]) + [1] for b in range(batch)]


def greet(place, digits):
    sem = pltpu.get_barrier_semaphore()
    for digit in digits:
        pl.semaphore_signal(sem, inc=1, device_id={"seq": flipped(place, digit)}, device_id_type=MESH)
    pl.semaphore_wait(sem, len(digits))


def block_gathers(count, batch, out, sources, send_sem, receive_sem):
    place = lax.axis_index("seq")
    orders = digit_orders(count, batch)
    steps = len(orders[0])
    started = []

    def copy(b, mask, step):
        digit = orders[b][step]
        block = out(b).at[flipped(place, mask)]
        return pltpu.make_async_remote_copy(
            src_ref=sources(b) if mask == 0 else block,
            dst_ref=block,
            send_sem=send_sem.at[b, step, mask],
            recv_sem=receive_sem.at[b, mask | digit],
            device_id={"seq": flipped(place, digit)},
            device_id_type=MESH,
        )

    def pass_on(b, mask, first):
        for step in range(first, steps):
            one = copy(b, mask, step)
            one.start()
            started.append(one)

    def arrive(b, mask, level):
        block = out(b).at[flipped(place, mask)]
        pltpu.make_async_remote_copy(
            src_ref=block,
            dst_ref=block,
            send_sem=send_sem.at[b, 0, mask],
            recv_sem=receive_sem.at[b, mask],
            device_id={"seq": flipped(place, orders[b][level])},
            device_id_type=MESH,
        ).wait_recv()
        pass_on(b, mask, level + 1)

    begins = [functools.partial(pass_on, b, 0, 0) for b in range(batch)]
    arrivals = []
    for level in range(steps):
        for turn in range(1 << level):
            for b in range(batch):
                mask = orders[b][level]
                for i in range(level):
                    if turn >> i & 1:
                        mask |= orders[b][i]
                arrivals.append((1.0 if level == steps - 1 else 4.0, functools.partial(arrive, b, mask, level)))

    def drain():
        for one in started:
            one.wait_send()

    return begins, arrivals, drain


def gather_kernel(count, batch, own_ref, out_ref, local_sem, send_sem, receive_sem):
    place = lax.axis_index("seq")
    greet(place, digit_orders(count, 1)[0])
    local = [
        pltpu.make_async_copy(own_ref.at[b], out_ref.at[b, place], local_sem.at[b]) for b in range(batch)
    ]
    for copy in local:
        copy.start()
    begins, arrivals, drain = block_gathers(
        count, batch, lambda b: out_ref.at[b], lambda b: own_ref.at[b], send_sem, receive_sem
    )
    for begin in begins:
        begin()
    for _, event in arrivals:
        event()
    drain()
    for copy in local:
        copy.wait()


def gather_blocks(own):
    batch, rows, columns = own.shape
    count = lax.axis_size("seq")
    steps = count.bit_length() - 1
    any_place = pl.BlockSpec(memory_space=pl.ANY)
    out = pl.pallas_call(
        functools.partial(gather_kernel, count, batch),
        in_specs=[any_place],
        out_specs=any_place,
        out_shape=jax.ShapeDtypeStruct((batch, count, rows, columns), LOW),
        scratch_shapes=[
            pltpu.SemaphoreType.DMA((batch,)),
            pltpu.SemaphoreType.DMA((batch, steps, count)),
            pltpu.SemaphoreType.DMA((batch, count)),
        ],
        compiler_params=params(4, collective_id=3, has_side_effects=True),
        cost_estimate=takes(41),
        name="gather_blocks",
    )(own)
    return out.reshape(batch, count * rows, columns)


def block_sums(count, batch, parts, finish, slots, send_sem, receive_sem, near):
    place = lax.axis_index("seq")
    orders = [order[::-1] for order in digit_orders(count, batch)]
    steps = len(orders[0])

    def masks_at(b, step):
        found = [0]
        for digit in orders[b][step + 1 :][::-1]:
            found = [mask | digit for mask in found] + found
        return found

    numbers = {}
    for b in range(batch):
        place_in = 0
        for step in range(steps):
            for mask in masks_at(b, step):
                numbers[b, step, mask] = place_in
                place_in += 1

    def slot(b, step, mask):
        return slots.at[b, numbers[b, step, mask]]

    def transfer(b, step, mask):
        digit = orders[b][step]
        number = numbers[b, step, mask]
        if step == 0:
            source = parts(b).at[flipped(place, mask | digit)]
        else:
            source = slot(b, step - 1, mask | digit)
        return pltpu.make_async_remote_copy(
            src_ref=source,
            dst_ref=slots.at[b, number],
            send_sem=send_sem.at[b, number],
            recv_sem=receive_sem.at[b, number],
            device_id={"seq": flipped(place, digit)},
            device_id_type=MESH,
        )

    started = []

    def begin():
        for turn in range(count // 2):
            for b in range(batch):
                copy = transfer(b, 0, masks_at(b, 0)[turn])
                copy.start()
                started.append(copy)

    def take(b, step, mask):
        transfer(b, step, mask).wait_recv()
        held = parts(b).at[flipped(place, mask)] if step == 0 else slot(b, step - 1, mask)
        total = held[...].astype(F32) + slot(b, step, mask)[...].astype(F32)
        if step == steps - 1:
            finish(b, total)
        else:
            slot(b, step, mask)[...] = total.astype(LOW)
            if mask & orders[b][step + 1]:
                copy = transfer(b, step + 1, mask & ~orders[b][step + 1])
                copy.start()
                started.append(copy)

    events = []
    for step in range(steps):
        for turn in range(len(masks_at(0, step))):
            for b in range(batch):
                events.append((near if step == 0 else 4.0, functools.partial(take, b, step, masks_at(b, step)[turn])))

    def drain():
        for copy in started:
            copy.wait_send()

    return begin, events, drain


def interleaved(*lists):
    spent = [0.0] * len(lists)
    whole = [sum(time for time, _ in calls) for calls in lists]
    taken = [0] * len(lists)
    while any(taken[i] < len(calls) for i, calls in enumerate(lists)):
        i = min((i for i, calls in enumerate(lists) if taken[i] < len(calls)), key=lambda i: spent[i])
        time, call = lists[i][taken[i]]
        call()
        spent[i] += time / whole[i]
        taken[i] += 1

def scatter_kernel(
    pieces, count, seq_count, batch, head_dim,
    parts_ref, hidden_hbm, wd_hbm, middle_ref, valid_ref, kraw_ref, cos_ref, sin_ref, kgain_ref,
    dkv_ref, output_ref, dkgain_ref,
    wd_ref, hidden_ref, load_sem, hidden_sem, slots, send_sem, receive_sem,
    part_ref, own_ref, right_ref, left_ref, *sems,
):
    rows, model = own_ref.shape[1], own_ref.shape[2]
    tall = count * rows
    keys = kraw_ref.shape[2]
    line = Line(pieces, count, part_ref, own_ref, right_ref, left_ref, sems)
    load = pltpu.make_async_copy(wd_hbm, wd_ref, load_sem)

    def hidden_copy(p):
        return pltpu.make_async_copy(hidden_hbm.at[:, p], hidden_ref.at[p % 2], hidden_sem.at[p % 2])

    load.start()
    hidden_copy(0).start()
    dkgain_ref[...] = jnp.zeros_like(dkgain_ref)
    line.barrier(digit_orders(seq_count, 1)[0])

    def finish(b, total):
        for h in range(keys // head_dim):
            columns = slice(h * head_dim, (h + 1) * head_dim)
            grad, gain_grad = norm_turn_back(
                total[:, columns], kraw_ref[b, :, columns], kgain_ref[...], cos_ref[...], sin_ref[...]
            )
            dkv_ref[b, :, columns] = grad.astype(LOW)
            dkgain_ref[...] = dkgain_ref[...] + gain_grad
        dkv_ref[b, :, keys:] = total[:, keys:].astype(LOW)

    first, events, drain = block_sums(
        seq_count, batch, lambda b: parts_ref.at[b], finish, slots, send_sem, receive_sem, 4.0
    )

    def begin(p):
        if p == 0:
            load.wait()
        if p + 1 < pieces:
            hidden_copy(p + 1).start()
        hidden_copy(p).wait()
        hidden = hidden_ref[p % 2].reshape(tall, hidden_ref.shape[-1])
        part_ref[...] = mm(hidden, wd_ref[...]).reshape(count, rows, model)
        line.keep_own(p)

    def own(p):
        line.finish_own(p)
        output_ref[p] = (valid_ref[p] * (middle_ref[p] + own_ref[p])).astype(LOW)

    first()
    interleaved(line_steps(line, begin, own), events)
    drain()
    line.drain()


def line_steps(line, begin, own):
    steps = []
    for k in range(line.pieces + 1):
        for i in range(line.count - 1):
            if i == 0 and k < line.pieces:
                steps.append((1.0, functools.partial(begin, k)))
            if k < line.pieces:
                steps.append((8.0, functools.partial(line.send_sums, k, line.count - 1 - i)))
            if i == 0 and k > 0:
                steps.append((1.0, functools.partial(own, k - 1)))
    return steps


def scatter_blocks(parts, hidden, wd, middle, valid, kraw, cosine, sine, kgain):
    seq_count, batch = lax.axis_size("seq"), parts.shape[0]
    rows, columns = parts.shape[1] // seq_count, parts.shape[2]
    count, pieces, piece_rows, units = hidden.shape
    model, head_dim = wd.shape[1], kgain.shape[1]
    any_place = pl.BlockSpec(memory_space=pl.ANY)
    return pl.pallas_call(
        functools.partial(scatter_kernel, pieces, count, seq_count, batch, head_dim),
        in_specs=[WHOLE, any_place, any_place] + [WHOLE] * 6,
        out_specs=[WHOLE] * 3,
        out_shape=[
            jax.ShapeDtypeStruct((batch, rows, columns), LOW),
            jax.ShapeDtypeStruct((pieces, piece_rows, model), LOW),
            shape_of(1, head_dim, F32),
        ],
        scratch_shapes=[
            pltpu.VMEM(wd.shape, LOW),
            pltpu.VMEM((2, count, piece_rows, units), LOW),
            pltpu.SemaphoreType.DMA,
            pltpu.SemaphoreType.DMA((2,)),
            pltpu.VMEM((batch, seq_count - 1, rows, columns), LOW),
            pltpu.SemaphoreType.DMA((batch, seq_count - 1)),
            pltpu.SemaphoreType.DMA((batch, seq_count - 1)),
        ]
        + line_scratch(pieces, count, piece_rows, model, F32, False),
        compiler_params=params(46, collective_id=4, has_side_effects=True),
        cost_estimate=takes(10),
        name="scatter_blocks",
    )(
        parts.reshape(batch, seq_count, rows, columns), hidden, wd, middle, valid, kraw, cosine, sine, kgain
    )


def last_kernel(
    pieces, count, seq_count, streams, halves,
    dq_ref, dkv_ref, dgate_ref, wq_ref, wk_ref, wv_ref, wg_ref, tok_ref, residual_ref, gain_ref,
    dmid_ref, dqgain_ref, dkgain_ref, *refs,
):
    grads, refs = refs[:streams], refs[streams:]
    input_ref, total_ref, sums = refs[0], refs[1], refs[2 : 2 + streams]
    (
        slots, scatter_send, scatter_receive, gather_send, gather_receive, mine_ref, mine_sem,
        dgain_ref, turns_ref, round_ref, mixed_ref, round_send, round_receive, mixed_send, mixed_receive,
        part_ref, own_ref, right_ref, left_ref, *sems,
    ) = refs[2 + streams :]
    rows, model = own_ref.shape[1], own_ref.shape[2]
    tall = count * rows
    place_seq = lax.axis_index("seq")
    digits = digit_orders(seq_count, 1)[0]
    line = Line(pieces, count, part_ref, own_ref, right_ref, left_ref, sems)
    line.barrier_all(digits)
    dgain_ref[...] = jnp.zeros_like(dgain_ref)

    begins, arrivals, gather_drain = block_gathers(
        seq_count, streams, lambda b: sums[b], lambda b: mine_ref.at[b], gather_send, gather_receive
    )

    def keep(b):
        return pltpu.make_async_copy(mine_ref.at[b], sums[b].at[place_seq], mine_sem.at[b])

    def finish(b, total):
        mine_ref[b] = total.astype(LOW)
        begins[b]()
        keep(b).start()

    first, events, scatter_drain = block_sums(
        seq_count, streams, lambda b: grads[b], finish, slots, scatter_send, scatter_receive, 1.0
    )

    def begin(p):
        b, half = p // halves, p % halves
        dq = dq_ref[b, :, half].reshape(tall, dq_ref.shape[-1])
        dkv = dkv_ref[b, :, half].reshape(tall, dkv_ref.shape[-1])
        dgate = dgate_ref[b, :, half].reshape(tall, dgate_ref.shape[-1])
        nk = dkv.shape[1] // 2
        total = mm_t(dq, wq_ref[...]) + mm_t(dgate, wg_ref[...])
        total = total + mm_t(dkv[:, :nk], wk_ref[...]) + mm_t(dkv[:, nk:], wv_ref[...])
        part_ref[...] = total.reshape(count, rows, model)
        line.keep_own(p)

    def own(p):
        line.finish_own(p)
        x = tok_ref[p].astype(F32)
        grad = own_ref[p]
        inverse = inverse_rms(x)
        dgain_ref[...] = dgain_ref[...] + jnp.sum(grad * x * inverse, axis=0, keepdims=True)
        input_ref[p] = residual_ref[p] + norm_back(grad, x, gain_ref[...])

    width = model // count
    lines = width // 128
    rounds = [
        pltpu.make_async_remote_copy(
            src_ref=turns_ref.at[i],
            dst_ref=round_ref.at[i],
            send_sem=round_send.at[i],
            recv_sem=round_receive.at[i],
            device_id={"seq": flipped(place_seq, digit)},
            device_id_type=MESH,
        )
        for i, digit in enumerate(digits)
    ]
    done = len(digits)
    shares = []
    for distance in range(1, count):
        other = lax.rem(line.place + distance, count)
        shares.append(
            pltpu.make_async_remote_copy(
                src_ref=turns_ref.at[done, other],
                dst_ref=mixed_ref.at[distance - 1],
                send_sem=mixed_send.at[distance - 1],
                recv_sem=mixed_receive.at[distance - 1],
                device_id={"head": other},
                device_id_type=MESH,
            )
        )

    def pack():
        turns_ref[0] = jnp.zeros(turns_ref.shape[1:], F32)
        for t in range(count):
            for i in range(lines):
                span = slice(t * width + i * 128, t * width + (i + 1) * 128)
                turns_ref[0, t, i : i + 1, :] = dgain_ref[:, span]
                turns_ref[0, t, lines + i : lines + i + 1, :] = dmid_ref[:, span]
            turns_ref[0, t, 2 * lines : 2 * lines + 1, :] = dqgain_ref[...]
            turns_ref[0, t, 2 * lines + 1 : 2 * lines + 2, :] = dkgain_ref[...]
        rounds[0].start()

    def one_round(i):
        rounds[i].wait_recv()
        turns_ref[i + 1] = turns_ref[i] + round_ref[i]
        for copy in rounds[i + 1 : i + 2] if i + 1 < done else shares:
            copy.start()

    def total():
        found = turns_ref[done, line.place]
        for i, copy in enumerate(shares):
            copy.wait_recv()
            found = found + mixed_ref[i]
        total_ref[...] = found

    steps = line_steps(line, begin, own) + [(1.0, pack)]
    steps += [(4.0, functools.partial(one_round, i)) for i in range(done)] + [(4.0, total)]
    first()
    interleaved(steps, events + arrivals)
    for copy in rounds + shares:
        copy.wait_send()
    for b in range(streams):
        keep(b).wait()
    scatter_drain()
    gather_drain()
    line.drain()


def last_step(dq, dkv, dgate, wq, wk, wv, wg, tok, residual, gain, dmid, dqgain, dkgain, grads):
    batch, count, halves, rows, nq = dq.shape
    pieces, model = batch * halves, wq.shape[0]
    seq_count, streams = lax.axis_size("seq"), len(grads)
    tall, columns = grads[0].shape
    block = tall // seq_count
    steps = seq_count.bit_length() - 1
    lines = 8 * ((2 * (model // count // 128) + 2 + 7) // 8)
    return pl.pallas_call(
        functools.partial(last_kernel, pieces, count, seq_count, streams, halves),
        in_specs=[WHOLE] * (13 + streams),
        out_specs=[WHOLE] * 2 + [pl.BlockSpec(memory_space=pl.ANY)] * streams,
        out_shape=[jax.ShapeDtypeStruct((pieces, rows, model), F32), shape_of(lines, 128, F32)]
        + [jax.ShapeDtypeStruct((seq_count, block, columns), LOW)] * streams,
        scratch_shapes=[
            pltpu.VMEM((streams, seq_count - 1, block, columns), LOW),
            pltpu.SemaphoreType.DMA((streams, seq_count - 1)),
            pltpu.SemaphoreType.DMA((streams, seq_count - 1)),
            pltpu.SemaphoreType.DMA((streams, steps, seq_count)),
            pltpu.SemaphoreType.DMA((streams, seq_count)),
            pltpu.VMEM((streams, block, columns), LOW),
            pltpu.SemaphoreType.DMA((streams,)),
            pltpu.VMEM((1, model), F32),
            pltpu.VMEM((steps + 1, count, lines, 128), F32),
            pltpu.VMEM((steps, count, lines, 128), F32),
            pltpu.VMEM((count - 1, lines, 128), F32),
            pltpu.SemaphoreType.DMA((steps,)),
            pltpu.SemaphoreType.DMA((steps,)),
            pltpu.SemaphoreType.DMA((count - 1,)),
            pltpu.SemaphoreType.DMA((count - 1,)),
        ]
        + line_scratch(pieces, count, rows, model, F32, False),
        compiler_params=params(60, collective_id=5, has_side_effects=True),
        cost_estimate=takes(5),
        name="last",
    )(
        dq, dkv, dgate, wq, wk, wv, wg, tok, residual, gain, dmid, dqgain, dkgain,
        *[grad.reshape(seq_count, block, columns) for grad in grads],
    )


def widen_kernel(input_ref, output_ref, dq_ref, dkv_ref, dgate_ref, out_ref, *refs):
    ff_refs, refs = refs[:3], refs[3:]
    input_out, output_out, dq_out, dk_out, dv_out, dgate_out, out_out, *ff_outs = refs
    keys = dk_out.shape[1]
    input_out[...] = jnp.stack([input_ref[b] for b in range(input_ref.shape[0])], axis=1)
    output_out[...] = jnp.stack([output_ref[b].astype(F32) for b in range(input_ref.shape[0])], axis=1).astype(LOW)
    dq_out[...] = dq_ref[...].astype(F32)
    dk_out[...] = dkv_ref[:, :keys].astype(F32)
    dv_out[...] = dkv_ref[:, keys:].astype(F32)
    dgate_out[...] = dgate_ref[...].astype(F32)
    out_out[...] = out_ref[...].astype(F32).T
    for ref, out in zip(ff_refs, ff_outs):
        out[...] = ref[...].astype(F32)


def widen(input_grad, output, dq, dkv, dgate, out, ff, steps=8):
    batch, rows, model = input_grad.shape
    columns, keys = dq.shape[1], dkv.shape[1] // 2

    def tall(array):
        return pl.BlockSpec((array.shape[0] // steps, array.shape[1]), lambda i: (i, 0))

    def wide(array):
        return jax.ShapeDtypeStruct(array.shape, F32)

    outs = [
        jax.ShapeDtypeStruct((rows, batch, model), F32), jax.ShapeDtypeStruct((rows, batch, model), LOW),
        wide(dq), shape_of(model, keys, F32), shape_of(model, keys, F32), wide(dgate), shape_of(columns, model, F32),
    ] + [wide(x) for x in ff]
    specs = [pl.BlockSpec((rows // steps, batch, model), lambda i: (i, 0, 0))] * 2
    specs += [tall(x) for x in outs[2:6]]
    specs += [pl.BlockSpec((columns, model // steps), lambda i: (0, i))]
    specs += [tall(x) for x in ff]
    return pl.pallas_call(
        widen_kernel,
        grid=(steps,),
        in_specs=[pl.BlockSpec((batch, rows // steps, model), lambda i: (0, i, 0))] * 2
        + [tall(x) for x in (dq, dkv, dgate, out, *ff)],
        out_specs=specs,
        out_shape=outs,
        compiler_params=params(58),
        cost_estimate=takes(25),
        name="widen",
    )(input_grad, output, dq, dkv, dgate, out, *ff)


def turn_tables(positions, head_dim):
    half_dim = head_dim // 2
    inverse = THETA ** (-(jnp.arange(half_dim, dtype=F32) * 2.0) / head_dim)
    angles = positions.astype(F32)[:, None] * inverse[None, :]
    cosine, sine = jnp.cos(angles), jnp.sin(angles)
    return jnp.concatenate([cosine, cosine], axis=1), jnp.concatenate([-sine, sine], axis=1)


def norm_back(grad, values, gain):
    inverse = inverse_rms(values)
    grad = grad * gain
    mean = jnp.mean(grad * values, axis=-1, keepdims=True)
    return inverse * (grad - values * (inverse * inverse * mean))


def gather(value, axis):
    return lax.all_gather(value, axis, axis=0, tiled=True)


def on_device(
    tokens, cotangent, lengths,
    query_weight, key_weight, value_weight, gating_weight, output_weight,
    swiglu_gate, swiglu_lift, swiglu_down,
    input_gain, middle_gain, query_gain, key_gain,
):
    block_index = lax.axis_index("seq")
    part_index = lax.axis_index("head")
    parts = lax.axis_size("head")
    local_rows, batch, model = tokens.shape
    head_dim = query_gain.shape[0]
    block_rows = local_rows * parts
    flat_rows = block_rows * batch
    group = query_weight.shape[1] // key_weight.shape[1]
    nq, nk = query_weight.shape[1], key_weight.shape[1]
    halves = 2
    pieces, rows = batch * halves, local_rows // halves

    query_start = block_index * block_rows
    positions = query_start + jnp.arange(block_rows, dtype=jnp.int32)
    cosine, sine = turn_tables(positions, head_dim)
    gain_in, gain_mid = input_gain[None, :], middle_gain[None, :]
    gain_q, gain_k = query_gain[None, :], key_gain[None, :]
    local_pos = query_start + part_index * local_rows + jnp.arange(local_rows, dtype=jnp.int32)
    place = jnp.concatenate([query_start[None], lengths]).astype(jnp.int32)
    valid = (local_pos[None, :] < lengths[:, None]).astype(F32)[..., None]
    tok = jnp.transpose(tokens, (1, 0, 2)).reshape(pieces, rows, model)

    normed, qraw, q, kraw, kv_own, gate = [
        x.reshape(batch, block_rows, x.shape[-1])
        for x in front_step(
            tok, gain_in, cosine, sine, gain_q, gain_k,
            query_weight, key_weight, value_weight, gating_weight, parts,
        )
    ]
    kv_own, masked_own = lax.optimization_barrier(
        (kv_own, valid * jnp.transpose(cotangent, (1, 0, 2)).astype(F32))
    )
    kv = gather_blocks(kv_own)
    masked = gather(masked_own.astype(LOW).reshape(batch * local_rows, model), "head")
    att, acted, inv = attend(place, q, kv, gate, group, head_dim)
    middle, dgain_mid, normed_mid, hidden, dg, dl, dn_mid = middle_step(
        acted.reshape(batch, parts, halves, rows, nq), tok, gain_mid, output_weight,
        masked.reshape(parts, pieces, rows, model), swiglu_gate, swiglu_lift, swiglu_down, parts,
    )

    def flat(array):
        return array.reshape(flat_rows, array.shape[-1])

    normed_mid = flat(normed_mid)
    ff_grads = (
        t_mm(normed_mid, flat(dg)).astype(LOW),
        t_mm(normed_mid, flat(dl)).astype(LOW),
        t_mm(flat(hidden), masked).astype(LOW),
    )
    dn_mid, ff_grads = lax.optimization_barrier((dn_mid, ff_grads))
    ff_grads = lax.psum(ff_grads, "seq")
    residual, r = residual_step(
        dn_mid, middle, masked_own.reshape(pieces, rows, model), gain_mid, batch
    )
    r = r.reshape(batch, block_rows, model)
    dq, dkv_all, dgate, dgain_q = attend_back(
        place, q, kv, r, output_weight, att, gate, inv, qraw, cosine, sine, gain_q, group
    )
    dkv, output, dgain_k = scatter_blocks(
        dkv_all, hidden, swiglu_down, middle, valid.reshape(pieces, rows, 1), kraw, cosine, sine, gain_k
    )
    grads = [
        t_mm(flat(normed), flat(dq)).astype(LOW),
        t_mm(flat(normed), flat(dkv)).astype(LOW),
        t_mm(flat(normed), flat(dgate)).astype(LOW),
        t_mm(flat(r), flat(acted)).astype(LOW),
    ]

    def pieced(array):
        return array.reshape(batch, parts, halves, rows, array.shape[-1])

    input_grad, gains, *grads = last_step(
        pieced(dq), pieced(dkv), pieced(dgate), query_weight, key_weight, value_weight, gating_weight,
        tok, residual, gain_in, dgain_mid, dgain_q, dgain_k, grads,
    )
    input_grad, output, dq_weight, dk_weight, dv_weight, dgate_weight, out_weight, *ff_sums = widen(
        input_grad.reshape(batch, local_rows, model),
        output.reshape(batch, local_rows, model),
        *[x.reshape(model, x.shape[-1]) for x in grads],
        ff_grads,
    )
    share = model // parts
    lines = share // 128
    head_share = head_dim // parts

    def head_gain(line):
        return lax.dynamic_slice(gains[line], (part_index * head_share,), (head_share,))

    return (
        output,
        input_grad,
        dq_weight,
        dk_weight,
        dv_weight,
        dgate_weight,
        out_weight,
        *ff_sums,
        gains[:lines].reshape(share),
        gains[lines : 2 * lines].reshape(share),
        head_gain(2 * lines),
        head_gain(2 * lines + 1),
    )


def solution(mesh):
    return jax.shard_map(
        on_device,
        mesh=mesh,
        in_specs=(
            P(("seq", "head"), None, None),
            P(("seq", "head"), None, None),
            P(),
            P(None, "head"),
            P(None, "head"),
            P(None, "head"),
            P(None, "head"),
            P("head", None),
            P(None, "head"),
            P(None, "head"),
            P("head", None),
            P(),
            P(),
            P(),
            P(),
        ),
        out_specs=(
            P(("seq", "head"), None, None),
            P(("seq", "head"), None, None),
            P(None, "head"),
            P(None, "head"),
            P(None, "head"),
            P(None, "head"),
            P("head", None),
            P(None, "head"),
            P(None, "head"),
            P("head", None),
            P("head"),
            P("head"),
            P("head"),
            P("head"),
        ),
        check_vma=False,
    )
```

```python
import functools

import jax
import jax.numpy as jnp
from jax import lax
from jax.experimental import pallas as pl
from jax.experimental.pallas import tpu as pltpu
from jax.sharding import PartitionSpec as P

EPS = 1e-06
THETA = 1000000.0
LOG2E = 1.4426950408889634
MIB = 1024 * 1024
LOW = jnp.bfloat16
F32 = jnp.float32
MESH = pl.DeviceIdType.MESH


def mm(left, right):
    return jnp.dot(left, right, preferred_element_type=F32)


def mm_t(left, right):
    return lax.dot_general(left, right, (((1,), (1,)), ((), ())), preferred_element_type=F32)


def t_mm(left, right):
    return lax.dot_general(left, right, (((0,), (0,)), ((), ())), preferred_element_type=F32)


def shape_of(rows, columns, kind):
    return jax.ShapeDtypeStruct((rows, columns), kind)


def params(mib, **extra):
    return pltpu.CompilerParams(vmem_limit_bytes=mib * MIB, **extra)


def takes(microseconds):
    return pl.CostEstimate(
        flops=int(microseconds * 1.15e9), bytes_accessed=int(microseconds * 3.69e6), transcendentals=0
    )


WHOLE = pl.BlockSpec(memory_space=pltpu.VMEM)
SCALARS = pl.BlockSpec(memory_space=pltpu.SMEM)


def full_block(array):
    return pl.BlockSpec(array.shape, lambda i: (0,) * len(array.shape))


def inverse_rms(values):
    return lax.rsqrt(jnp.mean(values * values, axis=-1, keepdims=True) + EPS)


def turn(values, cosine, sine):
    return values * cosine + pltpu.roll(values, values.shape[-1] // 2, 1) * sine


def turn_back(grads, cosine, sine):
    return grads * cosine + pltpu.roll(grads * sine, grads.shape[-1] // 2, 1)


def live_blocks(place_ref, rows, first=0):
    start, length = place_ref[0], place_ref[1 + first + pl.program_id(0)]
    whole = jnp.minimum(start // rows, length // rows)
    end = jnp.minimum(start // rows + 1, (length + rows - 1) // rows)
    end = jnp.where(start < length, end, 0)
    return jnp.minimum(whole, end), end, start, length


def attend_kernel(
    group, head_dim, place_ref, q_ref, kv_ref, gate_ref, att_ref, acted_ref, inv_ref, acc_ref, sum_ref
):
    rows = q_ref.shape[1]
    heads = q_ref.shape[2] // head_dim
    kv_heads = heads // group
    factor = head_dim ** (-0.5) * LOG2E
    acc_ref[...] = jnp.zeros_like(acc_ref)
    sum_ref[...] = jnp.zeros_like(sum_ref)
    whole, end, start, length = live_blocks(place_ref, rows)

    def one_block(j, masked, width=1):
        tall = width * rows
        span = pl.ds(pl.multiple_of(j * rows, rows), tall)
        if masked:
            key_pos = j * rows + lax.broadcasted_iota(jnp.int32, (rows, rows), 1)
            query_pos = start + lax.broadcasted_iota(jnp.int32, (rows, rows), 0)
            allowed = (key_pos <= query_pos) & (key_pos < length)
        for h in range(heads):
            c = h // group
            keys = kv_ref[0, span, c * head_dim : (c + 1) * head_dim]
            values = kv_ref[0, span, (kv_heads + c) * head_dim : (kv_heads + c + 1) * head_dim]
            weights = jnp.exp2(mm_t(q_ref[0, :, h * head_dim : (h + 1) * head_dim], keys) * factor)
            if masked:
                weights = jnp.where(allowed, weights, 0.0)
            total = weights[:, :128]
            for piece in range(1, tall // 128):
                total = total + weights[:, piece * 128 : (piece + 1) * 128]
            sum_ref[h] = sum_ref[h] + total
            acc_ref[h] = acc_ref[h] + mm(weights.astype(LOW), values)

    def plain(j, carry):
        one_block(j, False)
        return carry

    def pair(j, carry):
        one_block(2 * j, False, 2)
        return carry

    def edge(j, carry):
        one_block(j, True)
        return carry

    lax.fori_loop(0, whole // 2, pair, 0)
    lax.fori_loop(whole // 2 * 2, whole, plain, 0)
    lax.fori_loop(whole, end, edge, 0)
    lane = lax.broadcasted_iota(jnp.int32, inv_ref.shape[1:], 1)
    kept = jnp.zeros(inv_ref.shape[1:], F32)
    for h in range(heads):
        total = jnp.sum(sum_ref[h], axis=1, keepdims=True)
        inverse = 1.0 / jnp.where(total > 0.0, total, 1.0)
        attended = acc_ref[h] * inverse
        columns = slice(h * head_dim, (h + 1) * head_dim)
        att_ref[0, :, columns] = attended
        acted_ref[0, :, columns] = (attended * jax.nn.sigmoid(gate_ref[0, :, columns])).astype(LOW)
        kept = jnp.where(lane == h, inverse, kept)
    inv_ref[0] = kept


def by_sequence(array):
    return pl.BlockSpec((1,) + array.shape[1:], lambda b: (b,) + (0,) * (len(array.shape) - 1))


def attend(place, q, kv, gate, group, head_dim):
    batch, rows, width = q.shape
    heads = width // head_dim
    outs = [
        jax.ShapeDtypeStruct((batch, rows, width), F32),
        jax.ShapeDtypeStruct((batch, rows, width), LOW),
        jax.ShapeDtypeStruct((batch, rows, 128), F32),
    ]
    return pl.pallas_call(
        functools.partial(attend_kernel, group, head_dim),
        grid=(batch,),
        in_specs=[SCALARS, by_sequence(q), by_sequence(kv), by_sequence(gate)],
        out_specs=[by_sequence(x) for x in outs],
        out_shape=outs,
        scratch_shapes=[
            pltpu.VMEM((heads, rows, head_dim), F32),
            pltpu.VMEM((heads, rows, 128), F32),
        ],
        compiler_params=params(58),
        cost_estimate=takes(18),
        name="attend",
    )(place, q, kv, gate)


def norm_turn_back(grad, raw, head_gain, cosine, sine):
    grad = turn_back(grad, cosine, sine)
    inverse = inverse_rms(raw)
    gain_grad = jnp.sum(grad * raw * inverse, axis=0, keepdims=True)
    grad = grad * head_gain
    mean = jnp.mean(grad * raw, axis=-1, keepdims=True)
    return inverse * (grad - raw * (inverse * inverse * mean)), gain_grad


class HeadsBack:
    def __init__(
        self, group, start, length, q, kv, wo, att, gate, inv, qraw, cos, sin, qgain,
        dq, dkv, dgate, scaled, corr, acc,
    ):
        self.group, self.start, self.length = group, start, length
        self.q, self.kv, self.wo, self.att, self.gate, self.inv, self.qraw = q, kv, wo, att, gate, inv, qraw
        self.cos, self.sin, self.qgain = cos, sin, qgain
        self.dq, self.dkv, self.dgate, self.scaled, self.corr, self.acc = dq, dkv, dgate, scaled, corr, acc
        self.rows, self.head_dim = q.shape[0], cos.shape[1]
        self.heads = q.shape[1] // self.head_dim
        self.kv_heads = self.heads // group
        self.scale = self.head_dim ** (-0.5)

    def columns(self, h):
        return slice(h * self.head_dim, (h + 1) * self.head_dim)

    def begin(self, r):
        acted_grad = mm_t(r, self.wo[...])
        lane = lax.broadcasted_iota(jnp.int32, self.inv.shape, 1)
        kept = jnp.zeros(self.inv.shape, F32)
        for h in range(self.heads):
            columns = self.columns(h)
            sigmoid = jax.nn.sigmoid(self.gate[:, columns])
            attended = self.att[:, columns]
            grad = acted_grad[:, columns]
            self.dgate[:, columns] = (grad * attended * sigmoid * (1.0 - sigmoid)).astype(LOW)
            grad = grad * sigmoid
            inverse = self.inv[:, h : h + 1]
            self.scaled[:, columns] = (grad * inverse).astype(LOW)
            total = jnp.sum(grad * attended, axis=1, keepdims=True) * inverse
            kept = jnp.where(lane == h, total, kept)
        self.corr[...] = kept.T
        self.acc[...] = jnp.zeros_like(self.acc)

    def block(self, j, masked, width=1):
        rows, group = self.rows, self.group
        tall = width * rows
        span = pl.ds(pl.multiple_of(j * rows, rows), tall)
        if masked:
            key_pos = j * rows + lax.broadcasted_iota(jnp.int32, (tall, rows), 0)
            query_pos = self.start + lax.broadcasted_iota(jnp.int32, (tall, rows), 1)
            allowed = (key_pos <= query_pos) & (key_pos < self.length)
        for c in range(self.kv_heads):
            key_columns, value_columns = self.columns(c), self.columns(self.kv_heads + c)
            keys = self.kv[span, key_columns]
            values = self.kv[span, value_columns]
            dk = jnp.zeros((tall, self.head_dim), F32)
            dv = jnp.zeros((tall, self.head_dim), F32)
            for h in range(c * group, (c + 1) * group):
                queries = self.q[:, self.columns(h)]
                scaled = self.scaled[:, self.columns(h)]
                weights = jnp.exp2(mm_t(keys, queries) * (self.scale * LOG2E))
                if masked:
                    weights = jnp.where(allowed, weights, 0.0)
                dv = dv + mm(weights.astype(LOW), scaled)
                score = (weights * (mm_t(values, scaled) - self.corr[h : h + 1, :])).astype(LOW)
                dk = dk + mm(score, queries)
                self.acc[h] = self.acc[h] + t_mm(keys, score)
            self.dkv[span, key_columns] = (dk * self.scale).astype(LOW)
            self.dkv[span, value_columns] = dv.astype(LOW)

    def clear(self, j):
        span = pl.ds(pl.multiple_of(j * self.rows, self.rows), self.rows)
        self.dkv[span, :] = jnp.zeros((self.rows, self.dkv.shape[1]), LOW)

    def end(self):
        gain_total = jnp.zeros((1, self.head_dim), F32)
        for h in range(self.heads):
            columns = self.columns(h)
            grad, gain_grad = norm_turn_back(
                self.acc[h].T * self.scale, self.qraw[:, columns], self.qgain[...], self.cos[...], self.sin[...]
            )
            self.dq[:, columns] = grad.astype(LOW)
            gain_total = gain_total + gain_grad
        return gain_total


def heads_back_scratch(heads, rows, head_dim):
    return [
        pltpu.VMEM((rows, heads * head_dim), LOW),
        pltpu.VMEM((128, rows), F32),
        pltpu.VMEM((heads, head_dim, rows), F32),
    ]


def attend_back_kernel(
    group,
    place_ref, q_ref, kv_ref, r_ref, wo_ref, att_ref, gate_ref, inv_ref, qraw_ref, cos_ref, sin_ref, qgain_ref,
    first_gain_ref, first_dq, first_dkv, first_dgate,
    dq_ref, dkv_ref, dgate_ref, dqgain_ref,
    scaled_ref, corr_ref, acc_ref,
):
    del first_dq, first_dkv, first_dgate
    rows = q_ref.shape[1]
    whole, end, start, length = live_blocks(place_ref, rows, 1)
    back = HeadsBack(
        group, start, length, q_ref.at[0], kv_ref.at[0], wo_ref, att_ref.at[0], gate_ref.at[0], inv_ref.at[0],
        qraw_ref.at[0], cos_ref, sin_ref, qgain_ref, dq_ref.at[0], dkv_ref.at[0], dgate_ref.at[0],
        scaled_ref, corr_ref, acc_ref,
    )
    back.begin(r_ref[0])

    def plain(j, carry):
        back.block(j, False)
        return carry

    def pair(j, carry):
        back.block(2 * j, False, 2)
        return carry

    def edge(j, carry):
        back.block(j, True)
        return carry

    def empty(j, carry):
        back.clear(j)
        return carry

    lax.fori_loop(0, whole // 2, pair, 0)
    lax.fori_loop(whole // 2 * 2, whole, plain, 0)
    lax.fori_loop(whole, end, edge, 0)
    lax.fori_loop(end, dkv_ref.shape[1] // rows, empty, 0)
    gain_total = back.end()

    @pl.when(pl.program_id(0) == 0)
    def _():
        dqgain_ref[...] = first_gain_ref[...] + gain_total

    @pl.when(pl.program_id(0) > 0)
    def _():
        dqgain_ref[...] = dqgain_ref[...] + gain_total


def attend_back(place, q, kv, r, wo, att, gate, inv, qraw, cosine, sine, qgain, group, first_gain, firsts):
    batch, rows, width = q.shape
    head_dim = qgain.shape[1]
    any_place = pl.BlockSpec(memory_space=pl.ANY)

    def later(array):
        return pl.BlockSpec((1,) + array.shape[1:], lambda b: (b + 1,) + (0,) * (len(array.shape) - 1))

    line = pl.BlockSpec((1, head_dim), lambda b: (0, 0))
    return pl.pallas_call(
        functools.partial(attend_back_kernel, group),
        grid=(batch - 1,),
        in_specs=[SCALARS, later(q), later(kv), later(r), full_block(wo)]
        + [later(x) for x in (att, gate, inv, qraw)]
        + [full_block(x) for x in (cosine, sine, qgain, first_gain)]
        + [any_place] * 3,
        out_specs=[later(x) for x in firsts] + [line],
        out_shape=[jax.ShapeDtypeStruct(x.shape, x.dtype) for x in firsts] + [shape_of(1, head_dim, F32)],
        scratch_shapes=heads_back_scratch(width // head_dim, rows, head_dim),
        input_output_aliases={13: 0, 14: 1, 15: 2},
        compiler_params=params(58),
        cost_estimate=takes(3),
        name="attend_back",
    )(place, q, kv, r, wo, att, gate, inv, qraw, cosine, sine, qgain, first_gain, *firsts)


class Line:
    def __init__(self, pieces, count, part_ref, own_ref, right_ref, left_ref, sems, spread=None):
        self.sums = part_ref is not None
        self.pieces, self.count = pieces, count
        self.place = lax.axis_index("head")
        self.part_ref, self.own_ref = part_ref, own_ref
        self.right_ref, self.left_ref = right_ref, left_ref
        self.sems = sems
        self.spread = spread

    def barrier(self, digits=()):
        sem = pltpu.get_barrier_semaphore()
        place, count = self.place, self.count
        for digit in digits:
            partner = flipped(lax.axis_index("seq"), digit)
            pl.semaphore_signal(sem, inc=1, device_id={"seq": partner}, device_id_type=MESH)

        @pl.when(place > 0)
        def _():
            pl.semaphore_signal(sem, inc=1, device_id={"head": place - 1}, device_id_type=MESH)

        @pl.when(place < count - 1)
        def _():
            pl.semaphore_signal(sem, inc=1, device_id={"head": place + 1}, device_id_type=MESH)

        inside = (place > 0) & (place < count - 1)

        @pl.when(inside)
        def _():
            pl.semaphore_wait(sem, 2 + len(digits))

        @pl.when(jnp.logical_not(inside))
        def _():
            pl.semaphore_wait(sem, 1 + len(digits))

    def barrier_all(self, digits):
        sem = pltpu.get_barrier_semaphore()
        for digit in digits:
            partner = flipped(lax.axis_index("seq"), digit)
            pl.semaphore_signal(sem, inc=1, device_id={"seq": partner}, device_id_type=MESH)
        for distance in range(1, self.count):
            other = lax.rem(self.place + distance, self.count)
            pl.semaphore_signal(sem, inc=1, device_id={"head": other}, device_id_type=MESH)
        pl.semaphore_wait(sem, self.count - 1 + len(digits))

    def copy(self, ref, send, receive, p, t, step):
        return pltpu.make_async_remote_copy(
            src_ref=ref,
            dst_ref=ref,
            send_sem=self.sems[send].at[p, t],
            recv_sem=self.sems[receive].at[p, t],
            device_id={"head": jnp.clip(self.place + step, 0, self.count - 1)},
            device_id_type=MESH,
        )

    def sum_copy(self, p, t, step):
        ref = self.right_ref if step > 0 else self.left_ref
        base = 0 if step > 0 else 2
        return self.copy(ref.at[p, t], base, base + 1, p, t, step)

    def spread_copy(self, p, t, step):
        first = 4 if self.sums else 0
        return self.copy(self.spread(p, t), first if step > 0 else first + 1, first + 2, p, t, step)

    def send_sums(self, p, distance):
        place, count = self.place, self.count
        for step, ref in ((1, self.right_ref), (-1, self.left_ref)):
            t = place + step * distance
            first = place == (0 if step > 0 else count - 1)

            @pl.when((t >= 0) & (t < count))
            def _(t=t, step=step, ref=ref, first=first):
                @pl.when(first)
                def _():
                    ref[p, t] = self.part_ref[t].astype(LOW)

                @pl.when(jnp.logical_not(first))
                def _():
                    self.sum_copy(p, t, step).wait_recv()
                    ref[p, t] = (ref[p, t].astype(F32) + self.part_ref[t].astype(F32)).astype(LOW)

                self.sum_copy(p, t, step).start()

    def keep_own(self, p):
        self.own_ref[p] = self.part_ref[self.place].astype(F32)

    def finish_own(self, p):
        place, count = self.place, self.count
        for step, ref, inner in ((1, self.right_ref, place > 0), (-1, self.left_ref, place < count - 1)):

            @pl.when(inner)
            def _(step=step, ref=ref):
                self.sum_copy(p, place, step).wait_recv()
                self.own_ref[p] = self.own_ref[p] + ref[p, place].astype(F32)

    def hand_out(self, p):
        place, count = self.place, self.count

        @pl.when(place < count - 1)
        def _():
            self.spread_copy(p, place, 1).start()

        @pl.when(place > 0)
        def _():
            self.spread_copy(p, place, -1).start()

    def hand_on(self, p, distance):
        place, count = self.place, self.count
        for step, more in ((1, place < count - 1), (-1, place > 0)):
            t = place - step * distance

            @pl.when((t >= 0) & (t < count))
            def _(t=t, step=step, more=more):
                self.spread_copy(p, t, step).wait_recv()

                @pl.when(more)
                def _():
                    self.spread_copy(p, t, step).start()

    def drain(self):
        place, count = self.place, self.count

        def one(p, carry):
            for t in range(count):
                if self.sums:

                    @pl.when(t > place)
                    def _(t=t):
                        self.sum_copy(p, t, 1).wait_send()

                    @pl.when(t < place)
                    def _(t=t):
                        self.sum_copy(p, t, -1).wait_send()

                if self.spread is not None:

                    @pl.when((t <= place) & (place < count - 1))
                    def _(t=t):
                        self.spread_copy(p, t, 1).wait_send()

                    @pl.when((t >= place) & (place > 0))
                    def _(t=t):
                        self.spread_copy(p, t, -1).wait_send()

            return carry

        lax.fori_loop(0, self.pieces, one, 0)


def line_scratch(pieces, count, rows, model, part_kind, spread):
    slots = (pieces, count)
    scratch = [
        pltpu.VMEM((pieces, rows, model), F32),
        pltpu.VMEM((pieces, count, rows, model), LOW),
        pltpu.VMEM((pieces, count, rows, model), LOW),
    ] + [pltpu.SemaphoreType.DMA(slots)] * (7 if spread else 4)
    if part_kind is not None:
        scratch = [pltpu.VMEM((count, rows, model), part_kind)] + scratch
    return scratch


def both_ways(index, limit, body):
    @pl.when((index >= 0) & (index < limit))
    def _():
        body(index)


def front_kernel(
    pieces, count, head_dim,
    tok_ref, gain_ref, cos_ref, sin_ref, qgain_ref, kgain_ref, wq_ref, wk_ref, wv_ref, wg_ref,
    normed_ref, qraw_ref, q_ref, kraw_ref, kv_ref, gate_ref,
    all_ref, *sems,
):
    rows, model = tok_ref.shape[1], tok_ref.shape[2]
    tall = count * rows
    line = Line(pieces, count, None, None, None, None, sems, spread=lambda p, t: all_ref.at[p, t])
    line.barrier()
    for p in range(pieces):
        all_ref[p, line.place] = tok_ref[p]

    def project(p):
        b, half = p // 2, p % 2

        def keep(ref, value):
            ref[b, :, half] = value.astype(ref.dtype).reshape(count, rows, value.shape[-1])

        x = all_ref[p].reshape(tall, model).astype(F32)
        normed = (x * inverse_rms(x) * gain_ref[...]).astype(LOW)
        keep(normed_ref, normed)
        cosine = cos_ref[:, half].reshape(tall, head_dim)
        sine = sin_ref[:, half].reshape(tall, head_dim)

        def turned(raw, head_gain):
            parts = []
            for h in range(raw.shape[1] // head_dim):
                part = raw[:, h * head_dim : (h + 1) * head_dim]
                parts.append(turn(part * inverse_rms(part) * head_gain, cosine, sine).astype(LOW))
            return parts

        raw = mm(normed, wk_ref[...])
        keep(kraw_ref, raw)
        values = mm(normed, wv_ref[...]).astype(LOW)
        keep(kv_ref, jnp.concatenate(turned(raw, kgain_ref[...]) + [values], axis=1))
        raw = mm(normed, wq_ref[...])
        keep(qraw_ref, raw)
        keep(q_ref, jnp.concatenate(turned(raw, qgain_ref[...]), axis=1))
        keep(gate_ref, mm(normed, wg_ref[...]))

    def turn_once(k, carry):
        both_ways(k, pieces, line.hand_out)
        for distance in range(1, count):
            both_ways(k - 1, pieces, lambda p, d=distance: line.hand_on(p, d))
        both_ways(k - 1, pieces, project)
        return carry

    lax.fori_loop(0, pieces + 1, turn_once, 0)
    line.drain()


def front_step(tok, gain, cosine, sine, qgain, kgain, wq, wk, wv, wg, count):
    pieces, rows, model = tok.shape
    batch = pieces // 2
    head_dim = qgain.shape[1]
    nq, nk = wq.shape[1], wk.shape[1]

    def wide(columns, kind):
        return jax.ShapeDtypeStruct((batch, count, 2, rows, columns), kind)

    slots = (pieces, count)
    return pl.pallas_call(
        functools.partial(front_kernel, pieces, count, head_dim),
        in_specs=[WHOLE] * 10,
        out_specs=[WHOLE] * 6,
        out_shape=[
            wide(model, LOW), wide(nq, F32), wide(nq, LOW), wide(nk, F32), wide(2 * nk, LOW), wide(nq, F32)
        ],
        scratch_shapes=[pltpu.VMEM((pieces, count, rows, model), LOW)]
        + [pltpu.SemaphoreType.DMA(slots)] * 3,
        compiler_params=params(34, collective_id=2, has_side_effects=True),
        cost_estimate=takes(95),
        name="front",
    )(
        tok, gain, cosine.reshape(count, 2, rows, head_dim), sine.reshape(count, 2, rows, head_dim),
        qgain, kgain, wq, wk, wv, wg,
    )


def middle_kernel(
    pieces, count,
    acted_ref, tok_ref, gain_ref, wo_ref, masked_hbm, wg_hbm, wl_hbm, wd_hbm,
    middle_ref, dgain_ref, normed_hbm, hidden_hbm, dg_hbm, dl_hbm, dn_hbm,
    mid_ref, wg_ref, wl_ref, wd_ref, masked_ref, normed_ref, hidden_ref, dg_ref, dl_ref, dn_ref, acc_ref,
    load_sem, masked_sem, store_sem,
    part_ref, own_ref, right_ref, left_ref, *sems,
):
    rows, model = own_ref.shape[1], own_ref.shape[2]
    tall = count * rows
    hidden = wg_ref.shape[1]
    line = Line(
        pieces, count, part_ref, own_ref, right_ref, left_ref, sems, spread=lambda p, t: mid_ref.at[p, t]
    )
    place = line.place
    loads = [
        pltpu.make_async_copy(source, target, load_sem.at[i])
        for i, (source, target) in enumerate(((wg_hbm, wg_ref), (wl_hbm, wl_ref), (wd_hbm, wd_ref)))
    ]
    line.barrier()
    for load in loads:
        load.start()
    dgain_ref[...] = jnp.zeros_like(dgain_ref)
    tiles = 3
    tile = hidden // tiles

    def masked_copy(p):
        return pltpu.make_async_copy(masked_hbm.at[:, p], masked_ref, masked_sem)

    def stores(p):
        pairs = (
            (normed_ref, normed_hbm), (hidden_ref, hidden_hbm), (dg_ref, dg_hbm), (dl_ref, dl_hbm),
            (dn_ref, dn_hbm),
        )
        return [
            pltpu.make_async_copy(source, target.at[:, p], store_sem.at[i])
            for i, (source, target) in enumerate(pairs)
        ]

    def begin(p):
        acted = acted_ref[p // 2, :, p % 2].reshape(tall, acted_ref.shape[-1])
        part_ref[...] = mm(acted, wo_ref[...]).reshape(count, rows, model)
        line.keep_own(p)

    def own(p):
        line.finish_own(p)
        middle = own_ref[p] + tok_ref[p].astype(F32)
        middle_ref[p] = middle
        mid_ref[p, place] = middle.astype(LOW)
        line.hand_out(p)

    def units_begin(p):
        line.hand_on(p, count - 1)

        @pl.when(p > 0)
        def _():
            for store in stores(p - 1):
                store.wait()

        x = mid_ref[p].reshape(tall, model).astype(F32)
        normed = (x * inverse_rms(x) * gain_ref[...]).astype(LOW)
        normed_ref[...] = normed.reshape(count, rows, model)
        masked_copy(p).wait()

        @pl.when(p == 0)
        def _():
            for load in loads:
                load.wait()

    def units_tile(i):
        span = slice(i * tile, (i + 1) * tile)
        normed = normed_ref[...].reshape(tall, model)
        gate = mm(normed, wg_ref[:, span])
        lift = mm(normed, wl_ref[:, span])
        grad = mm_t(masked_ref[...].reshape(tall, model), wd_ref[span, :])
        sigmoid = jax.nn.sigmoid(gate)
        silu = gate * sigmoid
        lift_grad = (grad * silu).astype(LOW)
        gate_grad = (grad * lift * (sigmoid + silu * (1.0 - sigmoid))).astype(LOW)
        hidden_ref[:, :, span] = (silu * lift).astype(LOW).reshape(count, rows, tile)
        dg_ref[:, :, span] = gate_grad.reshape(count, rows, tile)
        dl_ref[:, :, span] = lift_grad.reshape(count, rows, tile)
        part = mm_t(gate_grad, wg_ref[:, span]) + mm_t(lift_grad, wl_ref[:, span])
        if i == 0:
            acc_ref[...] = part
        else:
            acc_ref[...] = acc_ref[...] + part

    def units_end(p):
        total = acc_ref[...]
        dn_ref[...] = total.astype(LOW).reshape(count, rows, model)
        x = mid_ref[p].reshape(tall, model).astype(F32)
        dgain_ref[...] = dgain_ref[...] + jnp.sum(total * x * inverse_rms(x), axis=0, keepdims=True)
        for store in stores(p):
            store.start()

        @pl.when(p < pieces - 1)
        def _():
            masked_copy(p + 1).start()

    masked_copy(0).start()

    def turn_once(k, carry):
        both_ways(k, pieces, begin)
        for i in range(max(tiles, count - 1)):
            if i < count - 1:
                both_ways(k, pieces, lambda p, i=i: line.send_sums(p, count - 1 - i))
            if i == 0:
                both_ways(k - 1, pieces, own)
                both_ways(k - 2, pieces, units_begin)
            elif i < count - 1:
                both_ways(k - 1, pieces, lambda p, i=i: line.hand_on(p, i))
            if i < tiles:
                both_ways(k - 2, pieces, lambda p, i=i: units_tile(i))
        both_ways(k - 2, pieces, units_end)
        return carry

    lax.fori_loop(0, pieces + 2, turn_once, 0)
    for store in stores(pieces - 1):
        store.wait()
    line.drain()


def middle_step(acted, tok, gain, wo, masked, wg, wl, wd, count):
    pieces, rows, model = tok.shape
    hidden = wg.shape[1]
    any_place = pl.BlockSpec(memory_space=pl.ANY)

    def wide(columns, kind=LOW):
        return jax.ShapeDtypeStruct((count, pieces, rows, columns), kind)

    def room(columns, kind=LOW):
        return pltpu.VMEM((count, rows, columns), kind)

    return pl.pallas_call(
        functools.partial(middle_kernel, pieces, count),
        in_specs=[WHOLE] * 4 + [any_place] * 4,
        out_specs=[WHOLE] * 2 + [any_place] * 5,
        out_shape=[
            jax.ShapeDtypeStruct((pieces, rows, model), F32), shape_of(1, model, F32),
            wide(model), wide(hidden), wide(hidden), wide(hidden), wide(model),
        ],
        scratch_shapes=[
            pltpu.VMEM((pieces, count, rows, model), LOW),
            pltpu.VMEM(wg.shape, LOW), pltpu.VMEM(wl.shape, LOW), pltpu.VMEM(wd.shape, LOW),
            room(model), room(model), room(hidden), room(hidden), room(hidden), room(model),
            pltpu.VMEM((count * rows, model), F32),
            pltpu.SemaphoreType.DMA((3,)), pltpu.SemaphoreType.DMA, pltpu.SemaphoreType.DMA((5,)),
        ]
        + line_scratch(pieces, count, rows, model, F32, True),
        compiler_params=params(58, collective_id=0, has_side_effects=True),
        cost_estimate=takes(128),
        name="middle",
    )(acted, tok, gain, wo, masked, wg, wl, wd)


def flipped(place, mask):
    bit = 1
    while bit <= mask:
        if mask & bit:
            place = place + (1 - 2 * (place // bit % 2)) * bit
        bit *= 2
    return place


def digit_orders(count, batch):
    upper = [1 << i for i in range(1, count.bit_length() - 1)]
    return [(upper if b % 2 == 0 else upper[::-1]) + [1] for b in range(batch)]


def greet(place, digits):
    sem = pltpu.get_barrier_semaphore()
    for digit in digits:
        pl.semaphore_signal(sem, inc=1, device_id={"seq": flipped(place, digit)}, device_id_type=MESH)
    pl.semaphore_wait(sem, len(digits))


def block_gathers(count, batch, out, sources, send_sem, receive_sem):
    place = lax.axis_index("seq")
    orders = digit_orders(count, batch)
    steps = len(orders[0])
    started = []

    def copy(b, mask, step):
        digit = orders[b][step]
        block = out(b).at[flipped(place, mask)]
        return pltpu.make_async_remote_copy(
            src_ref=sources(b) if mask == 0 else block,
            dst_ref=block,
            send_sem=send_sem.at[b, step, mask],
            recv_sem=receive_sem.at[b, mask | digit],
            device_id={"seq": flipped(place, digit)},
            device_id_type=MESH,
        )

    def pass_on(b, mask, first):
        for step in range(first, steps):
            one = copy(b, mask, step)
            one.start()
            started.append(one)

    def arrive(b, mask, level):
        block = out(b).at[flipped(place, mask)]
        pltpu.make_async_remote_copy(
            src_ref=block,
            dst_ref=block,
            send_sem=send_sem.at[b, 0, mask],
            recv_sem=receive_sem.at[b, mask],
            device_id={"seq": flipped(place, orders[b][level])},
            device_id_type=MESH,
        ).wait_recv()
        pass_on(b, mask, level + 1)

    begins = [functools.partial(pass_on, b, 0, 0) for b in range(batch)]
    arrivals = []
    for level in range(steps):
        for turn in range(1 << level):
            for b in range(batch):
                mask = orders[b][level]
                for i in range(level):
                    if turn >> i & 1:
                        mask |= orders[b][i]
                arrivals.append((1.0 if level == steps - 1 else 4.0, functools.partial(arrive, b, mask, level)))

    def drain():
        for one in started:
            one.wait_send()

    return begins, arrivals, drain


def gather_kernel(count, batch, own_ref, out_ref, local_sem, send_sem, receive_sem):
    place = lax.axis_index("seq")
    greet(place, digit_orders(count, 1)[0])
    local = [
        pltpu.make_async_copy(own_ref.at[b], out_ref.at[b, place], local_sem.at[b]) for b in range(batch)
    ]
    for copy in local:
        copy.start()
    begins, arrivals, drain = block_gathers(
        count, batch, lambda b: out_ref.at[b], lambda b: own_ref.at[b], send_sem, receive_sem
    )
    for begin in begins:
        begin()
    for _, event in arrivals:
        event()
    drain()
    for copy in local:
        copy.wait()


def gather_blocks(own):
    batch, rows, columns = own.shape
    count = lax.axis_size("seq")
    steps = count.bit_length() - 1
    any_place = pl.BlockSpec(memory_space=pl.ANY)
    out = pl.pallas_call(
        functools.partial(gather_kernel, count, batch),
        in_specs=[any_place],
        out_specs=any_place,
        out_shape=jax.ShapeDtypeStruct((batch, count, rows, columns), LOW),
        scratch_shapes=[
            pltpu.SemaphoreType.DMA((batch,)),
            pltpu.SemaphoreType.DMA((batch, steps, count)),
            pltpu.SemaphoreType.DMA((batch, count)),
        ],
        compiler_params=params(4, collective_id=3, has_side_effects=True),
        cost_estimate=takes(41),
        name="gather_blocks",
    )(own)
    return out.reshape(batch, count * rows, columns)


def block_sums(count, batch, parts, finish, slots, send_sem, receive_sem, near):
    place = lax.axis_index("seq")
    orders = [order[::-1] for order in digit_orders(count, batch)]
    steps = len(orders[0])

    def masks_at(b, step):
        found = [0]
        for digit in orders[b][step + 1 :][::-1]:
            found = [mask | digit for mask in found] + found
        return found

    numbers = {}
    for b in range(batch):
        place_in = 0
        for step in range(steps):
            for mask in masks_at(b, step):
                numbers[b, step, mask] = place_in
                place_in += 1

    def slot(b, step, mask):
        return slots.at[b, numbers[b, step, mask]]

    def transfer(b, step, mask):
        digit = orders[b][step]
        number = numbers[b, step, mask]
        if step == 0:
            source = parts(b).at[flipped(place, mask | digit)]
        else:
            source = slot(b, step - 1, mask | digit)
        return pltpu.make_async_remote_copy(
            src_ref=source,
            dst_ref=slots.at[b, number],
            send_sem=send_sem.at[b, number],
            recv_sem=receive_sem.at[b, number],
            device_id={"seq": flipped(place, digit)},
            device_id_type=MESH,
        )

    started = []

    def begin():
        for turn in range(count // 2):
            for b in range(batch):
                copy = transfer(b, 0, masks_at(b, 0)[turn])
                copy.start()
                started.append(copy)

    def take(b, step, mask):
        transfer(b, step, mask).wait_recv()
        held = parts(b).at[flipped(place, mask)] if step == 0 else slot(b, step - 1, mask)
        total = held[...].astype(F32) + slot(b, step, mask)[...].astype(F32)
        if step == steps - 1:
            finish(b, total)
        else:
            slot(b, step, mask)[...] = total.astype(LOW)
            if mask & orders[b][step + 1]:
                copy = transfer(b, step + 1, mask & ~orders[b][step + 1])
                copy.start()
                started.append(copy)

    events = []
    for step in range(steps):
        for turn in range(len(masks_at(0, step))):
            for b in range(batch):
                events.append((near if step == 0 else 4.0, functools.partial(take, b, step, masks_at(b, step)[turn])))

    def drain():
        for copy in started:
            copy.wait_send()

    return begin, events, drain


def interleaved(*lists):
    spent = [0.0] * len(lists)
    whole = [sum(time for time, _ in calls) for calls in lists]
    taken = [0] * len(lists)
    while any(taken[i] < len(calls) for i, calls in enumerate(lists)):
        i = min((i for i, calls in enumerate(lists) if taken[i] < len(calls)), key=lambda i: spent[i])
        time, call = lists[i][taken[i]]
        call()
        spent[i] += time / whole[i]
        taken[i] += 1

def residual_kernel(
    pieces, count, halves, group, seq_count,
    place_ref, dn_ref, middle_ref, masked_ref, gain_ref, wo_ref, cos_ref, sin_ref, qgain_ref,
    q_hbm, kv_hbm, att_hbm, gate_hbm, inv_hbm, qraw_hbm,
    residual_ref, r_ref, dqgain_ref, dq_hbm, dkv_hbm, dgate_hbm,
    q_ref, kv_ref, att_ref, gate_ref, inv_ref, qraw_ref, dq_ref, dkv_ref, dgate_ref,
    scaled_ref, corr_ref, acc_ref, load_sem, store_sem, block_sem,
    part_ref, own_ref, right_ref, left_ref, *sems,
):
    rows, model = own_ref.shape[1], own_ref.shape[2]
    query_rows = q_ref.shape[0]
    line = Line(
        pieces, count, part_ref, own_ref, right_ref, left_ref, sems,
        spread=lambda p, t: r_ref.at[p // halves, t, p % halves],
    )
    pairs = (
        (q_hbm, q_ref), (kv_hbm, kv_ref), (att_hbm, att_ref), (gate_hbm, gate_ref), (inv_hbm, inv_ref),
        (qraw_hbm, qraw_ref),
    )
    loads = [
        pltpu.make_async_copy(source.at[0], target, load_sem.at[i]) for i, (source, target) in enumerate(pairs)
    ]
    stores = [
        pltpu.make_async_copy(dq_ref, dq_hbm.at[0], store_sem.at[0]),
        pltpu.make_async_copy(dgate_ref, dgate_hbm.at[0], store_sem.at[1]),
    ]
    line.barrier()
    for load in loads:
        load.start()
    block_index = lax.axis_index("seq")
    back = HeadsBack(
        group, block_index * query_rows, place_ref[1], q_ref, kv_ref, wo_ref, att_ref, gate_ref, inv_ref, qraw_ref,
        cos_ref, sin_ref, qgain_ref, dq_ref, dkv_ref, dgate_ref, scaled_ref, corr_ref, acc_ref,
    )

    def begin(p):
        part_ref[...] = dn_ref[:, p]
        line.keep_own(p)

    def own(p):
        line.finish_own(p)
        x = middle_ref[p].astype(LOW).astype(F32)
        residual = masked_ref[p] + norm_back(own_ref[p], x, gain_ref[...])
        residual_ref[p] = residual
        r_ref[p // halves, line.place, p % halves] = residual.astype(LOW)
        line.hand_out(p)

    def block_store(j):
        span = pl.ds(j * query_rows, query_rows)
        return pltpu.make_async_copy(dkv_ref.at[span, :], dkv_hbm.at[0, span, :], block_sem.at[j])

    def heads_begin():
        for load in loads:
            load.wait()
        back.begin(r_ref[0].reshape(query_rows, model))

    def heads_block(j):
        @pl.when(j <= block_index)
        def _():
            back.block(j, True)

        @pl.when(j > block_index)
        def _():
            back.clear(j)

        block_store(j).start()

    def heads_end():
        dqgain_ref[...] = back.end()
        for store in stores:
            store.start()

    steps = []
    for k in range(pieces + 1):
        for i in range(count - 1):
            if i == 0 and k < pieces:
                steps.append((1.0, functools.partial(begin, k)))
            if k < pieces:
                steps.append((8.0, functools.partial(line.send_sums, k, count - 1 - i)))
            if i == 0 and k > 0:
                steps.append((1.0, functools.partial(own, k - 1)))
            elif k > 0:
                steps.append((1.0 if k < pieces else 6.0, functools.partial(line.hand_on, k - 1, i)))
        if k > 0:
            steps.append((1.0 if k < pieces else 6.0, functools.partial(line.hand_on, k - 1, count - 1)))
        if k == halves:
            ready = len(steps)
    heads = [(3.0, heads_begin)]
    heads += [(3.0, functools.partial(heads_block, j)) for j in range(seq_count)]
    heads += [(2.0, heads_end)]
    for _, call in steps[:ready]:
        call()
    interleaved(steps[ready:], heads)
    for j in range(seq_count):
        block_store(j).wait()
    for store in stores:
        store.wait()
    line.drain()


def residual_step(dn, middle, masked, gain, place, wo, cosine, sine, qgain, q, kv, att, gate, inv, qraw, group):
    count, pieces, rows, model = dn.shape
    batch, query_rows, width = q.shape
    halves = pieces // batch
    head_dim = qgain.shape[1]
    seq_count = lax.axis_size("seq")
    any_place = pl.BlockSpec(memory_space=pl.ANY)
    held = (q, kv, att, gate, inv, qraw)
    return pl.pallas_call(
        functools.partial(residual_kernel, pieces, count, halves, group, seq_count),
        in_specs=[SCALARS] + [WHOLE] * 8 + [any_place] * 6,
        out_specs=[WHOLE] * 3 + [any_place] * 3,
        out_shape=[
            jax.ShapeDtypeStruct((pieces, rows, model), F32),
            jax.ShapeDtypeStruct((batch, count, halves, rows, model), LOW),
            shape_of(1, head_dim, F32),
            jax.ShapeDtypeStruct(q.shape, LOW),
            jax.ShapeDtypeStruct(kv.shape, LOW),
            jax.ShapeDtypeStruct(q.shape, LOW),
        ],
        scratch_shapes=[pltpu.VMEM(x.shape[1:], x.dtype) for x in held]
        + [pltpu.VMEM(q.shape[1:], LOW), pltpu.VMEM(kv.shape[1:], LOW), pltpu.VMEM(q.shape[1:], LOW)]
        + heads_back_scratch(width // head_dim, query_rows, head_dim)
        + [
            pltpu.SemaphoreType.DMA((6,)),
            pltpu.SemaphoreType.DMA((2,)),
            pltpu.SemaphoreType.DMA((seq_count,)),
        ]
        + line_scratch(pieces, count, rows, model, LOW, True),
        compiler_params=params(60, collective_id=1, has_side_effects=True),
        cost_estimate=takes(10),
        name="residual",
    )(place, dn, middle, masked, gain, wo, cosine, sine, qgain, *held)


def scatter_kernel(
    pieces, count, seq_count, batch, head_dim,
    parts_ref, hidden_hbm, wd_hbm, middle_ref, valid_ref, kraw_ref, cos_ref, sin_ref, kgain_ref,
    dkv_ref, output_ref, dkgain_ref,
    wd_ref, hidden_ref, load_sem, hidden_sem, slots, send_sem, receive_sem,
    part_ref, own_ref, right_ref, left_ref, *sems,
):
    rows, model = own_ref.shape[1], own_ref.shape[2]
    tall = count * rows
    keys = kraw_ref.shape[2]
    line = Line(pieces, count, part_ref, own_ref, right_ref, left_ref, sems)
    load = pltpu.make_async_copy(wd_hbm, wd_ref, load_sem)

    def hidden_copy(p):
        return pltpu.make_async_copy(hidden_hbm.at[:, p], hidden_ref.at[p % 2], hidden_sem.at[p % 2])

    load.start()
    hidden_copy(0).start()
    dkgain_ref[...] = jnp.zeros_like(dkgain_ref)
    line.barrier(digit_orders(seq_count, 1)[0])

    def finish(b, total):
        for h in range(keys // head_dim):
            columns = slice(h * head_dim, (h + 1) * head_dim)
            grad, gain_grad = norm_turn_back(
                total[:, columns], kraw_ref[b, :, columns], kgain_ref[...], cos_ref[...], sin_ref[...]
            )
            dkv_ref[b, :, columns] = grad.astype(LOW)
            dkgain_ref[...] = dkgain_ref[...] + gain_grad
        dkv_ref[b, :, keys:] = total[:, keys:].astype(LOW)

    first, events, drain = block_sums(
        seq_count, batch, lambda b: parts_ref.at[b], finish, slots, send_sem, receive_sem, 4.0
    )

    def begin(p):
        if p == 0:
            load.wait()
        if p + 1 < pieces:
            hidden_copy(p + 1).start()
        hidden_copy(p).wait()
        hidden = hidden_ref[p % 2].reshape(tall, hidden_ref.shape[-1])
        part_ref[...] = mm(hidden, wd_ref[...]).reshape(count, rows, model)
        line.keep_own(p)

    def own(p):
        line.finish_own(p)
        output_ref[p] = (valid_ref[p] * (middle_ref[p] + own_ref[p])).astype(LOW)

    first()
    interleaved(line_steps(line, begin, own), events)
    drain()
    line.drain()


def line_steps(line, begin, own):
    steps = []
    for k in range(line.pieces + 1):
        for i in range(line.count - 1):
            if i == 0 and k < line.pieces:
                steps.append((1.0, functools.partial(begin, k)))
            if k < line.pieces:
                steps.append((8.0, functools.partial(line.send_sums, k, line.count - 1 - i)))
            if i == 0 and k > 0:
                steps.append((1.0, functools.partial(own, k - 1)))
    return steps


def scatter_blocks(parts, hidden, wd, middle, valid, kraw, cosine, sine, kgain):
    seq_count, batch = lax.axis_size("seq"), parts.shape[0]
    rows, columns = parts.shape[1] // seq_count, parts.shape[2]
    count, pieces, piece_rows, units = hidden.shape
    model, head_dim = wd.shape[1], kgain.shape[1]
    any_place = pl.BlockSpec(memory_space=pl.ANY)
    return pl.pallas_call(
        functools.partial(scatter_kernel, pieces, count, seq_count, batch, head_dim),
        in_specs=[WHOLE, any_place, any_place] + [WHOLE] * 6,
        out_specs=[WHOLE] * 3,
        out_shape=[
            jax.ShapeDtypeStruct((batch, rows, columns), LOW),
            jax.ShapeDtypeStruct((pieces, piece_rows, model), LOW),
            shape_of(1, head_dim, F32),
        ],
        scratch_shapes=[
            pltpu.VMEM(wd.shape, LOW),
            pltpu.VMEM((2, count, piece_rows, units), LOW),
            pltpu.SemaphoreType.DMA,
            pltpu.SemaphoreType.DMA((2,)),
            pltpu.VMEM((batch, seq_count - 1, rows, columns), LOW),
            pltpu.SemaphoreType.DMA((batch, seq_count - 1)),
            pltpu.SemaphoreType.DMA((batch, seq_count - 1)),
        ]
        + line_scratch(pieces, count, piece_rows, model, F32, False),
        compiler_params=params(46, collective_id=4, has_side_effects=True),
        cost_estimate=takes(10),
        name="scatter_blocks",
    )(
        parts.reshape(batch, seq_count, rows, columns), hidden, wd, middle, valid, kraw, cosine, sine, kgain
    )


def last_kernel(
    pieces, count, seq_count, streams, halves,
    dq_ref, dkv_ref, dgate_ref, wq_ref, wk_ref, wv_ref, wg_ref, tok_ref, residual_ref, gain_ref,
    dmid_ref, dqgain_ref, dkgain_ref, *refs,
):
    grads, refs = refs[:streams], refs[streams:]
    input_ref, total_ref, sums = refs[0], refs[1], refs[2 : 2 + streams]
    (
        slots, scatter_send, scatter_receive, gather_send, gather_receive, mine_ref, mine_sem,
        dgain_ref, turns_ref, round_ref, mixed_ref, round_send, round_receive, mixed_send, mixed_receive,
        part_ref, own_ref, right_ref, left_ref, *sems,
    ) = refs[2 + streams :]
    rows, model = own_ref.shape[1], own_ref.shape[2]
    tall = count * rows
    place_seq = lax.axis_index("seq")
    digits = digit_orders(seq_count, 1)[0]
    line = Line(pieces, count, part_ref, own_ref, right_ref, left_ref, sems)
    line.barrier_all(digits)
    dgain_ref[...] = jnp.zeros_like(dgain_ref)

    begins, arrivals, gather_drain = block_gathers(
        seq_count, streams, lambda b: sums[b], lambda b: mine_ref.at[b], gather_send, gather_receive
    )

    def keep(b):
        return pltpu.make_async_copy(mine_ref.at[b], sums[b].at[place_seq], mine_sem.at[b])

    def finish(b, total):
        mine_ref[b] = total.astype(LOW)
        begins[b]()
        keep(b).start()

    first, events, scatter_drain = block_sums(
        seq_count, streams, lambda b: grads[b], finish, slots, scatter_send, scatter_receive, 1.0
    )

    def begin(p):
        b, half = p // halves, p % halves
        dq = dq_ref[b, :, half].reshape(tall, dq_ref.shape[-1])
        dkv = dkv_ref[b, :, half].reshape(tall, dkv_ref.shape[-1])
        dgate = dgate_ref[b, :, half].reshape(tall, dgate_ref.shape[-1])
        nk = dkv.shape[1] // 2
        total = mm_t(dq, wq_ref[...]) + mm_t(dgate, wg_ref[...])
        total = total + mm_t(dkv[:, :nk], wk_ref[...]) + mm_t(dkv[:, nk:], wv_ref[...])
        part_ref[...] = total.reshape(count, rows, model)
        line.keep_own(p)

    def own(p):
        line.finish_own(p)
        x = tok_ref[p].astype(F32)
        grad = own_ref[p]
        inverse = inverse_rms(x)
        dgain_ref[...] = dgain_ref[...] + jnp.sum(grad * x * inverse, axis=0, keepdims=True)
        input_ref[p] = residual_ref[p] + norm_back(grad, x, gain_ref[...])

    width = model // count
    lines = width // 128
    rounds = [
        pltpu.make_async_remote_copy(
            src_ref=turns_ref.at[i],
            dst_ref=round_ref.at[i],
            send_sem=round_send.at[i],
            recv_sem=round_receive.at[i],
            device_id={"seq": flipped(place_seq, digit)},
            device_id_type=MESH,
        )
        for i, digit in enumerate(digits)
    ]
    done = len(digits)
    shares = []
    for distance in range(1, count):
        other = lax.rem(line.place + distance, count)
        shares.append(
            pltpu.make_async_remote_copy(
                src_ref=turns_ref.at[done, other],
                dst_ref=mixed_ref.at[distance - 1],
                send_sem=mixed_send.at[distance - 1],
                recv_sem=mixed_receive.at[distance - 1],
                device_id={"head": other},
                device_id_type=MESH,
            )
        )

    def pack():
        turns_ref[0] = jnp.zeros(turns_ref.shape[1:], F32)
        for t in range(count):
            for i in range(lines):
                span = slice(t * width + i * 128, t * width + (i + 1) * 128)
                turns_ref[0, t, i : i + 1, :] = dgain_ref[:, span]
                turns_ref[0, t, lines + i : lines + i + 1, :] = dmid_ref[:, span]
            turns_ref[0, t, 2 * lines : 2 * lines + 1, :] = dqgain_ref[...]
            turns_ref[0, t, 2 * lines + 1 : 2 * lines + 2, :] = dkgain_ref[...]
        rounds[0].start()

    def one_round(i):
        rounds[i].wait_recv()
        turns_ref[i + 1] = turns_ref[i] + round_ref[i]
        for copy in rounds[i + 1 : i + 2] if i + 1 < done else shares:
            copy.start()

    def total():
        found = turns_ref[done, line.place]
        for i, copy in enumerate(shares):
            copy.wait_recv()
            found = found + mixed_ref[i]
        total_ref[...] = found

    steps = line_steps(line, begin, own) + [(1.0, pack)]
    steps += [(4.0, functools.partial(one_round, i)) for i in range(done)] + [(4.0, total)]
    first()
    interleaved(steps, events + arrivals)
    for copy in rounds + shares:
        copy.wait_send()
    for b in range(streams):
        keep(b).wait()
    scatter_drain()
    gather_drain()
    line.drain()


def last_step(dq, dkv, dgate, wq, wk, wv, wg, tok, residual, gain, dmid, dqgain, dkgain, grads):
    batch, count, halves, rows, nq = dq.shape
    pieces, model = batch * halves, wq.shape[0]
    seq_count, streams = lax.axis_size("seq"), len(grads)
    tall, columns = grads[0].shape
    block = tall // seq_count
    steps = seq_count.bit_length() - 1
    lines = 8 * ((2 * (model // count // 128) + 2 + 7) // 8)
    return pl.pallas_call(
        functools.partial(last_kernel, pieces, count, seq_count, streams, halves),
        in_specs=[WHOLE] * (13 + streams),
        out_specs=[WHOLE] * 2 + [pl.BlockSpec(memory_space=pl.ANY)] * streams,
        out_shape=[jax.ShapeDtypeStruct((pieces, rows, model), F32), shape_of(lines, 128, F32)]
        + [jax.ShapeDtypeStruct((seq_count, block, columns), LOW)] * streams,
        scratch_shapes=[
            pltpu.VMEM((streams, seq_count - 1, block, columns), LOW),
            pltpu.SemaphoreType.DMA((streams, seq_count - 1)),
            pltpu.SemaphoreType.DMA((streams, seq_count - 1)),
            pltpu.SemaphoreType.DMA((streams, steps, seq_count)),
            pltpu.SemaphoreType.DMA((streams, seq_count)),
            pltpu.VMEM((streams, block, columns), LOW),
            pltpu.SemaphoreType.DMA((streams,)),
            pltpu.VMEM((1, model), F32),
            pltpu.VMEM((steps + 1, count, lines, 128), F32),
            pltpu.VMEM((steps, count, lines, 128), F32),
            pltpu.VMEM((count - 1, lines, 128), F32),
            pltpu.SemaphoreType.DMA((steps,)),
            pltpu.SemaphoreType.DMA((steps,)),
            pltpu.SemaphoreType.DMA((count - 1,)),
            pltpu.SemaphoreType.DMA((count - 1,)),
        ]
        + line_scratch(pieces, count, rows, model, F32, False),
        compiler_params=params(60, collective_id=5, has_side_effects=True),
        cost_estimate=takes(5),
        name="last",
    )(
        dq, dkv, dgate, wq, wk, wv, wg, tok, residual, gain, dmid, dqgain, dkgain,
        *[grad.reshape(seq_count, block, columns) for grad in grads],
    )


def widen_kernel(input_ref, output_ref, dq_ref, dkv_ref, dgate_ref, out_ref, *refs):
    ff_refs, refs = refs[:3], refs[3:]
    input_out, output_out, dq_out, dk_out, dv_out, dgate_out, out_out, *ff_outs = refs
    keys = dk_out.shape[1]
    input_out[...] = jnp.stack([input_ref[b] for b in range(input_ref.shape[0])], axis=1)
    output_out[...] = jnp.stack([output_ref[b].astype(F32) for b in range(input_ref.shape[0])], axis=1).astype(LOW)
    dq_out[...] = dq_ref[...].astype(F32)
    dk_out[...] = dkv_ref[:, :keys].astype(F32)
    dv_out[...] = dkv_ref[:, keys:].astype(F32)
    dgate_out[...] = dgate_ref[...].astype(F32)
    out_out[...] = out_ref[...].astype(F32).T
    for ref, out in zip(ff_refs, ff_outs):
        out[...] = ref[...].astype(F32)


def widen(input_grad, output, dq, dkv, dgate, out, ff, steps=8):
    batch, rows, model = input_grad.shape
    columns, keys = dq.shape[1], dkv.shape[1] // 2

    def tall(array):
        return pl.BlockSpec((array.shape[0] // steps, array.shape[1]), lambda i: (i, 0))

    def wide(array):
        return jax.ShapeDtypeStruct(array.shape, F32)

    outs = [
        jax.ShapeDtypeStruct((rows, batch, model), F32), jax.ShapeDtypeStruct((rows, batch, model), LOW),
        wide(dq), shape_of(model, keys, F32), shape_of(model, keys, F32), wide(dgate), shape_of(columns, model, F32),
    ] + [wide(x) for x in ff]
    specs = [pl.BlockSpec((rows // steps, batch, model), lambda i: (i, 0, 0))] * 2
    specs += [tall(x) for x in outs[2:6]]
    specs += [pl.BlockSpec((columns, model // steps), lambda i: (0, i))]
    specs += [tall(x) for x in ff]
    return pl.pallas_call(
        widen_kernel,
        grid=(steps,),
        in_specs=[pl.BlockSpec((batch, rows // steps, model), lambda i: (0, i, 0))] * 2
        + [tall(x) for x in (dq, dkv, dgate, out, *ff)],
        out_specs=specs,
        out_shape=outs,
        compiler_params=params(58),
        cost_estimate=takes(25),
        name="widen",
    )(input_grad, output, dq, dkv, dgate, out, *ff)


def turn_tables(positions, head_dim):
    half_dim = head_dim // 2
    inverse = THETA ** (-(jnp.arange(half_dim, dtype=F32) * 2.0) / head_dim)
    angles = positions.astype(F32)[:, None] * inverse[None, :]
    cosine, sine = jnp.cos(angles), jnp.sin(angles)
    return jnp.concatenate([cosine, cosine], axis=1), jnp.concatenate([-sine, sine], axis=1)


def norm_back(grad, values, gain):
    inverse = inverse_rms(values)
    grad = grad * gain
    mean = jnp.mean(grad * values, axis=-1, keepdims=True)
    return inverse * (grad - values * (inverse * inverse * mean))


def gather(value, axis):
    return lax.all_gather(value, axis, axis=0, tiled=True)


def on_device(
    tokens, cotangent, lengths,
    query_weight, key_weight, value_weight, gating_weight, output_weight,
    swiglu_gate, swiglu_lift, swiglu_down,
    input_gain, middle_gain, query_gain, key_gain,
):
    block_index = lax.axis_index("seq")
    part_index = lax.axis_index("head")
    parts = lax.axis_size("head")
    local_rows, batch, model = tokens.shape
    head_dim = query_gain.shape[0]
    block_rows = local_rows * parts
    flat_rows = block_rows * batch
    group = query_weight.shape[1] // key_weight.shape[1]
    nq, nk = query_weight.shape[1], key_weight.shape[1]
    halves = 2
    pieces, rows = batch * halves, local_rows // halves

    query_start = block_index * block_rows
    positions = query_start + jnp.arange(block_rows, dtype=jnp.int32)
    cosine, sine = turn_tables(positions, head_dim)
    gain_in, gain_mid = input_gain[None, :], middle_gain[None, :]
    gain_q, gain_k = query_gain[None, :], key_gain[None, :]
    local_pos = query_start + part_index * local_rows + jnp.arange(local_rows, dtype=jnp.int32)
    place = jnp.concatenate([query_start[None], lengths]).astype(jnp.int32)
    valid = (local_pos[None, :] < lengths[:, None]).astype(F32)[..., None]
    tok = jnp.transpose(tokens, (1, 0, 2)).reshape(pieces, rows, model)

    normed, qraw, q, kraw, kv_own, gate = [
        x.reshape(batch, block_rows, x.shape[-1])
        for x in front_step(
            tok, gain_in, cosine, sine, gain_q, gain_k,
            query_weight, key_weight, value_weight, gating_weight, parts,
        )
    ]
    kv_own, masked_own = lax.optimization_barrier(
        (kv_own, valid * jnp.transpose(cotangent, (1, 0, 2)).astype(F32))
    )
    kv = gather_blocks(kv_own)
    masked = gather(masked_own.astype(LOW).reshape(batch * local_rows, model), "head")
    att, acted, inv = attend(place, q, kv, gate, group, head_dim)
    middle, dgain_mid, normed_mid, hidden, dg, dl, dn_mid = middle_step(
        acted.reshape(batch, parts, halves, rows, nq), tok, gain_mid, output_weight,
        masked.reshape(parts, pieces, rows, model), swiglu_gate, swiglu_lift, swiglu_down, parts,
    )

    def flat(array):
        return array.reshape(flat_rows, array.shape[-1])

    normed_mid = flat(normed_mid)
    ff_grads = (
        t_mm(normed_mid, flat(dg)).astype(LOW),
        t_mm(normed_mid, flat(dl)).astype(LOW),
        t_mm(flat(hidden), masked).astype(LOW),
    )
    dn_mid, ff_grads = lax.optimization_barrier((dn_mid, ff_grads))
    ff_grads = lax.psum(ff_grads, "seq")
    residual, r, dgain_q, *firsts = residual_step(
        dn_mid, middle, masked_own.reshape(pieces, rows, model), gain_mid,
        place, output_weight, cosine, sine, gain_q, q, kv, att, gate, inv, qraw, group,
    )
    r = r.reshape(batch, block_rows, model)
    dq, dkv_all, dgate, dgain_q = attend_back(
        place, q, kv, r, output_weight, att, gate, inv, qraw, cosine, sine, gain_q, group, dgain_q, firsts
    )
    dkv, output, dgain_k = scatter_blocks(
        dkv_all, hidden, swiglu_down, middle, valid.reshape(pieces, rows, 1), kraw, cosine, sine, gain_k
    )
    grads = [
        t_mm(flat(normed), flat(dq)).astype(LOW),
        t_mm(flat(normed), flat(dkv)).astype(LOW),
        t_mm(flat(normed), flat(dgate)).astype(LOW),
        t_mm(flat(r), flat(acted)).astype(LOW),
    ]

    def pieced(array):
        return array.reshape(batch, parts, halves, rows, array.shape[-1])

    input_grad, gains, *grads = last_step(
        pieced(dq), pieced(dkv), pieced(dgate), query_weight, key_weight, value_weight, gating_weight,
        tok, residual, gain_in, dgain_mid, dgain_q, dgain_k, grads,
    )
    input_grad, output, dq_weight, dk_weight, dv_weight, dgate_weight, out_weight, *ff_sums = widen(
        input_grad.reshape(batch, local_rows, model),
        output.reshape(batch, local_rows, model),
        *[x.reshape(model, x.shape[-1]) for x in grads],
        ff_grads,
    )
    share = model // parts
    lines = share // 128
    head_share = head_dim // parts

    def head_gain(line):
        return lax.dynamic_slice(gains[line], (part_index * head_share,), (head_share,))

    return (
        output,
        input_grad,
        dq_weight,
        dk_weight,
        dv_weight,
        dgate_weight,
        out_weight,
        *ff_sums,
        gains[:lines].reshape(share),
        gains[lines : 2 * lines].reshape(share),
        head_gain(2 * lines),
        head_gain(2 * lines + 1),
    )


def solution(mesh):
    return jax.shard_map(
        on_device,
        mesh=mesh,
        in_specs=(
            P(("seq", "head"), None, None),
            P(("seq", "head"), None, None),
            P(),
            P(None, "head"),
            P(None, "head"),
            P(None, "head"),
            P(None, "head"),
            P("head", None),
            P(None, "head"),
            P(None, "head"),
            P("head", None),
            P(),
            P(),
            P(),
            P(),
        ),
        out_specs=(
            P(("seq", "head"), None, None),
            P(("seq", "head"), None, None),
            P(None, "head"),
            P(None, "head"),
            P(None, "head"),
            P(None, "head"),
            P("head", None),
            P(None, "head"),
            P(None, "head"),
            P("head", None),
            P("head"),
            P("head"),
            P("head"),
            P("head"),
        ),
        check_vma=False,
    )
```

```python
import functools

import jax
import jax.numpy as jnp
from jax import lax
from jax.experimental import pallas as pl
from jax.experimental.pallas import tpu as pltpu
from jax.sharding import PartitionSpec as P

EPS = 1e-06
THETA = 1000000.0
LOG2E = 1.4426950408889634
MIB = 1024 * 1024
LOW = jnp.bfloat16
F32 = jnp.float32
MESH = pl.DeviceIdType.MESH


def mm(left, right):
    return jnp.dot(left, right, preferred_element_type=F32)


def mm_t(left, right):
    return lax.dot_general(left, right, (((1,), (1,)), ((), ())), preferred_element_type=F32)


def t_mm(left, right):
    return lax.dot_general(left, right, (((0,), (0,)), ((), ())), preferred_element_type=F32)


def shape_of(rows, columns, kind):
    return jax.ShapeDtypeStruct((rows, columns), kind)


def params(mib, **extra):
    return pltpu.CompilerParams(vmem_limit_bytes=mib * MIB, **extra)


def takes(microseconds):
    return pl.CostEstimate(
        flops=int(microseconds * 1.15e9), bytes_accessed=int(microseconds * 3.69e6), transcendentals=0
    )


WHOLE = pl.BlockSpec(memory_space=pltpu.VMEM)
SCALARS = pl.BlockSpec(memory_space=pltpu.SMEM)


def full_block(array):
    return pl.BlockSpec(array.shape, lambda i: (0,) * len(array.shape))


def inverse_rms(values):
    return lax.rsqrt(jnp.mean(values * values, axis=-1, keepdims=True) + EPS)


def turn(values, cosine, sine):
    return values * cosine + pltpu.roll(values, values.shape[-1] // 2, 1) * sine


def turn_back(grads, cosine, sine):
    return grads * cosine + pltpu.roll(grads * sine, grads.shape[-1] // 2, 1)


def live_blocks(place_ref, rows, first=0):
    start, length = place_ref[0], place_ref[1 + first + pl.program_id(0)]
    whole = jnp.minimum(start // rows, length // rows)
    end = jnp.minimum(start // rows + 1, (length + rows - 1) // rows)
    end = jnp.where(start < length, end, 0)
    return jnp.minimum(whole, end), end, start, length


def attend_kernel(
    group, head_dim, place_ref, q_ref, kv_ref, gate_ref, att_ref, acted_ref, inv_ref, acc_ref, sum_ref
):
    rows = q_ref.shape[1]
    heads = q_ref.shape[2] // head_dim
    kv_heads = heads // group
    factor = head_dim ** (-0.5) * LOG2E
    acc_ref[...] = jnp.zeros_like(acc_ref)
    sum_ref[...] = jnp.zeros_like(sum_ref)
    whole, end, start, length = live_blocks(place_ref, rows)

    def one_block(j, masked, width=1):
        tall = width * rows
        span = pl.ds(pl.multiple_of(j * rows, rows), tall)
        if masked:
            key_pos = j * rows + lax.broadcasted_iota(jnp.int32, (rows, rows), 1)
            query_pos = start + lax.broadcasted_iota(jnp.int32, (rows, rows), 0)
            allowed = (key_pos <= query_pos) & (key_pos < length)
        for h in range(heads):
            c = h // group
            keys = kv_ref[0, span, c * head_dim : (c + 1) * head_dim]
            values = kv_ref[0, span, (kv_heads + c) * head_dim : (kv_heads + c + 1) * head_dim]
            weights = jnp.exp2(mm_t(q_ref[0, :, h * head_dim : (h + 1) * head_dim], keys) * factor)
            if masked:
                weights = jnp.where(allowed, weights, 0.0)
            total = weights[:, :128]
            for piece in range(1, tall // 128):
                total = total + weights[:, piece * 128 : (piece + 1) * 128]
            sum_ref[h] = sum_ref[h] + total
            acc_ref[h] = acc_ref[h] + mm(weights.astype(LOW), values)

    def plain(j, carry):
        one_block(j, False)
        return carry

    def pair(j, carry):
        one_block(2 * j, False, 2)
        return carry

    def edge(j, carry):
        one_block(j, True)
        return carry

    lax.fori_loop(0, whole // 2, pair, 0)
    lax.fori_loop(whole // 2 * 2, whole, plain, 0)
    lax.fori_loop(whole, end, edge, 0)
    lane = lax.broadcasted_iota(jnp.int32, inv_ref.shape[1:], 1)
    kept = jnp.zeros(inv_ref.shape[1:], F32)
    for h in range(heads):
        total = jnp.sum(sum_ref[h], axis=1, keepdims=True)
        inverse = 1.0 / jnp.where(total > 0.0, total, 1.0)
        attended = acc_ref[h] * inverse
        columns = slice(h * head_dim, (h + 1) * head_dim)
        att_ref[0, :, columns] = attended
        acted_ref[0, :, columns] = (attended * jax.nn.sigmoid(gate_ref[0, :, columns])).astype(LOW)
        kept = jnp.where(lane == h, inverse, kept)
    inv_ref[0] = kept


def by_sequence(array):
    return pl.BlockSpec((1,) + array.shape[1:], lambda b: (b,) + (0,) * (len(array.shape) - 1))


def attend(place, q, kv, gate, group, head_dim):
    batch, rows, width = q.shape
    heads = width // head_dim
    outs = [
        jax.ShapeDtypeStruct((batch, rows, width), F32),
        jax.ShapeDtypeStruct((batch, rows, width), LOW),
        jax.ShapeDtypeStruct((batch, rows, 128), F32),
    ]
    return pl.pallas_call(
        functools.partial(attend_kernel, group, head_dim),
        grid=(batch,),
        in_specs=[SCALARS, by_sequence(q), by_sequence(kv), by_sequence(gate)],
        out_specs=[by_sequence(x) for x in outs],
        out_shape=outs,
        scratch_shapes=[
            pltpu.VMEM((heads, rows, head_dim), F32),
            pltpu.VMEM((heads, rows, 128), F32),
        ],
        compiler_params=params(58),
        cost_estimate=takes(18),
        name="attend",
    )(place, q, kv, gate)


def norm_turn_back(grad, raw, head_gain, cosine, sine):
    grad = turn_back(grad, cosine, sine)
    inverse = inverse_rms(raw)
    gain_grad = jnp.sum(grad * raw * inverse, axis=0, keepdims=True)
    grad = grad * head_gain
    mean = jnp.mean(grad * raw, axis=-1, keepdims=True)
    return inverse * (grad - raw * (inverse * inverse * mean)), gain_grad


class HeadsBack:
    def __init__(
        self, group, start, length, q, kv, wo, att, gate, inv, qraw, cos, sin, qgain,
        dq, dkv, dgate, scaled, corr, acc,
    ):
        self.group, self.start, self.length = group, start, length
        self.q, self.kv, self.wo, self.att, self.gate, self.inv, self.qraw = q, kv, wo, att, gate, inv, qraw
        self.cos, self.sin, self.qgain = cos, sin, qgain
        self.dq, self.dkv, self.dgate, self.scaled, self.corr, self.acc = dq, dkv, dgate, scaled, corr, acc
        self.rows, self.head_dim = q.shape[0], cos.shape[1]
        self.heads = q.shape[1] // self.head_dim
        self.kv_heads = self.heads // group
        self.scale = self.head_dim ** (-0.5)

    def columns(self, h):
        return slice(h * self.head_dim, (h + 1) * self.head_dim)

    def begin(self, r):
        acted_grad = mm_t(r, self.wo[...])
        lane = lax.broadcasted_iota(jnp.int32, self.inv.shape, 1)
        kept = jnp.zeros(self.inv.shape, F32)
        for h in range(self.heads):
            columns = self.columns(h)
            sigmoid = jax.nn.sigmoid(self.gate[:, columns])
            attended = self.att[:, columns]
            grad = acted_grad[:, columns]
            self.dgate[:, columns] = (grad * attended * sigmoid * (1.0 - sigmoid)).astype(LOW)
            grad = grad * sigmoid
            inverse = self.inv[:, h : h + 1]
            self.scaled[:, columns] = (grad * inverse).astype(LOW)
            total = jnp.sum(grad * attended, axis=1, keepdims=True) * inverse
            kept = jnp.where(lane == h, total, kept)
        self.corr[...] = kept.T
        self.acc[...] = jnp.zeros_like(self.acc)

    def block(self, j, masked, width=1):
        rows, group = self.rows, self.group
        tall = width * rows
        span = pl.ds(pl.multiple_of(j * rows, rows), tall)
        if masked:
            key_pos = j * rows + lax.broadcasted_iota(jnp.int32, (tall, rows), 0)
            query_pos = self.start + lax.broadcasted_iota(jnp.int32, (tall, rows), 1)
            allowed = (key_pos <= query_pos) & (key_pos < self.length)
        for c in range(self.kv_heads):
            key_columns, value_columns = self.columns(c), self.columns(self.kv_heads + c)
            keys = self.kv[span, key_columns]
            values = self.kv[span, value_columns]
            dk = jnp.zeros((tall, self.head_dim), F32)
            dv = jnp.zeros((tall, self.head_dim), F32)
            for h in range(c * group, (c + 1) * group):
                queries = self.q[:, self.columns(h)]
                scaled = self.scaled[:, self.columns(h)]
                weights = jnp.exp2(mm_t(keys, queries) * (self.scale * LOG2E))
                if masked:
                    weights = jnp.where(allowed, weights, 0.0)
                dv = dv + mm(weights.astype(LOW), scaled)
                score = (weights * (mm_t(values, scaled) - self.corr[h : h + 1, :])).astype(LOW)
                dk = dk + mm(score, queries)
                self.acc[h] = self.acc[h] + t_mm(keys, score)
            self.dkv[span, key_columns] = (dk * self.scale).astype(LOW)
            self.dkv[span, value_columns] = dv.astype(LOW)

    def clear(self, j):
        span = pl.ds(pl.multiple_of(j * self.rows, self.rows), self.rows)
        self.dkv[span, :] = jnp.zeros((self.rows, self.dkv.shape[1]), LOW)

    def end(self):
        gain_total = jnp.zeros((1, self.head_dim), F32)
        for h in range(self.heads):
            columns = self.columns(h)
            grad, gain_grad = norm_turn_back(
                self.acc[h].T * self.scale, self.qraw[:, columns], self.qgain[...], self.cos[...], self.sin[...]
            )
            self.dq[:, columns] = grad.astype(LOW)
            gain_total = gain_total + gain_grad
        return gain_total


def heads_back_scratch(heads, rows, head_dim):
    return [
        pltpu.VMEM((rows, heads * head_dim), LOW),
        pltpu.VMEM((128, rows), F32),
        pltpu.VMEM((heads, head_dim, rows), F32),
    ]


def attend_back_kernel(
    group,
    place_ref, q_ref, kv_ref, r_ref, wo_ref, att_ref, gate_ref, inv_ref, qraw_ref, cos_ref, sin_ref, qgain_ref,
    first_gain_ref, first_dq, first_dkv, first_dgate,
    dq_ref, dkv_ref, dgate_ref, dqgain_ref,
    scaled_ref, corr_ref, acc_ref,
):
    del first_dq, first_dkv, first_dgate
    rows = q_ref.shape[1]
    whole, end, start, length = live_blocks(place_ref, rows, 1)
    back = HeadsBack(
        group, start, length, q_ref.at[0], kv_ref.at[0], wo_ref, att_ref.at[0], gate_ref.at[0], inv_ref.at[0],
        qraw_ref.at[0], cos_ref, sin_ref, qgain_ref, dq_ref.at[0], dkv_ref.at[0], dgate_ref.at[0],
        scaled_ref, corr_ref, acc_ref,
    )
    back.begin(r_ref[0])

    def plain(j, carry):
        back.block(j, False)
        return carry

    def pair(j, carry):
        back.block(2 * j, False, 2)
        return carry

    def edge(j, carry):
        back.block(j, True)
        return carry

    def empty(j, carry):
        back.clear(j)
        return carry

    lax.fori_loop(0, whole // 2, pair, 0)
    lax.fori_loop(whole // 2 * 2, whole, plain, 0)
    lax.fori_loop(whole, end, edge, 0)
    lax.fori_loop(end, dkv_ref.shape[1] // rows, empty, 0)
    gain_total = back.end()

    @pl.when(pl.program_id(0) == 0)
    def _():
        dqgain_ref[...] = first_gain_ref[...] + gain_total

    @pl.when(pl.program_id(0) > 0)
    def _():
        dqgain_ref[...] = dqgain_ref[...] + gain_total


def attend_back(place, q, kv, r, wo, att, gate, inv, qraw, cosine, sine, qgain, group, first_gain, firsts):
    batch, rows, width = q.shape
    head_dim = qgain.shape[1]
    any_place = pl.BlockSpec(memory_space=pl.ANY)

    def later(array):
        return pl.BlockSpec((1,) + array.shape[1:], lambda b: (b + 1,) + (0,) * (len(array.shape) - 1))

    line = pl.BlockSpec((1, head_dim), lambda b: (0, 0))
    return pl.pallas_call(
        functools.partial(attend_back_kernel, group),
        grid=(batch - 1,),
        in_specs=[SCALARS, later(q), later(kv), later(r), full_block(wo)]
        + [later(x) for x in (att, gate, inv, qraw)]
        + [full_block(x) for x in (cosine, sine, qgain, first_gain)]
        + [any_place] * 3,
        out_specs=[later(x) for x in firsts] + [line],
        out_shape=[jax.ShapeDtypeStruct(x.shape, x.dtype) for x in firsts] + [shape_of(1, head_dim, F32)],
        scratch_shapes=heads_back_scratch(width // head_dim, rows, head_dim),
        input_output_aliases={13: 0, 14: 1, 15: 2},
        compiler_params=params(58),
        cost_estimate=takes(3),
        name="attend_back",
    )(place, q, kv, r, wo, att, gate, inv, qraw, cosine, sine, qgain, first_gain, *firsts)


class Line:
    def __init__(self, pieces, count, part_ref, own_ref, right_ref, left_ref, sems, spread=None):
        self.sums = part_ref is not None
        self.pieces, self.count = pieces, count
        self.place = lax.axis_index("head")
        self.part_ref, self.own_ref = part_ref, own_ref
        self.right_ref, self.left_ref = right_ref, left_ref
        self.sems = sems
        self.spread = spread

    def barrier(self, digits=()):
        sem = pltpu.get_barrier_semaphore()
        place, count = self.place, self.count
        for digit in digits:
            partner = flipped(lax.axis_index("seq"), digit)
            pl.semaphore_signal(sem, inc=1, device_id={"seq": partner}, device_id_type=MESH)

        @pl.when(place > 0)
        def _():
            pl.semaphore_signal(sem, inc=1, device_id={"head": place - 1}, device_id_type=MESH)

        @pl.when(place < count - 1)
        def _():
            pl.semaphore_signal(sem, inc=1, device_id={"head": place + 1}, device_id_type=MESH)

        inside = (place > 0) & (place < count - 1)

        @pl.when(inside)
        def _():
            pl.semaphore_wait(sem, 2 + len(digits))

        @pl.when(jnp.logical_not(inside))
        def _():
            pl.semaphore_wait(sem, 1 + len(digits))

    def barrier_all(self, digits):
        sem = pltpu.get_barrier_semaphore()
        for digit in digits:
            partner = flipped(lax.axis_index("seq"), digit)
            pl.semaphore_signal(sem, inc=1, device_id={"seq": partner}, device_id_type=MESH)
        for distance in range(1, self.count):
            other = lax.rem(self.place + distance, self.count)
            pl.semaphore_signal(sem, inc=1, device_id={"head": other}, device_id_type=MESH)
        pl.semaphore_wait(sem, self.count - 1 + len(digits))

    def copy(self, ref, send, receive, p, t, step):
        return pltpu.make_async_remote_copy(
            src_ref=ref,
            dst_ref=ref,
            send_sem=self.sems[send].at[p, t],
            recv_sem=self.sems[receive].at[p, t],
            device_id={"head": jnp.clip(self.place + step, 0, self.count - 1)},
            device_id_type=MESH,
        )

    def sum_copy(self, p, t, step):
        ref = self.right_ref if step > 0 else self.left_ref
        base = 0 if step > 0 else 2
        return self.copy(ref.at[p, t], base, base + 1, p, t, step)

    def spread_copy(self, p, t, step):
        first = 4 if self.sums else 0
        return self.copy(self.spread(p, t), first if step > 0 else first + 1, first + 2, p, t, step)

    def send_sums(self, p, distance):
        place, count = self.place, self.count
        for step, ref in ((1, self.right_ref), (-1, self.left_ref)):
            t = place + step * distance
            first = place == (0 if step > 0 else count - 1)

            @pl.when((t >= 0) & (t < count))
            def _(t=t, step=step, ref=ref, first=first):
                @pl.when(first)
                def _():
                    ref[p, t] = self.part_ref[t].astype(LOW)

                @pl.when(jnp.logical_not(first))
                def _():
                    self.sum_copy(p, t, step).wait_recv()
                    ref[p, t] = (ref[p, t].astype(F32) + self.part_ref[t].astype(F32)).astype(LOW)

                self.sum_copy(p, t, step).start()

    def keep_own(self, p):
        self.own_ref[p] = self.part_ref[self.place].astype(F32)

    def finish_own(self, p):
        place, count = self.place, self.count
        for step, ref, inner in ((1, self.right_ref, place > 0), (-1, self.left_ref, place < count - 1)):

            @pl.when(inner)
            def _(step=step, ref=ref):
                self.sum_copy(p, place, step).wait_recv()
                self.own_ref[p] = self.own_ref[p] + ref[p, place].astype(F32)

    def hand_out(self, p):
        place, count = self.place, self.count

        @pl.when(place < count - 1)
        def _():
            self.spread_copy(p, place, 1).start()

        @pl.when(place > 0)
        def _():
            self.spread_copy(p, place, -1).start()

    def hand_on(self, p, distance):
        place, count = self.place, self.count
        for step, more in ((1, place < count - 1), (-1, place > 0)):
            t = place - step * distance

            @pl.when((t >= 0) & (t < count))
            def _(t=t, step=step, more=more):
                self.spread_copy(p, t, step).wait_recv()

                @pl.when(more)
                def _():
                    self.spread_copy(p, t, step).start()

    def drain(self):
        place, count = self.place, self.count

        def one(p, carry):
            for t in range(count):
                if self.sums:

                    @pl.when(t > place)
                    def _(t=t):
                        self.sum_copy(p, t, 1).wait_send()

                    @pl.when(t < place)
                    def _(t=t):
                        self.sum_copy(p, t, -1).wait_send()

                if self.spread is not None:

                    @pl.when((t <= place) & (place < count - 1))
                    def _(t=t):
                        self.spread_copy(p, t, 1).wait_send()

                    @pl.when((t >= place) & (place > 0))
                    def _(t=t):
                        self.spread_copy(p, t, -1).wait_send()

            return carry

        lax.fori_loop(0, self.pieces, one, 0)


def line_scratch(pieces, count, rows, model, part_kind, spread):
    slots = (pieces, count)
    scratch = [
        pltpu.VMEM((pieces, rows, model), F32),
        pltpu.VMEM((pieces, count, rows, model), LOW),
        pltpu.VMEM((pieces, count, rows, model), LOW),
    ] + [pltpu.SemaphoreType.DMA(slots)] * (7 if spread else 4)
    if part_kind is not None:
        scratch = [pltpu.VMEM((count, rows, model), part_kind)] + scratch
    return scratch


def both_ways(index, limit, body):
    @pl.when((index >= 0) & (index < limit))
    def _():
        body(index)


def front_kernel(
    pieces, count, head_dim,
    tok_ref, gain_ref, cos_ref, sin_ref, qgain_ref, kgain_ref, wq_hbm, wk_hbm, wv_hbm, wg_hbm,
    normed_hbm, qraw_hbm, q_hbm, kraw_hbm, kv_hbm, gate_hbm,
    all_ref, normed_ref, qraw_ref, q_ref, kraw_ref, kv_ref, gate_ref, store_sem,
    wq_ref, wk_ref, wv_ref, wg_ref, load_sem, *sems,
):
    rows, model = tok_ref.shape[1], tok_ref.shape[2]
    tall = count * rows
    line = Line(pieces, count, None, None, None, None, sems, spread=lambda p, t: all_ref.at[p, t])
    weights = ((wq_hbm, wq_ref), (wk_hbm, wk_ref), (wv_hbm, wv_ref), (wg_hbm, wg_ref))
    loads = [pltpu.make_async_copy(*pair, load_sem.at[i]) for i, pair in enumerate(weights)]
    for load in loads:
        load.start()
    line.barrier()
    for p in range(pieces):
        all_ref[p, line.place] = tok_ref[p]

    def stores(p):
        pairs = (
            (normed_ref, normed_hbm), (qraw_ref, qraw_hbm), (q_ref, q_hbm), (kraw_ref, kraw_hbm), (kv_ref, kv_hbm),
            (gate_ref, gate_hbm),
        )
        return [
            pltpu.make_async_copy(source, target.at[p // 2, :, p % 2], store_sem.at[i])
            for i, (source, target) in enumerate(pairs)
        ]

    def project(p):
        half = p % 2

        @pl.when(p == 0)
        def _():
            for load in loads:
                load.wait()

        @pl.when(p > 0)
        def _():
            for store in stores(p - 1):
                store.wait()

        def keep(ref, value):
            ref[...] = value.astype(ref.dtype).reshape(count, rows, value.shape[-1])

        x = all_ref[p].reshape(tall, model).astype(F32)
        normed = (x * inverse_rms(x) * gain_ref[...]).astype(LOW)
        keep(normed_ref, normed)
        cosine = cos_ref[:, half].reshape(tall, head_dim)
        sine = sin_ref[:, half].reshape(tall, head_dim)

        def turned(raw, head_gain):
            parts = []
            for h in range(raw.shape[1] // head_dim):
                part = raw[:, h * head_dim : (h + 1) * head_dim]
                parts.append(turn(part * inverse_rms(part) * head_gain, cosine, sine).astype(LOW))
            return parts

        raw = mm(normed, wk_ref[...])
        keep(kraw_ref, raw)
        values = mm(normed, wv_ref[...]).astype(LOW)
        keep(kv_ref, jnp.concatenate(turned(raw, kgain_ref[...]) + [values], axis=1))
        raw = mm(normed, wq_ref[...])
        keep(qraw_ref, raw)
        keep(q_ref, jnp.concatenate(turned(raw, qgain_ref[...]), axis=1))
        keep(gate_ref, mm(normed, wg_ref[...]))
        for store in stores(p):
            store.start()

    def turn_once(k, carry):
        both_ways(k, pieces, line.hand_out)
        for distance in range(1, count):
            both_ways(k - 1, pieces, lambda p, d=distance: line.hand_on(p, d))
        both_ways(k - 1, pieces, project)
        return carry

    lax.fori_loop(0, pieces + 1, turn_once, 0)
    for store in stores(pieces - 1):
        store.wait()
    line.drain()


def front_step(tok, gain, cosine, sine, qgain, kgain, wq, wk, wv, wg, count):
    pieces, rows, model = tok.shape
    batch = pieces // 2
    head_dim = qgain.shape[1]
    nq, nk = wq.shape[1], wk.shape[1]

    def wide(columns, kind):
        return jax.ShapeDtypeStruct((batch, count, 2, rows, columns), kind)

    slots = (pieces, count)
    kinds = [(model, LOW), (nq, F32), (nq, LOW), (nk, F32), (2 * nk, LOW), (nq, F32)]
    return pl.pallas_call(
        functools.partial(front_kernel, pieces, count, head_dim),
        in_specs=[WHOLE] * 6 + [pl.BlockSpec(memory_space=pl.ANY)] * 4,
        out_specs=[pl.BlockSpec(memory_space=pl.ANY)] * 6,
        out_shape=[wide(*kind) for kind in kinds],
        scratch_shapes=[pltpu.VMEM((pieces, count, rows, model), LOW)]
        + [pltpu.VMEM((count, rows, columns), kind) for columns, kind in kinds]
        + [pltpu.SemaphoreType.DMA((6,))]
        + [pltpu.VMEM(x.shape, LOW) for x in (wq, wk, wv, wg)]
        + [pltpu.SemaphoreType.DMA((4,))]
        + [pltpu.SemaphoreType.DMA(slots)] * 3,
        compiler_params=params(58, collective_id=2, has_side_effects=True),
        cost_estimate=takes(95),
        name="front",
    )(
        tok, gain, cosine.reshape(count, 2, rows, head_dim), sine.reshape(count, 2, rows, head_dim),
        qgain, kgain, wq, wk, wv, wg,
    )


def middle_kernel(
    pieces, count,
    acted_ref, tok_ref, gain_ref, wo_ref, masked_hbm, wg_hbm, wl_hbm, wd_hbm,
    middle_ref, dgain_ref, normed_hbm, hidden_hbm, dg_hbm, dl_hbm, dn_hbm,
    mid_ref, wg_ref, wl_ref, wd_ref, masked_ref, normed_ref, hidden_ref, dg_ref, dl_ref, dn_ref, acc_ref,
    load_sem, masked_sem, store_sem,
    part_ref, own_ref, right_ref, left_ref, *sems,
):
    rows, model = own_ref.shape[1], own_ref.shape[2]
    tall = count * rows
    hidden = wg_ref.shape[1]
    line = Line(
        pieces, count, part_ref, own_ref, right_ref, left_ref, sems, spread=lambda p, t: mid_ref.at[p, t]
    )
    place = line.place
    loads = [
        pltpu.make_async_copy(source, target, load_sem.at[i])
        for i, (source, target) in enumerate(((wg_hbm, wg_ref), (wl_hbm, wl_ref), (wd_hbm, wd_ref)))
    ]
    line.barrier()
    for load in loads:
        load.start()
    dgain_ref[...] = jnp.zeros_like(dgain_ref)
    tiles = 3
    tile = hidden // tiles

    def masked_copy(p):
        return pltpu.make_async_copy(masked_hbm.at[:, p], masked_ref, masked_sem)

    def stores(p):
        pairs = (
            (normed_ref, normed_hbm), (hidden_ref, hidden_hbm), (dg_ref, dg_hbm), (dl_ref, dl_hbm),
            (dn_ref, dn_hbm),
        )
        return [
            pltpu.make_async_copy(source, target.at[:, p], store_sem.at[i])
            for i, (source, target) in enumerate(pairs)
        ]

    def begin(p):
        acted = acted_ref[p // 2, :, p % 2].reshape(tall, acted_ref.shape[-1])
        part_ref[...] = mm(acted, wo_ref[...]).reshape(count, rows, model)
        line.keep_own(p)

    def own(p):
        line.finish_own(p)
        middle = own_ref[p] + tok_ref[p].astype(F32)
        middle_ref[p] = middle
        mid_ref[p, place] = middle.astype(LOW)
        line.hand_out(p)

    def units_begin(p):
        line.hand_on(p, count - 1)

        @pl.when(p > 0)
        def _():
            for store in stores(p - 1):
                store.wait()

        x = mid_ref[p].reshape(tall, model).astype(F32)
        normed = (x * inverse_rms(x) * gain_ref[...]).astype(LOW)
        normed_ref[...] = normed.reshape(count, rows, model)
        masked_copy(p).wait()

        @pl.when(p == 0)
        def _():
            for load in loads:
                load.wait()

    def units_tile(i):
        span = slice(i * tile, (i + 1) * tile)
        normed = normed_ref[...].reshape(tall, model)
        gate = mm(normed, wg_ref[:, span])
        lift = mm(normed, wl_ref[:, span])
        grad = mm_t(masked_ref[...].reshape(tall, model), wd_ref[span, :])
        sigmoid = jax.nn.sigmoid(gate)
        silu = gate * sigmoid
        lift_grad = (grad * silu).astype(LOW)
        gate_grad = (grad * lift * (sigmoid + silu * (1.0 - sigmoid))).astype(LOW)
        hidden_ref[:, :, span] = (silu * lift).astype(LOW).reshape(count, rows, tile)
        dg_ref[:, :, span] = gate_grad.reshape(count, rows, tile)
        dl_ref[:, :, span] = lift_grad.reshape(count, rows, tile)
        part = mm_t(gate_grad, wg_ref[:, span]) + mm_t(lift_grad, wl_ref[:, span])
        if i == 0:
            acc_ref[...] = part
        else:
            acc_ref[...] = acc_ref[...] + part

    def units_end(p):
        total = acc_ref[...]
        dn_ref[...] = total.astype(LOW).reshape(count, rows, model)
        x = mid_ref[p].reshape(tall, model).astype(F32)
        dgain_ref[...] = dgain_ref[...] + jnp.sum(total * x * inverse_rms(x), axis=0, keepdims=True)
        for store in stores(p):
            store.start()

        @pl.when(p < pieces - 1)
        def _():
            masked_copy(p + 1).start()

    masked_copy(0).start()

    def turn_once(k, carry):
        both_ways(k, pieces, begin)
        for i in range(max(tiles, count - 1)):
            if i < count - 1:
                both_ways(k, pieces, lambda p, i=i: line.send_sums(p, count - 1 - i))
            if i == 0:
                both_ways(k - 1, pieces, own)
                both_ways(k - 2, pieces, units_begin)
            elif i < count - 1:
                both_ways(k - 1, pieces, lambda p, i=i: line.hand_on(p, i))
            if i < tiles:
                both_ways(k - 2, pieces, lambda p, i=i: units_tile(i))
        both_ways(k - 2, pieces, units_end)
        return carry

    lax.fori_loop(0, pieces + 2, turn_once, 0)
    for store in stores(pieces - 1):
        store.wait()
    line.drain()


def middle_step(acted, tok, gain, wo, masked, wg, wl, wd, count):
    pieces, rows, model = tok.shape
    hidden = wg.shape[1]
    any_place = pl.BlockSpec(memory_space=pl.ANY)

    def wide(columns, kind=LOW):
        return jax.ShapeDtypeStruct((count, pieces, rows, columns), kind)

    def room(columns, kind=LOW):
        return pltpu.VMEM((count, rows, columns), kind)

    return pl.pallas_call(
        functools.partial(middle_kernel, pieces, count),
        in_specs=[WHOLE] * 4 + [any_place] * 4,
        out_specs=[WHOLE] * 2 + [any_place] * 5,
        out_shape=[
            jax.ShapeDtypeStruct((pieces, rows, model), F32), shape_of(1, model, F32),
            wide(model), wide(hidden), wide(hidden), wide(hidden), wide(model),
        ],
        scratch_shapes=[
            pltpu.VMEM((pieces, count, rows, model), LOW),
            pltpu.VMEM(wg.shape, LOW), pltpu.VMEM(wl.shape, LOW), pltpu.VMEM(wd.shape, LOW),
            room(model), room(model), room(hidden), room(hidden), room(hidden), room(model),
            pltpu.VMEM((count * rows, model), F32),
            pltpu.SemaphoreType.DMA((3,)), pltpu.SemaphoreType.DMA, pltpu.SemaphoreType.DMA((5,)),
        ]
        + line_scratch(pieces, count, rows, model, F32, True),
        compiler_params=params(58, collective_id=0, has_side_effects=True),
        cost_estimate=takes(128),
        name="middle",
    )(acted, tok, gain, wo, masked, wg, wl, wd)


def flipped(place, mask):
    bit = 1
    while bit <= mask:
        if mask & bit:
            place = place + (1 - 2 * (place // bit % 2)) * bit
        bit *= 2
    return place


def digit_orders(count, batch):
    upper = [1 << i for i in range(1, count.bit_length() - 1)]
    return [(upper if b % 2 == 0 else upper[::-1]) + [1] for b in range(batch)]


def greet(place, digits):
    sem = pltpu.get_barrier_semaphore()
    for digit in digits:
        pl.semaphore_signal(sem, inc=1, device_id={"seq": flipped(place, digit)}, device_id_type=MESH)
    pl.semaphore_wait(sem, len(digits))


def block_gathers(count, batch, out, sources, send_sem, receive_sem):
    place = lax.axis_index("seq")
    orders = digit_orders(count, batch)
    steps = len(orders[0])
    started = []

    def copy(b, mask, step):
        digit = orders[b][step]
        block = out(b).at[flipped(place, mask)]
        return pltpu.make_async_remote_copy(
            src_ref=sources(b) if mask == 0 else block,
            dst_ref=block,
            send_sem=send_sem.at[b, step, mask],
            recv_sem=receive_sem.at[b, mask | digit],
            device_id={"seq": flipped(place, digit)},
            device_id_type=MESH,
        )

    def pass_on(b, mask, first):
        for step in range(first, steps):
            one = copy(b, mask, step)
            one.start()
            started.append(one)

    def arrive(b, mask, level):
        block = out(b).at[flipped(place, mask)]
        pltpu.make_async_remote_copy(
            src_ref=block,
            dst_ref=block,
            send_sem=send_sem.at[b, 0, mask],
            recv_sem=receive_sem.at[b, mask],
            device_id={"seq": flipped(place, orders[b][level])},
            device_id_type=MESH,
        ).wait_recv()
        pass_on(b, mask, level + 1)

    begins = [functools.partial(pass_on, b, 0, 0) for b in range(batch)]
    arrivals = []
    for level in range(steps):
        for turn in range(1 << level):
            for b in range(batch):
                mask = orders[b][level]
                for i in range(level):
                    if turn >> i & 1:
                        mask |= orders[b][i]
                arrivals.append((1.0 if level == steps - 1 else 4.0, functools.partial(arrive, b, mask, level)))

    def drain():
        for one in started:
            one.wait_send()

    return begins, arrivals, drain


def gather_kernel(count, batch, own_ref, out_ref, local_sem, send_sem, receive_sem):
    place = lax.axis_index("seq")
    greet(place, digit_orders(count, 1)[0])
    local = [
        pltpu.make_async_copy(own_ref.at[b], out_ref.at[b, place], local_sem.at[b]) for b in range(batch)
    ]
    for copy in local:
        copy.start()
    begins, arrivals, drain = block_gathers(
        count, batch, lambda b: out_ref.at[b], lambda b: own_ref.at[b], send_sem, receive_sem
    )
    for begin in begins:
        begin()
    for _, event in arrivals:
        event()
    drain()
    for copy in local:
        copy.wait()


def gather_blocks(own):
    batch, rows, columns = own.shape
    count = lax.axis_size("seq")
    steps = count.bit_length() - 1
    any_place = pl.BlockSpec(memory_space=pl.ANY)
    out = pl.pallas_call(
        functools.partial(gather_kernel, count, batch),
        in_specs=[any_place],
        out_specs=any_place,
        out_shape=jax.ShapeDtypeStruct((batch, count, rows, columns), LOW),
        scratch_shapes=[
            pltpu.SemaphoreType.DMA((batch,)),
            pltpu.SemaphoreType.DMA((batch, steps, count)),
            pltpu.SemaphoreType.DMA((batch, count)),
        ],
        compiler_params=params(58, collective_id=3, has_side_effects=True),
        cost_estimate=takes(41),
        name="gather_blocks",
    )(own)
    return out.reshape(batch, count * rows, columns)


def block_sums(count, batch, parts, finish, slots, send_sem, receive_sem, kept_ref, kept_sem, near):
    place = lax.axis_index("seq")
    orders = [order[::-1] for order in digit_orders(count, batch)]
    steps = len(orders[0])

    def masks_at(b, step):
        found = [0]
        for digit in orders[b][step + 1 :][::-1]:
            found = [mask | digit for mask in found] + found
        return found

    numbers = {}
    for b in range(batch):
        place_in = 0
        for step in range(steps):
            for mask in masks_at(b, step):
                numbers[b, step, mask] = place_in
                place_in += 1

    def slot(b, step, mask):
        return slots.at[b, numbers[b, step, mask]]

    def transfer(b, step, mask):
        digit = orders[b][step]
        number = numbers[b, step, mask]
        if step == 0:
            source = parts(b).at[flipped(place, mask | digit)]
        else:
            source = slot(b, step - 1, mask | digit)
        return pltpu.make_async_remote_copy(
            src_ref=source,
            dst_ref=slots.at[b, number],
            send_sem=send_sem.at[b, number],
            recv_sem=receive_sem.at[b, number],
            device_id={"seq": flipped(place, digit)},
            device_id_type=MESH,
        )

    started = []

    def kept(b, turn):
        mask = masks_at(b, 0)[turn]
        return pltpu.make_async_copy(
            parts(b).at[flipped(place, mask)], kept_ref.at[b, turn], kept_sem.at[b, turn]
        )

    def begin():
        for turn in range(count // 2):
            for b in range(batch):
                copy = transfer(b, 0, masks_at(b, 0)[turn])
                copy.start()
                started.append(copy)
        for turn in range(count // 2):
            for b in range(batch):
                kept(b, turn).start()

    def take(b, step, mask):
        transfer(b, step, mask).wait_recv()
        if step == 0:
            turn = masks_at(b, 0).index(mask)
            kept(b, turn).wait()
            held = kept_ref.at[b, turn]
        else:
            held = slot(b, step - 1, mask)
        total = held[...].astype(F32) + slot(b, step, mask)[...].astype(F32)
        if step == steps - 1:
            finish(b, total)
        else:
            slot(b, step, mask)[...] = total.astype(LOW)
            if mask & orders[b][step + 1]:
                copy = transfer(b, step + 1, mask & ~orders[b][step + 1])
                copy.start()
                started.append(copy)

    events = []
    for step in range(steps):
        for turn in range(len(masks_at(0, step))):
            for b in range(batch):
                events.append((near if step == 0 else 4.0, functools.partial(take, b, step, masks_at(b, step)[turn])))

    def drain():
        for copy in started:
            copy.wait_send()

    return begin, events, drain


def interleaved(*lists):
    spent = [0.0] * len(lists)
    whole = [sum(time for time, _ in calls) for calls in lists]
    taken = [0] * len(lists)
    while any(taken[i] < len(calls) for i, calls in enumerate(lists)):
        i = min((i for i, calls in enumerate(lists) if taken[i] < len(calls)), key=lambda i: spent[i])
        time, call = lists[i][taken[i]]
        call()
        spent[i] += time / whole[i]
        taken[i] += 1

def residual_kernel(
    pieces, count, halves, group, seq_count,
    place_ref, dn_ref, middle_ref, masked_ref, gain_ref, wo_ref, cos_ref, sin_ref, qgain_ref,
    q_hbm, kv_hbm, att_hbm, gate_hbm, inv_hbm, qraw_hbm,
    residual_ref, r_ref, dqgain_ref, dq_hbm, dkv_hbm, dgate_hbm,
    q_ref, kv_ref, att_ref, gate_ref, inv_ref, qraw_ref, dq_ref, dkv_ref, dgate_ref,
    scaled_ref, corr_ref, acc_ref, load_sem, store_sem, block_sem,
    part_ref, own_ref, right_ref, left_ref, *sems,
):
    rows, model = own_ref.shape[1], own_ref.shape[2]
    query_rows = q_ref.shape[0]
    line = Line(
        pieces, count, part_ref, own_ref, right_ref, left_ref, sems,
        spread=lambda p, t: r_ref.at[p // halves, t, p % halves],
    )
    pairs = (
        (q_hbm, q_ref), (kv_hbm, kv_ref), (att_hbm, att_ref), (gate_hbm, gate_ref), (inv_hbm, inv_ref),
        (qraw_hbm, qraw_ref),
    )
    loads = [
        pltpu.make_async_copy(source.at[0], target, load_sem.at[i]) for i, (source, target) in enumerate(pairs)
    ]
    stores = [
        pltpu.make_async_copy(dq_ref, dq_hbm.at[0], store_sem.at[0]),
        pltpu.make_async_copy(dgate_ref, dgate_hbm.at[0], store_sem.at[1]),
    ]
    line.barrier()
    for load in loads:
        load.start()
    block_index = lax.axis_index("seq")
    back = HeadsBack(
        group, block_index * query_rows, place_ref[1], q_ref, kv_ref, wo_ref, att_ref, gate_ref, inv_ref, qraw_ref,
        cos_ref, sin_ref, qgain_ref, dq_ref, dkv_ref, dgate_ref, scaled_ref, corr_ref, acc_ref,
    )

    def begin(p):
        part_ref[...] = dn_ref[:, p]
        line.keep_own(p)

    def own(p):
        line.finish_own(p)
        x = middle_ref[p].astype(LOW).astype(F32)
        residual = masked_ref[p].astype(F32) + norm_back(own_ref[p], x, gain_ref[...])
        residual_ref[p] = residual
        r_ref[p // halves, line.place, p % halves] = residual.astype(LOW)
        line.hand_out(p)

    def block_store(j):
        span = pl.ds(j * query_rows, query_rows)
        return pltpu.make_async_copy(dkv_ref.at[span, :], dkv_hbm.at[0, span, :], block_sem.at[j])

    def heads_begin():
        for load in loads:
            load.wait()
        back.begin(r_ref[0].reshape(query_rows, model))

    def heads_block(j):
        @pl.when(j <= block_index)
        def _():
            back.block(j, True)

        @pl.when(j > block_index)
        def _():
            back.clear(j)

        block_store(j).start()

    def heads_end():
        dqgain_ref[...] = back.end()
        for store in stores:
            store.start()

    steps = []
    for k in range(pieces + 1):
        for i in range(count - 1):
            if i == 0 and k < pieces:
                steps.append((1.0, functools.partial(begin, k)))
            if k < pieces:
                steps.append((8.0, functools.partial(line.send_sums, k, count - 1 - i)))
            if i == 0 and k > 0:
                steps.append((1.0, functools.partial(own, k - 1)))
            elif k > 0:
                steps.append((1.0 if k < pieces else 6.0, functools.partial(line.hand_on, k - 1, i)))
        if k > 0:
            steps.append((1.0 if k < pieces else 6.0, functools.partial(line.hand_on, k - 1, count - 1)))
        if k == halves:
            ready = len(steps)
    heads = [(3.0, heads_begin)]
    heads += [(3.0, functools.partial(heads_block, j)) for j in range(seq_count)]
    heads += [(2.0, heads_end)]
    for _, call in steps[:ready]:
        call()
    interleaved(steps[ready:], heads)
    for j in range(seq_count):
        block_store(j).wait()
    for store in stores:
        store.wait()
    line.drain()


def residual_step(dn, middle, masked, gain, place, wo, cosine, sine, qgain, q, kv, att, gate, inv, qraw, group):
    count, pieces, rows, model = dn.shape
    batch, query_rows, width = q.shape
    halves = pieces // batch
    head_dim = qgain.shape[1]
    seq_count = lax.axis_size("seq")
    any_place = pl.BlockSpec(memory_space=pl.ANY)
    held = (q, kv, att, gate, inv, qraw)
    return pl.pallas_call(
        functools.partial(residual_kernel, pieces, count, halves, group, seq_count),
        in_specs=[SCALARS] + [WHOLE] * 8 + [any_place] * 6,
        out_specs=[WHOLE] * 3 + [any_place] * 3,
        out_shape=[
            jax.ShapeDtypeStruct((pieces, rows, model), F32),
            jax.ShapeDtypeStruct((batch, count, halves, rows, model), LOW),
            shape_of(1, head_dim, F32),
            jax.ShapeDtypeStruct(q.shape, LOW),
            jax.ShapeDtypeStruct(kv.shape, LOW),
            jax.ShapeDtypeStruct(q.shape, LOW),
        ],
        scratch_shapes=[pltpu.VMEM(x.shape[1:], x.dtype) for x in held]
        + [pltpu.VMEM(q.shape[1:], LOW), pltpu.VMEM(kv.shape[1:], LOW), pltpu.VMEM(q.shape[1:], LOW)]
        + heads_back_scratch(width // head_dim, query_rows, head_dim)
        + [
            pltpu.SemaphoreType.DMA((6,)),
            pltpu.SemaphoreType.DMA((2,)),
            pltpu.SemaphoreType.DMA((seq_count,)),
        ]
        + line_scratch(pieces, count, rows, model, LOW, True),
        compiler_params=params(60, collective_id=1, has_side_effects=True),
        cost_estimate=takes(10),
        name="residual",
    )(place, dn, middle, masked, gain, wo, cosine, sine, qgain, *held)


def scatter_kernel(
    pieces, count, seq_count, batch, head_dim,
    parts_ref, hidden_hbm, wd_hbm, middle_ref, valid_ref, kraw_ref, cos_ref, sin_ref, kgain_ref,
    dkv_ref, output_ref, dkgain_ref,
    wd_ref, hidden_ref, load_sem, hidden_sem, kept_ref, kept_sem, slots, send_sem, receive_sem,
    part_ref, own_ref, right_ref, left_ref, *sems,
):
    rows, model = own_ref.shape[1], own_ref.shape[2]
    tall = count * rows
    keys = kraw_ref.shape[2]
    line = Line(pieces, count, part_ref, own_ref, right_ref, left_ref, sems)
    load = pltpu.make_async_copy(wd_hbm, wd_ref, load_sem)

    def hidden_copy(p):
        return pltpu.make_async_copy(hidden_hbm.at[:, p], hidden_ref.at[p % 2], hidden_sem.at[p % 2])

    load.start()
    hidden_copy(0).start()
    dkgain_ref[...] = jnp.zeros_like(dkgain_ref)
    line.barrier(digit_orders(seq_count, 1)[0])

    def finish(b, total):
        for h in range(keys // head_dim):
            columns = slice(h * head_dim, (h + 1) * head_dim)
            grad, gain_grad = norm_turn_back(
                total[:, columns], kraw_ref[b, :, columns], kgain_ref[...], cos_ref[...], sin_ref[...]
            )
            dkv_ref[b, :, columns] = grad.astype(LOW)
            dkgain_ref[...] = dkgain_ref[...] + gain_grad
        dkv_ref[b, :, keys:] = total[:, keys:].astype(LOW)

    first, events, drain = block_sums(
        seq_count, batch, lambda b: parts_ref.at[b], finish, slots, send_sem, receive_sem, kept_ref, kept_sem, 4.0
    )

    def begin(p):
        if p == 0:
            load.wait()
        if p + 1 < pieces:
            hidden_copy(p + 1).start()
        hidden_copy(p).wait()
        hidden = hidden_ref[p % 2].reshape(tall, hidden_ref.shape[-1])
        part_ref[...] = mm(hidden, wd_ref[...]).reshape(count, rows, model)
        line.keep_own(p)

    def own(p):
        line.finish_own(p)
        output_ref[p] = (valid_ref[p] * (middle_ref[p] + own_ref[p])).astype(LOW)

    first()
    interleaved(line_steps(line, begin, own), events)
    drain()
    line.drain()


def line_steps(line, begin, own):
    steps = []
    for k in range(line.pieces + 1):
        for i in range(line.count - 1):
            if i == 0 and k < line.pieces:
                steps.append((1.0, functools.partial(begin, k)))
            if k < line.pieces:
                steps.append((8.0, functools.partial(line.send_sums, k, line.count - 1 - i)))
            if i == 0 and k > 0:
                steps.append((1.0, functools.partial(own, k - 1)))
    return steps


def scatter_blocks(parts, hidden, wd, middle, valid, kraw, cosine, sine, kgain):
    seq_count, batch = lax.axis_size("seq"), parts.shape[0]
    rows, columns = parts.shape[1] // seq_count, parts.shape[2]
    count, pieces, piece_rows, units = hidden.shape
    model, head_dim = wd.shape[1], kgain.shape[1]
    any_place = pl.BlockSpec(memory_space=pl.ANY)
    return pl.pallas_call(
        functools.partial(scatter_kernel, pieces, count, seq_count, batch, head_dim),
        in_specs=[any_place] * 3 + [WHOLE] * 6,
        out_specs=[WHOLE] * 3,
        out_shape=[
            jax.ShapeDtypeStruct((batch, rows, columns), LOW),
            jax.ShapeDtypeStruct((pieces, piece_rows, model), LOW),
            shape_of(1, head_dim, F32),
        ],
        scratch_shapes=[
            pltpu.VMEM(wd.shape, LOW),
            pltpu.VMEM((2, count, piece_rows, units), LOW),
            pltpu.SemaphoreType.DMA,
            pltpu.SemaphoreType.DMA((2,)),
            pltpu.VMEM((batch, seq_count // 2, rows, columns), LOW),
            pltpu.SemaphoreType.DMA((batch, seq_count // 2)),
            pltpu.VMEM((batch, seq_count - 1, rows, columns), LOW),
            pltpu.SemaphoreType.DMA((batch, seq_count - 1)),
            pltpu.SemaphoreType.DMA((batch, seq_count - 1)),
        ]
        + line_scratch(pieces, count, piece_rows, model, F32, False),
        compiler_params=params(58, collective_id=4, has_side_effects=True),
        cost_estimate=takes(10),
        name="scatter_blocks",
    )(
        parts.reshape(batch, seq_count, rows, columns), hidden, wd, middle, valid, kraw, cosine, sine, kgain
    )


def last_kernel(
    pieces, count, seq_count, streams, halves,
    dq_ref, dkv_ref, dgate_ref, gain_ref, dmid_ref, dqgain_ref, dkgain_ref,
    wq_hbm, wk_hbm, wv_hbm, wg_hbm, tok_hbm, residual_hbm, *refs,
):
    grads, refs = refs[:streams], refs[streams:]
    input_ref, total_ref, sums = refs[0], refs[1], refs[2 : 2 + streams]
    (
        wq_ref, wk_ref, wv_ref, wg_ref, tok_ref, residual_ref, load_sem, kept_ref, kept_sem,
        slots, scatter_send, scatter_receive, gather_send, gather_receive, mine_ref, mine_sem,
        dgain_ref, turns_ref, round_ref, mixed_ref, round_send, round_receive, mixed_send, mixed_receive,
        part_ref, own_ref, right_ref, left_ref, *sems,
    ) = refs[2 + streams :]
    rows, model = own_ref.shape[1], own_ref.shape[2]
    tall = count * rows
    place_seq = lax.axis_index("seq")
    digits = digit_orders(seq_count, 1)[0]
    line = Line(pieces, count, part_ref, own_ref, right_ref, left_ref, sems)
    pairs = (
        (wq_hbm, wq_ref), (wg_hbm, wg_ref), (wk_hbm, wk_ref), (wv_hbm, wv_ref), (tok_hbm, tok_ref),
        (residual_hbm, residual_ref),
    )
    loads = [pltpu.make_async_copy(*pair, load_sem.at[i]) for i, pair in enumerate(pairs)]
    for load in loads:
        load.start()
    line.barrier_all(digits)
    dgain_ref[...] = jnp.zeros_like(dgain_ref)

    begins, arrivals, gather_drain = block_gathers(
        seq_count, streams, lambda b: sums[b], lambda b: mine_ref.at[b], gather_send, gather_receive
    )

    def keep(b):
        return pltpu.make_async_copy(mine_ref.at[b], sums[b].at[place_seq], mine_sem.at[b])

    def finish(b, total):
        mine_ref[b] = total.astype(LOW)
        begins[b]()
        keep(b).start()

    first, events, scatter_drain = block_sums(
        seq_count, streams, lambda b: grads[b], finish, slots, scatter_send, scatter_receive, kept_ref, kept_sem, 1.0
    )

    def begin(p):
        if p == 0:
            for load in loads[:4]:
                load.wait()
        b, half = p // halves, p % halves
        dq = dq_ref[b, :, half].reshape(tall, dq_ref.shape[-1])
        dkv = dkv_ref[b, :, half].reshape(tall, dkv_ref.shape[-1])
        dgate = dgate_ref[b, :, half].reshape(tall, dgate_ref.shape[-1])
        nk = dkv.shape[1] // 2
        total = mm_t(dq, wq_ref[...]) + mm_t(dgate, wg_ref[...])
        total = total + mm_t(dkv[:, :nk], wk_ref[...]) + mm_t(dkv[:, nk:], wv_ref[...])
        part_ref[...] = total.reshape(count, rows, model)
        line.keep_own(p)

    def own(p):
        if p == 0:
            for load in loads[4:]:
                load.wait()
        line.finish_own(p)
        x = tok_ref[p].astype(F32)
        grad = own_ref[p]
        inverse = inverse_rms(x)
        dgain_ref[...] = dgain_ref[...] + jnp.sum(grad * x * inverse, axis=0, keepdims=True)
        input_ref[p] = residual_ref[p] + norm_back(grad, x, gain_ref[...])

    width = model // count
    lines = width // 128
    rounds = [
        pltpu.make_async_remote_copy(
            src_ref=turns_ref.at[i],
            dst_ref=round_ref.at[i],
            send_sem=round_send.at[i],
            recv_sem=round_receive.at[i],
            device_id={"seq": flipped(place_seq, digit)},
            device_id_type=MESH,
        )
        for i, digit in enumerate(digits)
    ]
    done = len(digits)
    shares = []
    for distance in range(1, count):
        other = lax.rem(line.place + distance, count)
        shares.append(
            pltpu.make_async_remote_copy(
                src_ref=turns_ref.at[done, other],
                dst_ref=mixed_ref.at[distance - 1],
                send_sem=mixed_send.at[distance - 1],
                recv_sem=mixed_receive.at[distance - 1],
                device_id={"head": other},
                device_id_type=MESH,
            )
        )

    def pack():
        turns_ref[0] = jnp.zeros(turns_ref.shape[1:], F32)
        for t in range(count):
            for i in range(lines):
                span = slice(t * width + i * 128, t * width + (i + 1) * 128)
                turns_ref[0, t, i : i + 1, :] = dgain_ref[:, span]
                turns_ref[0, t, lines + i : lines + i + 1, :] = dmid_ref[:, span]
            turns_ref[0, t, 2 * lines : 2 * lines + 1, :] = dqgain_ref[...]
            turns_ref[0, t, 2 * lines + 1 : 2 * lines + 2, :] = dkgain_ref[...]
        rounds[0].start()

    def one_round(i):
        rounds[i].wait_recv()
        turns_ref[i + 1] = turns_ref[i] + round_ref[i]
        for copy in rounds[i + 1 : i + 2] if i + 1 < done else shares:
            copy.start()

    def total():
        found = turns_ref[done, line.place]
        for i, copy in enumerate(shares):
            copy.wait_recv()
            found = found + mixed_ref[i]
        total_ref[...] = found

    steps = line_steps(line, begin, own) + [(1.0, pack)]
    steps += [(4.0, functools.partial(one_round, i)) for i in range(done)] + [(4.0, total)]
    first()
    interleaved(steps, events + arrivals)
    for copy in rounds + shares:
        copy.wait_send()
    for b in range(streams):
        keep(b).wait()
    scatter_drain()
    gather_drain()
    line.drain()


def last_step(dq, dkv, dgate, wq, wk, wv, wg, tok, residual, gain, dmid, dqgain, dkgain, grads):
    batch, count, halves, rows, nq = dq.shape
    pieces, model = batch * halves, wq.shape[0]
    seq_count, streams = lax.axis_size("seq"), len(grads)
    tall, columns = grads[0].shape
    block = tall // seq_count
    steps = seq_count.bit_length() - 1
    lines = 8 * ((2 * (model // count // 128) + 2 + 7) // 8)
    return pl.pallas_call(
        functools.partial(last_kernel, pieces, count, seq_count, streams, halves),
        in_specs=[WHOLE] * 7 + [pl.BlockSpec(memory_space=pl.ANY)] * (6 + streams),
        out_specs=[WHOLE] * 2 + [pl.BlockSpec(memory_space=pl.ANY)] * streams,
        out_shape=[jax.ShapeDtypeStruct((pieces, rows, model), F32), shape_of(lines, 128, F32)]
        + [jax.ShapeDtypeStruct((seq_count, block, columns), LOW)] * streams,
        scratch_shapes=[pltpu.VMEM(x.shape, x.dtype) for x in (wq, wk, wv, wg, tok, residual)]
        + [
            pltpu.SemaphoreType.DMA((6,)),
            pltpu.VMEM((streams, seq_count // 2, block, columns), LOW),
            pltpu.SemaphoreType.DMA((streams, seq_count // 2)),
            pltpu.VMEM((streams, seq_count - 1, block, columns), LOW),
            pltpu.SemaphoreType.DMA((streams, seq_count - 1)),
            pltpu.SemaphoreType.DMA((streams, seq_count - 1)),
            pltpu.SemaphoreType.DMA((streams, steps, seq_count)),
            pltpu.SemaphoreType.DMA((streams, seq_count)),
            pltpu.VMEM((streams, block, columns), LOW),
            pltpu.SemaphoreType.DMA((streams,)),
            pltpu.VMEM((1, model), F32),
            pltpu.VMEM((steps + 1, count, lines, 128), F32),
            pltpu.VMEM((steps, count, lines, 128), F32),
            pltpu.VMEM((count - 1, lines, 128), F32),
            pltpu.SemaphoreType.DMA((steps,)),
            pltpu.SemaphoreType.DMA((steps,)),
            pltpu.SemaphoreType.DMA((count - 1,)),
            pltpu.SemaphoreType.DMA((count - 1,)),
        ]
        + line_scratch(pieces, count, rows, model, F32, False),
        compiler_params=params(60, collective_id=5, has_side_effects=True),
        cost_estimate=takes(5),
        name="last",
    )(
        dq, dkv, dgate, gain, dmid, dqgain, dkgain, wq, wk, wv, wg, tok, residual,
        *[grad.reshape(seq_count, block, columns) for grad in grads],
    )


def widen_kernel(input_ref, output_ref, dq_ref, dkv_ref, dgate_ref, out_ref, *refs):
    ff_refs, refs = refs[:3], refs[3:]
    input_out, output_out, dq_out, dk_out, dv_out, dgate_out, out_out, *ff_outs = refs
    keys = dk_out.shape[1]
    input_out[...] = jnp.stack([input_ref[b] for b in range(input_ref.shape[0])], axis=1)
    output_out[...] = jnp.stack([output_ref[b].astype(F32) for b in range(input_ref.shape[0])], axis=1).astype(LOW)
    dq_out[...] = dq_ref[...].astype(F32)
    dk_out[...] = dkv_ref[:, :keys].astype(F32)
    dv_out[...] = dkv_ref[:, keys:].astype(F32)
    dgate_out[...] = dgate_ref[...].astype(F32)
    out_out[...] = out_ref[...].astype(F32).T
    for ref, out in zip(ff_refs, ff_outs):
        out[...] = ref[...].astype(F32)


def widen(input_grad, output, dq, dkv, dgate, out, ff, steps=8):
    batch, rows, model = input_grad.shape
    columns, keys = dq.shape[1], dkv.shape[1] // 2

    def tall(array):
        return pl.BlockSpec((array.shape[0] // steps, array.shape[1]), lambda i: (i, 0))

    def wide(array):
        return jax.ShapeDtypeStruct(array.shape, F32)

    outs = [
        jax.ShapeDtypeStruct((rows, batch, model), F32), jax.ShapeDtypeStruct((rows, batch, model), LOW),
        wide(dq), shape_of(model, keys, F32), shape_of(model, keys, F32), wide(dgate), shape_of(columns, model, F32),
    ] + [wide(x) for x in ff]
    specs = [pl.BlockSpec((rows // steps, batch, model), lambda i: (i, 0, 0))] * 2
    specs += [tall(x) for x in outs[2:6]]
    specs += [pl.BlockSpec((columns, model // steps), lambda i: (0, i))]
    specs += [tall(x) for x in ff]
    return pl.pallas_call(
        widen_kernel,
        grid=(steps,),
        in_specs=[pl.BlockSpec((batch, rows // steps, model), lambda i: (0, i, 0))] * 2
        + [tall(x) for x in (dq, dkv, dgate, out, *ff)],
        out_specs=specs,
        out_shape=outs,
        compiler_params=params(58),
        cost_estimate=takes(25),
        name="widen",
    )(input_grad, output, dq, dkv, dgate, out, *ff)


def turn_tables(positions, head_dim):
    half_dim = head_dim // 2
    lane = jnp.arange(head_dim, dtype=jnp.int32)
    inverse = THETA ** (-((lane % half_dim).astype(F32) * 2.0) / head_dim)
    angles = positions.astype(F32)[:, None] * inverse[None, :]
    return jnp.cos(angles), jnp.where(lane < half_dim, -1.0, 1.0)[None, :] * jnp.sin(angles)


def norm_back(grad, values, gain):
    inverse = inverse_rms(values)
    grad = grad * gain
    mean = jnp.mean(grad * values, axis=-1, keepdims=True)
    return inverse * (grad - values * (inverse * inverse * mean))


def gather(value, axis):
    return lax.all_gather(value, axis, axis=0, tiled=True)


def on_device(
    tokens, cotangent, lengths,
    query_weight, key_weight, value_weight, gating_weight, output_weight,
    swiglu_gate, swiglu_lift, swiglu_down,
    input_gain, middle_gain, query_gain, key_gain,
):
    block_index = lax.axis_index("seq")
    part_index = lax.axis_index("head")
    parts = lax.axis_size("head")
    local_rows, batch, model = tokens.shape
    head_dim = query_gain.shape[0]
    block_rows = local_rows * parts
    flat_rows = block_rows * batch
    group = query_weight.shape[1] // key_weight.shape[1]
    nq, nk = query_weight.shape[1], key_weight.shape[1]
    halves = 2
    pieces, rows = batch * halves, local_rows // halves

    query_start = block_index * block_rows
    positions = query_start + jnp.arange(block_rows, dtype=jnp.int32)
    cosine, sine = lax.optimization_barrier(turn_tables(positions, head_dim))
    gain_in, gain_mid = input_gain[None, :], middle_gain[None, :]
    gain_q, gain_k = query_gain[None, :], key_gain[None, :]
    local_pos = query_start + part_index * local_rows + jnp.arange(local_rows, dtype=jnp.int32)
    place = jnp.concatenate([query_start[None], lengths]).astype(jnp.int32)
    valid = (local_pos[None, :] < lengths[:, None]).astype(F32)[..., None]
    tok = jnp.transpose(tokens, (1, 0, 2)).reshape(pieces, rows, model)

    normed, qraw, q, kraw, kv_own, gate = [
        x.reshape(batch, block_rows, x.shape[-1])
        for x in front_step(
            tok, gain_in, cosine, sine, gain_q, gain_k,
            query_weight, key_weight, value_weight, gating_weight, parts,
        )
    ]
    masked_own = (valid * jnp.transpose(cotangent, (1, 0, 2)).astype(F32)).astype(LOW)
    kv_own, masked_own = lax.optimization_barrier((kv_own, masked_own))
    kv = gather_blocks(kv_own)
    masked = gather(masked_own.reshape(batch * local_rows, model), "head")
    att, acted, inv = attend(place, q, kv, gate, group, head_dim)
    middle, dgain_mid, normed_mid, hidden, dg, dl, dn_mid = middle_step(
        acted.reshape(batch, parts, halves, rows, nq), tok, gain_mid, output_weight,
        masked.reshape(parts, pieces, rows, model), swiglu_gate, swiglu_lift, swiglu_down, parts,
    )

    def flat(array):
        return array.reshape(flat_rows, array.shape[-1])

    normed_mid = flat(normed_mid)
    ff_grads = (
        t_mm(normed_mid, flat(dg)).astype(LOW),
        t_mm(normed_mid, flat(dl)).astype(LOW),
        t_mm(flat(hidden), masked).astype(LOW),
    )
    dn_mid, ff_grads = lax.optimization_barrier((dn_mid, ff_grads))
    ff_grads = lax.psum(ff_grads, "seq")
    residual, r, dgain_q, *firsts = residual_step(
        dn_mid, middle, masked_own.reshape(pieces, rows, model), gain_mid,
        place, output_weight, cosine, sine, gain_q, q, kv, att, gate, inv, qraw, group,
    )
    r = r.reshape(batch, block_rows, model)
    dq, dkv_all, dgate, dgain_q = attend_back(
        place, q, kv, r, output_weight, att, gate, inv, qraw, cosine, sine, gain_q, group, dgain_q, firsts
    )
    dkv, output, dgain_k = scatter_blocks(
        dkv_all, hidden, swiglu_down, middle, valid.reshape(pieces, rows, 1), kraw, cosine, sine, gain_k
    )
    grads = [
        t_mm(flat(normed), flat(dq)).astype(LOW),
        t_mm(flat(normed), flat(dkv)).astype(LOW),
        t_mm(flat(normed), flat(dgate)).astype(LOW),
        t_mm(flat(r), flat(acted)).astype(LOW),
    ]

    def pieced(array):
        return array.reshape(batch, parts, halves, rows, array.shape[-1])

    input_grad, gains, *grads = last_step(
        pieced(dq), pieced(dkv), pieced(dgate), query_weight, key_weight, value_weight, gating_weight,
        tok, residual, gain_in, dgain_mid, dgain_q, dgain_k, grads,
    )
    input_grad, output, dq_weight, dk_weight, dv_weight, dgate_weight, out_weight, *ff_sums = widen(
        input_grad.reshape(batch, local_rows, model),
        output.reshape(batch, local_rows, model),
        *[x.reshape(model, x.shape[-1]) for x in grads],
        ff_grads,
    )
    share = model // parts
    lines = share // 128
    head_share = head_dim // parts

    def head_gain(line):
        return lax.dynamic_slice(gains[line], (part_index * head_share,), (head_share,))

    return (
        output,
        input_grad,
        dq_weight,
        dk_weight,
        dv_weight,
        dgate_weight,
        out_weight,
        *ff_sums,
        gains[:lines].reshape(share),
        gains[lines : 2 * lines].reshape(share),
        head_gain(2 * lines),
        head_gain(2 * lines + 1),
    )


def solution(mesh):
    return jax.shard_map(
        on_device,
        mesh=mesh,
        in_specs=(
            P(("seq", "head"), None, None),
            P(("seq", "head"), None, None),
            P(),
            P(None, "head"),
            P(None, "head"),
            P(None, "head"),
            P(None, "head"),
            P("head", None),
            P(None, "head"),
            P(None, "head"),
            P("head", None),
            P(),
            P(),
            P(),
            P(),
        ),
        out_specs=(
            P(("seq", "head"), None, None),
            P(("seq", "head"), None, None),
            P(None, "head"),
            P(None, "head"),
            P(None, "head"),
            P(None, "head"),
            P("head", None),
            P(None, "head"),
            P(None, "head"),
            P("head", None),
            P("head"),
            P("head"),
            P("head"),
            P("head"),
        ),
        check_vma=False,
    )
```

```python
import functools

import jax
import jax.numpy as jnp
from jax import lax
from jax.experimental import pallas as pl
from jax.experimental.pallas import tpu as pltpu
from jax.sharding import PartitionSpec as P

EPS = 1e-06
THETA = 1000000.0
LOG2E = 1.4426950408889634
MIB = 1024 * 1024
LOW = jnp.bfloat16
F32 = jnp.float32
MESH = pl.DeviceIdType.MESH


def mm(left, right):
    return jnp.dot(left, right, preferred_element_type=F32)


def mm_t(left, right):
    return lax.dot_general(left, right, (((1,), (1,)), ((), ())), preferred_element_type=F32)


def t_mm(left, right):
    return lax.dot_general(left, right, (((0,), (0,)), ((), ())), preferred_element_type=F32)


def shape_of(rows, columns, kind):
    return jax.ShapeDtypeStruct((rows, columns), kind)


def params(mib, **extra):
    return pltpu.CompilerParams(vmem_limit_bytes=mib * MIB, **extra)


def takes(microseconds):
    return pl.CostEstimate(
        flops=int(microseconds * 1.15e9), bytes_accessed=int(microseconds * 3.69e6), transcendentals=0
    )


WHOLE = pl.BlockSpec(memory_space=pltpu.VMEM)
SCALARS = pl.BlockSpec(memory_space=pltpu.SMEM)


def full_block(array):
    return pl.BlockSpec(array.shape, lambda i: (0,) * len(array.shape))


def inverse_rms(values):
    return lax.rsqrt(jnp.mean(values * values, axis=-1, keepdims=True) + EPS)


def turn(values, cosine, sine):
    return values * cosine + pltpu.roll(values, values.shape[-1] // 2, 1) * sine


def turn_back(grads, cosine, sine):
    return grads * cosine + pltpu.roll(grads * sine, grads.shape[-1] // 2, 1)


def live_blocks(place_ref, rows, first=0):
    start, length = place_ref[0], place_ref[1 + first + pl.program_id(0)]
    whole = jnp.minimum(start // rows, length // rows)
    end = jnp.minimum(start // rows + 1, (length + rows - 1) // rows)
    end = jnp.where(start < length, end, 0)
    return jnp.minimum(whole, end), end, start, length


def attend_kernel(
    group, head_dim, place_ref, q_ref, kv_ref, gate_ref, att_ref, acted_ref, inv_ref, acc_ref, sum_ref
):
    rows = q_ref.shape[1]
    heads = q_ref.shape[2] // head_dim
    kv_heads = heads // group
    factor = head_dim ** (-0.5) * LOG2E
    acc_ref[...] = jnp.zeros_like(acc_ref)
    sum_ref[...] = jnp.zeros_like(sum_ref)
    whole, end, start, length = live_blocks(place_ref, rows)

    def one_block(j, masked, width=1):
        tall = width * rows
        span = pl.ds(pl.multiple_of(j * rows, rows), tall)
        if masked:
            key_pos = j * rows + lax.broadcasted_iota(jnp.int32, (rows, rows), 1)
            query_pos = start + lax.broadcasted_iota(jnp.int32, (rows, rows), 0)
            allowed = (key_pos <= query_pos) & (key_pos < length)
        for h in range(heads):
            c = h // group
            keys = kv_ref[0, span, c * head_dim : (c + 1) * head_dim]
            values = kv_ref[0, span, (kv_heads + c) * head_dim : (kv_heads + c + 1) * head_dim]
            weights = jnp.exp2(mm_t(q_ref[0, :, h * head_dim : (h + 1) * head_dim], keys) * factor)
            if masked:
                weights = jnp.where(allowed, weights, 0.0)
            total = weights[:, :128]
            for piece in range(1, tall // 128):
                total = total + weights[:, piece * 128 : (piece + 1) * 128]
            sum_ref[h] = sum_ref[h] + total
            acc_ref[h] = acc_ref[h] + mm(weights.astype(LOW), values)

    def plain(j, carry):
        one_block(j, False)
        return carry

    def pair(j, carry):
        one_block(2 * j, False, 2)
        return carry

    def edge(j, carry):
        one_block(j, True)
        return carry

    lax.fori_loop(0, whole // 2, pair, 0)
    lax.fori_loop(whole // 2 * 2, whole, plain, 0)
    lax.fori_loop(whole, end, edge, 0)
    lane = lax.broadcasted_iota(jnp.int32, inv_ref.shape[1:], 1)
    kept = jnp.zeros(inv_ref.shape[1:], F32)
    for h in range(heads):
        total = jnp.sum(sum_ref[h], axis=1, keepdims=True)
        inverse = 1.0 / jnp.where(total > 0.0, total, 1.0)
        attended = acc_ref[h] * inverse
        columns = slice(h * head_dim, (h + 1) * head_dim)
        att_ref[0, :, columns] = attended
        acted_ref[0, :, columns] = (attended * jax.nn.sigmoid(gate_ref[0, :, columns])).astype(LOW)
        kept = jnp.where(lane == h, inverse, kept)
    inv_ref[0] = kept


def by_sequence(array):
    return pl.BlockSpec((1,) + array.shape[1:], lambda b: (b,) + (0,) * (len(array.shape) - 1))


def attend(place, q, kv, gate, group, head_dim):
    batch, rows, width = q.shape
    heads = width // head_dim
    outs = [
        jax.ShapeDtypeStruct((batch, rows, width), F32),
        jax.ShapeDtypeStruct((batch, rows, width), LOW),
        jax.ShapeDtypeStruct((batch, rows, 128), F32),
    ]
    return pl.pallas_call(
        functools.partial(attend_kernel, group, head_dim),
        grid=(batch,),
        in_specs=[SCALARS, by_sequence(q), by_sequence(kv), by_sequence(gate)],
        out_specs=[by_sequence(x) for x in outs],
        out_shape=outs,
        scratch_shapes=[
            pltpu.VMEM((heads, rows, head_dim), F32),
            pltpu.VMEM((heads, rows, 128), F32),
        ],
        compiler_params=params(58),
        cost_estimate=takes(18),
        name="attend",
    )(place, q, kv, gate)


def norm_turn_back(grad, raw, head_gain, cosine, sine):
    grad = turn_back(grad, cosine, sine)
    inverse = inverse_rms(raw)
    gain_grad = jnp.sum(grad * raw * inverse, axis=0, keepdims=True)
    grad = grad * head_gain
    mean = jnp.mean(grad * raw, axis=-1, keepdims=True)
    return inverse * (grad - raw * (inverse * inverse * mean)), gain_grad


class HeadsBack:
    def __init__(
        self, group, start, length, q, kv, wo, att, gate, inv, qraw, cos, sin, qgain,
        dq, dkv, dgate, scaled, corr, acc,
    ):
        self.group, self.start, self.length = group, start, length
        self.q, self.kv, self.wo, self.att, self.gate, self.inv, self.qraw = q, kv, wo, att, gate, inv, qraw
        self.cos, self.sin, self.qgain = cos, sin, qgain
        self.dq, self.dkv, self.dgate, self.scaled, self.corr, self.acc = dq, dkv, dgate, scaled, corr, acc
        self.rows, self.head_dim = q.shape[0], cos.shape[1]
        self.heads = q.shape[1] // self.head_dim
        self.kv_heads = self.heads // group
        self.scale = self.head_dim ** (-0.5)

    def columns(self, h):
        return slice(h * self.head_dim, (h + 1) * self.head_dim)

    def begin(self, r):
        acted_grad = mm_t(r, self.wo[...])
        lane = lax.broadcasted_iota(jnp.int32, self.inv.shape, 1)
        kept = jnp.zeros(self.inv.shape, F32)
        for h in range(self.heads):
            columns = self.columns(h)
            sigmoid = jax.nn.sigmoid(self.gate[:, columns])
            attended = self.att[:, columns]
            grad = acted_grad[:, columns]
            self.dgate[:, columns] = (grad * attended * sigmoid * (1.0 - sigmoid)).astype(LOW)
            grad = grad * sigmoid
            inverse = self.inv[:, h : h + 1]
            self.scaled[:, columns] = (grad * inverse).astype(LOW)
            total = jnp.sum(grad * attended, axis=1, keepdims=True) * inverse
            kept = jnp.where(lane == h, total, kept)
        self.corr[...] = kept.T
        self.acc[...] = jnp.zeros_like(self.acc)

    def block(self, j, masked, width=1):
        rows, group = self.rows, self.group
        tall = width * rows
        span = pl.ds(pl.multiple_of(j * rows, rows), tall)
        if masked:
            key_pos = j * rows + lax.broadcasted_iota(jnp.int32, (tall, rows), 0)
            query_pos = self.start + lax.broadcasted_iota(jnp.int32, (tall, rows), 1)
            allowed = (key_pos <= query_pos) & (key_pos < self.length)
        for c in range(self.kv_heads):
            key_columns, value_columns = self.columns(c), self.columns(self.kv_heads + c)
            keys = self.kv[span, key_columns]
            values = self.kv[span, value_columns]
            dk = jnp.zeros((tall, self.head_dim), F32)
            dv = jnp.zeros((tall, self.head_dim), F32)
            for h in range(c * group, (c + 1) * group):
                queries = self.q[:, self.columns(h)]
                scaled = self.scaled[:, self.columns(h)]
                weights = jnp.exp2(mm_t(keys, queries) * (self.scale * LOG2E))
                if masked:
                    weights = jnp.where(allowed, weights, 0.0)
                dv = dv + mm(weights.astype(LOW), scaled)
                score = (weights * (mm_t(values, scaled) - self.corr[h : h + 1, :])).astype(LOW)
                dk = dk + mm(score, queries)
                self.acc[h] = self.acc[h] + t_mm(keys, score)
            self.dkv[span, key_columns] = (dk * self.scale).astype(LOW)
            self.dkv[span, value_columns] = dv.astype(LOW)

    def clear(self, j):
        span = pl.ds(pl.multiple_of(j * self.rows, self.rows), self.rows)
        self.dkv[span, :] = jnp.zeros((self.rows, self.dkv.shape[1]), LOW)

    def end(self):
        gain_total = jnp.zeros((1, self.head_dim), F32)
        for h in range(self.heads):
            columns = self.columns(h)
            grad, gain_grad = norm_turn_back(
                self.acc[h].T * self.scale, self.qraw[:, columns], self.qgain[...], self.cos[...], self.sin[...]
            )
            self.dq[:, columns] = grad.astype(LOW)
            gain_total = gain_total + gain_grad
        return gain_total


def heads_back_scratch(heads, rows, head_dim):
    return [
        pltpu.VMEM((rows, heads * head_dim), LOW),
        pltpu.VMEM((128, rows), F32),
        pltpu.VMEM((heads, head_dim, rows), F32),
    ]


def attend_back_kernel(
    group,
    place_ref, q_ref, kv_ref, r_ref, wo_ref, att_ref, gate_ref, inv_ref, qraw_ref, cos_ref, sin_ref, qgain_ref,
    first_gain_ref, first_dq, first_dkv, first_dgate,
    dq_ref, dkv_ref, dgate_ref, dqgain_ref,
    scaled_ref, corr_ref, acc_ref,
):
    del first_dq, first_dkv, first_dgate
    rows = q_ref.shape[1]
    whole, end, start, length = live_blocks(place_ref, rows, 1)
    back = HeadsBack(
        group, start, length, q_ref.at[0], kv_ref.at[0], wo_ref, att_ref.at[0], gate_ref.at[0], inv_ref.at[0],
        qraw_ref.at[0], cos_ref, sin_ref, qgain_ref, dq_ref.at[0], dkv_ref.at[0], dgate_ref.at[0],
        scaled_ref, corr_ref, acc_ref,
    )
    back.begin(r_ref[0])

    def plain(j, carry):
        back.block(j, False)
        return carry

    def pair(j, carry):
        back.block(2 * j, False, 2)
        return carry

    def edge(j, carry):
        back.block(j, True)
        return carry

    def empty(j, carry):
        back.clear(j)
        return carry

    lax.fori_loop(0, whole // 2, pair, 0)
    lax.fori_loop(whole // 2 * 2, whole, plain, 0)
    lax.fori_loop(whole, end, edge, 0)
    lax.fori_loop(end, dkv_ref.shape[1] // rows, empty, 0)
    gain_total = back.end()

    @pl.when(pl.program_id(0) == 0)
    def _():
        dqgain_ref[...] = first_gain_ref[...] + gain_total

    @pl.when(pl.program_id(0) > 0)
    def _():
        dqgain_ref[...] = dqgain_ref[...] + gain_total


def attend_back(place, q, kv, r, wo, att, gate, inv, qraw, cosine, sine, qgain, group, first_gain, firsts):
    batch, rows, width = q.shape
    head_dim = qgain.shape[1]
    any_place = pl.BlockSpec(memory_space=pl.ANY)

    def later(array):
        return pl.BlockSpec((1,) + array.shape[1:], lambda b: (b + 1,) + (0,) * (len(array.shape) - 1))

    line = pl.BlockSpec((1, head_dim), lambda b: (0, 0))
    return pl.pallas_call(
        functools.partial(attend_back_kernel, group),
        grid=(batch - 1,),
        in_specs=[SCALARS, later(q), later(kv), later(r), full_block(wo)]
        + [later(x) for x in (att, gate, inv, qraw)]
        + [full_block(x) for x in (cosine, sine, qgain, first_gain)]
        + [any_place] * 3,
        out_specs=[later(x) for x in firsts] + [line],
        out_shape=[jax.ShapeDtypeStruct(x.shape, x.dtype) for x in firsts] + [shape_of(1, head_dim, F32)],
        scratch_shapes=heads_back_scratch(width // head_dim, rows, head_dim),
        input_output_aliases={13: 0, 14: 1, 15: 2},
        compiler_params=params(58),
        cost_estimate=takes(3),
        name="attend_back",
    )(place, q, kv, r, wo, att, gate, inv, qraw, cosine, sine, qgain, first_gain, *firsts)


class Line:
    def __init__(self, pieces, count, part_ref, own_ref, right_ref, left_ref, sems, spread=None):
        self.sums = part_ref is not None
        self.pieces, self.count = pieces, count
        self.place = lax.axis_index("head")
        self.part_ref, self.own_ref = part_ref, own_ref
        self.right_ref, self.left_ref = right_ref, left_ref
        self.sems = sems
        self.spread = spread

    def barrier(self, digits=()):
        sem = pltpu.get_barrier_semaphore()
        place, count = self.place, self.count
        for digit in digits:
            partner = flipped(lax.axis_index("seq"), digit)
            pl.semaphore_signal(sem, inc=1, device_id={"seq": partner}, device_id_type=MESH)

        @pl.when(place > 0)
        def _():
            pl.semaphore_signal(sem, inc=1, device_id={"head": place - 1}, device_id_type=MESH)

        @pl.when(place < count - 1)
        def _():
            pl.semaphore_signal(sem, inc=1, device_id={"head": place + 1}, device_id_type=MESH)

        inside = (place > 0) & (place < count - 1)

        @pl.when(inside)
        def _():
            pl.semaphore_wait(sem, 2 + len(digits))

        @pl.when(jnp.logical_not(inside))
        def _():
            pl.semaphore_wait(sem, 1 + len(digits))

    def barrier_all(self, digits):
        sem = pltpu.get_barrier_semaphore()
        for digit in digits:
            partner = flipped(lax.axis_index("seq"), digit)
            pl.semaphore_signal(sem, inc=1, device_id={"seq": partner}, device_id_type=MESH)
        for distance in range(1, self.count):
            other = lax.rem(self.place + distance, self.count)
            pl.semaphore_signal(sem, inc=1, device_id={"head": other}, device_id_type=MESH)
        pl.semaphore_wait(sem, self.count - 1 + len(digits))

    def copy(self, ref, send, receive, p, t, step):
        return pltpu.make_async_remote_copy(
            src_ref=ref,
            dst_ref=ref,
            send_sem=self.sems[send].at[p, t],
            recv_sem=self.sems[receive].at[p, t],
            device_id={"head": jnp.clip(self.place + step, 0, self.count - 1)},
            device_id_type=MESH,
        )

    def sum_copy(self, p, t, step):
        ref = self.right_ref if step > 0 else self.left_ref
        base = 0 if step > 0 else 2
        return self.copy(ref.at[p, t], base, base + 1, p, t, step)

    def spread_copy(self, p, t, step):
        first = 4 if self.sums else 0
        return self.copy(self.spread(p, t), first if step > 0 else first + 1, first + 2, p, t, step)

    def send_sums(self, p, distance):
        place, count = self.place, self.count
        for step, ref in ((1, self.right_ref), (-1, self.left_ref)):
            t = place + step * distance
            first = place == (0 if step > 0 else count - 1)

            @pl.when((t >= 0) & (t < count))
            def _(t=t, step=step, ref=ref, first=first):
                @pl.when(first)
                def _():
                    ref[p, t] = self.part_ref[t].astype(LOW)

                @pl.when(jnp.logical_not(first))
                def _():
                    self.sum_copy(p, t, step).wait_recv()
                    ref[p, t] = (ref[p, t].astype(F32) + self.part_ref[t].astype(F32)).astype(LOW)

                self.sum_copy(p, t, step).start()

    def keep_own(self, p):
        self.own_ref[p] = self.part_ref[self.place].astype(F32)

    def finish_own(self, p):
        place, count = self.place, self.count
        for step, ref, inner in ((1, self.right_ref, place > 0), (-1, self.left_ref, place < count - 1)):

            @pl.when(inner)
            def _(step=step, ref=ref):
                self.sum_copy(p, place, step).wait_recv()
                self.own_ref[p] = self.own_ref[p] + ref[p, place].astype(F32)

    def hand_out(self, p):
        place, count = self.place, self.count

        @pl.when(place < count - 1)
        def _():
            self.spread_copy(p, place, 1).start()

        @pl.when(place > 0)
        def _():
            self.spread_copy(p, place, -1).start()

    def hand_on(self, p, distance):
        place, count = self.place, self.count
        for step, more in ((1, place < count - 1), (-1, place > 0)):
            t = place - step * distance

            @pl.when((t >= 0) & (t < count))
            def _(t=t, step=step, more=more):
                self.spread_copy(p, t, step).wait_recv()

                @pl.when(more)
                def _():
                    self.spread_copy(p, t, step).start()

    def drain(self):
        place, count = self.place, self.count

        def one(p, carry):
            for t in range(count):
                if self.sums:

                    @pl.when(t > place)
                    def _(t=t):
                        self.sum_copy(p, t, 1).wait_send()

                    @pl.when(t < place)
                    def _(t=t):
                        self.sum_copy(p, t, -1).wait_send()

                if self.spread is not None:

                    @pl.when((t <= place) & (place < count - 1))
                    def _(t=t):
                        self.spread_copy(p, t, 1).wait_send()

                    @pl.when((t >= place) & (place > 0))
                    def _(t=t):
                        self.spread_copy(p, t, -1).wait_send()

            return carry

        lax.fori_loop(0, self.pieces, one, 0)


def line_scratch(pieces, count, rows, model, part_kind, spread):
    slots = (pieces, count)
    scratch = [
        pltpu.VMEM((pieces, rows, model), F32),
        pltpu.VMEM((pieces, count, rows, model), LOW),
        pltpu.VMEM((pieces, count, rows, model), LOW),
    ] + [pltpu.SemaphoreType.DMA(slots)] * (7 if spread else 4)
    if part_kind is not None:
        scratch = [pltpu.VMEM((count, rows, model), part_kind)] + scratch
    return scratch


def both_ways(index, limit, body):
    @pl.when((index >= 0) & (index < limit))
    def _():
        body(index)


def front_kernel(
    pieces, count, head_dim,
    tok_ref, gain_ref, cos_ref, sin_ref, qgain_ref, kgain_ref, wq_hbm, wk_hbm, wv_hbm, wg_hbm,
    normed_hbm, qraw_hbm, q_hbm, kraw_hbm, kv_hbm, gate_hbm,
    all_ref, normed_ref, qraw_ref, q_ref, kraw_ref, kv_ref, gate_ref, store_sem,
    wq_ref, wk_ref, wv_ref, wg_ref, load_sem, *sems,
):
    rows, model = tok_ref.shape[1], tok_ref.shape[2]
    tall = count * rows
    line = Line(pieces, count, None, None, None, None, sems, spread=lambda p, t: all_ref.at[p, t])
    weights = ((wq_hbm, wq_ref), (wk_hbm, wk_ref), (wv_hbm, wv_ref), (wg_hbm, wg_ref))
    loads = [pltpu.make_async_copy(*pair, load_sem.at[i]) for i, pair in enumerate(weights)]
    for load in loads:
        load.start()
    line.barrier()
    for p in range(pieces):
        all_ref[p, line.place] = tok_ref[p]

    def stores(p):
        pairs = (
            (normed_ref, normed_hbm), (qraw_ref, qraw_hbm), (q_ref, q_hbm), (kraw_ref, kraw_hbm), (kv_ref, kv_hbm),
            (gate_ref, gate_hbm),
        )
        return [
            pltpu.make_async_copy(source, target.at[p // 2, :, p % 2], store_sem.at[i])
            for i, (source, target) in enumerate(pairs)
        ]

    def project(p):
        half = p % 2

        @pl.when(p == 0)
        def _():
            for load in loads:
                load.wait()

        @pl.when(p > 0)
        def _():
            for store in stores(p - 1):
                store.wait()

        def keep(ref, value):
            ref[...] = value.astype(ref.dtype).reshape(count, rows, value.shape[-1])

        x = all_ref[p].reshape(tall, model).astype(F32)
        normed = (x * inverse_rms(x) * gain_ref[...]).astype(LOW)
        keep(normed_ref, normed)
        cosine = cos_ref[:, half].reshape(tall, head_dim)
        sine = sin_ref[:, half].reshape(tall, head_dim)

        def turned(raw, head_gain):
            parts = []
            for h in range(raw.shape[1] // head_dim):
                part = raw[:, h * head_dim : (h + 1) * head_dim]
                parts.append(turn(part * inverse_rms(part) * head_gain, cosine, sine).astype(LOW))
            return parts

        raw = mm(normed, wk_ref[...])
        keep(kraw_ref, raw)
        values = mm(normed, wv_ref[...]).astype(LOW)
        keep(kv_ref, jnp.concatenate(turned(raw, kgain_ref[...]) + [values], axis=1))
        raw = mm(normed, wq_ref[...])
        keep(qraw_ref, raw)
        keep(q_ref, jnp.concatenate(turned(raw, qgain_ref[...]), axis=1))
        keep(gate_ref, mm(normed, wg_ref[...]))
        for store in stores(p):
            store.start()

    def turn_once(k, carry):
        both_ways(k, pieces, line.hand_out)
        for distance in range(1, count):
            both_ways(k - 1, pieces, lambda p, d=distance: line.hand_on(p, d))
        both_ways(k - 1, pieces, project)
        return carry

    lax.fori_loop(0, pieces + 1, turn_once, 0)
    for store in stores(pieces - 1):
        store.wait()
    line.drain()


def front_step(tok, gain, cosine, sine, qgain, kgain, wq, wk, wv, wg, count):
    pieces, rows, model = tok.shape
    batch = pieces // 2
    head_dim = qgain.shape[1]
    nq, nk = wq.shape[1], wk.shape[1]

    def wide(columns, kind):
        return jax.ShapeDtypeStruct((batch, count, 2, rows, columns), kind)

    slots = (pieces, count)
    kinds = [(model, LOW), (nq, F32), (nq, LOW), (nk, F32), (2 * nk, LOW), (nq, F32)]
    return pl.pallas_call(
        functools.partial(front_kernel, pieces, count, head_dim),
        in_specs=[WHOLE] * 6 + [pl.BlockSpec(memory_space=pl.ANY)] * 4,
        out_specs=[pl.BlockSpec(memory_space=pl.ANY)] * 6,
        out_shape=[wide(*kind) for kind in kinds],
        scratch_shapes=[pltpu.VMEM((pieces, count, rows, model), LOW)]
        + [pltpu.VMEM((count, rows, columns), kind) for columns, kind in kinds]
        + [pltpu.SemaphoreType.DMA((6,))]
        + [pltpu.VMEM(x.shape, LOW) for x in (wq, wk, wv, wg)]
        + [pltpu.SemaphoreType.DMA((4,))]
        + [pltpu.SemaphoreType.DMA(slots)] * 3,
        compiler_params=params(58, collective_id=2, has_side_effects=True),
        cost_estimate=takes(95),
        name="front",
    )(
        tok, gain, cosine.reshape(count, 2, rows, head_dim), sine.reshape(count, 2, rows, head_dim),
        qgain, kgain, wq, wk, wv, wg,
    )


def middle_kernel(
    pieces, count,
    acted_ref, tok_ref, gain_ref, wo_ref, masked_hbm, wg_hbm, wl_hbm, wd_hbm,
    middle_ref, dgain_ref, normed_hbm, hidden_hbm, dg_hbm, dl_hbm, dn_hbm,
    mid_ref, wg_ref, wl_ref, wd_ref, masked_ref, normed_ref, hidden_ref, dg_ref, dl_ref, dn_ref, acc_ref,
    load_sem, masked_sem, store_sem,
    part_ref, own_ref, right_ref, left_ref, *sems,
):
    rows, model = own_ref.shape[1], own_ref.shape[2]
    tall = count * rows
    hidden = wg_ref.shape[1]
    line = Line(
        pieces, count, part_ref, own_ref, right_ref, left_ref, sems, spread=lambda p, t: mid_ref.at[p, t]
    )
    place = line.place
    loads = [
        pltpu.make_async_copy(source, target, load_sem.at[i])
        for i, (source, target) in enumerate(((wg_hbm, wg_ref), (wl_hbm, wl_ref), (wd_hbm, wd_ref)))
    ]
    line.barrier()
    for load in loads:
        load.start()
    dgain_ref[...] = jnp.zeros_like(dgain_ref)
    tiles = 3
    tile = hidden // tiles

    def masked_copy(p):
        return pltpu.make_async_copy(masked_hbm.at[:, p], masked_ref, masked_sem)

    def stores(p):
        pairs = (
            (normed_ref, normed_hbm), (hidden_ref, hidden_hbm), (dg_ref, dg_hbm), (dl_ref, dl_hbm),
            (dn_ref, dn_hbm),
        )
        return [
            pltpu.make_async_copy(source, target.at[:, p], store_sem.at[i])
            for i, (source, target) in enumerate(pairs)
        ]

    def begin(p):
        acted = acted_ref[p // 2, :, p % 2].reshape(tall, acted_ref.shape[-1])
        part_ref[...] = mm(acted, wo_ref[...]).reshape(count, rows, model)
        line.keep_own(p)

    def own(p):
        line.finish_own(p)
        middle = own_ref[p] + tok_ref[p].astype(F32)
        middle_ref[p] = middle
        mid_ref[p, place] = middle.astype(LOW)
        line.hand_out(p)

    def units_begin(p):
        line.hand_on(p, count - 1)

        @pl.when(p > 0)
        def _():
            for store in stores(p - 1):
                store.wait()

        x = mid_ref[p].reshape(tall, model).astype(F32)
        normed = (x * inverse_rms(x) * gain_ref[...]).astype(LOW)
        normed_ref[...] = normed.reshape(count, rows, model)
        masked_copy(p).wait()

        @pl.when(p == 0)
        def _():
            for load in loads:
                load.wait()

    def units_tile(i):
        span = slice(i * tile, (i + 1) * tile)
        normed = normed_ref[...].reshape(tall, model)
        gate = mm(normed, wg_ref[:, span])
        lift = mm(normed, wl_ref[:, span])
        grad = mm_t(masked_ref[...].reshape(tall, model), wd_ref[span, :])
        sigmoid = jax.nn.sigmoid(gate)
        silu = gate * sigmoid
        lift_grad = (grad * silu).astype(LOW)
        gate_grad = (grad * lift * (sigmoid + silu * (1.0 - sigmoid))).astype(LOW)
        hidden_ref[:, :, span] = (silu * lift).astype(LOW).reshape(count, rows, tile)
        dg_ref[:, :, span] = gate_grad.reshape(count, rows, tile)
        dl_ref[:, :, span] = lift_grad.reshape(count, rows, tile)
        part = mm_t(gate_grad, wg_ref[:, span]) + mm_t(lift_grad, wl_ref[:, span])
        if i == 0:
            acc_ref[...] = part
        else:
            acc_ref[...] = acc_ref[...] + part

    def units_end(p):
        total = acc_ref[...]
        dn_ref[...] = total.astype(LOW).reshape(count, rows, model)
        x = mid_ref[p].reshape(tall, model).astype(F32)
        dgain_ref[...] = dgain_ref[...] + jnp.sum(total * x * inverse_rms(x), axis=0, keepdims=True)
        for store in stores(p):
            store.start()

        @pl.when(p < pieces - 1)
        def _():
            masked_copy(p + 1).start()

    masked_copy(0).start()

    def turn_once(k, carry):
        both_ways(k, pieces, begin)
        for i in range(max(tiles, count - 1)):
            if i < count - 1:
                both_ways(k, pieces, lambda p, i=i: line.send_sums(p, count - 1 - i))
            if i == 0:
                both_ways(k - 1, pieces, own)
                both_ways(k - 2, pieces, units_begin)
            elif i < count - 1:
                both_ways(k - 1, pieces, lambda p, i=i: line.hand_on(p, i))
            if i < tiles:
                both_ways(k - 2, pieces, lambda p, i=i: units_tile(i))
        both_ways(k - 2, pieces, units_end)
        return carry

    lax.fori_loop(0, pieces + 2, turn_once, 0)
    for store in stores(pieces - 1):
        store.wait()
    line.drain()


def middle_step(acted, tok, gain, wo, masked, wg, wl, wd, count):
    pieces, rows, model = tok.shape
    hidden = wg.shape[1]
    any_place = pl.BlockSpec(memory_space=pl.ANY)

    def wide(columns, kind=LOW):
        return jax.ShapeDtypeStruct((count, pieces, rows, columns), kind)

    def room(columns, kind=LOW):
        return pltpu.VMEM((count, rows, columns), kind)

    return pl.pallas_call(
        functools.partial(middle_kernel, pieces, count),
        in_specs=[WHOLE] * 4 + [any_place] * 4,
        out_specs=[WHOLE] * 2 + [any_place] * 5,
        out_shape=[
            jax.ShapeDtypeStruct((pieces, rows, model), F32), shape_of(1, model, F32),
            wide(model), wide(hidden), wide(hidden), wide(hidden), wide(model),
        ],
        scratch_shapes=[
            pltpu.VMEM((pieces, count, rows, model), LOW),
            pltpu.VMEM(wg.shape, LOW), pltpu.VMEM(wl.shape, LOW), pltpu.VMEM(wd.shape, LOW),
            room(model), room(model), room(hidden), room(hidden), room(hidden), room(model),
            pltpu.VMEM((count * rows, model), F32),
            pltpu.SemaphoreType.DMA((3,)), pltpu.SemaphoreType.DMA, pltpu.SemaphoreType.DMA((5,)),
        ]
        + line_scratch(pieces, count, rows, model, F32, True),
        compiler_params=params(58, collective_id=0, has_side_effects=True),
        cost_estimate=takes(128),
        name="middle",
    )(acted, tok, gain, wo, masked, wg, wl, wd)


def flipped(place, mask):
    bit = 1
    while bit <= mask:
        if mask & bit:
            place = place + (1 - 2 * (place // bit % 2)) * bit
        bit *= 2
    return place


def digit_orders(count, batch):
    upper = [1 << i for i in range(1, count.bit_length() - 1)]
    return [(upper if b % 2 == 0 else upper[::-1]) + [1] for b in range(batch)]


def greet(place, digits):
    sem = pltpu.get_barrier_semaphore()
    for digit in digits:
        pl.semaphore_signal(sem, inc=1, device_id={"seq": flipped(place, digit)}, device_id_type=MESH)
    pl.semaphore_wait(sem, len(digits))


def block_gathers(count, batch, out, sources, send_sem, receive_sem):
    place = lax.axis_index("seq")
    orders = digit_orders(count, batch)
    steps = len(orders[0])
    started = []

    def copy(b, mask, step):
        digit = orders[b][step]
        block = out(b).at[flipped(place, mask)]
        return pltpu.make_async_remote_copy(
            src_ref=sources(b) if mask == 0 else block,
            dst_ref=block,
            send_sem=send_sem.at[b, step, mask],
            recv_sem=receive_sem.at[b, mask | digit],
            device_id={"seq": flipped(place, digit)},
            device_id_type=MESH,
        )

    def pass_on(b, mask, first):
        for step in range(first, steps):
            one = copy(b, mask, step)
            one.start()
            started.append(one)

    def arrive(b, mask, level):
        block = out(b).at[flipped(place, mask)]
        pltpu.make_async_remote_copy(
            src_ref=block,
            dst_ref=block,
            send_sem=send_sem.at[b, 0, mask],
            recv_sem=receive_sem.at[b, mask],
            device_id={"seq": flipped(place, orders[b][level])},
            device_id_type=MESH,
        ).wait_recv()
        pass_on(b, mask, level + 1)

    begins = [functools.partial(pass_on, b, 0, 0) for b in range(batch)]
    arrivals = []
    for level in range(steps):
        for turn in range(1 << level):
            for b in range(batch):
                mask = orders[b][level]
                for i in range(level):
                    if turn >> i & 1:
                        mask |= orders[b][i]
                arrivals.append((1.0 if level == steps - 1 else 4.0, functools.partial(arrive, b, mask, level)))

    def drain():
        for one in started:
            one.wait_send()

    return begins, arrivals, drain


def gather_kernel(count, batch, own_ref, out_ref, local_sem, send_sem, receive_sem):
    place = lax.axis_index("seq")
    greet(place, digit_orders(count, 1)[0])
    local = [
        pltpu.make_async_copy(own_ref.at[b], out_ref.at[b, place], local_sem.at[b]) for b in range(batch)
    ]
    for copy in local:
        copy.start()
    begins, arrivals, drain = block_gathers(
        count, batch, lambda b: out_ref.at[b], lambda b: own_ref.at[b], send_sem, receive_sem
    )
    for begin in begins:
        begin()
    for _, event in arrivals:
        event()
    drain()
    for copy in local:
        copy.wait()


def gather_blocks(own):
    batch, rows, columns = own.shape
    count = lax.axis_size("seq")
    steps = count.bit_length() - 1
    any_place = pl.BlockSpec(memory_space=pl.ANY)
    out = pl.pallas_call(
        functools.partial(gather_kernel, count, batch),
        in_specs=[any_place],
        out_specs=any_place,
        out_shape=jax.ShapeDtypeStruct((batch, count, rows, columns), LOW),
        scratch_shapes=[
            pltpu.SemaphoreType.DMA((batch,)),
            pltpu.SemaphoreType.DMA((batch, steps, count)),
            pltpu.SemaphoreType.DMA((batch, count)),
        ],
        compiler_params=params(58, collective_id=3, has_side_effects=True),
        cost_estimate=takes(41),
        name="gather_blocks",
    )(own)
    return out.reshape(batch, count * rows, columns)


def block_sums(count, batch, parts, finish, slots, send_sem, receive_sem, kept_ref, kept_sem, near):
    place = lax.axis_index("seq")
    orders = [order[::-1] for order in digit_orders(count, batch)]
    steps = len(orders[0])

    def masks_at(b, step):
        found = [0]
        for digit in orders[b][step + 1 :][::-1]:
            found = [mask | digit for mask in found] + found
        return found

    numbers = {}
    for b in range(batch):
        place_in = 0
        for step in range(steps):
            for mask in masks_at(b, step):
                numbers[b, step, mask] = place_in
                place_in += 1

    def slot(b, step, mask):
        return slots.at[b, numbers[b, step, mask]]

    def transfer(b, step, mask):
        digit = orders[b][step]
        number = numbers[b, step, mask]
        if step == 0:
            source = parts(b).at[flipped(place, mask | digit)]
        else:
            source = slot(b, step - 1, mask | digit)
        return pltpu.make_async_remote_copy(
            src_ref=source,
            dst_ref=slots.at[b, number],
            send_sem=send_sem.at[b, number],
            recv_sem=receive_sem.at[b, number],
            device_id={"seq": flipped(place, digit)},
            device_id_type=MESH,
        )

    started = []

    def kept(b, turn):
        mask = masks_at(b, 0)[turn]
        return pltpu.make_async_copy(
            parts(b).at[flipped(place, mask)], kept_ref.at[b, turn], kept_sem.at[b, turn]
        )

    def begin():
        for turn in range(count // 2):
            for b in range(batch):
                copy = transfer(b, 0, masks_at(b, 0)[turn])
                copy.start()
                started.append(copy)
        for turn in range(count // 2):
            for b in range(batch):
                kept(b, turn).start()

    def take(b, step, mask):
        transfer(b, step, mask).wait_recv()
        if step == 0:
            turn = masks_at(b, 0).index(mask)
            kept(b, turn).wait()
            held = kept_ref.at[b, turn]
        else:
            held = slot(b, step - 1, mask)
        total = held[...].astype(F32) + slot(b, step, mask)[...].astype(F32)
        if step == steps - 1:
            finish(b, total)
        else:
            slot(b, step, mask)[...] = total.astype(LOW)
            if mask & orders[b][step + 1]:
                copy = transfer(b, step + 1, mask & ~orders[b][step + 1])
                copy.start()
                started.append(copy)

    events = []
    for step in range(steps):
        for turn in range(len(masks_at(0, step))):
            for b in range(batch):
                events.append((near if step == 0 else 4.0, functools.partial(take, b, step, masks_at(b, step)[turn])))

    def drain():
        for copy in started:
            copy.wait_send()

    return begin, events, drain


def interleaved(*lists):
    spent = [0.0] * len(lists)
    whole = [sum(time for time, _ in calls) for calls in lists]
    taken = [0] * len(lists)
    while any(taken[i] < len(calls) for i, calls in enumerate(lists)):
        i = min((i for i, calls in enumerate(lists) if taken[i] < len(calls)), key=lambda i: spent[i])
        time, call = lists[i][taken[i]]
        call()
        spent[i] += time / whole[i]
        taken[i] += 1

def residual_kernel(
    pieces, count, halves, group, seq_count,
    place_ref, masked_ref, gain_ref, cos_ref, sin_ref, qgain_ref,
    dn_hbm, middle_hbm, wo_hbm, q_hbm, kv_hbm, att_hbm, gate_hbm, inv_hbm, qraw_hbm,
    residual_ref, r_ref, dqgain_ref, dq_hbm, dkv_hbm, dgate_hbm,
    q_ref, kv_ref, att_ref, gate_ref, inv_ref, qraw_ref, dq_ref, dkv_ref, dgate_ref,
    scaled_ref, corr_ref, acc_ref, load_sem, store_sem, block_sem,
    dn_ref, middle_ref, wo_ref, dn_sem, middle_sem, wo_sem,
    part_ref, own_ref, right_ref, left_ref, *sems,
):
    rows, model = own_ref.shape[1], own_ref.shape[2]
    query_rows = q_ref.shape[0]
    line = Line(
        pieces, count, part_ref, own_ref, right_ref, left_ref, sems,
        spread=lambda p, t: r_ref.at[p // halves, t, p % halves],
    )
    pairs = (
        (q_hbm, q_ref), (kv_hbm, kv_ref), (att_hbm, att_ref), (gate_hbm, gate_ref), (inv_hbm, inv_ref),
        (qraw_hbm, qraw_ref),
    )
    loads = [
        pltpu.make_async_copy(source.at[0], target, load_sem.at[i]) for i, (source, target) in enumerate(pairs)
    ]
    stores = [
        pltpu.make_async_copy(dq_ref, dq_hbm.at[0], store_sem.at[0]),
        pltpu.make_async_copy(dgate_ref, dgate_hbm.at[0], store_sem.at[1]),
    ]
    dn_loads = [pltpu.make_async_copy(dn_hbm.at[:, p], dn_ref.at[:, p], dn_sem.at[p]) for p in range(pieces)]
    middle_load = pltpu.make_async_copy(middle_hbm, middle_ref, middle_sem)
    loads.append(pltpu.make_async_copy(wo_hbm, wo_ref, wo_sem))
    for load in dn_loads + [middle_load]:
        load.start()
    line.barrier()
    for load in loads:
        load.start()
    block_index = lax.axis_index("seq")
    back = HeadsBack(
        group, block_index * query_rows, place_ref[1], q_ref, kv_ref, wo_ref, att_ref, gate_ref, inv_ref, qraw_ref,
        cos_ref, sin_ref, qgain_ref, dq_ref, dkv_ref, dgate_ref, scaled_ref, corr_ref, acc_ref,
    )

    def begin(p):
        dn_loads[p].wait()
        part_ref[...] = dn_ref[:, p]
        line.keep_own(p)

    def own(p):
        if p == 0:
            middle_load.wait()
        line.finish_own(p)
        x = middle_ref[p].astype(LOW).astype(F32)
        residual = masked_ref[p].astype(F32) + norm_back(own_ref[p], x, gain_ref[...])
        residual_ref[p] = residual
        r_ref[p // halves, line.place, p % halves] = residual.astype(LOW)
        line.hand_out(p)

    def block_store(j):
        span = pl.ds(j * query_rows, query_rows)
        return pltpu.make_async_copy(dkv_ref.at[span, :], dkv_hbm.at[0, span, :], block_sem.at[j])

    def heads_begin():
        for load in loads:
            load.wait()
        back.begin(r_ref[0].reshape(query_rows, model))

    def heads_block(j):
        @pl.when(j <= block_index)
        def _():
            back.block(j, True)

        @pl.when(j > block_index)
        def _():
            back.clear(j)

        block_store(j).start()

    def heads_end():
        dqgain_ref[...] = back.end()
        for store in stores:
            store.start()

    steps = []
    for k in range(pieces + 1):
        for i in range(count - 1):
            if i == 0 and k < pieces:
                steps.append((1.0, functools.partial(begin, k)))
            if k < pieces:
                steps.append((8.0, functools.partial(line.send_sums, k, count - 1 - i)))
            if i == 0 and k > 0:
                steps.append((1.0, functools.partial(own, k - 1)))
            elif k > 0:
                steps.append((1.0 if k < pieces else 6.0, functools.partial(line.hand_on, k - 1, i)))
        if k > 0:
            steps.append((1.0 if k < pieces else 6.0, functools.partial(line.hand_on, k - 1, count - 1)))
        if k == halves:
            ready = len(steps)
    heads = [(3.0, heads_begin)]
    heads += [(3.0, functools.partial(heads_block, j)) for j in range(seq_count)]
    heads += [(2.0, heads_end)]
    for _, call in steps[:ready]:
        call()
    interleaved(steps[ready:], heads)
    for j in range(seq_count):
        block_store(j).wait()
    for store in stores:
        store.wait()
    line.drain()


def residual_step(dn, middle, masked, gain, place, wo, cosine, sine, qgain, q, kv, att, gate, inv, qraw, group):
    count, pieces, rows, model = dn.shape
    batch, query_rows, width = q.shape
    halves = pieces // batch
    head_dim = qgain.shape[1]
    seq_count = lax.axis_size("seq")
    any_place = pl.BlockSpec(memory_space=pl.ANY)
    held = (q, kv, att, gate, inv, qraw)
    return pl.pallas_call(
        functools.partial(residual_kernel, pieces, count, halves, group, seq_count),
        in_specs=[SCALARS] + [WHOLE] * 5 + [any_place] * 9,
        out_specs=[WHOLE] * 3 + [any_place] * 3,
        out_shape=[
            jax.ShapeDtypeStruct((pieces, rows, model), F32),
            jax.ShapeDtypeStruct((batch, count, halves, rows, model), LOW),
            shape_of(1, head_dim, F32),
            jax.ShapeDtypeStruct(q.shape, LOW),
            jax.ShapeDtypeStruct(kv.shape, LOW),
            jax.ShapeDtypeStruct(q.shape, LOW),
        ],
        scratch_shapes=[pltpu.VMEM(x.shape[1:], x.dtype) for x in held]
        + [pltpu.VMEM(q.shape[1:], LOW), pltpu.VMEM(kv.shape[1:], LOW), pltpu.VMEM(q.shape[1:], LOW)]
        + heads_back_scratch(width // head_dim, query_rows, head_dim)
        + [
            pltpu.SemaphoreType.DMA((6,)),
            pltpu.SemaphoreType.DMA((2,)),
            pltpu.SemaphoreType.DMA((seq_count,)),
        ]
        + [pltpu.VMEM(x.shape, x.dtype) for x in (dn, middle, wo)]
        + [pltpu.SemaphoreType.DMA((pieces,)), pltpu.SemaphoreType.DMA, pltpu.SemaphoreType.DMA]
        + line_scratch(pieces, count, rows, model, LOW, True),
        compiler_params=params(60, collective_id=1, has_side_effects=True),
        cost_estimate=takes(10),
        name="residual",
    )(place, masked, gain, cosine, sine, qgain, dn, middle, wo, *held)


def scatter_kernel(
    pieces, count, seq_count, batch, head_dim,
    parts_ref, hidden_hbm, wd_hbm, middle_hbm, valid_ref, kraw_ref, cos_ref, sin_ref, kgain_ref,
    dkv_ref, output_ref, dkgain_ref,
    wd_ref, middle_ref, hidden_ref, load_sem, middle_sem, hidden_sem, kept_ref, kept_sem, slots, send_sem, receive_sem,
    part_ref, own_ref, right_ref, left_ref, *sems,
):
    rows, model = own_ref.shape[1], own_ref.shape[2]
    tall = count * rows
    keys = kraw_ref.shape[2]
    line = Line(pieces, count, part_ref, own_ref, right_ref, left_ref, sems)
    load = pltpu.make_async_copy(wd_hbm, wd_ref, load_sem)

    def hidden_copy(p):
        return pltpu.make_async_copy(hidden_hbm.at[:, p], hidden_ref.at[p % 2], hidden_sem.at[p % 2])

    middle_load = pltpu.make_async_copy(middle_hbm, middle_ref, middle_sem)
    load.start()
    hidden_copy(0).start()
    middle_load.start()
    dkgain_ref[...] = jnp.zeros_like(dkgain_ref)
    line.barrier(digit_orders(seq_count, 1)[0])

    def finish(b, total):
        for h in range(keys // head_dim):
            columns = slice(h * head_dim, (h + 1) * head_dim)
            grad, gain_grad = norm_turn_back(
                total[:, columns], kraw_ref[b, :, columns], kgain_ref[...], cos_ref[...], sin_ref[...]
            )
            dkv_ref[b, :, columns] = grad.astype(LOW)
            dkgain_ref[...] = dkgain_ref[...] + gain_grad
        dkv_ref[b, :, keys:] = total[:, keys:].astype(LOW)

    first, events, drain = block_sums(
        seq_count, batch, lambda b: parts_ref.at[b], finish, slots, send_sem, receive_sem, kept_ref, kept_sem, 4.0
    )

    def begin(p):
        if p == 0:
            load.wait()
        if p + 1 < pieces:
            hidden_copy(p + 1).start()
        hidden_copy(p).wait()
        hidden = hidden_ref[p % 2].reshape(tall, hidden_ref.shape[-1])
        part_ref[...] = mm(hidden, wd_ref[...]).reshape(count, rows, model)
        line.keep_own(p)

    def own(p):
        if p == 0:
            middle_load.wait()
        line.finish_own(p)
        output_ref[p] = (valid_ref[p] * (middle_ref[p] + own_ref[p])).astype(LOW)

    first()
    interleaved(line_steps(line, begin, own), events)
    drain()
    line.drain()


def line_steps(line, begin, own):
    steps = []
    for k in range(line.pieces + 1):
        for i in range(line.count - 1):
            if i == 0 and k < line.pieces:
                steps.append((1.0, functools.partial(begin, k)))
            if k < line.pieces:
                steps.append((8.0, functools.partial(line.send_sums, k, line.count - 1 - i)))
            if i == 0 and k > 0:
                steps.append((1.0, functools.partial(own, k - 1)))
    return steps


def scatter_blocks(parts, hidden, wd, middle, valid, kraw, cosine, sine, kgain):
    seq_count, batch = lax.axis_size("seq"), parts.shape[0]
    rows, columns = parts.shape[1] // seq_count, parts.shape[2]
    count, pieces, piece_rows, units = hidden.shape
    model, head_dim = wd.shape[1], kgain.shape[1]
    any_place = pl.BlockSpec(memory_space=pl.ANY)
    return pl.pallas_call(
        functools.partial(scatter_kernel, pieces, count, seq_count, batch, head_dim),
        in_specs=[any_place] * 4 + [WHOLE] * 5,
        out_specs=[WHOLE] * 3,
        out_shape=[
            jax.ShapeDtypeStruct((batch, rows, columns), LOW),
            jax.ShapeDtypeStruct((pieces, piece_rows, model), LOW),
            shape_of(1, head_dim, F32),
        ],
        scratch_shapes=[
            pltpu.VMEM(wd.shape, LOW),
            pltpu.VMEM(middle.shape, F32),
            pltpu.VMEM((2, count, piece_rows, units), LOW),
            pltpu.SemaphoreType.DMA,
            pltpu.SemaphoreType.DMA,
            pltpu.SemaphoreType.DMA((2,)),
            pltpu.VMEM((batch, seq_count // 2, rows, columns), LOW),
            pltpu.SemaphoreType.DMA((batch, seq_count // 2)),
            pltpu.VMEM((batch, seq_count - 1, rows, columns), LOW),
            pltpu.SemaphoreType.DMA((batch, seq_count - 1)),
            pltpu.SemaphoreType.DMA((batch, seq_count - 1)),
        ]
        + line_scratch(pieces, count, piece_rows, model, F32, False),
        compiler_params=params(58, collective_id=4, has_side_effects=True),
        cost_estimate=takes(10),
        name="scatter_blocks",
    )(
        parts.reshape(batch, seq_count, rows, columns), hidden, wd, middle, valid, kraw, cosine, sine, kgain
    )


def last_kernel(
    pieces, count, seq_count, streams, halves,
    dq_ref, dkv_ref, dgate_ref, gain_ref, dmid_ref, dqgain_ref, dkgain_ref,
    wq_hbm, wk_hbm, wv_hbm, wg_hbm, tok_hbm, residual_hbm, *refs,
):
    grads, refs = refs[:streams], refs[streams:]
    input_ref, total_ref, sums = refs[0], refs[1], refs[2 : 2 + streams]
    (
        wq_ref, wk_ref, wv_ref, wg_ref, tok_ref, residual_ref, load_sem, kept_ref, kept_sem,
        slots, scatter_send, scatter_receive, gather_send, gather_receive, mine_ref, mine_sem,
        dgain_ref, turns_ref, round_ref, mixed_ref, round_send, round_receive, mixed_send, mixed_receive,
        part_ref, own_ref, right_ref, left_ref, *sems,
    ) = refs[2 + streams :]
    rows, model = own_ref.shape[1], own_ref.shape[2]
    tall = count * rows
    place_seq = lax.axis_index("seq")
    digits = digit_orders(seq_count, 1)[0]
    line = Line(pieces, count, part_ref, own_ref, right_ref, left_ref, sems)
    pairs = (
        (wq_hbm, wq_ref), (wg_hbm, wg_ref), (wk_hbm, wk_ref), (wv_hbm, wv_ref), (tok_hbm, tok_ref),
        (residual_hbm, residual_ref),
    )
    loads = [pltpu.make_async_copy(*pair, load_sem.at[i]) for i, pair in enumerate(pairs)]
    for load in loads:
        load.start()
    line.barrier_all(digits)
    dgain_ref[...] = jnp.zeros_like(dgain_ref)

    begins, arrivals, gather_drain = block_gathers(
        seq_count, streams, lambda b: sums[b], lambda b: mine_ref.at[b], gather_send, gather_receive
    )

    def keep(b):
        return pltpu.make_async_copy(mine_ref.at[b], sums[b].at[place_seq], mine_sem.at[b])

    def finish(b, total):
        mine_ref[b] = total.astype(LOW)
        begins[b]()
        keep(b).start()

    first, events, scatter_drain = block_sums(
        seq_count, streams, lambda b: grads[b], finish, slots, scatter_send, scatter_receive, kept_ref, kept_sem, 1.0
    )

    def begin(p):
        if p == 0:
            for load in loads[:4]:
                load.wait()
        b, half = p // halves, p % halves
        dq = dq_ref[b, :, half].reshape(tall, dq_ref.shape[-1])
        dkv = dkv_ref[b, :, half].reshape(tall, dkv_ref.shape[-1])
        dgate = dgate_ref[b, :, half].reshape(tall, dgate_ref.shape[-1])
        nk = dkv.shape[1] // 2
        total = mm_t(dq, wq_ref[...]) + mm_t(dgate, wg_ref[...])
        total = total + mm_t(dkv[:, :nk], wk_ref[...]) + mm_t(dkv[:, nk:], wv_ref[...])
        part_ref[...] = total.reshape(count, rows, model)
        line.keep_own(p)

    def own(p):
        if p == 0:
            for load in loads[4:]:
                load.wait()
        line.finish_own(p)
        x = tok_ref[p].astype(F32)
        grad = own_ref[p]
        inverse = inverse_rms(x)
        dgain_ref[...] = dgain_ref[...] + jnp.sum(grad * x * inverse, axis=0, keepdims=True)
        input_ref[p] = residual_ref[p] + norm_back(grad, x, gain_ref[...])

    width = model // count
    lines = width // 128
    rounds = [
        pltpu.make_async_remote_copy(
            src_ref=turns_ref.at[i],
            dst_ref=round_ref.at[i],
            send_sem=round_send.at[i],
            recv_sem=round_receive.at[i],
            device_id={"seq": flipped(place_seq, digit)},
            device_id_type=MESH,
        )
        for i, digit in enumerate(digits)
    ]
    done = len(digits)
    shares = []
    for distance in range(1, count):
        other = lax.rem(line.place + distance, count)
        shares.append(
            pltpu.make_async_remote_copy(
                src_ref=turns_ref.at[done, other],
                dst_ref=mixed_ref.at[distance - 1],
                send_sem=mixed_send.at[distance - 1],
                recv_sem=mixed_receive.at[distance - 1],
                device_id={"head": other},
                device_id_type=MESH,
            )
        )

    def pack():
        turns_ref[0] = jnp.zeros(turns_ref.shape[1:], F32)
        for t in range(count):
            for i in range(lines):
                span = slice(t * width + i * 128, t * width + (i + 1) * 128)
                turns_ref[0, t, i : i + 1, :] = dgain_ref[:, span]
                turns_ref[0, t, lines + i : lines + i + 1, :] = dmid_ref[:, span]
            turns_ref[0, t, 2 * lines : 2 * lines + 1, :] = dqgain_ref[...]
            turns_ref[0, t, 2 * lines + 1 : 2 * lines + 2, :] = dkgain_ref[...]
        rounds[0].start()

    def one_round(i):
        rounds[i].wait_recv()
        turns_ref[i + 1] = turns_ref[i] + round_ref[i]
        for copy in rounds[i + 1 : i + 2] if i + 1 < done else shares:
            copy.start()

    def total():
        found = turns_ref[done, line.place]
        for i, copy in enumerate(shares):
            copy.wait_recv()
            found = found + mixed_ref[i]
        total_ref[...] = found

    steps = line_steps(line, begin, own) + [(1.0, pack)]
    steps += [(4.0, functools.partial(one_round, i)) for i in range(done)] + [(4.0, total)]
    first()
    interleaved(steps, events + arrivals)
    for copy in rounds + shares:
        copy.wait_send()
    for b in range(streams):
        keep(b).wait()
    scatter_drain()
    gather_drain()
    line.drain()


def last_step(dq, dkv, dgate, wq, wk, wv, wg, tok, residual, gain, dmid, dqgain, dkgain, grads):
    batch, count, halves, rows, nq = dq.shape
    pieces, model = batch * halves, wq.shape[0]
    seq_count, streams = lax.axis_size("seq"), len(grads)
    tall, columns = grads[0].shape
    block = tall // seq_count
    steps = seq_count.bit_length() - 1
    lines = 8 * ((2 * (model // count // 128) + 2 + 7) // 8)
    return pl.pallas_call(
        functools.partial(last_kernel, pieces, count, seq_count, streams, halves),
        in_specs=[WHOLE] * 7 + [pl.BlockSpec(memory_space=pl.ANY)] * (6 + streams),
        out_specs=[WHOLE] * 2 + [pl.BlockSpec(memory_space=pl.ANY)] * streams,
        out_shape=[jax.ShapeDtypeStruct((pieces, rows, model), F32), shape_of(lines, 128, F32)]
        + [jax.ShapeDtypeStruct((seq_count, block, columns), LOW)] * streams,
        scratch_shapes=[pltpu.VMEM(x.shape, x.dtype) for x in (wq, wk, wv, wg, tok, residual)]
        + [
            pltpu.SemaphoreType.DMA((6,)),
            pltpu.VMEM((streams, seq_count // 2, block, columns), LOW),
            pltpu.SemaphoreType.DMA((streams, seq_count // 2)),
            pltpu.VMEM((streams, seq_count - 1, block, columns), LOW),
            pltpu.SemaphoreType.DMA((streams, seq_count - 1)),
            pltpu.SemaphoreType.DMA((streams, seq_count - 1)),
            pltpu.SemaphoreType.DMA((streams, steps, seq_count)),
            pltpu.SemaphoreType.DMA((streams, seq_count)),
            pltpu.VMEM((streams, block, columns), LOW),
            pltpu.SemaphoreType.DMA((streams,)),
            pltpu.VMEM((1, model), F32),
            pltpu.VMEM((steps + 1, count, lines, 128), F32),
            pltpu.VMEM((steps, count, lines, 128), F32),
            pltpu.VMEM((count - 1, lines, 128), F32),
            pltpu.SemaphoreType.DMA((steps,)),
            pltpu.SemaphoreType.DMA((steps,)),
            pltpu.SemaphoreType.DMA((count - 1,)),
            pltpu.SemaphoreType.DMA((count - 1,)),
        ]
        + line_scratch(pieces, count, rows, model, F32, False),
        compiler_params=params(60, collective_id=5, has_side_effects=True),
        cost_estimate=takes(5),
        name="last",
    )(
        dq, dkv, dgate, gain, dmid, dqgain, dkgain, wq, wk, wv, wg, tok, residual,
        *[grad.reshape(seq_count, block, columns) for grad in grads],
    )


def widen_kernel(input_ref, output_ref, dq_ref, dkv_ref, dgate_ref, out_ref, *refs):
    ff_refs, refs = refs[:3], refs[3:]
    input_out, output_out, dq_out, dk_out, dv_out, dgate_out, out_out, *ff_outs = refs
    keys = dk_out.shape[1]
    input_out[...] = jnp.stack([input_ref[b] for b in range(input_ref.shape[0])], axis=1)
    output_out[...] = jnp.stack([output_ref[b].astype(F32) for b in range(input_ref.shape[0])], axis=1).astype(LOW)
    dq_out[...] = dq_ref[...].astype(F32)
    dk_out[...] = dkv_ref[:, :keys].astype(F32)
    dv_out[...] = dkv_ref[:, keys:].astype(F32)
    dgate_out[...] = dgate_ref[...].astype(F32)
    out_out[...] = out_ref[...].astype(F32).T
    for ref, out in zip(ff_refs, ff_outs):
        out[...] = ref[...].astype(F32)


def widen(input_grad, output, dq, dkv, dgate, out, ff, steps=4):
    batch, rows, model = input_grad.shape
    columns, keys = dq.shape[1], dkv.shape[1] // 2

    def tall(array):
        return pl.BlockSpec((array.shape[0] // steps, array.shape[1]), lambda i: (i, 0))

    def wide(array):
        return jax.ShapeDtypeStruct(array.shape, F32)

    outs = [
        jax.ShapeDtypeStruct((rows, batch, model), F32), jax.ShapeDtypeStruct((rows, batch, model), LOW),
        wide(dq), shape_of(model, keys, F32), shape_of(model, keys, F32), wide(dgate), shape_of(columns, model, F32),
    ] + [wide(x) for x in ff]
    specs = [pl.BlockSpec((rows // steps, batch, model), lambda i: (i, 0, 0))] * 2
    specs += [tall(x) for x in outs[2:6]]
    specs += [pl.BlockSpec((columns, model // steps), lambda i: (0, i))]
    specs += [tall(x) for x in ff]
    return pl.pallas_call(
        widen_kernel,
        grid=(steps,),
        in_specs=[pl.BlockSpec((batch, rows // steps, model), lambda i: (0, i, 0))] * 2
        + [tall(x) for x in (dq, dkv, dgate, out, *ff)],
        out_specs=specs,
        out_shape=outs,
        compiler_params=params(58),
        cost_estimate=takes(25),
        name="widen",
    )(input_grad, output, dq, dkv, dgate, out, *ff)


def turn_tables(positions, head_dim):
    half_dim = head_dim // 2
    lane = jnp.arange(head_dim, dtype=jnp.int32)
    inverse = THETA ** (-((lane % half_dim).astype(F32) * 2.0) / head_dim)
    angles = positions.astype(F32)[:, None] * inverse[None, :]
    return jnp.cos(angles), jnp.where(lane < half_dim, -1.0, 1.0)[None, :] * jnp.sin(angles)


def norm_back(grad, values, gain):
    inverse = inverse_rms(values)
    grad = grad * gain
    mean = jnp.mean(grad * values, axis=-1, keepdims=True)
    return inverse * (grad - values * (inverse * inverse * mean))


def gather(value, axis):
    return lax.all_gather(value, axis, axis=0, tiled=True)


def on_device(
    tokens, cotangent, lengths,
    query_weight, key_weight, value_weight, gating_weight, output_weight,
    swiglu_gate, swiglu_lift, swiglu_down,
    input_gain, middle_gain, query_gain, key_gain,
):
    block_index = lax.axis_index("seq")
    part_index = lax.axis_index("head")
    parts = lax.axis_size("head")
    local_rows, batch, model = tokens.shape
    head_dim = query_gain.shape[0]
    block_rows = local_rows * parts
    flat_rows = block_rows * batch
    group = query_weight.shape[1] // key_weight.shape[1]
    nq, nk = query_weight.shape[1], key_weight.shape[1]
    halves = 2
    pieces, rows = batch * halves, local_rows // halves

    query_start = block_index * block_rows
    positions = query_start + jnp.arange(block_rows, dtype=jnp.int32)
    cosine, sine = lax.optimization_barrier(turn_tables(positions, head_dim))
    gain_in, gain_mid = input_gain[None, :], middle_gain[None, :]
    gain_q, gain_k = query_gain[None, :], key_gain[None, :]
    local_pos = query_start + part_index * local_rows + jnp.arange(local_rows, dtype=jnp.int32)
    place = jnp.concatenate([query_start[None], lengths]).astype(jnp.int32)
    valid = (local_pos[None, :] < lengths[:, None]).astype(F32)[..., None]
    tok = jnp.transpose(tokens, (1, 0, 2)).reshape(pieces, rows, model)

    normed, qraw, q, kraw, kv_own, gate = [
        x.reshape(batch, block_rows, x.shape[-1])
        for x in front_step(
            tok, gain_in, cosine, sine, gain_q, gain_k,
            query_weight, key_weight, value_weight, gating_weight, parts,
        )
    ]
    masked_own = (valid * jnp.transpose(cotangent, (1, 0, 2)).astype(F32)).astype(LOW)
    kv_own, masked_own = lax.optimization_barrier((kv_own, masked_own))
    kv = gather_blocks(kv_own)
    masked = gather(masked_own.reshape(batch * local_rows, model), "head")
    att, acted, inv = attend(place, q, kv, gate, group, head_dim)
    middle, dgain_mid, normed_mid, hidden, dg, dl, dn_mid = middle_step(
        acted.reshape(batch, parts, halves, rows, nq), tok, gain_mid, output_weight,
        masked.reshape(parts, pieces, rows, model), swiglu_gate, swiglu_lift, swiglu_down, parts,
    )

    def flat(array):
        return array.reshape(flat_rows, array.shape[-1])

    normed_mid = flat(normed_mid)
    ff_grads = (
        t_mm(normed_mid, flat(dg)).astype(LOW),
        t_mm(normed_mid, flat(dl)).astype(LOW),
        t_mm(flat(hidden), masked).astype(LOW),
    )
    dn_mid, ff_grads = lax.optimization_barrier((dn_mid, ff_grads))
    ff_grads = lax.psum(ff_grads, "seq")
    residual, r, dgain_q, *firsts = residual_step(
        dn_mid, middle, masked_own.reshape(pieces, rows, model), gain_mid,
        place, output_weight, cosine, sine, gain_q, q, kv, att, gate, inv, qraw, group,
    )
    r = r.reshape(batch, block_rows, model)
    dq, dkv_all, dgate, dgain_q = attend_back(
        place, q, kv, r, output_weight, att, gate, inv, qraw, cosine, sine, gain_q, group, dgain_q, firsts
    )
    dkv, output, dgain_k = scatter_blocks(
        dkv_all, hidden, swiglu_down, middle, valid.reshape(pieces, rows, 1), kraw, cosine, sine, gain_k
    )
    grads = [
        t_mm(flat(normed), flat(dq)).astype(LOW),
        t_mm(flat(normed), flat(dkv)).astype(LOW),
        t_mm(flat(normed), flat(dgate)).astype(LOW),
        t_mm(flat(r), flat(acted)).astype(LOW),
    ]

    def pieced(array):
        return array.reshape(batch, parts, halves, rows, array.shape[-1])

    input_grad, gains, *grads = last_step(
        pieced(dq), pieced(dkv), pieced(dgate), query_weight, key_weight, value_weight, gating_weight,
        tok, residual, gain_in, dgain_mid, dgain_q, dgain_k, grads,
    )
    input_grad, output, dq_weight, dk_weight, dv_weight, dgate_weight, out_weight, *ff_sums = widen(
        input_grad.reshape(batch, local_rows, model),
        output.reshape(batch, local_rows, model),
        *[x.reshape(model, x.shape[-1]) for x in grads],
        ff_grads,
    )
    share = model // parts
    lines = share // 128
    head_share = head_dim // parts

    def head_gain(line):
        return lax.dynamic_slice(gains[line], (part_index * head_share,), (head_share,))

    return (
        output,
        input_grad,
        dq_weight,
        dk_weight,
        dv_weight,
        dgate_weight,
        out_weight,
        *ff_sums,
        gains[:lines].reshape(share),
        gains[lines : 2 * lines].reshape(share),
        head_gain(2 * lines),
        head_gain(2 * lines + 1),
    )


def solution(mesh):
    return jax.shard_map(
        on_device,
        mesh=mesh,
        in_specs=(
            P(("seq", "head"), None, None),
            P(("seq", "head"), None, None),
            P(),
            P(None, "head"),
            P(None, "head"),
            P(None, "head"),
            P(None, "head"),
            P("head", None),
            P(None, "head"),
            P(None, "head"),
            P("head", None),
            P(),
            P(),
            P(),
            P(),
        ),
        out_specs=(
            P(("seq", "head"), None, None),
            P(("seq", "head"), None, None),
            P(None, "head"),
            P(None, "head"),
            P(None, "head"),
            P(None, "head"),
            P("head", None),
            P(None, "head"),
            P(None, "head"),
            P("head", None),
            P("head"),
            P("head"),
            P("head"),
            P("head"),
        ),
        check_vma=False,
    )
```

```python
import functools

import jax
import jax.numpy as jnp
from jax import lax
from jax.experimental import pallas as pl
from jax.experimental.pallas import tpu as pltpu
from jax.sharding import PartitionSpec as P

EPS = 1e-06
THETA = 1000000.0
LOG2E = 1.4426950408889634
MIB = 1024 * 1024
LOW = jnp.bfloat16
F32 = jnp.float32
MESH = pl.DeviceIdType.MESH


def mm(left, right):
    return jnp.dot(left, right, preferred_element_type=F32)


def mm_t(left, right):
    return lax.dot_general(left, right, (((1,), (1,)), ((), ())), preferred_element_type=F32)


def t_mm(left, right):
    return lax.dot_general(left, right, (((0,), (0,)), ((), ())), preferred_element_type=F32)


def shape_of(rows, columns, kind):
    return jax.ShapeDtypeStruct((rows, columns), kind)


def params(mib, **extra):
    return pltpu.CompilerParams(vmem_limit_bytes=mib * MIB, **extra)


def takes(microseconds):
    return pl.CostEstimate(
        flops=int(microseconds * 1.15e9), bytes_accessed=int(microseconds * 3.69e6), transcendentals=0
    )


WHOLE = pl.BlockSpec(memory_space=pltpu.VMEM)
SCALARS = pl.BlockSpec(memory_space=pltpu.SMEM)


def full_block(array):
    return pl.BlockSpec(array.shape, lambda i: (0,) * len(array.shape))


def inverse_rms(values):
    return lax.rsqrt(jnp.mean(values * values, axis=-1, keepdims=True) + EPS)


def turn(values, cosine, sine):
    return values * cosine + pltpu.roll(values, values.shape[-1] // 2, 1) * sine


def turn_back(grads, cosine, sine):
    return grads * cosine + pltpu.roll(grads * sine, grads.shape[-1] // 2, 1)


def live_blocks(place_ref, rows, first=0):
    start, length = place_ref[0], place_ref[1 + first + pl.program_id(0)]
    whole = jnp.minimum(start // rows, length // rows)
    end = jnp.minimum(start // rows + 1, (length + rows - 1) // rows)
    end = jnp.where(start < length, end, 0)
    return jnp.minimum(whole, end), end, start, length


def attend_kernel(
    group, head_dim, place_ref, q_ref, kv_ref, gate_ref, att_ref, acted_ref, inv_ref, acc_ref, sum_ref
):
    rows = q_ref.shape[1]
    heads = q_ref.shape[2] // head_dim
    kv_heads = heads // group
    factor = head_dim ** (-0.5) * LOG2E
    acc_ref[...] = jnp.zeros_like(acc_ref)
    sum_ref[...] = jnp.zeros_like(sum_ref)
    whole, end, start, length = live_blocks(place_ref, rows)

    def one_block(j, masked, width=1):
        tall = width * rows
        span = pl.ds(pl.multiple_of(j * rows, rows), tall)
        if masked:
            key_pos = j * rows + lax.broadcasted_iota(jnp.int32, (rows, rows), 1)
            query_pos = start + lax.broadcasted_iota(jnp.int32, (rows, rows), 0)
            allowed = (key_pos <= query_pos) & (key_pos < length)
        for h in range(heads):
            c = h // group
            keys = kv_ref[0, span, c * head_dim : (c + 1) * head_dim]
            values = kv_ref[0, span, (kv_heads + c) * head_dim : (kv_heads + c + 1) * head_dim]
            weights = jnp.exp2(mm_t(q_ref[0, :, h * head_dim : (h + 1) * head_dim], keys) * factor)
            if masked:
                weights = jnp.where(allowed, weights, 0.0)
            total = weights[:, :128]
            for piece in range(1, tall // 128):
                total = total + weights[:, piece * 128 : (piece + 1) * 128]
            sum_ref[h] = sum_ref[h] + total
            acc_ref[h] = acc_ref[h] + mm(weights.astype(LOW), values)

    def plain(j, carry):
        one_block(j, False)
        return carry

    def pair(j, carry):
        one_block(2 * j, False, 2)
        return carry

    def edge(j, carry):
        one_block(j, True)
        return carry

    lax.fori_loop(0, whole // 2, pair, 0)
    lax.fori_loop(whole // 2 * 2, whole, plain, 0)
    lax.fori_loop(whole, end, edge, 0)
    lane = lax.broadcasted_iota(jnp.int32, inv_ref.shape[1:], 1)
    kept = jnp.zeros(inv_ref.shape[1:], F32)
    for h in range(heads):
        total = jnp.sum(sum_ref[h], axis=1, keepdims=True)
        inverse = 1.0 / jnp.where(total > 0.0, total, 1.0)
        attended = acc_ref[h] * inverse
        columns = slice(h * head_dim, (h + 1) * head_dim)
        att_ref[0, :, columns] = attended
        acted_ref[0, :, columns] = (attended * jax.nn.sigmoid(gate_ref[0, :, columns])).astype(LOW)
        kept = jnp.where(lane == h, inverse, kept)
    inv_ref[0] = kept


def by_sequence(array):
    return pl.BlockSpec((1,) + array.shape[1:], lambda b: (b,) + (0,) * (len(array.shape) - 1))


def attend(place, q, kv, gate, group, head_dim):
    batch, rows, width = q.shape
    heads = width // head_dim
    outs = [
        jax.ShapeDtypeStruct((batch, rows, width), F32),
        jax.ShapeDtypeStruct((batch, rows, width), LOW),
        jax.ShapeDtypeStruct((batch, rows, 128), F32),
    ]
    return pl.pallas_call(
        functools.partial(attend_kernel, group, head_dim),
        grid=(batch,),
        in_specs=[SCALARS, by_sequence(q), by_sequence(kv), by_sequence(gate)],
        out_specs=[by_sequence(x) for x in outs],
        out_shape=outs,
        scratch_shapes=[
            pltpu.VMEM((heads, rows, head_dim), F32),
            pltpu.VMEM((heads, rows, 128), F32),
        ],
        compiler_params=params(58),
        cost_estimate=takes(18),
        name="attend",
    )(place, q, kv, gate)


def norm_turn_back(grad, raw, head_gain, cosine, sine):
    grad = turn_back(grad, cosine, sine)
    inverse = inverse_rms(raw)
    gain_grad = jnp.sum(grad * raw * inverse, axis=0, keepdims=True)
    grad = grad * head_gain
    mean = jnp.mean(grad * raw, axis=-1, keepdims=True)
    return inverse * (grad - raw * (inverse * inverse * mean)), gain_grad


class HeadsBack:
    def __init__(
        self, group, start, length, q, kv, wo, att, gate, inv, qraw, cos, sin, qgain,
        dq, dkv, dgate, scaled, corr, acc,
    ):
        self.group, self.start, self.length = group, start, length
        self.q, self.kv, self.wo, self.att, self.gate, self.inv, self.qraw = q, kv, wo, att, gate, inv, qraw
        self.cos, self.sin, self.qgain = cos, sin, qgain
        self.dq, self.dkv, self.dgate, self.scaled, self.corr, self.acc = dq, dkv, dgate, scaled, corr, acc
        self.rows, self.head_dim = q.shape[0], cos.shape[1]
        self.heads = q.shape[1] // self.head_dim
        self.kv_heads = self.heads // group
        self.scale = self.head_dim ** (-0.5)

    def columns(self, h):
        return slice(h * self.head_dim, (h + 1) * self.head_dim)

    def begin(self, r):
        acted_grad = mm_t(r, self.wo[...])
        lane = lax.broadcasted_iota(jnp.int32, self.inv.shape, 1)
        kept = jnp.zeros(self.inv.shape, F32)
        for h in range(self.heads):
            columns = self.columns(h)
            sigmoid = jax.nn.sigmoid(self.gate[:, columns])
            attended = self.att[:, columns]
            grad = acted_grad[:, columns]
            self.dgate[:, columns] = (grad * attended * sigmoid * (1.0 - sigmoid)).astype(LOW)
            grad = grad * sigmoid
            inverse = self.inv[:, h : h + 1]
            self.scaled[:, columns] = (grad * inverse).astype(LOW)
            total = jnp.sum(grad * attended, axis=1, keepdims=True) * inverse
            kept = jnp.where(lane == h, total, kept)
        self.corr[...] = kept.T
        self.acc[...] = jnp.zeros_like(self.acc)

    def block(self, j, masked, width=1):
        rows, group = self.rows, self.group
        tall = width * rows
        span = pl.ds(pl.multiple_of(j * rows, rows), tall)
        if masked:
            key_pos = j * rows + lax.broadcasted_iota(jnp.int32, (tall, rows), 0)
            query_pos = self.start + lax.broadcasted_iota(jnp.int32, (tall, rows), 1)
            allowed = (key_pos <= query_pos) & (key_pos < self.length)
        for c in range(self.kv_heads):
            key_columns, value_columns = self.columns(c), self.columns(self.kv_heads + c)
            keys = self.kv[span, key_columns]
            values = self.kv[span, value_columns]
            dk = jnp.zeros((tall, self.head_dim), F32)
            dv = jnp.zeros((tall, self.head_dim), F32)
            for h in range(c * group, (c + 1) * group):
                queries = self.q[:, self.columns(h)]
                scaled = self.scaled[:, self.columns(h)]
                weights = jnp.exp2(mm_t(keys, queries) * (self.scale * LOG2E))
                if masked:
                    weights = jnp.where(allowed, weights, 0.0)
                dv = dv + mm(weights.astype(LOW), scaled)
                score = (weights * (mm_t(values, scaled) - self.corr[h : h + 1, :])).astype(LOW)
                dk = dk + mm(score, queries)
                self.acc[h] = self.acc[h] + t_mm(keys, score)
            self.dkv[span, key_columns] = (dk * self.scale).astype(LOW)
            self.dkv[span, value_columns] = dv.astype(LOW)

    def clear(self, j):
        span = pl.ds(pl.multiple_of(j * self.rows, self.rows), self.rows)
        self.dkv[span, :] = jnp.zeros((self.rows, self.dkv.shape[1]), LOW)

    def end(self):
        gain_total = jnp.zeros((1, self.head_dim), F32)
        for h in range(self.heads):
            columns = self.columns(h)
            grad, gain_grad = norm_turn_back(
                self.acc[h].T * self.scale, self.qraw[:, columns], self.qgain[...], self.cos[...], self.sin[...]
            )
            self.dq[:, columns] = grad.astype(LOW)
            gain_total = gain_total + gain_grad
        return gain_total


def heads_back_scratch(heads, rows, head_dim):
    return [
        pltpu.VMEM((rows, heads * head_dim), LOW),
        pltpu.VMEM((128, rows), F32),
        pltpu.VMEM((heads, head_dim, rows), F32),
    ]


def attend_back_kernel(
    group,
    place_ref, q_ref, kv_ref, r_ref, wo_ref, att_ref, gate_ref, inv_ref, qraw_ref, cos_ref, sin_ref, qgain_ref,
    first_gain_ref, first_dq, first_dkv, first_dgate,
    dq_ref, dkv_ref, dgate_ref, dqgain_ref,
    scaled_ref, corr_ref, acc_ref,
):
    del first_dq, first_dkv, first_dgate
    rows = q_ref.shape[1]
    whole, end, start, length = live_blocks(place_ref, rows, 1)
    back = HeadsBack(
        group, start, length, q_ref.at[0], kv_ref.at[0], wo_ref, att_ref.at[0], gate_ref.at[0], inv_ref.at[0],
        qraw_ref.at[0], cos_ref, sin_ref, qgain_ref, dq_ref.at[0], dkv_ref.at[0], dgate_ref.at[0],
        scaled_ref, corr_ref, acc_ref,
    )
    back.begin(r_ref[0])

    def plain(j, carry):
        back.block(j, False)
        return carry

    def pair(j, carry):
        back.block(2 * j, False, 2)
        return carry

    def edge(j, carry):
        back.block(j, True)
        return carry

    def empty(j, carry):
        back.clear(j)
        return carry

    lax.fori_loop(0, whole // 2, pair, 0)
    lax.fori_loop(whole // 2 * 2, whole, plain, 0)
    lax.fori_loop(whole, end, edge, 0)
    lax.fori_loop(end, dkv_ref.shape[1] // rows, empty, 0)
    gain_total = back.end()

    @pl.when(pl.program_id(0) == 0)
    def _():
        dqgain_ref[...] = first_gain_ref[...] + gain_total

    @pl.when(pl.program_id(0) > 0)
    def _():
        dqgain_ref[...] = dqgain_ref[...] + gain_total


def attend_back(place, q, kv, r, wo, att, gate, inv, qraw, cosine, sine, qgain, group, first_gain, firsts):
    batch, rows, width = q.shape
    head_dim = qgain.shape[1]
    any_place = pl.BlockSpec(memory_space=pl.ANY)

    def later(array):
        return pl.BlockSpec((1,) + array.shape[1:], lambda b: (b + 1,) + (0,) * (len(array.shape) - 1))

    line = pl.BlockSpec((1, head_dim), lambda b: (0, 0))
    return pl.pallas_call(
        functools.partial(attend_back_kernel, group),
        grid=(batch - 1,),
        in_specs=[SCALARS, later(q), later(kv), later(r), full_block(wo)]
        + [later(x) for x in (att, gate, inv, qraw)]
        + [full_block(x) for x in (cosine, sine, qgain, first_gain)]
        + [any_place] * 3,
        out_specs=[later(x) for x in firsts] + [line],
        out_shape=[jax.ShapeDtypeStruct(x.shape, x.dtype) for x in firsts] + [shape_of(1, head_dim, F32)],
        scratch_shapes=heads_back_scratch(width // head_dim, rows, head_dim),
        input_output_aliases={13: 0, 14: 1, 15: 2},
        compiler_params=params(58),
        cost_estimate=takes(3),
        name="attend_back",
    )(place, q, kv, r, wo, att, gate, inv, qraw, cosine, sine, qgain, first_gain, *firsts)


class Line:
    def __init__(self, pieces, count, part_ref, own_ref, right_ref, left_ref, sems, spread=None):
        self.sums = part_ref is not None
        self.pieces, self.count = pieces, count
        self.place = lax.axis_index("head")
        self.part_ref, self.own_ref = part_ref, own_ref
        self.right_ref, self.left_ref = right_ref, left_ref
        self.sems = sems
        self.spread = spread

    def barrier(self, digits=()):
        sem = pltpu.get_barrier_semaphore()
        place, count = self.place, self.count
        for digit in digits:
            partner = flipped(lax.axis_index("seq"), digit)
            pl.semaphore_signal(sem, inc=1, device_id={"seq": partner}, device_id_type=MESH)

        @pl.when(place > 0)
        def _():
            pl.semaphore_signal(sem, inc=1, device_id={"head": place - 1}, device_id_type=MESH)

        @pl.when(place < count - 1)
        def _():
            pl.semaphore_signal(sem, inc=1, device_id={"head": place + 1}, device_id_type=MESH)

        inside = (place > 0) & (place < count - 1)

        @pl.when(inside)
        def _():
            pl.semaphore_wait(sem, 2 + len(digits))

        @pl.when(jnp.logical_not(inside))
        def _():
            pl.semaphore_wait(sem, 1 + len(digits))

    def barrier_all(self, digits):
        sem = pltpu.get_barrier_semaphore()
        for digit in digits:
            partner = flipped(lax.axis_index("seq"), digit)
            pl.semaphore_signal(sem, inc=1, device_id={"seq": partner}, device_id_type=MESH)
        for distance in range(1, self.count):
            other = lax.rem(self.place + distance, self.count)
            pl.semaphore_signal(sem, inc=1, device_id={"head": other}, device_id_type=MESH)
        pl.semaphore_wait(sem, self.count - 1 + len(digits))

    def copy(self, ref, send, receive, p, t, step):
        return pltpu.make_async_remote_copy(
            src_ref=ref,
            dst_ref=ref,
            send_sem=self.sems[send].at[p, t],
            recv_sem=self.sems[receive].at[p, t],
            device_id={"head": jnp.clip(self.place + step, 0, self.count - 1)},
            device_id_type=MESH,
        )

    def sum_copy(self, p, t, step):
        ref = self.right_ref if step > 0 else self.left_ref
        base = 0 if step > 0 else 2
        return self.copy(ref.at[p, t], base, base + 1, p, t, step)

    def spread_copy(self, p, t, step):
        first = 4 if self.sums else 0
        return self.copy(self.spread(p, t), first if step > 0 else first + 1, first + 2, p, t, step)

    def send_sums(self, p, distance):
        place, count = self.place, self.count
        for step, ref in ((1, self.right_ref), (-1, self.left_ref)):
            t = place + step * distance
            first = place == (0 if step > 0 else count - 1)

            @pl.when((t >= 0) & (t < count))
            def _(t=t, step=step, ref=ref, first=first):
                @pl.when(first)
                def _():
                    ref[p, t] = self.part_ref[t].astype(LOW)

                @pl.when(jnp.logical_not(first))
                def _():
                    self.sum_copy(p, t, step).wait_recv()
                    ref[p, t] = (ref[p, t].astype(F32) + self.part_ref[t].astype(F32)).astype(LOW)

                self.sum_copy(p, t, step).start()

    def keep_own(self, p):
        self.own_ref[p] = self.part_ref[self.place].astype(F32)

    def finish_own(self, p):
        place, count = self.place, self.count
        for step, ref, inner in ((1, self.right_ref, place > 0), (-1, self.left_ref, place < count - 1)):

            @pl.when(inner)
            def _(step=step, ref=ref):
                self.sum_copy(p, place, step).wait_recv()
                self.own_ref[p] = self.own_ref[p] + ref[p, place].astype(F32)

    def hand_out(self, p):
        place, count = self.place, self.count

        @pl.when(place < count - 1)
        def _():
            self.spread_copy(p, place, 1).start()

        @pl.when(place > 0)
        def _():
            self.spread_copy(p, place, -1).start()

    def hand_on(self, p, distance):
        place, count = self.place, self.count
        for step, more in ((1, place < count - 1), (-1, place > 0)):
            t = place - step * distance

            @pl.when((t >= 0) & (t < count))
            def _(t=t, step=step, more=more):
                self.spread_copy(p, t, step).wait_recv()

                @pl.when(more)
                def _():
                    self.spread_copy(p, t, step).start()

    def drain(self):
        place, count = self.place, self.count

        def one(p, carry):
            for t in range(count):
                if self.sums:

                    @pl.when(t > place)
                    def _(t=t):
                        self.sum_copy(p, t, 1).wait_send()

                    @pl.when(t < place)
                    def _(t=t):
                        self.sum_copy(p, t, -1).wait_send()

                if self.spread is not None:

                    @pl.when((t <= place) & (place < count - 1))
                    def _(t=t):
                        self.spread_copy(p, t, 1).wait_send()

                    @pl.when((t >= place) & (place > 0))
                    def _(t=t):
                        self.spread_copy(p, t, -1).wait_send()

            return carry

        lax.fori_loop(0, self.pieces, one, 0)


def line_scratch(pieces, count, rows, model, part_kind, spread):
    slots = (pieces, count)
    scratch = [
        pltpu.VMEM((pieces, rows, model), F32),
        pltpu.VMEM((pieces, count, rows, model), LOW),
        pltpu.VMEM((pieces, count, rows, model), LOW),
    ] + [pltpu.SemaphoreType.DMA(slots)] * (7 if spread else 4)
    if part_kind is not None:
        scratch = [pltpu.VMEM((count, rows, model), part_kind)] + scratch
    return scratch


def both_ways(index, limit, body):
    @pl.when((index >= 0) & (index < limit))
    def _():
        body(index)


def front_kernel(
    pieces, count, head_dim,
    tok_ref, gain_ref, cos_ref, sin_ref, qgain_ref, kgain_ref, wq_hbm, wk_hbm, wv_hbm, wg_hbm,
    normed_hbm, qraw_hbm, q_hbm, kraw_hbm, kv_hbm, gate_hbm,
    all_ref, normed_ref, qraw_ref, q_ref, kraw_ref, kv_ref, gate_ref, store_sem,
    wq_ref, wk_ref, wv_ref, wg_ref, load_sem, *sems,
):
    rows, model = tok_ref.shape[1], tok_ref.shape[2]
    tall = count * rows
    line = Line(pieces, count, None, None, None, None, sems, spread=lambda p, t: all_ref.at[p, t])
    weights = ((wq_hbm, wq_ref), (wk_hbm, wk_ref), (wv_hbm, wv_ref), (wg_hbm, wg_ref))
    loads = [pltpu.make_async_copy(*pair, load_sem.at[i]) for i, pair in enumerate(weights)]
    for load in loads:
        load.start()
    line.barrier()
    for p in range(pieces):
        all_ref[p, line.place] = tok_ref[p]

    def stores(p):
        pairs = (
            (normed_ref, normed_hbm), (qraw_ref, qraw_hbm), (q_ref, q_hbm), (kraw_ref, kraw_hbm), (kv_ref, kv_hbm),
            (gate_ref, gate_hbm),
        )
        return [
            pltpu.make_async_copy(source, target.at[p // 2, :, p % 2], store_sem.at[i])
            for i, (source, target) in enumerate(pairs)
        ]

    def project(p):
        half = p % 2

        @pl.when(p == 0)
        def _():
            for load in loads:
                load.wait()

        @pl.when(p > 0)
        def _():
            for store in stores(p - 1):
                store.wait()

        def keep(ref, value):
            ref[...] = value.astype(ref.dtype).reshape(count, rows, value.shape[-1])

        x = all_ref[p].reshape(tall, model).astype(F32)
        normed = (x * inverse_rms(x) * gain_ref[...]).astype(LOW)
        keep(normed_ref, normed)
        cosine = cos_ref[:, half].reshape(tall, head_dim)
        sine = sin_ref[:, half].reshape(tall, head_dim)

        def turned(raw, head_gain):
            parts = []
            for h in range(raw.shape[1] // head_dim):
                part = raw[:, h * head_dim : (h + 1) * head_dim]
                parts.append(turn(part * inverse_rms(part) * head_gain, cosine, sine).astype(LOW))
            return parts

        raw = mm(normed, wk_ref[...])
        keep(kraw_ref, raw)
        values = mm(normed, wv_ref[...]).astype(LOW)
        keep(kv_ref, jnp.concatenate(turned(raw, kgain_ref[...]) + [values], axis=1))
        raw = mm(normed, wq_ref[...])
        keep(qraw_ref, raw)
        keep(q_ref, jnp.concatenate(turned(raw, qgain_ref[...]), axis=1))
        keep(gate_ref, mm(normed, wg_ref[...]))
        for store in stores(p):
            store.start()

    def turn_once(k, carry):
        both_ways(k, pieces, line.hand_out)
        for distance in range(1, count):
            both_ways(k - 1, pieces, lambda p, d=distance: line.hand_on(p, d))
        both_ways(k - 1, pieces, project)
        return carry

    lax.fori_loop(0, pieces + 1, turn_once, 0)
    for store in stores(pieces - 1):
        store.wait()
    line.drain()


def front_step(tok, gain, cosine, sine, qgain, kgain, wq, wk, wv, wg, count):
    pieces, rows, model = tok.shape
    batch = pieces // 2
    head_dim = qgain.shape[1]
    nq, nk = wq.shape[1], wk.shape[1]

    def wide(columns, kind):
        return jax.ShapeDtypeStruct((batch, count, 2, rows, columns), kind)

    slots = (pieces, count)
    kinds = [(model, LOW), (nq, F32), (nq, LOW), (nk, F32), (2 * nk, LOW), (nq, F32)]
    return pl.pallas_call(
        functools.partial(front_kernel, pieces, count, head_dim),
        in_specs=[WHOLE] * 6 + [pl.BlockSpec(memory_space=pl.ANY)] * 4,
        out_specs=[pl.BlockSpec(memory_space=pl.ANY)] * 6,
        out_shape=[wide(*kind) for kind in kinds],
        scratch_shapes=[pltpu.VMEM((pieces, count, rows, model), LOW)]
        + [pltpu.VMEM((count, rows, columns), kind) for columns, kind in kinds]
        + [pltpu.SemaphoreType.DMA((6,))]
        + [pltpu.VMEM(x.shape, LOW) for x in (wq, wk, wv, wg)]
        + [pltpu.SemaphoreType.DMA((4,))]
        + [pltpu.SemaphoreType.DMA(slots)] * 3,
        compiler_params=params(58, collective_id=2, has_side_effects=True),
        cost_estimate=takes(95),
        name="front",
    )(
        tok, gain, cosine.reshape(count, 2, rows, head_dim), sine.reshape(count, 2, rows, head_dim),
        qgain, kgain, wq, wk, wv, wg,
    )


def middle_kernel(
    pieces, count,
    acted_ref, tok_ref, gain_ref, wo_ref, masked_hbm, wg_hbm, wl_hbm, wd_hbm,
    middle_ref, dgain_ref, normed_hbm, hidden_hbm, dg_hbm, dl_hbm, dn_hbm,
    mid_ref, wg_ref, wl_ref, wd_ref, masked_ref, normed_ref, hidden_ref, dg_ref, dl_ref, dn_ref, acc_ref,
    load_sem, masked_sem, store_sem,
    part_ref, own_ref, right_ref, left_ref, *sems,
):
    rows, model = own_ref.shape[1], own_ref.shape[2]
    tall = count * rows
    hidden = wg_ref.shape[1]
    line = Line(
        pieces, count, part_ref, own_ref, right_ref, left_ref, sems, spread=lambda p, t: mid_ref.at[p, t]
    )
    place = line.place
    loads = [
        pltpu.make_async_copy(source, target, load_sem.at[i])
        for i, (source, target) in enumerate(((wg_hbm, wg_ref), (wl_hbm, wl_ref), (wd_hbm, wd_ref)))
    ]
    line.barrier()
    for load in loads:
        load.start()
    dgain_ref[...] = jnp.zeros_like(dgain_ref)
    tiles = 3
    tile = hidden // tiles

    def masked_copy(p):
        return pltpu.make_async_copy(masked_hbm.at[:, p], masked_ref, masked_sem)

    def stores(p):
        pairs = (
            (normed_ref, normed_hbm), (hidden_ref, hidden_hbm), (dg_ref, dg_hbm), (dl_ref, dl_hbm),
            (dn_ref, dn_hbm),
        )
        return [
            pltpu.make_async_copy(source, target.at[:, p], store_sem.at[i])
            for i, (source, target) in enumerate(pairs)
        ]

    def begin(p):
        acted = acted_ref[p // 2, :, p % 2].reshape(tall, acted_ref.shape[-1])
        part_ref[...] = mm(acted, wo_ref[...]).reshape(count, rows, model)
        line.keep_own(p)

    def own(p):
        line.finish_own(p)
        middle = own_ref[p] + tok_ref[p].astype(F32)
        middle_ref[p] = middle
        mid_ref[p, place] = middle.astype(LOW)
        line.hand_out(p)

    def units_begin(p):
        line.hand_on(p, count - 1)

        @pl.when(p > 0)
        def _():
            for store in stores(p - 1):
                store.wait()

        x = mid_ref[p].reshape(tall, model).astype(F32)
        normed = (x * inverse_rms(x) * gain_ref[...]).astype(LOW)
        normed_ref[...] = normed.reshape(count, rows, model)
        masked_copy(p).wait()

        @pl.when(p == 0)
        def _():
            for load in loads:
                load.wait()

    def units_tile(i):
        span = slice(i * tile, (i + 1) * tile)
        normed = normed_ref[...].reshape(tall, model)
        gate = mm(normed, wg_ref[:, span])
        lift = mm(normed, wl_ref[:, span])
        grad = mm_t(masked_ref[...].reshape(tall, model), wd_ref[span, :])
        sigmoid = jax.nn.sigmoid(gate)
        silu = gate * sigmoid
        lift_grad = (grad * silu).astype(LOW)
        gate_grad = (grad * lift * (sigmoid + silu * (1.0 - sigmoid))).astype(LOW)
        hidden_ref[:, :, span] = (silu * lift).astype(LOW).reshape(count, rows, tile)
        dg_ref[:, :, span] = gate_grad.reshape(count, rows, tile)
        dl_ref[:, :, span] = lift_grad.reshape(count, rows, tile)
        part = mm_t(gate_grad, wg_ref[:, span]) + mm_t(lift_grad, wl_ref[:, span])
        if i == 0:
            acc_ref[...] = part
        else:
            acc_ref[...] = acc_ref[...] + part

    def units_end(p):
        total = acc_ref[...]
        dn_ref[...] = total.astype(LOW).reshape(count, rows, model)
        x = mid_ref[p].reshape(tall, model).astype(F32)
        dgain_ref[...] = dgain_ref[...] + jnp.sum(total * x * inverse_rms(x), axis=0, keepdims=True)
        for store in stores(p):
            store.start()

        @pl.when(p < pieces - 1)
        def _():
            masked_copy(p + 1).start()

    masked_copy(0).start()

    def turn_once(k, carry):
        both_ways(k, pieces, begin)
        for i in range(max(tiles, count - 1)):
            if i < count - 1:
                both_ways(k, pieces, lambda p, i=i: line.send_sums(p, count - 1 - i))
            if i == 0:
                both_ways(k - 1, pieces, own)
                both_ways(k - 2, pieces, units_begin)
            elif i < count - 1:
                both_ways(k - 1, pieces, lambda p, i=i: line.hand_on(p, i))
            if i < tiles:
                both_ways(k - 2, pieces, lambda p, i=i: units_tile(i))
        both_ways(k - 2, pieces, units_end)
        return carry

    lax.fori_loop(0, pieces + 2, turn_once, 0)
    for store in stores(pieces - 1):
        store.wait()
    line.drain()


def middle_step(acted, tok, gain, wo, masked, wg, wl, wd, count):
    pieces, rows, model = tok.shape
    hidden = wg.shape[1]
    any_place = pl.BlockSpec(memory_space=pl.ANY)

    def wide(columns, kind=LOW):
        return jax.ShapeDtypeStruct((count, pieces, rows, columns), kind)

    def room(columns, kind=LOW):
        return pltpu.VMEM((count, rows, columns), kind)

    return pl.pallas_call(
        functools.partial(middle_kernel, pieces, count),
        in_specs=[WHOLE] * 4 + [any_place] * 4,
        out_specs=[WHOLE] * 2 + [any_place] * 5,
        out_shape=[
            jax.ShapeDtypeStruct((pieces, rows, model), F32), shape_of(1, model, F32),
            wide(model), wide(hidden), wide(hidden), wide(hidden), wide(model),
        ],
        scratch_shapes=[
            pltpu.VMEM((pieces, count, rows, model), LOW),
            pltpu.VMEM(wg.shape, LOW), pltpu.VMEM(wl.shape, LOW), pltpu.VMEM(wd.shape, LOW),
            room(model), room(model), room(hidden), room(hidden), room(hidden), room(model),
            pltpu.VMEM((count * rows, model), F32),
            pltpu.SemaphoreType.DMA((3,)), pltpu.SemaphoreType.DMA, pltpu.SemaphoreType.DMA((5,)),
        ]
        + line_scratch(pieces, count, rows, model, F32, True),
        compiler_params=params(58, collective_id=0, has_side_effects=True),
        cost_estimate=takes(128),
        name="middle",
    )(acted, tok, gain, wo, masked, wg, wl, wd)


def flipped(place, mask):
    bit = 1
    while bit <= mask:
        if mask & bit:
            place = place + (1 - 2 * (place // bit % 2)) * bit
        bit *= 2
    return place


def digit_orders(count, batch):
    upper = [1 << i for i in range(1, count.bit_length() - 1)]
    return [(upper if b % 2 == 0 else upper[::-1]) + [1] for b in range(batch)]


def greet(place, digits):
    sem = pltpu.get_barrier_semaphore()
    for digit in digits:
        pl.semaphore_signal(sem, inc=1, device_id={"seq": flipped(place, digit)}, device_id_type=MESH)
    pl.semaphore_wait(sem, len(digits))


def block_gathers(count, batch, out, sources, send_sem, receive_sem):
    place = lax.axis_index("seq")
    orders = digit_orders(count, batch)
    steps = len(orders[0])
    started = []

    def copy(b, mask, step):
        digit = orders[b][step]
        block = out(b).at[flipped(place, mask)]
        return pltpu.make_async_remote_copy(
            src_ref=sources(b) if mask == 0 else block,
            dst_ref=block,
            send_sem=send_sem.at[b, step, mask],
            recv_sem=receive_sem.at[b, mask | digit],
            device_id={"seq": flipped(place, digit)},
            device_id_type=MESH,
        )

    def pass_on(b, mask, first):
        for step in range(first, steps):
            one = copy(b, mask, step)
            one.start()
            started.append(one)

    def arrive(b, mask, level):
        block = out(b).at[flipped(place, mask)]
        pltpu.make_async_remote_copy(
            src_ref=block,
            dst_ref=block,
            send_sem=send_sem.at[b, 0, mask],
            recv_sem=receive_sem.at[b, mask],
            device_id={"seq": flipped(place, orders[b][level])},
            device_id_type=MESH,
        ).wait_recv()
        pass_on(b, mask, level + 1)

    begins = [functools.partial(pass_on, b, 0, 0) for b in range(batch)]
    arrivals = []
    for level in range(steps):
        for turn in range(1 << level):
            for b in range(batch):
                mask = orders[b][level]
                for i in range(level):
                    if turn >> i & 1:
                        mask |= orders[b][i]
                arrivals.append((1.0 if level == steps - 1 else 4.0, functools.partial(arrive, b, mask, level)))

    def drain():
        for one in started:
            one.wait_send()

    return begins, arrivals, drain


def gather_kernel(count, batch, own_ref, out_ref, local_sem, send_sem, receive_sem):
    place = lax.axis_index("seq")
    greet(place, digit_orders(count, 1)[0])
    local = [
        pltpu.make_async_copy(own_ref.at[b], out_ref.at[b, place], local_sem.at[b]) for b in range(batch)
    ]
    for copy in local:
        copy.start()
    begins, arrivals, drain = block_gathers(
        count, batch, lambda b: out_ref.at[b], lambda b: own_ref.at[b], send_sem, receive_sem
    )
    for begin in begins:
        begin()
    for _, event in arrivals:
        event()
    drain()
    for copy in local:
        copy.wait()


def gather_blocks(own):
    batch, rows, columns = own.shape
    count = lax.axis_size("seq")
    steps = count.bit_length() - 1
    any_place = pl.BlockSpec(memory_space=pl.ANY)
    out = pl.pallas_call(
        functools.partial(gather_kernel, count, batch),
        in_specs=[any_place],
        out_specs=any_place,
        out_shape=jax.ShapeDtypeStruct((batch, count, rows, columns), LOW),
        scratch_shapes=[
            pltpu.SemaphoreType.DMA((batch,)),
            pltpu.SemaphoreType.DMA((batch, steps, count)),
            pltpu.SemaphoreType.DMA((batch, count)),
        ],
        compiler_params=params(58, collective_id=3, has_side_effects=True),
        cost_estimate=takes(41),
        name="gather_blocks",
    )(own)
    return out.reshape(batch, count * rows, columns)


def block_sums(count, batch, parts, finish, slots, send_sem, receive_sem, kept_ref, kept_sem, near):
    place = lax.axis_index("seq")
    orders = [order[::-1] for order in digit_orders(count, batch)]
    steps = len(orders[0])

    def masks_at(b, step):
        found = [0]
        for digit in orders[b][step + 1 :][::-1]:
            found = [mask | digit for mask in found] + found
        return found

    numbers = {}
    for b in range(batch):
        place_in = 0
        for step in range(steps):
            for mask in masks_at(b, step):
                numbers[b, step, mask] = place_in
                place_in += 1

    def slot(b, step, mask):
        return slots.at[b, numbers[b, step, mask]]

    def transfer(b, step, mask):
        digit = orders[b][step]
        number = numbers[b, step, mask]
        if step == 0:
            source = parts(b).at[flipped(place, mask | digit)]
        else:
            source = slot(b, step - 1, mask | digit)
        return pltpu.make_async_remote_copy(
            src_ref=source,
            dst_ref=slots.at[b, number],
            send_sem=send_sem.at[b, number],
            recv_sem=receive_sem.at[b, number],
            device_id={"seq": flipped(place, digit)},
            device_id_type=MESH,
        )

    started = []

    def kept(b, turn):
        mask = masks_at(b, 0)[turn]
        return pltpu.make_async_copy(
            parts(b).at[flipped(place, mask)], kept_ref.at[b, turn], kept_sem.at[b, turn]
        )

    def begin():
        for turn in range(count // 2):
            for b in range(batch):
                copy = transfer(b, 0, masks_at(b, 0)[turn])
                copy.start()
                started.append(copy)
        for turn in range(count // 2):
            for b in range(batch):
                kept(b, turn).start()

    def take(b, step, mask):
        transfer(b, step, mask).wait_recv()
        if step == 0:
            turn = masks_at(b, 0).index(mask)
            kept(b, turn).wait()
            held = kept_ref.at[b, turn]
        else:
            held = slot(b, step - 1, mask)
        total = held[...].astype(F32) + slot(b, step, mask)[...].astype(F32)
        if step == steps - 1:
            finish(b, total)
        else:
            slot(b, step, mask)[...] = total.astype(LOW)
            if mask & orders[b][step + 1]:
                copy = transfer(b, step + 1, mask & ~orders[b][step + 1])
                copy.start()
                started.append(copy)

    events = []
    for step in range(steps):
        for turn in range(len(masks_at(0, step))):
            for b in range(batch):
                events.append((near if step == 0 else 4.0, functools.partial(take, b, step, masks_at(b, step)[turn])))

    def drain():
        for copy in started:
            copy.wait_send()

    return begin, events, drain


def interleaved(*lists):
    spent = [0.0] * len(lists)
    whole = [sum(time for time, _ in calls) for calls in lists]
    taken = [0] * len(lists)
    while any(taken[i] < len(calls) for i, calls in enumerate(lists)):
        i = min((i for i, calls in enumerate(lists) if taken[i] < len(calls)), key=lambda i: spent[i])
        time, call = lists[i][taken[i]]
        call()
        spent[i] += time / whole[i]
        taken[i] += 1

def residual_kernel(
    pieces, count, halves, group, seq_count,
    place_ref, masked_ref, gain_ref, cos_ref, sin_ref, qgain_ref,
    dn_hbm, middle_hbm, wo_hbm, q_hbm, kv_hbm, att_hbm, gate_hbm, inv_hbm, qraw_hbm,
    residual_ref, r_ref, dqgain_ref, dq_hbm, dkv_hbm, dgate_hbm,
    q_ref, kv_ref, att_ref, gate_ref, inv_ref, qraw_ref, dq_ref, dkv_ref, dgate_ref,
    scaled_ref, corr_ref, acc_ref, load_sem, store_sem, block_sem,
    dn_ref, middle_ref, wo_ref, dn_sem, middle_sem, wo_sem,
    part_ref, own_ref, right_ref, left_ref, *sems,
):
    rows, model = own_ref.shape[1], own_ref.shape[2]
    query_rows = q_ref.shape[0]
    line = Line(
        pieces, count, part_ref, own_ref, right_ref, left_ref, sems,
        spread=lambda p, t: r_ref.at[p // halves, t, p % halves],
    )
    pairs = (
        (q_hbm, q_ref), (kv_hbm, kv_ref), (att_hbm, att_ref), (gate_hbm, gate_ref), (inv_hbm, inv_ref),
        (qraw_hbm, qraw_ref),
    )
    loads = [
        pltpu.make_async_copy(source.at[0], target, load_sem.at[i]) for i, (source, target) in enumerate(pairs)
    ]
    stores = [
        pltpu.make_async_copy(dq_ref, dq_hbm.at[0], store_sem.at[0]),
        pltpu.make_async_copy(dgate_ref, dgate_hbm.at[0], store_sem.at[1]),
    ]
    dn_loads = [pltpu.make_async_copy(dn_hbm.at[:, p], dn_ref.at[:, p], dn_sem.at[p]) for p in range(pieces)]
    middle_load = pltpu.make_async_copy(middle_hbm, middle_ref, middle_sem)
    loads.append(pltpu.make_async_copy(wo_hbm, wo_ref, wo_sem))
    for load in dn_loads + [middle_load]:
        load.start()
    line.barrier()
    for load in loads:
        load.start()
    block_index = lax.axis_index("seq")
    back = HeadsBack(
        group, block_index * query_rows, place_ref[1], q_ref, kv_ref, wo_ref, att_ref, gate_ref, inv_ref, qraw_ref,
        cos_ref, sin_ref, qgain_ref, dq_ref, dkv_ref, dgate_ref, scaled_ref, corr_ref, acc_ref,
    )

    def begin(p):
        dn_loads[p].wait()
        part_ref[...] = dn_ref[:, p]
        line.keep_own(p)

    def own(p):
        if p == 0:
            middle_load.wait()
        line.finish_own(p)
        x = middle_ref[p].astype(LOW).astype(F32)
        residual = masked_ref[p].astype(F32) + norm_back(own_ref[p], x, gain_ref[...])
        residual_ref[p] = residual
        r_ref[p // halves, line.place, p % halves] = residual.astype(LOW)
        line.hand_out(p)

    def block_store(j):
        span = pl.ds(j * query_rows, query_rows)
        return pltpu.make_async_copy(dkv_ref.at[span, :], dkv_hbm.at[0, span, :], block_sem.at[j])

    def heads_begin():
        for load in loads:
            load.wait()
        back.begin(r_ref[0].reshape(query_rows, model))

    def heads_block(j):
        @pl.when(j <= block_index)
        def _():
            back.block(j, True)

        @pl.when(j > block_index)
        def _():
            back.clear(j)

        block_store(j).start()

    def heads_end():
        dqgain_ref[...] = back.end()
        for store in stores:
            store.start()

    steps = []
    for k in range(pieces + 1):
        for i in range(count - 1):
            if i == 0 and k < pieces:
                steps.append((1.0, functools.partial(begin, k)))
            if k < pieces:
                steps.append((8.0, functools.partial(line.send_sums, k, count - 1 - i)))
            if i == 0 and k > 0:
                steps.append((1.0, functools.partial(own, k - 1)))
            elif k > 0:
                steps.append((1.0 if k < pieces else 6.0, functools.partial(line.hand_on, k - 1, i)))
        if k > 0:
            steps.append((1.0 if k < pieces else 6.0, functools.partial(line.hand_on, k - 1, count - 1)))
        if k == halves:
            ready = len(steps)
    heads = [(3.0, heads_begin)]
    heads += [(3.0, functools.partial(heads_block, j)) for j in range(seq_count)]
    heads += [(2.0, heads_end)]
    heads += [(5.0, lambda: None)]
    for _, call in steps[:ready]:
        call()
    interleaved(steps[ready:], heads)
    for j in range(seq_count):
        block_store(j).wait()
    for store in stores:
        store.wait()
    line.drain()


def residual_step(dn, middle, masked, gain, place, wo, cosine, sine, qgain, q, kv, att, gate, inv, qraw, group):
    count, pieces, rows, model = dn.shape
    batch, query_rows, width = q.shape
    halves = pieces // batch
    head_dim = qgain.shape[1]
    seq_count = lax.axis_size("seq")
    any_place = pl.BlockSpec(memory_space=pl.ANY)
    held = (q, kv, att, gate, inv, qraw)
    return pl.pallas_call(
        functools.partial(residual_kernel, pieces, count, halves, group, seq_count),
        in_specs=[SCALARS] + [WHOLE] * 5 + [any_place] * 9,
        out_specs=[WHOLE] * 3 + [any_place] * 3,
        out_shape=[
            jax.ShapeDtypeStruct((pieces, rows, model), F32),
            jax.ShapeDtypeStruct((batch, count, halves, rows, model), LOW),
            shape_of(1, head_dim, F32),
            jax.ShapeDtypeStruct(q.shape, LOW),
            jax.ShapeDtypeStruct(kv.shape, LOW),
            jax.ShapeDtypeStruct(q.shape, LOW),
        ],
        scratch_shapes=[pltpu.VMEM(x.shape[1:], x.dtype) for x in held]
        + [pltpu.VMEM(q.shape[1:], LOW), pltpu.VMEM(kv.shape[1:], LOW), pltpu.VMEM(q.shape[1:], LOW)]
        + heads_back_scratch(width // head_dim, query_rows, head_dim)
        + [
            pltpu.SemaphoreType.DMA((6,)),
            pltpu.SemaphoreType.DMA((2,)),
            pltpu.SemaphoreType.DMA((seq_count,)),
        ]
        + [pltpu.VMEM(x.shape, x.dtype) for x in (dn, middle, wo)]
        + [pltpu.SemaphoreType.DMA((pieces,)), pltpu.SemaphoreType.DMA, pltpu.SemaphoreType.DMA]
        + line_scratch(pieces, count, rows, model, LOW, True),
        compiler_params=params(60, collective_id=1, has_side_effects=True),
        cost_estimate=takes(10),
        name="residual",
    )(place, masked, gain, cosine, sine, qgain, dn, middle, wo, *held)


def scatter_kernel(
    pieces, count, seq_count, batch, head_dim,
    parts_ref, hidden_hbm, wd_hbm, middle_hbm, valid_ref, kraw_ref, cos_ref, sin_ref, kgain_ref,
    dkv_ref, output_ref, dkgain_ref,
    wd_ref, middle_ref, hidden_ref, load_sem, middle_sem, hidden_sem, kept_ref, kept_sem, slots, send_sem, receive_sem,
    part_ref, own_ref, right_ref, left_ref, *sems,
):
    rows, model = own_ref.shape[1], own_ref.shape[2]
    tall = count * rows
    keys = kraw_ref.shape[2]
    line = Line(pieces, count, part_ref, own_ref, right_ref, left_ref, sems)
    load = pltpu.make_async_copy(wd_hbm, wd_ref, load_sem)

    def hidden_copy(p):
        return pltpu.make_async_copy(hidden_hbm.at[:, p], hidden_ref.at[p % 2], hidden_sem.at[p % 2])

    middle_load = pltpu.make_async_copy(middle_hbm, middle_ref, middle_sem)
    load.start()
    hidden_copy(0).start()
    middle_load.start()
    dkgain_ref[...] = jnp.zeros_like(dkgain_ref)
    line.barrier(digit_orders(seq_count, 1)[0])

    def finish(b, total):
        for h in range(keys // head_dim):
            columns = slice(h * head_dim, (h + 1) * head_dim)
            grad, gain_grad = norm_turn_back(
                total[:, columns], kraw_ref[b, :, columns], kgain_ref[...], cos_ref[...], sin_ref[...]
            )
            dkv_ref[b, :, columns] = grad.astype(LOW)
            dkgain_ref[...] = dkgain_ref[...] + gain_grad
        dkv_ref[b, :, keys:] = total[:, keys:].astype(LOW)

    first, events, drain = block_sums(
        seq_count, batch, lambda b: parts_ref.at[b], finish, slots, send_sem, receive_sem, kept_ref, kept_sem, 4.0
    )

    def begin(p):
        if p == 0:
            load.wait()
        if p + 1 < pieces:
            hidden_copy(p + 1).start()
        hidden_copy(p).wait()
        hidden = hidden_ref[p % 2].reshape(tall, hidden_ref.shape[-1])
        part_ref[...] = mm(hidden, wd_ref[...]).reshape(count, rows, model)
        line.keep_own(p)

    def own(p):
        if p == 0:
            middle_load.wait()
        line.finish_own(p)
        output_ref[p] = (valid_ref[p] * (middle_ref[p] + own_ref[p])).astype(LOW)

    first()
    interleaved(line_steps(line, begin, own), events)
    drain()
    line.drain()


def line_steps(line, begin, own):
    steps = []
    for k in range(line.pieces + 1):
        for i in range(line.count - 1):
            if i == 0 and k < line.pieces:
                steps.append((1.0, functools.partial(begin, k)))
            if k < line.pieces:
                steps.append((8.0, functools.partial(line.send_sums, k, line.count - 1 - i)))
            if i == 0 and k > 0:
                steps.append((1.0, functools.partial(own, k - 1)))
    return steps


def scatter_blocks(parts, hidden, wd, middle, valid, kraw, cosine, sine, kgain):
    seq_count, batch = lax.axis_size("seq"), parts.shape[0]
    rows, columns = parts.shape[1] // seq_count, parts.shape[2]
    count, pieces, piece_rows, units = hidden.shape
    model, head_dim = wd.shape[1], kgain.shape[1]
    any_place = pl.BlockSpec(memory_space=pl.ANY)
    return pl.pallas_call(
        functools.partial(scatter_kernel, pieces, count, seq_count, batch, head_dim),
        in_specs=[any_place] * 4 + [WHOLE] * 5,
        out_specs=[WHOLE] * 3,
        out_shape=[
            jax.ShapeDtypeStruct((batch, rows, columns), LOW),
            jax.ShapeDtypeStruct((pieces, piece_rows, model), LOW),
            shape_of(1, head_dim, F32),
        ],
        scratch_shapes=[
            pltpu.VMEM(wd.shape, LOW),
            pltpu.VMEM(middle.shape, F32),
            pltpu.VMEM((2, count, piece_rows, units), LOW),
            pltpu.SemaphoreType.DMA,
            pltpu.SemaphoreType.DMA,
            pltpu.SemaphoreType.DMA((2,)),
            pltpu.VMEM((batch, seq_count // 2, rows, columns), LOW),
            pltpu.SemaphoreType.DMA((batch, seq_count // 2)),
            pltpu.VMEM((batch, seq_count - 1, rows, columns), LOW),
            pltpu.SemaphoreType.DMA((batch, seq_count - 1)),
            pltpu.SemaphoreType.DMA((batch, seq_count - 1)),
        ]
        + line_scratch(pieces, count, piece_rows, model, F32, False),
        compiler_params=params(58, collective_id=4, has_side_effects=True),
        cost_estimate=takes(10),
        name="scatter_blocks",
    )(
        parts.reshape(batch, seq_count, rows, columns), hidden, wd, middle, valid, kraw, cosine, sine, kgain
    )


def last_kernel(
    pieces, count, seq_count, streams, halves,
    dq_ref, dkv_ref, dgate_ref, gain_ref, dmid_ref, dqgain_ref, dkgain_ref,
    wq_hbm, wk_hbm, wv_hbm, wg_hbm, tok_hbm, residual_hbm, *refs,
):
    grads, refs = refs[:streams], refs[streams:]
    input_ref, total_ref, sums = refs[0], refs[1], refs[2 : 2 + streams]
    (
        wq_ref, wk_ref, wv_ref, wg_ref, tok_ref, residual_ref, load_sem, kept_ref, kept_sem,
        slots, scatter_send, scatter_receive, gather_send, gather_receive, mine_ref, mine_sem,
        dgain_ref, turns_ref, round_ref, mixed_ref, round_send, round_receive, mixed_send, mixed_receive,
        part_ref, own_ref, right_ref, left_ref, *sems,
    ) = refs[2 + streams :]
    rows, model = own_ref.shape[1], own_ref.shape[2]
    tall = count * rows
    place_seq = lax.axis_index("seq")
    digits = digit_orders(seq_count, 1)[0]
    line = Line(pieces, count, part_ref, own_ref, right_ref, left_ref, sems)
    pairs = (
        (wq_hbm, wq_ref), (wg_hbm, wg_ref), (wk_hbm, wk_ref), (wv_hbm, wv_ref), (tok_hbm, tok_ref),
        (residual_hbm, residual_ref),
    )
    loads = [pltpu.make_async_copy(*pair, load_sem.at[i]) for i, pair in enumerate(pairs)]
    for load in loads:
        load.start()
    line.barrier_all(digits)
    dgain_ref[...] = jnp.zeros_like(dgain_ref)

    begins, arrivals, gather_drain = block_gathers(
        seq_count, streams, lambda b: sums[b], lambda b: mine_ref.at[b], gather_send, gather_receive
    )

    def keep(b):
        return pltpu.make_async_copy(mine_ref.at[b], sums[b].at[place_seq], mine_sem.at[b])

    def finish(b, total):
        mine_ref[b] = total.astype(LOW)
        begins[b]()
        keep(b).start()

    first, events, scatter_drain = block_sums(
        seq_count, streams, lambda b: grads[b], finish, slots, scatter_send, scatter_receive, kept_ref, kept_sem, 1.0
    )

    def begin(p):
        if p == 0:
            for load in loads[:4]:
                load.wait()
        b, half = p // halves, p % halves
        dq = dq_ref[b, :, half].reshape(tall, dq_ref.shape[-1])
        dkv = dkv_ref[b, :, half].reshape(tall, dkv_ref.shape[-1])
        dgate = dgate_ref[b, :, half].reshape(tall, dgate_ref.shape[-1])
        nk = dkv.shape[1] // 2
        total = mm_t(dq, wq_ref[...]) + mm_t(dgate, wg_ref[...])
        total = total + mm_t(dkv[:, :nk], wk_ref[...]) + mm_t(dkv[:, nk:], wv_ref[...])
        part_ref[...] = total.reshape(count, rows, model)
        line.keep_own(p)

    def own(p):
        if p == 0:
            for load in loads[4:]:
                load.wait()
        line.finish_own(p)
        x = tok_ref[p].astype(F32)
        grad = own_ref[p]
        inverse = inverse_rms(x)
        dgain_ref[...] = dgain_ref[...] + jnp.sum(grad * x * inverse, axis=0, keepdims=True)
        input_ref[p] = residual_ref[p] + norm_back(grad, x, gain_ref[...])

    width = model // count
    lines = width // 128
    rounds = [
        pltpu.make_async_remote_copy(
            src_ref=turns_ref.at[i],
            dst_ref=round_ref.at[i],
            send_sem=round_send.at[i],
            recv_sem=round_receive.at[i],
            device_id={"seq": flipped(place_seq, digit)},
            device_id_type=MESH,
        )
        for i, digit in enumerate(digits)
    ]
    done = len(digits)
    shares = []
    for distance in range(1, count):
        other = lax.rem(line.place + distance, count)
        shares.append(
            pltpu.make_async_remote_copy(
                src_ref=turns_ref.at[done, other],
                dst_ref=mixed_ref.at[distance - 1],
                send_sem=mixed_send.at[distance - 1],
                recv_sem=mixed_receive.at[distance - 1],
                device_id={"head": other},
                device_id_type=MESH,
            )
        )

    def pack():
        turns_ref[0] = jnp.zeros(turns_ref.shape[1:], F32)
        for t in range(count):
            for i in range(lines):
                span = slice(t * width + i * 128, t * width + (i + 1) * 128)
                turns_ref[0, t, i : i + 1, :] = dgain_ref[:, span]
                turns_ref[0, t, lines + i : lines + i + 1, :] = dmid_ref[:, span]
            turns_ref[0, t, 2 * lines : 2 * lines + 1, :] = dqgain_ref[...]
            turns_ref[0, t, 2 * lines + 1 : 2 * lines + 2, :] = dkgain_ref[...]
        rounds[0].start()

    def one_round(i):
        rounds[i].wait_recv()
        turns_ref[i + 1] = turns_ref[i] + round_ref[i]
        for copy in rounds[i + 1 : i + 2] if i + 1 < done else shares:
            copy.start()

    def total():
        found = turns_ref[done, line.place]
        for i, copy in enumerate(shares):
            copy.wait_recv()
            found = found + mixed_ref[i]
        total_ref[...] = found

    steps = line_steps(line, begin, own) + [(1.0, pack)]
    steps += [(4.0, functools.partial(one_round, i)) for i in range(done)] + [(4.0, total)]
    first()
    interleaved(steps, events + arrivals)
    for copy in rounds + shares:
        copy.wait_send()
    for b in range(streams):
        keep(b).wait()
    scatter_drain()
    gather_drain()
    line.drain()


def last_step(dq, dkv, dgate, wq, wk, wv, wg, tok, residual, gain, dmid, dqgain, dkgain, grads):
    batch, count, halves, rows, nq = dq.shape
    pieces, model = batch * halves, wq.shape[0]
    seq_count, streams = lax.axis_size("seq"), len(grads)
    tall, columns = grads[0].shape
    block = tall // seq_count
    steps = seq_count.bit_length() - 1
    lines = 8 * ((2 * (model // count // 128) + 2 + 7) // 8)
    return pl.pallas_call(
        functools.partial(last_kernel, pieces, count, seq_count, streams, halves),
        in_specs=[WHOLE] * 7 + [pl.BlockSpec(memory_space=pl.ANY)] * (6 + streams),
        out_specs=[WHOLE] * 2 + [pl.BlockSpec(memory_space=pl.ANY)] * streams,
        out_shape=[jax.ShapeDtypeStruct((pieces, rows, model), F32), shape_of(lines, 128, F32)]
        + [jax.ShapeDtypeStruct((seq_count, block, columns), LOW)] * streams,
        scratch_shapes=[pltpu.VMEM(x.shape, x.dtype) for x in (wq, wk, wv, wg, tok, residual)]
        + [
            pltpu.SemaphoreType.DMA((6,)),
            pltpu.VMEM((streams, seq_count // 2, block, columns), LOW),
            pltpu.SemaphoreType.DMA((streams, seq_count // 2)),
            pltpu.VMEM((streams, seq_count - 1, block, columns), LOW),
            pltpu.SemaphoreType.DMA((streams, seq_count - 1)),
            pltpu.SemaphoreType.DMA((streams, seq_count - 1)),
            pltpu.SemaphoreType.DMA((streams, steps, seq_count)),
            pltpu.SemaphoreType.DMA((streams, seq_count)),
            pltpu.VMEM((streams, block, columns), LOW),
            pltpu.SemaphoreType.DMA((streams,)),
            pltpu.VMEM((1, model), F32),
            pltpu.VMEM((steps + 1, count, lines, 128), F32),
            pltpu.VMEM((steps, count, lines, 128), F32),
            pltpu.VMEM((count - 1, lines, 128), F32),
            pltpu.SemaphoreType.DMA((steps,)),
            pltpu.SemaphoreType.DMA((steps,)),
            pltpu.SemaphoreType.DMA((count - 1,)),
            pltpu.SemaphoreType.DMA((count - 1,)),
        ]
        + line_scratch(pieces, count, rows, model, F32, False),
        compiler_params=params(60, collective_id=5, has_side_effects=True),
        cost_estimate=takes(5),
        name="last",
    )(
        dq, dkv, dgate, gain, dmid, dqgain, dkgain, wq, wk, wv, wg, tok, residual,
        *[grad.reshape(seq_count, block, columns) for grad in grads],
    )


def widen_kernel(input_ref, output_ref, dq_ref, dkv_ref, dgate_ref, out_ref, *refs):
    ff_refs, refs = refs[:3], refs[3:]
    input_out, output_out, dq_out, dk_out, dv_out, dgate_out, out_out, *ff_outs = refs
    keys = dk_out.shape[1]
    input_out[...] = jnp.stack([input_ref[b] for b in range(input_ref.shape[0])], axis=1)
    output_out[...] = jnp.stack([output_ref[b].astype(F32) for b in range(input_ref.shape[0])], axis=1).astype(LOW)
    dq_out[...] = dq_ref[...].astype(F32)
    dk_out[...] = dkv_ref[:, :keys].astype(F32)
    dv_out[...] = dkv_ref[:, keys:].astype(F32)
    dgate_out[...] = dgate_ref[...].astype(F32)
    out_out[...] = out_ref[...].astype(F32).T
    for ref, out in zip(ff_refs, ff_outs):
        out[...] = ref[...].astype(F32)


def widen(input_grad, output, dq, dkv, dgate, out, ff, steps=4):
    batch, rows, model = input_grad.shape
    columns, keys = dq.shape[1], dkv.shape[1] // 2

    def tall(array):
        return pl.BlockSpec((array.shape[0] // steps, array.shape[1]), lambda i: (i, 0))

    def wide(array):
        return jax.ShapeDtypeStruct(array.shape, F32)

    outs = [
        jax.ShapeDtypeStruct((rows, batch, model), F32), jax.ShapeDtypeStruct((rows, batch, model), LOW),
        wide(dq), shape_of(model, keys, F32), shape_of(model, keys, F32), wide(dgate), shape_of(columns, model, F32),
    ] + [wide(x) for x in ff]
    specs = [pl.BlockSpec((rows // steps, batch, model), lambda i: (i, 0, 0))] * 2
    specs += [tall(x) for x in outs[2:6]]
    specs += [pl.BlockSpec((columns, model // steps), lambda i: (0, i))]
    specs += [tall(x) for x in ff]
    return pl.pallas_call(
        widen_kernel,
        grid=(steps,),
        in_specs=[pl.BlockSpec((batch, rows // steps, model), lambda i: (0, i, 0))] * 2
        + [tall(x) for x in (dq, dkv, dgate, out, *ff)],
        out_specs=specs,
        out_shape=outs,
        compiler_params=params(58),
        cost_estimate=takes(25),
        name="widen",
    )(input_grad, output, dq, dkv, dgate, out, *ff)


def turn_tables(positions, head_dim):
    half_dim = head_dim // 2
    lane = jnp.arange(head_dim, dtype=jnp.int32)
    inverse = THETA ** (-((lane % half_dim).astype(F32) * 2.0) / head_dim)
    angles = positions.astype(F32)[:, None] * inverse[None, :]
    return jnp.cos(angles), jnp.where(lane < half_dim, -1.0, 1.0)[None, :] * jnp.sin(angles)


def norm_back(grad, values, gain):
    inverse = inverse_rms(values)
    grad = grad * gain
    mean = jnp.mean(grad * values, axis=-1, keepdims=True)
    return inverse * (grad - values * (inverse * inverse * mean))


def gather(value, axis):
    return lax.all_gather(value, axis, axis=0, tiled=True)


def on_device(
    tokens, cotangent, lengths,
    query_weight, key_weight, value_weight, gating_weight, output_weight,
    swiglu_gate, swiglu_lift, swiglu_down,
    input_gain, middle_gain, query_gain, key_gain,
):
    block_index = lax.axis_index("seq")
    part_index = lax.axis_index("head")
    parts = lax.axis_size("head")
    local_rows, batch, model = tokens.shape
    head_dim = query_gain.shape[0]
    block_rows = local_rows * parts
    flat_rows = block_rows * batch
    group = query_weight.shape[1] // key_weight.shape[1]
    nq, nk = query_weight.shape[1], key_weight.shape[1]
    halves = 2
    pieces, rows = batch * halves, local_rows // halves

    query_start = block_index * block_rows
    positions = query_start + jnp.arange(block_rows, dtype=jnp.int32)
    cosine, sine = lax.optimization_barrier(turn_tables(positions, head_dim))
    gain_in, gain_mid = input_gain[None, :], middle_gain[None, :]
    gain_q, gain_k = query_gain[None, :], key_gain[None, :]
    local_pos = query_start + part_index * local_rows + jnp.arange(local_rows, dtype=jnp.int32)
    place = jnp.concatenate([query_start[None], lengths]).astype(jnp.int32)
    valid = (local_pos[None, :] < lengths[:, None]).astype(F32)[..., None]
    tok = jnp.transpose(tokens, (1, 0, 2)).reshape(pieces, rows, model)

    normed, qraw, q, kraw, kv_own, gate = [
        x.reshape(batch, block_rows, x.shape[-1])
        for x in front_step(
            tok, gain_in, cosine, sine, gain_q, gain_k,
            query_weight, key_weight, value_weight, gating_weight, parts,
        )
    ]
    masked_own = (valid * jnp.transpose(cotangent, (1, 0, 2)).astype(F32)).astype(LOW)
    kv_own, masked_own = lax.optimization_barrier((kv_own, masked_own))
    kv = gather_blocks(kv_own)
    masked = gather(masked_own.reshape(batch * local_rows, model), "head")
    att, acted, inv = attend(place, q, kv, gate, group, head_dim)
    middle, dgain_mid, normed_mid, hidden, dg, dl, dn_mid = middle_step(
        acted.reshape(batch, parts, halves, rows, nq), tok, gain_mid, output_weight,
        masked.reshape(parts, pieces, rows, model), swiglu_gate, swiglu_lift, swiglu_down, parts,
    )

    def flat(array):
        return array.reshape(flat_rows, array.shape[-1])

    normed_mid = flat(normed_mid)
    ff_grads = (
        t_mm(normed_mid, flat(dg)).astype(LOW),
        t_mm(normed_mid, flat(dl)).astype(LOW),
        t_mm(flat(hidden), masked).astype(LOW),
    )
    dn_mid, ff_grads = lax.optimization_barrier((dn_mid, ff_grads))
    ff_grads = lax.psum(ff_grads, "seq")
    residual, r, dgain_q, *firsts = residual_step(
        dn_mid, middle, masked_own.reshape(pieces, rows, model), gain_mid,
        place, output_weight, cosine, sine, gain_q, q, kv, att, gate, inv, qraw, group,
    )
    r = r.reshape(batch, block_rows, model)
    dq, dkv_all, dgate, dgain_q = attend_back(
        place, q, kv, r, output_weight, att, gate, inv, qraw, cosine, sine, gain_q, group, dgain_q, firsts
    )
    dkv, output, dgain_k = scatter_blocks(
        dkv_all, hidden, swiglu_down, middle, valid.reshape(pieces, rows, 1), kraw, cosine, sine, gain_k
    )
    grads = [
        t_mm(flat(normed), flat(dq)).astype(LOW),
        t_mm(flat(normed), flat(dkv)).astype(LOW),
        t_mm(flat(normed), flat(dgate)).astype(LOW),
        t_mm(flat(r), flat(acted)).astype(LOW),
    ]

    def pieced(array):
        return array.reshape(batch, parts, halves, rows, array.shape[-1])

    input_grad, gains, *grads = last_step(
        pieced(dq), pieced(dkv), pieced(dgate), query_weight, key_weight, value_weight, gating_weight,
        tok, residual, gain_in, dgain_mid, dgain_q, dgain_k, grads,
    )
    input_grad, output, dq_weight, dk_weight, dv_weight, dgate_weight, out_weight, *ff_sums = widen(
        input_grad.reshape(batch, local_rows, model),
        output.reshape(batch, local_rows, model),
        *[x.reshape(model, x.shape[-1]) for x in grads],
        ff_grads,
    )
    share = model // parts
    lines = share // 128
    head_share = head_dim // parts

    def head_gain(line):
        return lax.dynamic_slice(gains[line], (part_index * head_share,), (head_share,))

    return (
        output,
        input_grad,
        dq_weight,
        dk_weight,
        dv_weight,
        dgate_weight,
        out_weight,
        *ff_sums,
        gains[:lines].reshape(share),
        gains[lines : 2 * lines].reshape(share),
        head_gain(2 * lines),
        head_gain(2 * lines + 1),
    )


def solution(mesh):
    return jax.shard_map(
        on_device,
        mesh=mesh,
        in_specs=(
            P(("seq", "head"), None, None),
            P(("seq", "head"), None, None),
            P(),
            P(None, "head"),
            P(None, "head"),
            P(None, "head"),
            P(None, "head"),
            P("head", None),
            P(None, "head"),
            P(None, "head"),
            P("head", None),
            P(),
            P(),
            P(),
            P(),
        ),
        out_specs=(
            P(("seq", "head"), None, None),
            P(("seq", "head"), None, None),
            P(None, "head"),
            P(None, "head"),
            P(None, "head"),
            P(None, "head"),
            P("head", None),
            P(None, "head"),
            P(None, "head"),
            P("head", None),
            P("head"),
            P("head"),
            P("head"),
            P("head"),
        ),
        check_vma=False,
    )
```
